32 devices in a mesh: dom: 8 (over y, x, core), grp: 4 (over z).
Axes of the slice: x: 2, y: 2, z: 4, core: 2. Of those that a mesh axis runs over, the one named last changes fastest.
Arguments:
- feats: bfloat16 [8, 4, 1024, 256], P('dom', 'grp'), may hold values from -6 to 6
- hop_noise: bfloat16 [2, 8, 4, 1024, 256], P(None, 'dom', 'grp'), may hold values from -4 to 4
- send_rows: int32 [8, 4, 8, 32], P('dom', 'grp'), may hold values from 0 to 1023
- tile_block: int32 [8, 4, 64], P('dom', 'grp'), may hold values from 0 to 7
- tile_src: int32 [8, 4, 64, 256], P('dom', 'grp'), may hold values from 0 to 1279
- tile_dst: int32 [8, 4, 64, 256], P('dom', 'grp'), may hold values from 0 to 128
- tile_count: int32 [8, 4], P('dom', 'grp'), may hold values from 1 to 64, as said below
- labels: int32 [8, 4, 32], P('dom', 'grp'), may hold values from 0 to 171
- w_first: bfloat16 [768, 1024], replicated, may hold values from -6 to 6
- w_second: bfloat16 [1024, 1024], replicated, may hold values from -0.75 to 0.75
- w_third: bfloat16 [1024, 172], replicated, may hold values from -2.5 to 2.5
- noise_first: float32 [768, 1024], P('dom'), may hold values from -0.75 to 0.75
- noise_second: float32 [1024, 1024], P('dom'), may hold values from -0.75 to 0.75
- noise_third: float32 [1024, 172], P('dom'), may hold values from -0.75 to 0.75
Outputs:
- hop_feats: bfloat16 [2, 8, 4, 1024, 256], P(None, 'dom', 'grp')
- grad_first: float32 [768, 1024], P('dom')
- grad_second: float32 [1024, 1024], P('dom')
- grad_third: float32 [1024, 172], P('dom')
The draws below stay inside these ranges and needn't reach their ends.
Inputs may be any that keep to these rules, and one draw needn't show every extreme that they name: `tile_count`: tiles at positions of a partition's count and beyond are ignored; the count 64 is reached by some partition in every draw. `tile_dst`: A value of 128 marks an empty slot. `tile_src`: values below 1024 are the partition's own nodes; value 1024 + p * 32 + j is the j-th row received from partition p of the group.
All inputs are finite; a program needn't handle non-finite values.
Results may differ from the reference program's by a relative error of at most 0.0044.
Values may be sent and summed in bfloat16 or wider, within the bound.
No kernel may reach another device: no remote copies, remote signals or barrier semaphores. Data moves between devices by JAX's collectives and lax.ppermute only.
A program may use at most 64 MiB of HBM per device.

```python
import jax
import jax.numpy as jnp
from jax import lax

FEAT = 256
HID = 1024
CLS = 172
HOPS = 2
BLOCK = 128
TILE_E = 256
TILE_MAX = 64
NODE_DEV = 1024
TRAIN_DEV = 32
BND = 32
D_IN = 768
N_DOM = 8
N_GRP = 4


def draw_tile_count(key, part):
    key = jax.random.fold_in(key, 11)
    first, second = jax.random.split(key)
    raw = jax.random.randint(first, (N_DOM, N_GRP), 0, TILE_MAX)
    counts = 1 + raw * raw // TILE_MAX
    chosen = jax.random.randint(second, (), 0, N_DOM * N_GRP)
    flat_ids = jnp.arange(N_DOM * N_GRP, dtype=jnp.int32).reshape(N_DOM, N_GRP)
    return jnp.where(flat_ids == chosen, TILE_MAX, counts).astype(jnp.int32)


def touch_ends(values, own_key, least, top_value):
    longest = values.shape.index(max(values.shape))
    spots = []
    for shift in (0, 1):
        where = [jax.random.randint(jax.random.fold_in(own_key, axis), (), 0, length) for axis, length in enumerate(values.shape)]
        where[longest] = (where[longest] + shift) % values.shape[longest]
        spots.append(tuple(where))
    return values.at[spots[0]].set(least).at[spots[1]].set(top_value)


def shard_levels(stream_key, dims, pieces, low, high):
    def one(position, parts):
        steps = jax.random.uniform(jax.random.fold_in(jax.random.fold_in(stream_key, 6), position), (parts,), jnp.float32, low / len(pieces), high / len(pieces))
        return jnp.repeat(jnp.exp(steps), dims[position] // parts).reshape((-1,) + (1,) * (len(dims) - position - 1))

    level = one(*pieces[0])
    for cut in pieces[1:]:
        level = level * one(*cut)
    return level


def gaussian(rng, dims, spread, limit, shards=(), held_as=jnp.bfloat16):
    level = shard_levels(rng, dims, shards, -0.22, 0.18) if shards else 1.0
    result = jax.random.normal(rng, dims, jnp.float32) * spread * level
    return jnp.minimum(jnp.maximum(result, -limit), limit).astype(held_as)


def setup_inputs(seed: int = 0) -> dict:
    streams_of = jax.random.split(jax.random.key(seed), 15)
    feats = gaussian(streams_of[0], (N_DOM, N_GRP, NODE_DEV, FEAT), 1.0, 6.0, ((0, 8), (1, 4)))
    hop_noise = gaussian(streams_of[1], (HOPS, N_DOM, N_GRP, NODE_DEV, FEAT), 0.25, 4.0, ((1, 8), (2, 4)))
    send_rows = touch_ends(jax.random.randint(streams_of[2], (N_DOM, N_GRP, N_DOM, BND), 0, NODE_DEV), jax.random.fold_in(streams_of[2], 1), 0, NODE_DEV - 1).astype(jnp.int32)
    tile_block = touch_ends(jax.random.randint(streams_of[3], (N_DOM, N_GRP, TILE_MAX), 0, NODE_DEV // BLOCK), jax.random.fold_in(streams_of[3], 1), 0, (NODE_DEV // BLOCK) - 1).astype(jnp.int32)
    tile_src = touch_ends(jax.random.randint(streams_of[4], (N_DOM, N_GRP, TILE_MAX, TILE_E), 0, NODE_DEV + N_DOM * BND), jax.random.fold_in(streams_of[4], 1), 0, (NODE_DEV + N_DOM * BND) - 1).astype(jnp.int32)
    tile_dst = touch_ends(jax.random.randint(streams_of[5], (N_DOM, N_GRP, TILE_MAX, TILE_E), 0, BLOCK + 1), jax.random.fold_in(streams_of[5], 1), 0, BLOCK).astype(jnp.int32)
    tile_count = draw_tile_count(jax.random.fold_in(streams_of[14], 71), 0)
    labels = touch_ends(jax.random.randint(streams_of[7], (N_DOM, N_GRP, TRAIN_DEV), 0, CLS), jax.random.fold_in(streams_of[7], 1), 0, CLS - 1).astype(jnp.int32)
    w_first = gaussian(streams_of[8], (D_IN, HID), 0.6, 6.0)
    w_second = gaussian(streams_of[9], (HID, HID), 0.05, 0.75)
    w_third = gaussian(streams_of[10], (HID, CLS), 0.17, 2.5)
    noise_first = gaussian(streams_of[11], (D_IN, HID), 0.05, 0.75, ((0, 8),), jnp.float32)
    noise_second = gaussian(streams_of[12], (HID, HID), 0.05, 0.75, ((0, 8),), jnp.float32)
    noise_third = gaussian(streams_of[13], (HID, CLS), 0.05, 0.75, ((0, 8),), jnp.float32)
    return {"feats": feats, "hop_noise": hop_noise, "send_rows": send_rows, "tile_block": tile_block, "tile_src": tile_src, "tile_dst": tile_dst, "tile_count": tile_count, "labels": labels, "w_first": w_first, "w_second": w_second, "w_third": w_third, "noise_first": noise_first, "noise_second": noise_second, "noise_third": noise_third}


clip_bound = 4.0
noise_mult = 1.0

def normalize(values):
    return (values * lax.rsqrt(lax.optimization_barrier(jnp.sum(values * values, -1, keepdims=True)) + 1e-06)).astype(jnp.bfloat16)

def silu_slope(values):
    sigma = jax.nn.sigmoid(values)
    return sigma * (1.0 + values * (1.0 - sigma))

def aggregate_one(table, blocks, sources, targets, count):
    tile_ids = jnp.arange(TILE_MAX, dtype=jnp.int32)
    live = (tile_ids < count)[:, None] & (targets < BLOCK)
    places = blocks[:, None] * BLOCK + targets
    places = jnp.where(live, places, NODE_DEV).astype(jnp.int32)
    gathered = table[sources.reshape(-1)].astype(jnp.float32)
    summed = jax.ops.segment_sum(gathered, places.reshape(-1), num_segments=NODE_DEV + 1)
    return summed[:NODE_DEV]

def group_work(group, feats, hop_noise, send_rows, tile_block, tile_src, tile_dst, tile_count, labels, w_first, w_second, w_third):
    current = normalize(feats[:, group].astype(jnp.float32))
    senders = send_rows[:, group]
    states = [current]
    for hop in range(HOPS):
        picked = jax.vmap(lambda own, wanted: own[wanted])(current, senders)
        ghosts = jnp.transpose(picked, (1, 0, 2, 3)).reshape(N_DOM, N_DOM * BND, FEAT)
        table = jnp.concatenate([current, ghosts], 1)
        summed = jax.vmap(aggregate_one)(table, tile_block[:, group], tile_src[:, group], tile_dst[:, group], tile_count[:, group])
        current = normalize(summed + hop_noise[hop][:, group].astype(jnp.float32))
        states.append(current)
    inputs = jnp.concatenate([state[:, :TRAIN_DEV] for state in states], -1).reshape(N_DOM * TRAIN_DEV, D_IN)
    z_one = jnp.dot(inputs, w_first, preferred_element_type=jnp.float32)
    h_one = jax.nn.silu(z_one).astype(jnp.bfloat16)
    z_two = jnp.dot(h_one, w_second, preferred_element_type=jnp.float32)
    h_two = jax.nn.silu(z_two).astype(jnp.bfloat16)
    logits = jnp.dot(h_two, w_third, preferred_element_type=jnp.float32)
    expo = jnp.exp(logits)
    probs = expo / lax.optimization_barrier(jnp.sum(expo, -1, keepdims=True))
    onehot = (labels[:, group].reshape(-1)[:, None] == jnp.arange(CLS, dtype=jnp.int32)[None, :]).astype(jnp.float32)
    d_three = (probs - onehot).astype(jnp.bfloat16)
    d_two = (jnp.dot(d_three, w_third.T, preferred_element_type=jnp.float32) * silu_slope(z_two)).astype(jnp.bfloat16)
    d_one = (jnp.dot(d_two, w_second.T, preferred_element_type=jnp.float32) * silu_slope(z_one)).astype(jnp.bfloat16)

    def squares(values):
        wide = values.astype(jnp.float32)
        return lax.optimization_barrier(jnp.sum(wide * wide, -1))
    norm = jnp.sqrt(squares(inputs) * squares(d_one) + squares(h_one) * squares(d_two) + squares(h_two) * squares(d_three))
    factor = (clip_bound / jnp.maximum(norm, clip_bound))[:, None]
    e_one = (d_one.astype(jnp.float32) * factor).astype(jnp.bfloat16)
    e_two = (d_two.astype(jnp.float32) * factor).astype(jnp.bfloat16)
    e_three = (d_three.astype(jnp.float32) * factor).astype(jnp.bfloat16)
    g_one = jnp.dot(inputs.T, e_one, preferred_element_type=jnp.float32)
    g_two = jnp.dot(h_one.T, e_two, preferred_element_type=jnp.float32)
    g_three = jnp.dot(h_two.T, e_three, preferred_element_type=jnp.float32)
    return (jnp.stack(states[1:]), g_one, g_two, g_three)

def reference(feats, hop_noise, send_rows, tile_block, tile_src, tile_dst, tile_count, labels, w_first, w_second, w_third, noise_first, noise_second, noise_third):

    def one_group(group):
        return group_work(group, feats, hop_noise, send_rows, tile_block, tile_src, tile_dst, tile_count, labels, w_first, w_second, w_third)
    stacked, g_one, g_two, g_three = lax.map(one_group, jnp.arange(N_GRP, dtype=jnp.int32))
    hop_feats = jnp.transpose(stacked, (1, 2, 0, 3, 4))
    scale = noise_mult * clip_bound
    grad_first = lax.optimization_barrier(jnp.sum(g_one, 0)) + scale * noise_first
    grad_second = lax.optimization_barrier(jnp.sum(g_two, 0)) + scale * noise_second
    grad_third = lax.optimization_barrier(jnp.sum(g_three, 0)) + scale * noise_third
    return (hop_feats, grad_first, grad_second, grad_third)
```

```python
import functools

import jax
import jax.numpy as jnp
from jax import lax
from jax.experimental import pallas as pl
from jax.experimental.pallas import tpu as pltpu
from jax.sharding import PartitionSpec as P

BLOCK = 128
LOW = 256
GROUP = 4
clip_bound = 4.0
noise_mult = 1.0

f32 = jnp.float32
bf16 = jnp.bfloat16
VMEM = pltpu.VMEM
SMEM = pltpu.SMEM


def params():
    return pltpu.CompilerParams(vmem_limit_bytes=56 * 1024 * 1024)


def normalize(values):
    return (values * lax.rsqrt(jnp.sum(values * values, -1, keepdims=True) + 1e-06)).astype(bf16)


def dot(left, right):
    return jnp.dot(left, right, preferred_element_type=f32)


def dot_nt(left, right):
    return lax.dot_general(left, right, (((1,), (1,)), ((), ())), preferred_element_type=f32)


def dot_tn(left, right):
    return lax.dot_general(left, right, (((0,), (0,)), ((), ())), preferred_element_type=f32)


def send(start, rows_ref, out_ref, turn_ref, pick_ref):
    parts, each = rows_ref.shape
    nodes = start.shape[0]
    turn_ref[:parts, :each] = rows_ref[...]
    columns = turn_ref[...].T
    spots = lax.broadcasted_iota(jnp.int32, (each, nodes), 1)
    for part in range(parts):
        wanted = columns[:each, part : part + 1]
        pick_ref[part * each : (part + 1) * each, :] = jnp.where(wanted == spots, 1.0, 0.0).astype(
            bf16
        )
    out = dot(pick_ref[...], start).astype(bf16)
    out_ref[...] = out.reshape(out_ref.shape)


def first_kernel(feats_ref, rows_ref, start_ref, out_ref, turn_ref, pick_ref):
    start = normalize(feats_ref[...].astype(f32))
    start_ref[...] = start
    send(start, rows_ref, out_ref, turn_ref, pick_ref)


def build_kernel(
    blocks_ref,
    count_ref,
    src_ref,
    dst_ref,
    start_ref,
    noise_ref,
    own_ref,
    ghost_ref,
    part_ref,
    flag_ref,
    own_rest_ref,
    ghost_rest_ref,
    sums_ref,
    rest_ref,
):
    nodes, cols = sums_ref.shape
    pieces = cols // LOW
    slots = src_ref.shape[1]
    count = count_ref[0]
    sums_ref[...] = jnp.zeros_like(sums_ref)
    low_ids = lax.broadcasted_iota(jnp.int32, (LOW, slots), 0)
    spot_ids = lax.broadcasted_iota(jnp.int32, (pieces * BLOCK, slots), 0)

    def turn(step, carry):
        for inner in range(GROUP):
            tile = step * GROUP + inner
            src = src_ref[pl.ds(tile, 1), :]
            dst = dst_ref[pl.ds(tile, 1), :]
            live = (dst < BLOCK) & (tile < count)
            spot = jnp.where(live, (src // LOW) * BLOCK + dst, -1)
            low = src % LOW
            low_hot = jnp.where(low_ids == low, 1.0, 0.0).astype(bf16)
            spot_hot = jnp.where(spot_ids == spot, 1.0, 0.0).astype(bf16)
            out = dot_nt(spot_hot, low_hot)
            base = pl.multiple_of(blocks_ref[tile] * BLOCK, BLOCK)
            for piece in range(pieces):
                sums_ref[pl.ds(base, BLOCK), piece * LOW : (piece + 1) * LOW] += out[
                    piece * BLOCK : (piece + 1) * BLOCK
                ]
        return carry

    lax.fori_loop(0, (count + GROUP - 1) // GROUP, turn, 0)
    own_ref[...] = sums_ref[:, :nodes].astype(bf16)
    ghost_ref[...] = sums_ref[:, nodes:].astype(bf16)
    part_ref[...] = dot(own_ref[...], start_ref[...]) + noise_ref[...].astype(f32)
    big = jnp.max(sums_ref[...]) > 256.0
    flag_ref[0] = big.astype(jnp.int32)

    @pl.when(big)
    def _():
        own_rest = (sums_ref[:, :nodes] - own_ref[...].astype(f32)).astype(bf16)
        part_ref[...] += dot(own_rest, start_ref[...])
        rest_ref[...] = own_rest
        pltpu.sync_copy(rest_ref, own_rest_ref)
        rest_ref[:, : cols - nodes] = (sums_ref[:, nodes:] - ghost_ref[...].astype(f32)).astype(bf16)
        pltpu.sync_copy(rest_ref.at[:, : cols - nodes], ghost_rest_ref)


def aggregate(flag_ref, part_ref, count_ref, rest_hbm, table, sums_ref, rest_ref):
    rows = sums_ref.shape[0]
    sums_ref[...] = part_ref[...] + dot(count_ref[...], table)

    @pl.when(flag_ref[0] > 0)
    def _():
        pltpu.sync_copy(rest_hbm.at[:rows], rest_ref)
        sums_ref[...] += dot(rest_ref[...], table)


def hop_kernel(
    flag_ref,
    part_ref,
    ghost_ref,
    rest_hbm,
    table_ref,
    rows_ref,
    start_ref,
    out_ref,
    sums_ref,
    rest_ref,
    turn_ref,
    pick_ref,
):
    width = start_ref.shape[1]
    table = table_ref[...].reshape(-1, width)
    aggregate(flag_ref, part_ref, ghost_ref, rest_hbm, table, sums_ref, rest_ref)
    start = normalize(sums_ref[...])
    start_ref[...] = start
    send(start, rows_ref, out_ref, turn_ref, pick_ref)


def own_kernel(flag_ref, own_ref, rest_hbm, start_ref, noise_ref, part_ref, rest_ref):
    start = start_ref[...]
    aggregate(flag_ref, noise_ref, own_ref, rest_hbm, start, part_ref, rest_ref)


def train_kernel(flag_ref, part_ref, ghost_ref, rest_hbm, table_ref, out_ref, sums_ref, rest_ref):
    table = table_ref[...].reshape(-1, out_ref.shape[1])
    aggregate(flag_ref, part_ref, ghost_ref, rest_hbm, table, sums_ref, rest_ref)
    out_ref[...] = normalize(sums_ref[...])


def last_kernel(
    flag_ref, part_ref, ghost_ref, rest_hbm, table_ref, start_ref, out_ref, sums_ref, rest_ref
):
    table = table_ref[...].reshape(-1, out_ref.shape[-1])
    aggregate(flag_ref, part_ref, ghost_ref, rest_hbm, table, sums_ref, rest_ref)
    out_ref[0, 0, 0] = start_ref[...]
    out_ref[1, 0, 0] = normalize(sums_ref[...])


def shares(ref, first, share):
    if share % 128 == 0:
        return ref[:, pl.ds(pl.multiple_of(first, 128), share)].astype(f32)
    length = ref.shape[1]
    rows = lax.broadcasted_iota(jnp.int32, (length, share), 0)
    cols = lax.broadcasted_iota(jnp.int32, (length, share), 1)
    return dot(ref[...], jnp.where(rows == cols + first, 1.0, 0.0).astype(bf16))


def lanes_sum(values):
    total = None
    for piece in range(values.shape[1] // 128):
        part = values[:, piece * 128 : (piece + 1) * 128].astype(f32)
        total = part * part if total is None else total + part * part
    return total


def classify_kernel(
    place_ref,
    label_ref,
    zero_ref,
    one_ref,
    two_ref,
    w_first_ref,
    w_second_ref,
    w_third_ref,
    n_first_ref,
    n_second_ref,
    n_third_ref,
    g_first_ref,
    g_second_ref,
    g_third_ref,
    in_ref,
    w_third_pad_ref,
    turn_ref,
    column_ref,
    h_one_ref,
    h_two_ref,
    slope_one_ref,
    slope_two_ref,
    d_one_ref,
    d_two_ref,
):
    classes = w_third_ref.shape[0]
    hid = w_second_ref.shape[0]
    width = zero_ref.shape[1]
    wide = w_third_pad_ref.shape[0]
    groups, train = label_ref.shape
    scale = noise_mult * clip_bound
    place = place_ref[0]

    @pl.when(pl.program_id(0) == 0)
    def _():
        g_first_ref[...] = scale * n_first_ref[...]
        g_second_ref[...] = scale * n_second_ref[...]
        g_third_ref[...] = scale * n_third_ref[...]
        w_third_pad_ref[...] = jnp.zeros_like(w_third_pad_ref)
        w_third_pad_ref[:classes, :] = w_third_ref[...]

    turn_ref[:groups, :train] = label_ref[...]
    turned = turn_ref[...].T
    for group in range(groups):
        column_ref[group * train : (group + 1) * train, :] = jnp.broadcast_to(
            turned[:train, group : group + 1], (train, 128)
        )
    for hop, ref in enumerate((zero_ref, one_ref, two_ref)):
        in_ref[:, hop * width : (hop + 1) * width] = ref[...]

    def activate(values, h_ref, slope_ref, cols):
        sigma = 0.5 + 0.5 * jnp.tanh(0.5 * values)
        out = values * sigma
        slope_ref[:, cols] = sigma + out * (1.0 - sigma)
        rounded = out.astype(bf16)
        h_ref[:, cols] = rounded
        return lanes_sum(rounded)

    step = 256
    cuts = [slice(at, at + step) for at in range(0, hid, step)]
    sq_in = lanes_sum(in_ref[...])
    sq_one = sum(
        activate(dot(in_ref[...], w_first_ref[:, cut]), h_one_ref, slope_one_ref, cut)
        for cut in cuts
    )
    sq_two = sum(
        activate(dot(h_one_ref[...], w_second_ref[:, cut]), h_two_ref, slope_two_ref, cut)
        for cut in cuts
    )
    logits = dot_nt(h_two_ref[...], w_third_pad_ref[...])
    ids = lax.broadcasted_iota(jnp.int32, (logits.shape[0], wide), 1)
    expo = jnp.where(ids < classes, jnp.exp(logits), 0.0)
    probs = expo / jnp.sum(expo, -1, keepdims=True)
    label = column_ref[:, :1]
    d_three = (probs - jnp.where(ids == label, 1.0, 0.0)).astype(bf16)
    sq_dthree = lanes_sum(d_three)

    def back(values, slope_ref, d_ref, cut):
        rounded = (values * slope_ref[:, cut]).astype(bf16)
        d_ref[:, cut] = rounded
        return lanes_sum(rounded)

    sq_dtwo = sum(
        back(dot(d_three, w_third_pad_ref[:, cut]), slope_two_ref, d_two_ref, cut)
        for cut in cuts
    )
    sq_done = sum(
        back(dot_nt(d_two_ref[...], w_second_ref[cut, :]), slope_one_ref, d_one_ref, cut)
        for cut in cuts
    )

    def total(values):
        return jnp.sum(values, -1, keepdims=True)

    norm = jnp.sqrt(
        total(sq_in) * total(sq_done)
        + total(sq_one) * total(sq_dtwo)
        + total(sq_two) * total(sq_dthree)
    )
    factor = clip_bound / jnp.maximum(norm, clip_bound)

    def left(ref, share):
        return (shares(ref, place * share, share) * factor).astype(bf16)

    share = g_second_ref.shape[0]
    g_first_ref[...] += dot_tn(left(in_ref, g_first_ref.shape[0]), d_one_ref[...])
    g_second_ref[...] += dot_tn(left(h_one_ref, share), d_two_ref[...])
    g_third_ref[...] += dot_tn(d_three, left(h_two_ref, share))[:classes, :]


def call(kernel, outs, ins, scratch, **more):
    return pl.pallas_call(
        kernel,
        out_shape=[jax.ShapeDtypeStruct(shape, dtype) for shape, dtype, _ in outs],
        in_specs=[pl.BlockSpec(memory_space=space) for _, space in ins],
        out_specs=[pl.BlockSpec(memory_space=space) for _, _, space in outs],
        scratch_shapes=scratch,
        compiler_params=params(),
        **more,
    )(*[value for value, _ in ins])


def local(
    feats,
    hop_noise,
    send_rows,
    tile_block,
    tile_src,
    tile_dst,
    tile_count,
    labels,
    w_first,
    w_second,
    w_third,
    noise_first,
    noise_second,
    noise_third,
):
    nodes, width = feats.shape[2:]
    parts, each = send_rows.shape[2:]
    ghosts = parts * each
    tiles = tile_src.shape[2]
    slots = tile_src.shape[3]
    train = labels.shape[2]
    classes = w_third.shape[1]
    hid = w_second.shape[0]
    d_in = w_first.shape[0]
    cols = nodes + ghosts
    rows = send_rows.reshape(parts, each)
    turn = VMEM((128, 128), jnp.int32)
    pick = VMEM((ghosts, nodes), bf16)

    def gather(value):
        return lax.all_gather(value, ("dom", "grp"), axis=0, tiled=True)

    every_label = gather(labels.reshape(1, train))
    start0, out0 = call(
        first_kernel,
        [((nodes, width), bf16, VMEM), ((parts, each, width), bf16, VMEM)],
        [(feats.reshape(nodes, width), VMEM), (rows, VMEM)],
        [turn, pick],
    )
    every0 = gather(start0[:train])
    table0 = lax.all_to_all(out0, "dom", split_axis=0, concat_axis=0, tiled=True)
    own, ghost, part1, flag, own_rest, ghost_rest = call(
        build_kernel,
        [
            ((nodes, nodes), bf16, VMEM),
            ((nodes, ghosts), bf16, VMEM),
            ((nodes, width), f32, VMEM),
            ((1,), jnp.int32, SMEM),
            ((nodes, nodes), bf16, pl.ANY),
            ((nodes, ghosts), bf16, pl.ANY),
        ],
        [
            (tile_block.reshape(tiles), SMEM),
            (tile_count.reshape(1), SMEM),
            (tile_src.reshape(tiles, slots), VMEM),
            (tile_dst.reshape(tiles, slots), VMEM),
            (start0, VMEM),
            (hop_noise[0, 0, 0], VMEM),
        ],
        [VMEM((nodes, cols), f32), VMEM((nodes, max(nodes, ghosts)), bf16)],
    )
    start1, out1 = call(
        hop_kernel,
        [
            ((nodes, width), bf16, VMEM),
            ((parts, each, width), bf16, VMEM),
        ],
        [
            (flag, SMEM),
            (part1, VMEM),
            (ghost, VMEM),
            (ghost_rest, pl.ANY),
            (table0, VMEM),
            (rows, VMEM),
        ],
        [VMEM((nodes, width), f32), VMEM((nodes, ghosts), bf16), turn, pick],
    )
    table1 = lax.all_to_all(out1, "dom", split_axis=0, concat_axis=0, tiled=True)
    every1 = gather(start1[:train])
    (part2,) = call(
        own_kernel,
        [((nodes, width), f32, VMEM)],
        [
            (flag, SMEM),
            (own, VMEM),
            (own_rest, pl.ANY),
            (start1, VMEM),
            (hop_noise[1, 0, 0], VMEM),
        ],
        [VMEM((nodes, nodes), bf16)],
    )
    (last,) = pl.pallas_call(
        train_kernel,
        grid=(1,),
        out_shape=[jax.ShapeDtypeStruct((train, width), bf16)],
        in_specs=[
            pl.BlockSpec(memory_space=SMEM),
            pl.BlockSpec((train, width), lambda i: (0, 0)),
            pl.BlockSpec((train, ghosts), lambda i: (0, 0)),
            pl.BlockSpec(memory_space=pl.ANY),
            pl.BlockSpec((parts, each, width), lambda i: (0, 0, 0)),
        ],
        out_specs=[pl.BlockSpec((train, width), lambda i: (0, 0))],
        scratch_shapes=[VMEM((train, width), f32), VMEM((train, ghosts), bf16)],
        compiler_params=params(),
    )(flag, part2, ghost, ghost_rest, table1)
    every2 = gather(last)
    (hop_feats,) = call(
        last_kernel,
        [((2, 1, 1, nodes, width), bf16, VMEM)],
        [
            (flag, SMEM),
            (part2, VMEM),
            (ghost, VMEM),
            (ghost_rest, pl.ANY),
            (table1, VMEM),
            (start1, VMEM),
        ],
        [VMEM((nodes, width), f32), VMEM((nodes, ghosts), bf16)],
    )
    total = every2.shape[0]
    chunk = min(total, 1024)
    wide = (classes + 255) // 256 * 256

    def fixed(value):
        return pl.BlockSpec(value.shape, lambda i: (0, 0))

    grads = pl.pallas_call(
        classify_kernel,
        grid=(total // chunk,),
        out_shape=[
            jax.ShapeDtypeStruct(value.shape, f32)
            for value in (noise_first, noise_second, noise_third.T)
        ],
        in_specs=[
            pl.BlockSpec(memory_space=SMEM),
            pl.BlockSpec((chunk // train, train), lambda i: (i, 0)),
        ]
        + [pl.BlockSpec((chunk, width), lambda i: (i, 0))] * 3
        + [
            fixed(value)
            for value in (w_first, w_second, w_third.T, noise_first, noise_second, noise_third.T)
        ],
        out_specs=[fixed(value) for value in (noise_first, noise_second, noise_third.T)],
        scratch_shapes=[
            VMEM((chunk, d_in), bf16),
            VMEM((wide, hid), bf16),
            VMEM((128, 128), jnp.int32),
            VMEM((chunk, 128), jnp.int32),
            VMEM((chunk, hid), bf16),
            VMEM((chunk, hid), bf16),
            VMEM((chunk, hid), f32),
            VMEM((chunk, hid), f32),
            VMEM((chunk, hid), bf16),
            VMEM((chunk, hid), bf16),
        ],
        compiler_params=params(),
    )(
        lax.axis_index("dom").reshape(1).astype(jnp.int32),
        every_label,
        every0,
        every1,
        every2,
        w_first,
        w_second,
        w_third.T,
        noise_first,
        noise_second,
        noise_third.T,
    )
    return (hop_feats, grads[0], grads[1], grads[2].T)


def solution(mesh):
    in_specs = (
        P("dom", "grp", None, None),
        P(None, "dom", "grp", None, None),
        P("dom", "grp", None, None),
        P("dom", "grp", None),
        P("dom", "grp", None, None),
        P("dom", "grp", None, None),
        P("dom", "grp"),
        P("dom", "grp", None),
        P(),
        P(),
        P(),
        P("dom", None),
        P("dom", None),
        P("dom", None),
    )
    out_specs = (P(None, "dom", "grp", None, None), P("dom", None), P("dom", None), P("dom", None))
    return jax.shard_map(local, mesh=mesh, in_specs=in_specs, out_specs=out_specs, check_vma=False)
```

```python
import functools

import jax
import jax.numpy as jnp
from jax import lax
from jax.experimental import pallas as pl
from jax.experimental.pallas import tpu as pltpu
from jax.sharding import PartitionSpec as P

BLOCK = 128
LOW = 256
GROUP = 4
clip_bound = 4.0
noise_mult = 1.0

f32 = jnp.float32
bf16 = jnp.bfloat16
VMEM = pltpu.VMEM
SMEM = pltpu.SMEM


FEW = 64


def params(mib):
    return pltpu.CompilerParams(vmem_limit_bytes=mib * 1024 * 1024)


def normalize(values):
    return (values * lax.rsqrt(jnp.sum(values * values, -1, keepdims=True) + 1e-06)).astype(bf16)


def dot(left, right):
    return jnp.dot(left, right, preferred_element_type=f32)


def dot_nt(left, right):
    return lax.dot_general(left, right, (((1,), (1,)), ((), ())), preferred_element_type=f32)


def dot_tn(left, right):
    return lax.dot_general(left, right, (((0,), (0,)), ((), ())), preferred_element_type=f32)


def send(start, rows_ref, out_ref, turn_ref, pick_ref):
    parts, each = rows_ref.shape
    nodes = start.shape[0]
    turn_ref[:parts, :each] = rows_ref[...]
    columns = turn_ref[...].T
    spots = lax.broadcasted_iota(jnp.int32, (each, nodes), 1)
    for part in range(parts):
        wanted = columns[:each, part : part + 1]
        pick_ref[part * each : (part + 1) * each, :] = jnp.where(wanted == spots, 1.0, 0.0).astype(
            bf16
        )
    out = dot(pick_ref[...], start).astype(bf16)
    out_ref[...] = out.reshape(out_ref.shape)


def spread(rows, out_ref):
    out_ref[...] = jnp.broadcast_to(rows[None], out_ref.shape)


def first_kernel(
    feats_ref, rows_ref, labels_ref, start_ref, out_ref, side_ref, turn_ref, pick_ref
):
    start = normalize(feats_ref[...].astype(f32))
    start_ref[...] = start
    send(start, rows_ref, out_ref, turn_ref, pick_ref)
    train = labels_ref.shape[1]
    turn_ref[:1, :train] = labels_ref[...]
    side_ref[:, :train, :] = jnp.broadcast_to(
        start[None, :train], (side_ref.shape[0], train, start.shape[1])
    )
    label = turn_ref[:16, :].astype(f32).astype(bf16)
    side_ref[:, train:, :128] = jnp.broadcast_to(label[None], (side_ref.shape[0], 16, 128))


def build_kernel(
    blocks_ref,
    count_ref,
    src_ref,
    dst_ref,
    start_ref,
    noise_ref,
    own_ref,
    ghost_ref,
    part_ref,
    flag_ref,
    own_rest_ref,
    ghost_rest_ref,
    sums_ref,
    rest_ref,
):
    nodes, cols = sums_ref.shape
    pieces = cols // LOW
    slots = src_ref.shape[1]
    count = count_ref[0]
    sums_ref[...] = jnp.zeros_like(sums_ref)
    low_ids = lax.broadcasted_iota(jnp.int32, (LOW, slots), 0)
    spot_ids = lax.broadcasted_iota(jnp.int32, (pieces * BLOCK, slots), 0)

    def turn(step, carry):
        for inner in range(GROUP):
            tile = step * GROUP + inner
            src = src_ref[pl.ds(tile, 1), :]
            dst = dst_ref[pl.ds(tile, 1), :]
            live = (dst < BLOCK) & (tile < count)
            spot = jnp.where(live, (src // LOW) * BLOCK + dst, -1)
            low = src % LOW
            low_hot = jnp.where(low_ids == low, 1.0, 0.0).astype(bf16)
            spot_hot = jnp.where(spot_ids == spot, 1.0, 0.0).astype(bf16)
            out = dot_nt(spot_hot, low_hot)
            base = pl.multiple_of(blocks_ref[tile] * BLOCK, BLOCK)
            for piece in range(pieces):
                sums_ref[pl.ds(base, BLOCK), piece * LOW : (piece + 1) * LOW] += out[
                    piece * BLOCK : (piece + 1) * BLOCK
                ]
        return carry

    lax.fori_loop(0, (count + GROUP - 1) // GROUP, turn, 0)
    own_ref[...] = sums_ref[:, :nodes].astype(bf16)
    ghost_ref[...] = sums_ref[:, nodes:].astype(bf16)
    part_ref[...] = dot(own_ref[...], start_ref[...]) + noise_ref[0, 0, 0].astype(f32)
    big = jnp.max(sums_ref[...]) > 256.0
    flag_ref[0] = big.astype(jnp.int32)

    @pl.when(big)
    def _():
        own_rest = (sums_ref[:, :nodes] - own_ref[...].astype(f32)).astype(bf16)
        part_ref[...] += dot(own_rest, start_ref[...])
        rest_ref[...] = own_rest
        pltpu.sync_copy(rest_ref, own_rest_ref)
        rest_ref[:, : cols - nodes] = (sums_ref[:, nodes:] - ghost_ref[...].astype(f32)).astype(bf16)
        pltpu.sync_copy(rest_ref.at[:, : cols - nodes], ghost_rest_ref)


def aggregate(flag_ref, part_ref, count_ref, rest_hbm, table, sums_ref, rest_ref):
    rows = sums_ref.shape[0]
    sums_ref[...] = part_ref.astype(f32) + dot(count_ref, table)

    @pl.when(flag_ref[0] > 0)
    def _():
        pltpu.sync_copy(rest_hbm.at[:rows], rest_ref)
        sums_ref[...] += dot(rest_ref[...], table)


def hop_kernel(
    flag_ref,
    part_ref,
    ghost_ref,
    rest_hbm,
    table_ref,
    rows_ref,
    start_ref,
    out_ref,
    side_ref,
    sums_ref,
    rest_ref,
    turn_ref,
    pick_ref,
):
    width = start_ref.shape[1]
    table = table_ref[...].reshape(-1, width)
    aggregate(flag_ref, part_ref[...], ghost_ref[...], rest_hbm, table, sums_ref, rest_ref)
    start = normalize(sums_ref[...])
    start_ref[...] = start
    send(start, rows_ref, out_ref, turn_ref, pick_ref)
    spread(start[: side_ref.shape[1]], side_ref)


def own_kernel(flag_ref, own_ref, rest_hbm, start_ref, noise_ref, part_ref, rest_ref):
    start = start_ref[...]
    aggregate(flag_ref, noise_ref[1, 0, 0], own_ref[...], rest_hbm, start, part_ref, rest_ref)


def train_kernel(flag_ref, part_ref, ghost_ref, rest_hbm, table_ref, out_ref, sums_ref, rest_ref):
    train, width = sums_ref.shape
    table = table_ref[...].reshape(-1, width)
    aggregate(
        flag_ref, part_ref[:train], ghost_ref[:train], rest_hbm, table, sums_ref, rest_ref
    )
    spread(normalize(sums_ref[...]), out_ref)


def last_kernel(
    flag_ref, part_ref, ghost_ref, rest_hbm, table_ref, start_ref, out_ref, sums_ref, rest_ref
):
    table = table_ref[...].reshape(-1, out_ref.shape[-1])
    aggregate(flag_ref, part_ref[...], ghost_ref[...], rest_hbm, table, sums_ref, rest_ref)
    out_ref[0, 0, 0] = start_ref[...]
    out_ref[1, 0, 0] = normalize(sums_ref[...])


def shares(ref, first, share):
    if share % 128 == 0:
        return ref[:, pl.ds(pl.multiple_of(first, 128), share)].astype(f32)
    length = ref.shape[1]
    rows = lax.broadcasted_iota(jnp.int32, (length, share), 0)
    cols = lax.broadcasted_iota(jnp.int32, (length, share), 1)
    return dot(ref[...], jnp.where(rows == cols + first, 1.0, 0.0).astype(bf16))


def lanes_sum(values):
    total = None
    for piece in range(values.shape[1] // 128):
        part = values[:, piece * 128 : (piece + 1) * 128].astype(f32)
        total = part * part if total is None else total + part * part
    return total


def classify_kernel(
    many,
    place_ref,
    label_ref,
    zero_ref,
    one_ref,
    two_ref,
    w_first_ref,
    w_second_ref,
    w_third_ref,
    n_first_ref,
    n_second_ref,
    n_third_ref,
    g_first_ref,
    g_second_ref,
    g_third_ref,
    in_ref,
    w_third_pad_ref,
    turn_ref,
    column_ref,
    h_one_ref,
    h_two_ref,
    slope_one_ref,
    slope_two_ref,
    d_one_ref,
    d_two_ref,
):
    classes = w_third_ref.shape[0]
    hid = w_second_ref.shape[0]
    width = zero_ref.shape[2]
    wide = w_third_pad_ref.shape[0]
    groups, train = label_ref.shape
    scale = noise_mult * clip_bound
    place = place_ref[0]

    def begin():
        g_first_ref[...] = scale * n_first_ref[...]
        g_second_ref[...] = scale * n_second_ref[...]
        g_third_ref[...] = scale * n_third_ref[...]
        w_third_pad_ref[...] = jnp.zeros_like(w_third_pad_ref)
        w_third_pad_ref[:classes, :] = w_third_ref[...]

    if many:
        pl.when(pl.program_id(0) == 0)(begin)
    else:
        begin()
    turn_ref[:groups, :train] = label_ref[...]
    turned = turn_ref[...].T
    for group in range(groups):
        column_ref[group * train : (group + 1) * train, :] = jnp.broadcast_to(
            turned[:train, group : group + 1], (train, 128)
        )
    for hop, ref in enumerate((zero_ref, one_ref, two_ref)):
        in_ref[:, hop * width : (hop + 1) * width] = ref[:, :train, :].reshape(-1, width)

    def activate(values, h_ref, slope_ref, cols):
        sigma = 0.5 + 0.5 * jnp.tanh(0.5 * values)
        out = values * sigma
        slope_ref[:, cols] = sigma + out * (1.0 - sigma)
        rounded = out.astype(bf16)
        h_ref[:, cols] = rounded
        return lanes_sum(rounded)

    step = 256
    cuts = [slice(at, at + step) for at in range(0, hid, step)]
    sq_in = lanes_sum(in_ref[...])
    sq_one = sum(
        activate(dot(in_ref[...], w_first_ref[:, cut]), h_one_ref, slope_one_ref, cut)
        for cut in cuts
    )
    sq_two = sum(
        activate(dot(h_one_ref[...], w_second_ref[:, cut]), h_two_ref, slope_two_ref, cut)
        for cut in cuts
    )
    logits = dot_nt(h_two_ref[...], w_third_pad_ref[...])
    ids = lax.broadcasted_iota(jnp.int32, (logits.shape[0], wide), 1)
    expo = jnp.where(ids < classes, jnp.exp(logits), 0.0)
    probs = expo / jnp.sum(expo, -1, keepdims=True)
    label = column_ref[:, :1]
    d_three = (probs - jnp.where(ids == label, 1.0, 0.0)).astype(bf16)
    sq_dthree = lanes_sum(d_three)

    def back(values, slope_ref, d_ref, cut):
        rounded = (values * slope_ref[:, cut]).astype(bf16)
        d_ref[:, cut] = rounded
        return lanes_sum(rounded)

    sq_dtwo = sum(
        back(dot(d_three, w_third_pad_ref[:, cut]), slope_two_ref, d_two_ref, cut)
        for cut in cuts
    )
    sq_done = sum(
        back(dot_nt(d_two_ref[...], w_second_ref[cut, :]), slope_one_ref, d_one_ref, cut)
        for cut in cuts
    )

    def total(values):
        return jnp.sum(values, -1, keepdims=True)

    norm = jnp.sqrt(
        total(sq_in) * total(sq_done)
        + total(sq_one) * total(sq_dtwo)
        + total(sq_two) * total(sq_dthree)
    )
    factor = clip_bound / jnp.maximum(norm, clip_bound)

    def left(ref, share):
        return (shares(ref, place * share, share) * factor).astype(bf16)

    share = g_second_ref.shape[0]
    g_first_ref[...] += dot_tn(left(in_ref, g_first_ref.shape[0]), d_one_ref[...])
    g_second_ref[...] += dot_tn(left(h_one_ref, share), d_two_ref[...])
    g_third_ref[...] += dot_tn(d_three, left(h_two_ref, share))[:classes, :]


def call(kernel, mib, outs, ins, scratch):
    def shape_of(shape, dtype, space):
        return VMEM(shape, dtype) if space is None else jax.ShapeDtypeStruct(shape, dtype)

    def block(space):
        return pl.BlockSpec(memory_space=VMEM if space is None else space)

    return pl.pallas_call(
        kernel,
        out_shape=[shape_of(*out) for out in outs],
        in_specs=[block(space) for _, space in ins],
        out_specs=[block(space) for _, _, space in outs],
        scratch_shapes=scratch,
        compiler_params=params(mib),
    )(
        *[
            pltpu.with_memory_space_constraint(value, VMEM) if space is None else value
            for value, space in ins
        ]
    )


def local(
    feats,
    hop_noise,
    send_rows,
    tile_block,
    tile_src,
    tile_dst,
    tile_count,
    labels,
    w_first,
    w_second,
    w_third,
    noise_first,
    noise_second,
    noise_third,
):
    nodes, width = feats.shape[2:]
    parts, each = send_rows.shape[2:]
    ghosts = parts * each
    tiles = tile_src.shape[2]
    slots = tile_src.shape[3]
    train = labels.shape[2]
    classes = w_third.shape[1]
    hid = w_second.shape[0]
    d_in = w_first.shape[0]
    cols = nodes + ghosts
    rows = send_rows.reshape(parts, each)
    turn = VMEM((128, 128), jnp.int32)
    pick = VMEM((ghosts, nodes), bf16)
    axes = ("dom", "grp")
    members = lax.axis_size(axes)
    few = members <= FEW
    copies = members if few else 1

    def gather(value):
        if few:
            return lax.all_to_all(value, axes, split_axis=0, concat_axis=0, tiled=True)
        return lax.all_gather(value, axes, axis=0, tiled=True)

    label_rows = labels.reshape(1, train)
    start0, out0, side0 = call(
        first_kernel,
        16,
        [
            ((nodes, width), bf16, None),
            ((parts, each, width), bf16, VMEM),
            ((copies, train + 16, width), bf16, VMEM),
        ],
        [(feats.reshape(nodes, width), VMEM), (rows, VMEM), (label_rows, VMEM)],
        [turn, pick],
    )
    table0 = lax.all_to_all(out0, "dom", split_axis=0, concat_axis=0, tiled=True)
    if few:
        every0 = gather(side0)
        every_label = every0[:, train, :train].astype(jnp.int32)
    else:
        every0 = gather(side0[:, :train])
        every_label = gather(label_rows)
    own, ghost, part1, flag, own_rest, ghost_rest = call(
        build_kernel,
        24,
        [
            ((nodes, nodes), bf16, None),
            ((nodes, ghosts), bf16, None),
            ((nodes, width), f32, None),
            ((1,), jnp.int32, SMEM),
            ((nodes, nodes), bf16, pl.ANY),
            ((nodes, ghosts), bf16, pl.ANY),
        ],
        [
            (tile_block.reshape(tiles), SMEM),
            (tile_count.reshape(1), SMEM),
            (tile_src.reshape(tiles, slots), VMEM),
            (tile_dst.reshape(tiles, slots), VMEM),
            (start0, None),
            (hop_noise, None),
        ],
        [VMEM((nodes, cols), f32), VMEM((nodes, max(nodes, ghosts)), bf16)],
    )
    start1, out1, side1 = call(
        hop_kernel,
        16,
        [
            ((nodes, width), bf16, None),
            ((parts, each, width), bf16, VMEM),
            ((copies, train, width), bf16, VMEM),
        ],
        [
            (flag, SMEM),
            (part1, None),
            (ghost, None),
            (ghost_rest, pl.ANY),
            (table0, None),
            (rows, VMEM),
        ],
        [VMEM((nodes, width), f32), VMEM((nodes, ghosts), bf16), turn, pick],
    )
    table1 = lax.all_to_all(out1, "dom", split_axis=0, concat_axis=0, tiled=True)
    every1 = gather(side1)
    (part2,) = call(
        own_kernel,
        12,
        [((nodes, width), f32, None)],
        [
            (flag, SMEM),
            (own, None),
            (own_rest, pl.ANY),
            (start1, None),
            (hop_noise, None),
        ],
        [VMEM((nodes, nodes), bf16)],
    )
    (last,) = call(
        train_kernel,
        8,
        [((copies, train, width), bf16, VMEM)],
        [
            (flag, SMEM),
            (part2, None),
            (ghost, None),
            (ghost_rest, pl.ANY),
            (table1, None),
        ],
        [VMEM((train, width), f32), VMEM((train, ghosts), bf16)],
    )
    every2 = gather(last)
    (hop_feats,) = call(
        last_kernel,
        12,
        [((2, 1, 1, nodes, width), bf16, VMEM)],
        [
            (flag, SMEM),
            (part2, None),
            (ghost, None),
            (ghost_rest, pl.ANY),
            (table1, None),
            (start1, None),
        ],
        [VMEM((nodes, width), f32), VMEM((nodes, ghosts), bf16)],
    )
    chunk = train * min(members, 32)
    groups = chunk // train
    wide = (classes + 255) // 256 * 256
    fixed = (w_first, w_second, w_third.T, noise_first, noise_second, noise_third.T)
    scratch = [
        VMEM((chunk, d_in), bf16),
        VMEM((wide, hid), bf16),
        VMEM((128, 128), jnp.int32),
        VMEM((chunk, 128), jnp.int32),
        VMEM((chunk, hid), bf16),
        VMEM((chunk, hid), bf16),
        VMEM((chunk, hid), f32),
        VMEM((chunk, hid), f32),
        VMEM((chunk, hid), bf16),
        VMEM((chunk, hid), bf16),
    ]
    place = lax.axis_index("dom").reshape(1).astype(jnp.int32)
    ins = (every_label, every0, every1, every2)
    if members == groups:
        first, second, third = call(
            functools.partial(classify_kernel, False),
            36,
            [(value.shape, f32, VMEM) for value in fixed[3:]],
            [(place, SMEM)] + [(value, None) for value in ins + fixed],
            scratch,
        )
    else:

        def whole(value):
            return pl.BlockSpec(value.shape, lambda i: (0, 0))

        def piece(value):
            return pl.BlockSpec(
                (groups,) + value.shape[1:], lambda i: (i,) + (0,) * (value.ndim - 1)
            )

        first, second, third = pl.pallas_call(
            functools.partial(classify_kernel, True),
            grid=(members // groups,),
            out_shape=[jax.ShapeDtypeStruct(value.shape, f32) for value in fixed[3:]],
            in_specs=[pl.BlockSpec(memory_space=SMEM)]
            + [piece(value) for value in ins]
            + [whole(value) for value in fixed],
            out_specs=[whole(value) for value in fixed[3:]],
            scratch_shapes=scratch,
            compiler_params=params(56),
        )(place, *ins, *fixed)
    return (hop_feats, first, second, third.T)


def solution(mesh):
    in_specs = (
        P("dom", "grp", None, None),
        P(None, "dom", "grp", None, None),
        P("dom", "grp", None, None),
        P("dom", "grp", None),
        P("dom", "grp", None, None),
        P("dom", "grp", None, None),
        P("dom", "grp"),
        P("dom", "grp", None),
        P(),
        P(),
        P(),
        P("dom", None),
        P("dom", None),
        P("dom", None),
    )
    out_specs = (P(None, "dom", "grp", None, None), P("dom", None), P("dom", None), P("dom", None))
    return jax.shard_map(local, mesh=mesh, in_specs=in_specs, out_specs=out_specs, check_vma=False)
```

```python
import functools

import jax
import jax.numpy as jnp
from jax import lax
from jax.experimental import pallas as pl
from jax.experimental.pallas import tpu as pltpu
from jax.sharding import PartitionSpec as P

BLOCK = 128
LOW = 256
GROUP = 4
clip_bound = 4.0
noise_mult = 1.0

f32 = jnp.float32
bf16 = jnp.bfloat16
VMEM = pltpu.VMEM
SMEM = pltpu.SMEM
HBM = pltpu.HBM
DMA = pltpu.SemaphoreType.DMA


FEW = 64


def params(mib):
    return pltpu.CompilerParams(vmem_limit_bytes=mib * 1024 * 1024)


def fetch(pairs, sems):
    copies = [pltpu.make_async_copy(*pair, sems.at[at]) for at, pair in enumerate(pairs)]
    for copy in copies:
        copy.start()
    return copies


def normalize(values):
    return (values * lax.rsqrt(jnp.sum(values * values, -1, keepdims=True) + 1e-06)).astype(bf16)


def dot(left, right):
    return jnp.dot(left, right, preferred_element_type=f32)


def dot_nt(left, right):
    return lax.dot_general(left, right, (((1,), (1,)), ((), ())), preferred_element_type=f32)


def dot_tn(left, right):
    return lax.dot_general(left, right, (((0,), (0,)), ((), ())), preferred_element_type=f32)


def send(start, rows_ref, out_ref, turn_ref, pick_ref):
    parts, each = rows_ref.shape
    nodes = start.shape[0]
    turn_ref[:parts, :each] = rows_ref[...]
    columns = turn_ref[...].T
    spots = lax.broadcasted_iota(jnp.int32, (each, nodes), 1)
    for part in range(parts):
        wanted = columns[:each, part : part + 1]
        pick_ref[part * each : (part + 1) * each, :] = jnp.where(wanted == spots, 1.0, 0.0).astype(
            bf16
        )
    out = dot(pick_ref[...], start).astype(bf16)
    out_ref[...] = out.reshape(out_ref.shape)


def spread(rows, out_ref):
    out_ref[...] = jnp.broadcast_to(rows[None], out_ref.shape)


def first_kernel(
    feats_hbm,
    rows_hbm,
    labels_hbm,
    start_ref,
    out_ref,
    side_ref,
    feats_ref,
    rows_ref,
    labels_ref,
    turn_ref,
    pick_ref,
    sems,
):
    sources = (feats_hbm.at[0, 0], rows_hbm.at[0, 0], labels_hbm.at[0])
    copies = fetch(zip(sources, (feats_ref, rows_ref, labels_ref)), sems)
    for copy in copies:
        copy.wait()
    start = normalize(feats_ref[...].astype(f32))
    start_ref[...] = start
    send(start, rows_ref, out_ref, turn_ref, pick_ref)
    train = labels_ref.shape[1]
    side_ref[:train, :] = start[:train]
    turn_ref[:1, :train] = labels_ref[...]
    side_ref[train:, :128] = turn_ref[:16, :].astype(f32).astype(bf16)


def build_kernel(
    blocks_ref,
    count_ref,
    src_hbm,
    dst_hbm,
    noise_hbm,
    start_ref,
    own_hbm,
    ghost_ref,
    part_ref,
    flag_ref,
    own_rest_ref,
    ghost_rest_ref,
    src_ref,
    dst_ref,
    noise_ref,
    low_ref,
    high_ref,
    spot_ref,
    sums_ref,
    rest_ref,
    own_ref,
    sems,
):
    copies = fetch(
        (
            (src_hbm.at[0, 0], src_ref),
            (dst_hbm.at[0, 0], dst_ref),
            (noise_hbm.at[0, 0, 0], noise_ref),
        ),
        sems,
    )
    nodes, cols = sums_ref.shape
    pieces = cols // LOW
    tiles, slots = src_ref.shape
    count = count_ref[0, 0]
    sums_ref[...] = jnp.zeros_like(sums_ref)
    for copy in copies:
        copy.wait()

    def sixteen(values):
        wide = jnp.broadcast_to(values.astype(f32)[:, None, :], (tiles, 16, slots))
        return wide.reshape(tiles * 16, slots).astype(bf16)

    src = src_ref[...]
    dst = dst_ref[...]
    tile_ids = lax.broadcasted_iota(jnp.int32, (tiles, slots), 0)
    low_ref[...] = sixteen(src % LOW)
    high_ref[...] = sixteen(src // LOW)
    spot_ref[...] = sixteen(jnp.where((dst < BLOCK) & (tile_ids < count), dst, -1))
    ids = lax.broadcasted_iota(jnp.int32, (LOW, slots), 0).astype(f32).astype(bf16)
    one = jnp.ones((), bf16)
    zero = jnp.zeros((), bf16)

    def hot(values, length):
        tall = jnp.concatenate([values] * (length // 16), 0)
        return jnp.where(ids[:length] == tall, one, zero)

    def turn(step, carry):
        for inner in range(GROUP):
            tile = step * GROUP + inner
            rows = pl.ds(pl.multiple_of(tile * 16, 16), 16)
            low, high, spot = low_ref[rows, :], high_ref[rows, :], spot_ref[rows, :]
            spots = [
                hot(jnp.where(high == piece, spot, -one), BLOCK) for piece in range(pieces)
            ]
            out = dot_nt(jnp.concatenate(spots, 0), hot(low, LOW))
            base = pl.multiple_of(blocks_ref[0, 0, tile] * BLOCK, BLOCK)
            for piece in range(pieces):
                sums_ref[pl.ds(base, BLOCK), piece * LOW : (piece + 1) * LOW] += out[
                    piece * BLOCK : (piece + 1) * BLOCK
                ]
        return carry

    lax.fori_loop(0, (count + GROUP - 1) // GROUP, turn, 0)
    top = jnp.zeros((BLOCK, LOW), f32)
    for first in range(0, nodes, BLOCK):
        for piece in range(pieces):
            values = sums_ref[first : first + BLOCK, piece * LOW : (piece + 1) * LOW]
            top = jnp.maximum(top, values)
            at = piece * LOW
            if at < nodes:
                own_ref[first : first + BLOCK, at : at + LOW] = values.astype(bf16)
            else:
                at -= nodes
                ghost_ref[first : first + BLOCK, at : at + LOW] = values.astype(bf16)
    own_copy = pltpu.make_async_copy(own_ref, own_hbm, sems.at[3])
    own_copy.start()
    part_ref[...] = dot(own_ref[...], start_ref[...]) + noise_ref[...].astype(f32)
    big = jnp.max(top) > 256.0
    flag_ref[0] = big.astype(jnp.int32)

    @pl.when(big)
    def _():
        own_rest = (sums_ref[:, :nodes] - own_ref[...].astype(f32)).astype(bf16)
        part_ref[...] += dot(own_rest, start_ref[...])
        rest_ref[:, :nodes] = own_rest
        pltpu.sync_copy(rest_ref.at[:, :nodes], own_rest_ref)
        rest_ref[:, : cols - nodes] = (sums_ref[:, nodes:] - ghost_ref[...].astype(f32)).astype(bf16)
        pltpu.sync_copy(rest_ref.at[:, : cols - nodes], ghost_rest_ref)

    own_copy.wait()


def aggregate(flag_ref, part_ref, count_ref, rest_hbm, table, sums_ref, rest_ref):
    rows = sums_ref.shape[0]
    sums_ref[...] = part_ref.astype(f32) + dot(count_ref, table)

    @pl.when(flag_ref[0] > 0)
    def _():
        pltpu.sync_copy(rest_hbm.at[:rows], rest_ref)
        sums_ref[...] += dot(rest_ref[...], table)


def hop_kernel(
    flag_ref,
    part_ref,
    ghost_ref,
    rest_hbm,
    table_ref,
    rows_ref,
    start_ref,
    out_ref,
    sums_ref,
    rest_ref,
    turn_ref,
    pick_ref,
):
    width = start_ref.shape[1]
    table = table_ref[...].reshape(-1, width)
    aggregate(flag_ref, part_ref[...], ghost_ref[...], rest_hbm, table, sums_ref, rest_ref)
    start = normalize(sums_ref[...])
    start_ref[...] = start
    send(start, rows_ref, out_ref, turn_ref, pick_ref)


def own_kernel(
    flag_ref, own_hbm, rest_hbm, noise_hbm, start_ref, part_ref, own_ref, noise_ref, rest_ref, sems
):
    copies = fetch(((own_hbm, own_ref), (noise_hbm.at[1, 0, 0], noise_ref)), sems)
    for copy in copies:
        copy.wait()
    start = start_ref[...]
    noise = noise_ref[...].astype(f32)
    aggregate(flag_ref, noise, own_ref[...], rest_hbm, start, part_ref, rest_ref)


def train_kernel(
    flag_ref,
    place_ref,
    part_ref,
    ghost_ref,
    rest_hbm,
    table_ref,
    start_ref,
    *refs,
):
    *piece_refs, out_ref, side_ref, sums_ref, rest_ref = refs
    train, width = sums_ref.shape
    table = table_ref[...].reshape(-1, width)
    aggregate(
        flag_ref, part_ref[:train], ghost_ref[:train], rest_hbm, table, sums_ref, rest_ref
    )
    spread(normalize(sums_ref[...]), out_ref)
    group, groups = place_ref[1], side_ref.shape[1] // train
    for shift in range(len(piece_refs) + 1):
        rows = piece_refs[shift - 1][...] if shift else start_ref[:train, :]
        at = pl.multiple_of(lax.rem(group + shift, groups) * train, train)
        side_ref[:, pl.ds(at, train), :] = jnp.broadcast_to(
            rows[None], (side_ref.shape[0], train, width)
        )


def last_kernel(
    flag_ref, part_ref, ghost_ref, rest_hbm, table_ref, start_ref, out_ref, sums_ref, rest_ref
):
    table = table_ref[...].reshape(-1, out_ref.shape[-1])
    aggregate(flag_ref, part_ref[...], ghost_ref[...], rest_hbm, table, sums_ref, rest_ref)
    out_ref[0, 0, 0] = start_ref[...]
    out_ref[1, 0, 0] = normalize(sums_ref[...])


def shares(ref, first, share):
    if share % 128 == 0:
        return ref[:, pl.ds(pl.multiple_of(first, 128), share)].astype(f32)
    length = ref.shape[1]
    rows = lax.broadcasted_iota(jnp.int32, (length, share), 0)
    cols = lax.broadcasted_iota(jnp.int32, (length, share), 1)
    return dot(ref[...], jnp.where(rows == cols + first, 1.0, 0.0).astype(bf16))


def lanes_sum(values):
    total = None
    for piece in range(values.shape[1] // 128):
        part = values[:, piece * 128 : (piece + 1) * 128].astype(f32)
        total = part * part if total is None else total + part * part
    return total


def classify_kernel(
    many,
    place_ref,
    label_ref,
    zero_in,
    one_in,
    two_ref,
    w_first_hbm,
    w_second_hbm,
    w_third_hbm,
    n_first_hbm,
    n_second_hbm,
    n_third_hbm,
    g_first_ref,
    g_second_ref,
    g_third_ref,
    zero_own,
    one_own,
    w_first_ref,
    w_second_ref,
    w_third_ref,
    n_first_ref,
    n_second_ref,
    n_third_ref,
    in_ref,
    w_third_pad_ref,
    turn_ref,
    column_ref,
    h_one_ref,
    h_two_ref,
    slope_one_ref,
    slope_two_ref,
    d_one_ref,
    d_two_ref,
    sems,
):
    classes = w_third_ref.shape[0]
    hid = w_second_ref.shape[0]
    width = two_ref.shape[2]
    wide = w_third_pad_ref.shape[0]
    groups, train = label_ref.shape
    scale = noise_mult * clip_bound
    place = place_ref[0]
    pairs = (
        (w_first_hbm, w_first_ref),
        (w_second_hbm, w_second_ref),
        (w_third_hbm, w_third_ref),
        (n_first_hbm, n_first_ref),
        (n_second_hbm, n_second_ref),
        (n_third_hbm, n_third_ref),
    )

    def set_noise():
        g_first_ref[...] = scale * n_first_ref[...]
        g_second_ref[...] = scale * n_second_ref[...]
        g_third_ref[...] = scale * n_third_ref[...]

    def pad():
        w_third_pad_ref[...] = jnp.zeros_like(w_third_pad_ref)
        w_third_pad_ref[:classes, :] = w_third_ref[...]

    if many:

        @pl.when(pl.program_id(0) == 0)
        def _():
            for copy in fetch(pairs, sems):
                copy.wait()
            set_noise()
            pad()

        zero_ref, one_ref = zero_in, one_in
    else:
        zero_ref, one_ref = zero_own, one_own
        copies = fetch(((zero_in, zero_own), (one_in, one_own)) + pairs, sems)

    turn_ref[:groups, :train] = label_ref[...]
    turned = turn_ref[...].T
    for group in range(groups):
        column_ref[group * train : (group + 1) * train, :] = jnp.broadcast_to(
            turned[:train, group : group + 1], (train, 128)
        )
    if not many:
        for copy in copies[:3]:
            copy.wait()
    for hop, ref in enumerate((zero_ref, one_ref, two_ref)):
        in_ref[:, hop * width : (hop + 1) * width] = ref[:, :train, :].reshape(-1, width)

    def activate(values, h_ref, slope_ref, cols):
        sigma = 0.5 + 0.5 * jnp.tanh(0.5 * values)
        out = values * sigma
        slope_ref[:, cols] = sigma + out * (1.0 - sigma)
        rounded = out.astype(bf16)
        h_ref[:, cols] = rounded
        return lanes_sum(rounded)

    step = 256
    cuts = [slice(at, at + step) for at in range(0, hid, step)]
    sq_in = lanes_sum(in_ref[...])
    sq_one = sum(
        activate(dot(in_ref[...], w_first_ref[:, cut]), h_one_ref, slope_one_ref, cut)
        for cut in cuts
    )
    if not many:
        copies[3].wait()
    sq_two = sum(
        activate(dot(h_one_ref[...], w_second_ref[:, cut]), h_two_ref, slope_two_ref, cut)
        for cut in cuts
    )
    if not many:
        copies[4].wait()
        pad()
    logits = dot_nt(h_two_ref[...], w_third_pad_ref[...])
    ids = lax.broadcasted_iota(jnp.int32, (logits.shape[0], wide), 1)
    expo = jnp.where(ids < classes, jnp.exp(logits), 0.0)
    probs = expo / jnp.sum(expo, -1, keepdims=True)
    label = column_ref[:, :1]
    d_three = (probs - jnp.where(ids == label, 1.0, 0.0)).astype(bf16)
    sq_dthree = lanes_sum(d_three)

    def back(values, slope_ref, d_ref, cut):
        rounded = (values * slope_ref[:, cut]).astype(bf16)
        d_ref[:, cut] = rounded
        return lanes_sum(rounded)

    sq_dtwo = sum(
        back(dot(d_three, w_third_pad_ref[:, cut]), slope_two_ref, d_two_ref, cut)
        for cut in cuts
    )
    sq_done = sum(
        back(dot_nt(d_two_ref[...], w_second_ref[cut, :]), slope_one_ref, d_one_ref, cut)
        for cut in cuts
    )

    def total(values):
        return jnp.sum(values, -1, keepdims=True)

    norm = jnp.sqrt(
        total(sq_in) * total(sq_done)
        + total(sq_one) * total(sq_dtwo)
        + total(sq_two) * total(sq_dthree)
    )
    factor = clip_bound / jnp.maximum(norm, clip_bound)

    def left(ref, share):
        return (shares(ref, place * share, share) * factor).astype(bf16)

    if not many:
        for copy in copies[5:]:
            copy.wait()
        set_noise()
    share = g_second_ref.shape[0]
    g_first_ref[...] += dot_tn(left(in_ref, g_first_ref.shape[0]), d_one_ref[...])
    g_second_ref[...] += dot_tn(left(h_one_ref, share), d_two_ref[...])
    g_third_ref[...] += dot_tn(d_three, left(h_two_ref, share))[:classes, :]


def call(kernel, mib, outs, ins, scratch):
    def shape_of(shape, dtype, space):
        if space is None or space is HBM:
            return (space or VMEM)(shape, dtype)
        return jax.ShapeDtypeStruct(shape, dtype)

    def block(space):
        return pl.BlockSpec(memory_space=VMEM if space is None else space)

    def held(value, space):
        if space is None or space is HBM:
            return pltpu.with_memory_space_constraint(value, space or VMEM)
        return value

    return pl.pallas_call(
        kernel,
        out_shape=[shape_of(*out) for out in outs],
        in_specs=[block(space) for _, space in ins],
        out_specs=[block(space) for _, _, space in outs],
        scratch_shapes=scratch,
        compiler_params=params(mib),
    )(*[held(value, space) for value, space in ins])


def local(
    feats,
    hop_noise,
    send_rows,
    tile_block,
    tile_src,
    tile_dst,
    tile_count,
    labels,
    w_first,
    w_second,
    w_third,
    noise_first,
    noise_second,
    noise_third,
):
    nodes, width = feats.shape[2:]
    parts, each = send_rows.shape[2:]
    ghosts = parts * each
    tiles = tile_src.shape[2]
    slots = tile_src.shape[3]
    train = labels.shape[2]
    classes = w_third.shape[1]
    hid = w_second.shape[0]
    d_in = w_first.shape[0]
    cols = nodes + ghosts
    rows = send_rows.reshape(parts, each)
    turn = VMEM((128, 128), jnp.int32)
    pick = VMEM((ghosts, nodes), bf16)
    axes = ("dom", "grp")
    members = lax.axis_size(axes)
    few = members <= FEW
    copies = members if few else 1

    def every(value, *names):
        for name in names:
            value = lax.all_gather(value, name, axis=0, tiled=True)
        return value

    start0, out0, side0 = call(
        first_kernel,
        16,
        [
            ((nodes, width), bf16, None),
            ((parts, each, width), bf16, VMEM),
            ((train + 16, width), bf16, VMEM),
        ],
        [(feats, HBM), (send_rows, HBM), (labels, HBM)],
        [
            VMEM((nodes, width), bf16),
            VMEM((parts, each), jnp.int32),
            VMEM((1, train), jnp.int32),
            turn,
            pick,
            DMA((3,)),
        ],
    )
    table0 = lax.all_to_all(out0, "dom", split_axis=0, concat_axis=0, tiled=True)
    if few:
        every0 = every(side0[None], "grp", "dom")
        every_label = every0[:, train, :train].astype(jnp.int32)
    else:
        every0 = every(side0[None, :train], axes)
        every_label = every(labels.reshape(1, train), axes)
    own, ghost, part1, flag, own_rest, ghost_rest = call(
        build_kernel,
        28,
        [
            ((nodes, nodes), bf16, HBM),
            ((nodes, ghosts), bf16, None),
            ((nodes, width), f32, None),
            ((1,), jnp.int32, SMEM),
            ((nodes, nodes), bf16, HBM),
            ((nodes, ghosts), bf16, HBM),
        ],
        [
            (tile_block, SMEM),
            (tile_count, SMEM),
            (tile_src, HBM),
            (tile_dst, HBM),
            (hop_noise, HBM),
            (start0, None),
        ],
        [
            VMEM((tiles, slots), jnp.int32),
            VMEM((tiles, slots), jnp.int32),
            VMEM((nodes, width), bf16),
            VMEM((tiles * 16, slots), bf16),
            VMEM((tiles * 16, slots), bf16),
            VMEM((tiles * 16, slots), bf16),
            VMEM((nodes, cols), f32),
            VMEM((nodes, max(nodes, ghosts)), bf16),
            VMEM((nodes, nodes), bf16),
            DMA((4,)),
        ],
    )
    start1, out1 = call(
        hop_kernel,
        16,
        [
            ((nodes, width), bf16, None),
            ((parts, each, width), bf16, VMEM),
        ],
        [
            (flag, SMEM),
            (part1, None),
            (ghost, None),
            (ghost_rest, HBM),
            (table0, None),
            (rows, VMEM),
        ],
        [VMEM((nodes, width), f32), VMEM((nodes, ghosts), bf16), turn, pick],
    )
    table1 = lax.all_to_all(out1, "dom", split_axis=0, concat_axis=0, tiled=True)
    (part2,) = call(
        own_kernel,
        16,
        [((nodes, width), f32, None)],
        [(flag, SMEM), (own, HBM), (own_rest, HBM), (hop_noise, HBM), (start1, None)],
        [
            VMEM((nodes, nodes), bf16),
            VMEM((nodes, width), bf16),
            VMEM((nodes, nodes), bf16),
            DMA((2,)),
        ],
    )
    place = jnp.stack([lax.axis_index("dom"), lax.axis_index("grp")]).astype(jnp.int32)
    grp = lax.axis_size("grp")
    pieces1 = []
    if few:
        pieces1 = [
            lax.ppermute(start1[:train], "grp", [((at + shift) % grp, at) for at in range(grp)])
            for shift in range(1, grp)
        ]
    last, side1 = call(
        train_kernel,
        12,
        [
            ((copies, train, width), bf16, VMEM),
            ((parts, (grp if few else 1) * train, width), bf16, VMEM),
        ],
        [
            (flag, SMEM),
            (place, SMEM),
            (part2, None),
            (ghost, None),
            (ghost_rest, HBM),
            (table1, None),
            (start1, None),
        ]
        + [(piece, None) for piece in pieces1],
        [VMEM((train, width), f32), VMEM((train, ghosts), bf16)],
    )
    if few:
        every2 = lax.all_to_all(last, axes, split_axis=0, concat_axis=0, tiled=True)
        every1 = lax.all_to_all(side1, "dom", split_axis=0, concat_axis=0, tiled=True)
        every1 = every1.reshape(members, train, width)
    else:
        every2 = every(last, axes)
        every1 = every(start1[None, :train], axes)
    (hop_feats,) = call(
        last_kernel,
        12,
        [((2, 1, 1, nodes, width), bf16, VMEM)],
        [
            (flag, SMEM),
            (part2, None),
            (ghost, None),
            (ghost_rest, HBM),
            (table1, None),
            (start1, None),
        ],
        [VMEM((nodes, width), f32), VMEM((nodes, ghosts), bf16)],
    )
    chunk = train * min(members, 32)
    groups = chunk // train
    wide = (classes + 255) // 256 * 256
    fixed = (w_first, w_second, w_third.T, noise_first, noise_second, noise_third.T)
    scratch = (
        [VMEM(value.shape, bf16) for value in (every0, every1)]
        if few
        else [VMEM((16, 128), bf16)] * 2
    )
    scratch += [VMEM(value.shape, value.dtype) for value in fixed]
    scratch += [
        VMEM((chunk, d_in), bf16),
        VMEM((wide, hid), bf16),
        VMEM((128, 128), jnp.int32),
        VMEM((chunk, 128), jnp.int32),
        VMEM((chunk, hid), bf16),
        VMEM((chunk, hid), bf16),
        VMEM((chunk, hid), f32),
        VMEM((chunk, hid), f32),
        VMEM((chunk, hid), bf16),
        VMEM((chunk, hid), bf16),
        DMA((8,)),
    ]
    ins = (every_label, every0, every1, every2)
    if members == groups:
        first, second, third = call(
            functools.partial(classify_kernel, False),
            44,
            [(value.shape, f32, VMEM) for value in fixed[3:]],
            [(place, SMEM), (every_label, VMEM), (every0, HBM), (every1, HBM), (every2, None)]
            + [(value, HBM) for value in fixed],
            scratch,
        )
    else:

        def whole(value):
            return pl.BlockSpec(value.shape, lambda i: (0, 0))

        def piece(value):
            return pl.BlockSpec(
                (groups,) + value.shape[1:], lambda i: (i,) + (0,) * (value.ndim - 1)
            )

        first, second, third = pl.pallas_call(
            functools.partial(classify_kernel, True),
            grid=(members // groups,),
            out_shape=[jax.ShapeDtypeStruct(value.shape, f32) for value in fixed[3:]],
            in_specs=[pl.BlockSpec(memory_space=SMEM)]
            + [piece(value) for value in ins]
            + [pl.BlockSpec(memory_space=HBM) for value in fixed],
            out_specs=[whole(value) for value in fixed[3:]],
            scratch_shapes=scratch,
            compiler_params=params(56),
        )(place, *ins, *fixed)
    return (hop_feats, first, second, third.T)


def solution(mesh):
    in_specs = (
        P("dom", "grp", None, None),
        P(None, "dom", "grp", None, None),
        P("dom", "grp", None, None),
        P("dom", "grp", None),
        P("dom", "grp", None, None),
        P("dom", "grp", None, None),
        P("dom", "grp"),
        P("dom", "grp", None),
        P(),
        P(),
        P(),
        P("dom", None),
        P("dom", None),
        P("dom", None),
    )
    out_specs = (P(None, "dom", "grp", None, None), P("dom", None), P("dom", None), P("dom", None))
    return jax.shard_map(local, mesh=mesh, in_specs=in_specs, out_specs=out_specs, check_vma=False)
```

```python
import functools

import jax
import jax.numpy as jnp
from jax import lax
from jax.experimental import pallas as pl
from jax.experimental.pallas import tpu as pltpu
from jax.sharding import PartitionSpec as P

BLOCK = 128
LOW = 256
GROUP = 4
clip_bound = 4.0
noise_mult = 1.0

f32 = jnp.float32
bf16 = jnp.bfloat16
VMEM = pltpu.VMEM
SMEM = pltpu.SMEM
HBM = pltpu.HBM
DMA = pltpu.SemaphoreType.DMA


FEW = 32


def params(mib):
    return pltpu.CompilerParams(vmem_limit_bytes=mib * 1024 * 1024)


def fetch(pairs, sems):
    copies = [pltpu.make_async_copy(*pair, sems.at[at]) for at, pair in enumerate(pairs)]
    for copy in copies:
        copy.start()
    return copies


def normalize(values):
    return (values * lax.rsqrt(jnp.sum(values * values, -1, keepdims=True) + 1e-06)).astype(bf16)


def dot(left, right):
    return jnp.dot(left, right, preferred_element_type=f32)


def dot_nt(left, right):
    return lax.dot_general(left, right, (((1,), (1,)), ((), ())), preferred_element_type=f32)


def dot_tn(left, right):
    return lax.dot_general(left, right, (((0,), (0,)), ((), ())), preferred_element_type=f32)


def send(start, rows_ref, out_ref, turn_ref, pick_ref):
    parts, each = rows_ref.shape
    nodes = start.shape[0]
    turn_ref[:parts, :each] = rows_ref[...]
    columns = turn_ref[...].T
    spots = lax.broadcasted_iota(jnp.int32, (each, nodes), 1)
    for part in range(parts):
        wanted = columns[:each, part : part + 1]
        pick_ref[part * each : (part + 1) * each, :] = jnp.where(wanted == spots, 1.0, 0.0).astype(
            bf16
        )
    out = dot(pick_ref[...], start).astype(bf16)
    out_ref[...] = out.reshape(out_ref.shape)


def spread(rows, out_ref):
    out_ref[...] = jnp.broadcast_to(rows[None], out_ref.shape)


def first_kernel(
    feats_hbm,
    rows_hbm,
    start_ref,
    out_ref,
    feats_ref,
    rows_ref,
    turn_ref,
    pick_ref,
    sems,
):
    copies = fetch(
        ((feats_hbm.at[0, 0], feats_ref), (rows_hbm.at[0, 0], rows_ref)), sems
    )
    for copy in copies:
        copy.wait()
    start = normalize(feats_ref[...].astype(f32))
    start_ref[...] = start
    send(start, rows_ref, out_ref, turn_ref, pick_ref)


def build_kernel(
    blocks_ref,
    count_ref,
    src_hbm,
    dst_hbm,
    noise_hbm,
    start_ref,
    own_hbm,
    ghost_ref,
    part_ref,
    flag_ref,
    own_rest_ref,
    ghost_rest_ref,
    src_ref,
    dst_ref,
    noise_ref,
    low_ref,
    high_ref,
    spot_ref,
    sums_ref,
    rest_ref,
    own_ref,
    sems,
):
    copies = fetch(
        (
            (src_hbm.at[0, 0], src_ref),
            (dst_hbm.at[0, 0], dst_ref),
            (noise_hbm.at[0, 0, 0], noise_ref),
        ),
        sems,
    )
    nodes, cols = sums_ref.shape
    pieces = cols // LOW
    tiles, slots = src_ref.shape
    count = count_ref[0, 0]
    own_ref[...] = jnp.zeros_like(own_ref)
    ghost_ref[...] = jnp.zeros_like(ghost_ref)
    for copy in copies:
        copy.wait()

    def sixteen(values):
        wide = jnp.broadcast_to(values.astype(f32)[:, None, :], (tiles, 16, slots))
        return wide.reshape(tiles * 16, slots).astype(bf16)

    src = src_ref[...]
    dst = dst_ref[...]
    tile_ids = lax.broadcasted_iota(jnp.int32, (tiles, slots), 0)
    high_ref[...] = sixteen(src // LOW)
    spot_ref[...] = sixteen(jnp.where((dst < BLOCK) & (tile_ids < count), dst, -1))
    low = (src % LOW).astype(f32).T
    for tile in range(tiles):
        low_ref[tile] = jnp.broadcast_to(low[:, tile : tile + 1], (slots, 128)).astype(bf16)
    ids = lax.broadcasted_iota(jnp.int32, (BLOCK, slots), 0).astype(f32).astype(bf16)
    lanes = lax.broadcasted_iota(jnp.int32, (slots, 128), 1).astype(f32)
    lanes = [(lanes + first).astype(bf16) for first in range(0, LOW, 128)]
    one = jnp.ones((), bf16)
    zero = jnp.zeros((), bf16)

    def turn(add, step, carry):
        for inner in range(GROUP):
            tile = step * GROUP + inner
            rows = pl.ds(pl.multiple_of(tile * 16, 16), 16)
            high, spot = high_ref[rows, :], spot_ref[rows, :]
            spots = []
            for piece in range(pieces):
                wanted = jnp.where(high == piece, spot, -one)
                tall = jnp.concatenate([wanted] * (BLOCK // 16), 0)
                spots.append(jnp.where(ids == tall, one, zero))
            low = low_ref[tile]
            low_hot = jnp.concatenate([jnp.where(low == ids, one, zero) for ids in lanes], 1)
            out = dot(jnp.concatenate(spots, 0), low_hot)
            base = pl.multiple_of(blocks_ref[0, 0, tile] * BLOCK, BLOCK)
            for piece in range(pieces):
                add(pl.ds(base, BLOCK), piece * LOW, out[piece * BLOCK : (piece + 1) * BLOCK])
        return carry

    def add_short(rows, at, values):
        ref, at = (own_ref, at) if at < nodes else (ghost_ref, at - nodes)
        ref[rows, at : at + LOW] += values.astype(bf16)

    def add_long(rows, at, values):
        sums_ref[rows, at : at + LOW] += values

    steps = (count + GROUP - 1) // GROUP
    lax.fori_loop(0, steps, functools.partial(turn, add_short), 0)
    top = ghost_ref[:BLOCK, :LOW]
    for first in range(0, nodes, BLOCK):
        for ref in (own_ref, ghost_ref):
            for at in range(0, ref.shape[1], LOW):
                top = jnp.maximum(top, ref[first : first + BLOCK, at : at + LOW])
    big = jnp.max(top.astype(f32)) >= 256.0
    flag_ref[0] = big.astype(jnp.int32)

    @pl.when(big)
    def _():
        sums_ref[...] = jnp.zeros_like(sums_ref)
        lax.fori_loop(0, steps, functools.partial(turn, add_long), 0)
        own_ref[...] = sums_ref[:, :nodes].astype(bf16)
        ghost_ref[...] = sums_ref[:, nodes:].astype(bf16)

    own_copy = pltpu.make_async_copy(own_ref, own_hbm, sems.at[3])
    own_copy.start()
    part_ref[...] = dot(own_ref[...], start_ref[...]) + noise_ref[...].astype(f32)

    @pl.when(big)
    def _():
        own_rest = (sums_ref[:, :nodes] - own_ref[...].astype(f32)).astype(bf16)
        part_ref[...] += dot(own_rest, start_ref[...])
        rest_ref[:, :nodes] = own_rest
        pltpu.sync_copy(rest_ref.at[:, :nodes], own_rest_ref)
        rest_ref[:, : cols - nodes] = (sums_ref[:, nodes:] - ghost_ref[...].astype(f32)).astype(bf16)
        pltpu.sync_copy(rest_ref.at[:, : cols - nodes], ghost_rest_ref)

    own_copy.wait()


def aggregate(flag_ref, part_ref, count_ref, rest_hbm, table, sums_ref, rest_ref):
    rows = sums_ref.shape[0]
    sums_ref[...] = part_ref.astype(f32) + dot(count_ref, table)

    @pl.when(flag_ref[0] > 0)
    def _():
        pltpu.sync_copy(rest_hbm.at[:rows], rest_ref)
        sums_ref[...] += dot(rest_ref[...], table)


def hop_kernel(
    flag_ref,
    part_ref,
    ghost_ref,
    rest_hbm,
    table_ref,
    rows_ref,
    old_ref,
    labels_ref,
    start_ref,
    out_ref,
    side_ref,
    sums_ref,
    rest_ref,
    turn_ref,
    pick_ref,
):
    width = start_ref.shape[1]
    table = table_ref[...].reshape(-1, width)
    aggregate(flag_ref, part_ref[...], ghost_ref[...], rest_hbm, table, sums_ref, rest_ref)
    start = normalize(sums_ref[...])
    start_ref[...] = start
    send(start, rows_ref, out_ref, turn_ref, pick_ref)
    train = labels_ref.shape[1]
    side_ref[:train, :] = old_ref[:train, :]
    side_ref[train : 2 * train, :] = start[:train]
    turn_ref[:1, :train] = labels_ref[...]
    side_ref[2 * train :, :128] = turn_ref[:16, :].astype(f32).astype(bf16)


def own_kernel(
    flag_ref, own_hbm, rest_hbm, noise_hbm, start_ref, part_ref, own_ref, noise_ref, rest_ref, sems
):
    copies = fetch(((own_hbm, own_ref), (noise_hbm.at[1, 0, 0], noise_ref)), sems)
    for copy in copies:
        copy.wait()
    start = start_ref[...]
    noise = noise_ref[...].astype(f32)
    aggregate(flag_ref, noise, own_ref[...], rest_hbm, start, part_ref, rest_ref)


def train_kernel(
    flag_ref, part_ref, ghost_ref, rest_hbm, table_ref, out_ref, token_ref, sums_ref, rest_ref
):
    train, width = sums_ref.shape
    table = table_ref[...].reshape(-1, width)
    aggregate(
        flag_ref, part_ref[:train], ghost_ref[:train], rest_hbm, table, sums_ref, rest_ref
    )
    spread(normalize(sums_ref[...]), out_ref)
    token_ref[...] = sums_ref[:8, :128]


def last_kernel(
    flag_ref,
    place_ref,
    token_ref,
    part_ref,
    ghost_ref,
    rest_hbm,
    table_ref,
    start_ref,
    *refs,
):
    *piece_refs, out_ref, side_ref, sums_ref, rest_ref, turn_ref = refs
    table = table_ref[...].reshape(-1, out_ref.shape[-1])
    aggregate(flag_ref, part_ref[...], ghost_ref[...], rest_hbm, table, sums_ref, rest_ref)
    out_ref[0, 0, 0] = start_ref[...]
    out_ref[1, 0, 0] = normalize(sums_ref[...])
    length = piece_refs[0].shape[0] - 16
    groups = len(piece_refs)
    if groups > 1:
        for shift, ref in enumerate(piece_refs):
            group = lax.rem(place_ref[1] + shift, groups)
            at = pl.multiple_of(group * length, length)
            side_ref[pl.ds(at, length), :] = ref[:length, :]
            turn_ref[pl.ds(group, 1), :] = ref[length:, :128].astype(f32)[:1]
        side_ref[groups * length :, :128] = turn_ref[:16, :].astype(bf16)


def shares(ref, first, share):
    if share % 128 == 0:
        return ref[:, pl.ds(pl.multiple_of(first, 128), share)].astype(f32)
    length = ref.shape[1]
    rows = lax.broadcasted_iota(jnp.int32, (length, share), 0)
    cols = lax.broadcasted_iota(jnp.int32, (length, share), 1)
    return dot(ref[...], jnp.where(rows == cols + first, 1.0, 0.0).astype(bf16))


def lanes_sum(values):
    total = None
    for piece in range(values.shape[1] // 128):
        part = values[:, piece * 128 : (piece + 1) * 128].astype(f32)
        total = part * part if total is None else total + part * part
    return total


def classify_kernel(
    many,
    place_ref,
    label_ref,
    zero_ref,
    one_ref,
    two_ref,
    side_refs,
    w_first_hbm,
    w_second_hbm,
    w_third_hbm,
    n_first_hbm,
    n_second_hbm,
    n_third_hbm,
    g_first_ref,
    g_second_ref,
    g_third_ref,
    w_first_ref,
    w_second_ref,
    w_third_ref,
    n_first_ref,
    n_second_ref,
    n_third_ref,
    in_ref,
    w_third_pad_ref,
    turn_ref,
    column_ref,
    h_one_ref,
    h_two_ref,
    slope_one_ref,
    slope_two_ref,
    d_one_ref,
    d_two_ref,
    sems,
):
    classes = w_third_ref.shape[0]
    hid = w_second_ref.shape[0]
    width = two_ref.shape[2]
    wide = w_third_pad_ref.shape[0]
    train = two_ref.shape[1]
    scale = noise_mult * clip_bound
    place = place_ref[0]
    pairs = (
        (w_first_hbm, w_first_ref),
        (w_second_hbm, w_second_ref),
        (w_third_hbm, w_third_ref),
        (n_first_hbm, n_first_ref),
        (n_second_hbm, n_second_ref),
        (n_third_hbm, n_third_ref),
    )

    def set_noise():
        g_first_ref[...] = scale * n_first_ref[...]
        g_second_ref[...] = scale * n_second_ref[...]
        g_third_ref[...] = scale * n_third_ref[...]

    def pad():
        w_third_pad_ref[...] = jnp.zeros_like(w_third_pad_ref)
        w_third_pad_ref[:classes, :] = w_third_ref[...]

    def column(row, turned, lane):
        column_ref[row : row + train, :] = jnp.broadcast_to(
            turned[:train, lane : lane + 1], (train, 128)
        ).astype(jnp.int32)

    if many:

        @pl.when(pl.program_id(0) == 0)
        def _():
            for copy in fetch(pairs, sems):
                copy.wait()
            set_noise()
            pad()

        groups = label_ref.shape[0]
        turn_ref[:groups, :train] = label_ref[...].astype(f32)
        turned = turn_ref[...].T
        for group in range(groups):
            column(group * train, turned, group)
        for hop, ref in enumerate((zero_ref, one_ref)):
            in_ref[:, hop * width : (hop + 1) * width] = ref[...].reshape(-1, width)
    else:
        copies = fetch(pairs[:1], sems)
        parts = len(side_refs)
        groups = two_ref.shape[0] // parts
        rows = groups * train
        for shift, ref in enumerate(side_refs):
            part = lax.rem(place - shift + parts, parts)
            at = pl.multiple_of(part * rows, rows)
            for group in range(groups):
                for hop in range(2):
                    first = (2 * group + hop) * train
                    in_ref[pl.ds(at + group * train, train), hop * width : (hop + 1) * width] = ref[
                        first : first + train, :
                    ]
            turn_ref[pl.ds(pl.multiple_of(part * 16, 16), 16), :] = ref[2 * rows :, :128].astype(f32)
        turned = turn_ref[...].T
        for part in range(parts):
            for group in range(groups):
                column((part * groups + group) * train, turned, part * 16 + group)
    in_ref[:, 2 * width :] = two_ref[...].reshape(-1, width)
    if not many:
        copies[0].wait()
        copies = fetch(pairs[1:], sems)

    def activate(values, h_ref, slope_ref, cols):
        sigma = 0.5 + 0.5 * jnp.tanh(0.5 * values)
        out = values * sigma
        slope_ref[:, cols] = sigma + out * (1.0 - sigma)
        rounded = out.astype(bf16)
        h_ref[:, cols] = rounded
        return lanes_sum(rounded)

    step = 256
    cuts = [slice(at, at + step) for at in range(0, hid, step)]
    sq_in = lanes_sum(in_ref[...])
    sq_one = sum(
        activate(dot(in_ref[...], w_first_ref[:, cut]), h_one_ref, slope_one_ref, cut)
        for cut in cuts
    )
    if not many:
        copies[0].wait()
    sq_two = sum(
        activate(dot(h_one_ref[...], w_second_ref[:, cut]), h_two_ref, slope_two_ref, cut)
        for cut in cuts
    )
    if not many:
        copies[1].wait()
        pad()
    logits = dot_nt(h_two_ref[...], w_third_pad_ref[...])
    ids = lax.broadcasted_iota(jnp.int32, (logits.shape[0], wide), 1)
    expo = jnp.where(ids < classes, jnp.exp(logits), 0.0)
    probs = expo / jnp.sum(expo, -1, keepdims=True)
    label = column_ref[:, :1]
    d_three = (probs - jnp.where(ids == label, 1.0, 0.0)).astype(bf16)
    sq_dthree = lanes_sum(d_three)

    def back(values, slope_ref, d_ref, cut):
        rounded = (values * slope_ref[:, cut]).astype(bf16)
        d_ref[:, cut] = rounded
        return lanes_sum(rounded)

    sq_dtwo = sum(
        back(dot(d_three, w_third_pad_ref[:, cut]), slope_two_ref, d_two_ref, cut)
        for cut in cuts
    )
    sq_done = sum(
        back(dot_nt(d_two_ref[...], w_second_ref[cut, :]), slope_one_ref, d_one_ref, cut)
        for cut in cuts
    )

    def total(values):
        return jnp.sum(values, -1, keepdims=True)

    norm = jnp.sqrt(
        total(sq_in) * total(sq_done)
        + total(sq_one) * total(sq_dtwo)
        + total(sq_two) * total(sq_dthree)
    )
    factor = clip_bound / jnp.maximum(norm, clip_bound)

    def left(ref, share):
        return (shares(ref, place * share, share) * factor).astype(bf16)

    if not many:
        for copy in copies[2:]:
            copy.wait()
        set_noise()
    share = g_second_ref.shape[0]
    g_first_ref[...] += dot_tn(left(in_ref, g_first_ref.shape[0]), d_one_ref[...])
    g_second_ref[...] += dot_tn(left(h_one_ref, share), d_two_ref[...])
    g_third_ref[...] += dot_tn(d_three, left(h_two_ref, share))[:classes, :]


def call(kernel, mib, outs, ins, scratch):
    def shape_of(shape, dtype, space):
        if space is None or space is HBM:
            return (space or VMEM)(shape, dtype)
        return jax.ShapeDtypeStruct(shape, dtype)

    def block(space):
        return pl.BlockSpec(memory_space=VMEM if space is None else space)

    def held(value, space):
        if space is None or space is HBM:
            return pltpu.with_memory_space_constraint(value, space or VMEM)
        return value

    return pl.pallas_call(
        kernel,
        out_shape=[shape_of(*out) for out in outs],
        in_specs=[block(space) for _, space in ins],
        out_specs=[block(space) for _, _, space in outs],
        scratch_shapes=scratch,
        compiler_params=params(mib),
    )(*[held(value, space) for value, space in ins])


def local(
    feats,
    hop_noise,
    send_rows,
    tile_block,
    tile_src,
    tile_dst,
    tile_count,
    labels,
    w_first,
    w_second,
    w_third,
    noise_first,
    noise_second,
    noise_third,
):
    nodes, width = feats.shape[2:]
    parts, each = send_rows.shape[2:]
    ghosts = parts * each
    tiles = tile_src.shape[2]
    slots = tile_src.shape[3]
    train = labels.shape[2]
    classes = w_third.shape[1]
    hid = w_second.shape[0]
    d_in = w_first.shape[0]
    cols = nodes + ghosts
    rows = send_rows.reshape(parts, each)
    turn = VMEM((128, 128), jnp.int32)
    pick = VMEM((ghosts, nodes), bf16)
    axes = ("dom", "grp")
    members = lax.axis_size(axes)
    few = members <= FEW and parts <= 8
    copies = members if few else 1

    def every(value, *names):
        for name in names:
            value = lax.all_gather(value, name, axis=0, tiled=True)
        return value

    start0, out0 = call(
        first_kernel,
        16,
        [((nodes, width), bf16, None), ((parts, each, width), bf16, None)],
        [(feats, HBM), (send_rows, HBM)],
        [VMEM((nodes, width), bf16), VMEM((parts, each), jnp.int32), turn, pick, DMA((2,))],
    )
    table0 = lax.all_to_all(out0, "dom", split_axis=0, concat_axis=0, tiled=True)
    own, ghost, part1, flag, own_rest, ghost_rest = call(
        build_kernel,
        28,
        [
            ((nodes, nodes), bf16, HBM),
            ((nodes, ghosts), bf16, None),
            ((nodes, width), f32, None),
            ((1,), jnp.int32, SMEM),
            ((nodes, nodes), bf16, HBM),
            ((nodes, ghosts), bf16, HBM),
        ],
        [
            (tile_block, SMEM),
            (tile_count, SMEM),
            (tile_src, HBM),
            (tile_dst, HBM),
            (hop_noise, HBM),
            (start0, None),
        ],
        [
            VMEM((tiles, slots), jnp.int32),
            VMEM((tiles, slots), jnp.int32),
            VMEM((nodes, width), bf16),
            VMEM((tiles, slots, 128), bf16),
            VMEM((tiles * 16, slots), bf16),
            VMEM((tiles * 16, slots), bf16),
            VMEM((nodes, cols), f32),
            VMEM((nodes, max(nodes, ghosts)), bf16),
            VMEM((nodes, nodes), bf16),
            DMA((4,)),
        ],
    )
    start1, out1, side = call(
        hop_kernel,
        16,
        [
            ((nodes, width), bf16, None),
            ((parts, each, width), bf16, None),
            ((2 * train + 16, width), bf16, None),
        ],
        [
            (flag, SMEM),
            (part1, None),
            (ghost, None),
            (ghost_rest, HBM),
            (table0, None),
            (rows, VMEM),
            (start0, None),
            (labels.reshape(1, train), VMEM),
        ],
        [VMEM((nodes, width), f32), VMEM((nodes, ghosts), bf16), turn, pick],
    )
    table1 = lax.all_to_all(out1, "dom", split_axis=0, concat_axis=0, tiled=True)
    (part2,) = call(
        own_kernel,
        16,
        [((nodes, width), f32, None)],
        [(flag, SMEM), (own, HBM), (own_rest, HBM), (hop_noise, HBM), (start1, None)],
        [
            VMEM((nodes, nodes), bf16),
            VMEM((nodes, width), bf16),
            VMEM((nodes, nodes), bf16),
            DMA((2,)),
        ],
    )
    place = jnp.stack([lax.axis_index("dom"), lax.axis_index("grp")]).astype(jnp.int32)
    grp = lax.axis_size("grp")

    def shifted(value, name, size, step):
        return [
            lax.ppermute(value, name, [((at + step * shift) % size, at) for at in range(size)])
            for shift in range(1, size)
        ]

    sides = [side] + (shifted(side, "grp", grp, 1) if few else [])
    last, token = call(
        train_kernel,
        12,
        [((copies, train, width), bf16, None), ((8, 128), f32, None)],
        [(flag, SMEM), (part2, None), (ghost, None), (ghost_rest, HBM), (table1, None)],
        [VMEM((train, width), f32), VMEM((train, ghosts), bf16)],
    )
    if few:
        every2 = lax.all_to_all(last, axes, split_axis=0, concat_axis=0, tiled=True)
    else:
        every0, every1, every2 = (
            every(value, axes) for value in (start0[None, :train], start1[None, :train], last)
        )
        every_label = every(labels.reshape(1, train), axes)
    hop_feats, side = call(
        last_kernel,
        12,
        [
            ((2, 1, 1, nodes, width), bf16, VMEM),
            ((len(sides) * 2 * train + 16, width), bf16, None),
        ],
        [
            (flag, SMEM),
            (place, SMEM),
            (token, None),
            (part2, None),
            (ghost, None),
            (ghost_rest, HBM),
            (table1, None),
            (start1, None),
        ]
        + [(value, None) for value in sides],
        [VMEM((nodes, width), f32), VMEM((nodes, ghosts), bf16), VMEM((128, 128), f32)],
    )
    sides = [side] + (shifted(side, "dom", parts, -1) if few else [])
    chunk = train * min(members, 32)
    groups = chunk // train
    wide = (classes + 255) // 256 * 256
    fixed = (w_first, w_second, w_third.T, noise_first, noise_second, noise_third.T)
    scratch = [VMEM(value.shape, value.dtype) for value in fixed]
    scratch += [
        VMEM((chunk, d_in), bf16),
        VMEM((wide, hid), bf16),
        VMEM((128, 128), f32),
        VMEM((chunk, 128), jnp.int32),
        VMEM((chunk, hid), bf16),
        VMEM((chunk, hid), bf16),
        VMEM((chunk, hid), f32),
        VMEM((chunk, hid), f32),
        VMEM((chunk, hid), bf16),
        VMEM((chunk, hid), bf16),
        DMA((6,)),
    ]
    if few:

        def classify(place_ref, *refs):
            sides_in, rest = refs[:parts], refs[parts:]
            classify_kernel(False, place_ref, None, None, None, rest[0], sides_in, *rest[1:])

        first, second, third = call(
            classify,
            44,
            [(value.shape, f32, VMEM) for value in fixed[3:]],
            [(place, SMEM)]
            + [(value, None) for value in sides]
            + [(every2, None)]
            + [(value, HBM) for value in fixed],
            scratch,
        )
    else:

        ins = (every_label, every0, every1, every2)

        def classify(place_ref, label_ref, zero_ref, one_ref, two_ref, *rest):
            classify_kernel(
                True, place_ref, label_ref, zero_ref, one_ref, two_ref, None, *rest
            )

        def whole(value):
            return pl.BlockSpec(value.shape, lambda i: (0, 0))

        def piece(value):
            return pl.BlockSpec(
                (groups,) + value.shape[1:], lambda i: (i,) + (0,) * (value.ndim - 1)
            )

        first, second, third = pl.pallas_call(
            classify,
            grid=(members // groups,),
            out_shape=[jax.ShapeDtypeStruct(value.shape, f32) for value in fixed[3:]],
            in_specs=[pl.BlockSpec(memory_space=SMEM)]
            + [piece(value) for value in ins]
            + [pl.BlockSpec(memory_space=HBM) for value in fixed],
            out_specs=[whole(value) for value in fixed[3:]],
            scratch_shapes=scratch,
            compiler_params=params(56),
        )(place, *ins, *fixed)
    return (hop_feats, first, second, third.T)


def solution(mesh):
    in_specs = (
        P("dom", "grp", None, None),
        P(None, "dom", "grp", None, None),
        P("dom", "grp", None, None),
        P("dom", "grp", None),
        P("dom", "grp", None, None),
        P("dom", "grp", None, None),
        P("dom", "grp"),
        P("dom", "grp", None),
        P(),
        P(),
        P(),
        P("dom", None),
        P("dom", None),
        P("dom", None),
    )
    out_specs = (P(None, "dom", "grp", None, None), P("dom", None), P("dom", None), P("dom", None))
    return jax.shard_map(local, mesh=mesh, in_specs=in_specs, out_specs=out_specs, check_vma=False)
```

```python
import functools

import jax
import jax.numpy as jnp
from jax import lax
from jax.experimental import pallas as pl
from jax.experimental.pallas import tpu as pltpu
from jax.sharding import PartitionSpec as P

BLOCK = 128
LOW = 512
GROUP = 4
clip_bound = 4.0
noise_mult = 1.0

f32 = jnp.float32
bf16 = jnp.bfloat16
VMEM = pltpu.VMEM
SMEM = pltpu.SMEM
HBM = pltpu.HBM
DMA = pltpu.SemaphoreType.DMA


FEW = 32


def params(mib):
    return pltpu.CompilerParams(vmem_limit_bytes=mib * 1024 * 1024)


def fetch(pairs, sems):
    copies = [pltpu.make_async_copy(*pair, sems.at[at]) for at, pair in enumerate(pairs)]
    for copy in copies:
        copy.start()
    return copies


def normalize(values):
    return (values * lax.rsqrt(jnp.sum(values * values, -1, keepdims=True) + 1e-06)).astype(bf16)


def dot(left, right):
    return jnp.dot(left, right, preferred_element_type=f32)


def dot_nt(left, right):
    return lax.dot_general(left, right, (((1,), (1,)), ((), ())), preferred_element_type=f32)


def dot_tn(left, right):
    return lax.dot_general(left, right, (((0,), (0,)), ((), ())), preferred_element_type=f32)


def send(start, rows_ref, out_ref, turn_ref, pick_ref):
    parts, each = rows_ref.shape
    nodes = start.shape[0]
    turn_ref[:parts, :each] = rows_ref[...]
    columns = turn_ref[...].T
    spots = lax.broadcasted_iota(jnp.int32, (each, nodes), 1)
    for part in range(parts):
        wanted = columns[:each, part : part + 1]
        pick_ref[part * each : (part + 1) * each, :] = jnp.where(wanted == spots, 1.0, 0.0).astype(
            bf16
        )
    out = dot(pick_ref[...], start).astype(bf16)
    out_ref[...] = out.reshape(out_ref.shape)


def spread(rows, out_ref):
    out_ref[...] = jnp.broadcast_to(rows[None], out_ref.shape)


def first_kernel(
    feats_hbm,
    rows_hbm,
    start_ref,
    out_ref,
    own_ref,
    feats_ref,
    rows_ref,
    turn_ref,
    pick_ref,
    sems,
):
    copies = fetch(
        ((feats_hbm.at[0, 0], feats_ref), (rows_hbm.at[0, 0], rows_ref)), sems
    )
    for copy in copies:
        copy.wait()
    start = normalize(feats_ref[...].astype(f32))
    start_ref[...] = start
    own_ref[...] = start[: own_ref.shape[0]]
    send(start, rows_ref, out_ref, turn_ref, pick_ref)


def build_kernel(
    blocks_ref,
    count_ref,
    src_hbm,
    dst_hbm,
    noise_hbm,
    start_ref,
    own_hbm,
    ghost_ref,
    part_ref,
    flag_ref,
    own_rest_ref,
    ghost_rest_ref,
    src_ref,
    dst_ref,
    noise_ref,
    low_ref,
    high_ref,
    spot_ref,
    sums_ref,
    rest_ref,
    own_ref,
    sems,
):
    copies = fetch(
        (
            (src_hbm.at[0, 0], src_ref),
            (dst_hbm.at[0, 0], dst_ref),
            (noise_hbm.at[0, 0, 0], noise_ref),
        ),
        sems,
    )
    nodes, cols = sums_ref.shape
    pieces = -(-cols // LOW)
    tiles, slots = src_ref.shape
    count = count_ref[0, 0]
    own_ref[...] = jnp.zeros_like(own_ref)
    ghost_ref[...] = jnp.zeros_like(ghost_ref)
    for copy in copies:
        copy.wait()

    def sixteen(values):
        wide = jnp.broadcast_to(values.astype(f32)[:, None, :], (tiles, 16, slots))
        return wide.reshape(tiles * 16, slots).astype(bf16)

    src = src_ref[...]
    dst = dst_ref[...]
    tile_ids = lax.broadcasted_iota(jnp.int32, (tiles, slots), 0)
    high_ref[...] = sixteen(src // LOW)
    spot_ref[...] = sixteen(jnp.where((dst < BLOCK) & (tile_ids < count), dst, -1))
    low = (src % LOW - LOW // 2).astype(f32).T
    for tile in range(tiles):
        low_ref[tile] = jnp.broadcast_to(low[:, tile : tile + 1], (slots, 128)).astype(bf16)
    ids = lax.broadcasted_iota(jnp.int32, (BLOCK, slots), 0).astype(f32).astype(bf16)
    lanes = lax.broadcasted_iota(jnp.int32, (slots, 128), 1).astype(f32)
    lanes = [(lanes + first).astype(bf16) for first in range(-LOW // 2, LOW // 2, 128)]
    one = jnp.ones((), bf16)
    zero = jnp.zeros((), bf16)

    def turn(add, step, carry):
        for inner in range(GROUP):
            tile = step * GROUP + inner
            rows = pl.ds(pl.multiple_of(tile * 16, 16), 16)
            high, spot = high_ref[rows, :], spot_ref[rows, :]
            spots = []
            for piece in range(pieces):
                wanted = jnp.where(high == piece, spot, -one)
                tall = jnp.concatenate([wanted] * (BLOCK // 16), 0)
                spots.append(jnp.where(ids == tall, one, zero))
            low = low_ref[tile]
            low_hot = jnp.concatenate([jnp.where(low == ids, one, zero) for ids in lanes], 1)
            out = dot(jnp.concatenate(spots, 0), low_hot)
            base = pl.multiple_of(blocks_ref[0, 0, tile] * BLOCK, BLOCK)
            for piece in range(pieces):
                add(pl.ds(base, BLOCK), piece * LOW, out[piece * BLOCK : (piece + 1) * BLOCK])
        return carry

    def add_short(rows, at, values):
        ref, at = (own_ref, at) if at < nodes else (ghost_ref, at - nodes)
        size = min(LOW, ref.shape[1] - at)
        ref[rows, at : at + size] += values[:, :size].astype(bf16)

    def add_long(rows, at, values):
        size = min(LOW, cols - at)
        sums_ref[rows, at : at + size] += values[:, :size]

    steps = (count + GROUP - 1) // GROUP
    lax.fori_loop(0, steps, functools.partial(turn, add_short), 0)
    top = ghost_ref[:BLOCK, :256]
    for first in range(0, nodes, BLOCK):
        for ref in (own_ref, ghost_ref):
            for at in range(0, ref.shape[1], 256):
                top = jnp.maximum(top, ref[first : first + BLOCK, at : at + 256])
    big = jnp.max(top.astype(f32)) >= 256.0
    flag_ref[0] = big.astype(jnp.int32)

    @pl.when(big)
    def _():
        sums_ref[...] = jnp.zeros_like(sums_ref)
        lax.fori_loop(0, steps, functools.partial(turn, add_long), 0)
        own_ref[...] = sums_ref[:, :nodes].astype(bf16)
        ghost_ref[...] = sums_ref[:, nodes:].astype(bf16)

    own_copy = pltpu.make_async_copy(own_ref, own_hbm, sems.at[3])
    own_copy.start()
    part_ref[...] = dot(own_ref[...], start_ref[...]) + noise_ref[...].astype(f32)

    @pl.when(big)
    def _():
        own_rest = (sums_ref[:, :nodes] - own_ref[...].astype(f32)).astype(bf16)
        part_ref[...] += dot(own_rest, start_ref[...])
        rest_ref[:, :nodes] = own_rest
        pltpu.sync_copy(rest_ref.at[:, :nodes], own_rest_ref)
        rest_ref[:, : cols - nodes] = (sums_ref[:, nodes:] - ghost_ref[...].astype(f32)).astype(bf16)
        pltpu.sync_copy(rest_ref.at[:, : cols - nodes], ghost_rest_ref)

    own_copy.wait()


def aggregate(flag_ref, part_ref, count_ref, rest_hbm, table, sums_ref, rest_ref):
    rows = sums_ref.shape[0]
    sums_ref[...] = part_ref.astype(f32) + dot(count_ref, table)

    @pl.when(flag_ref[0] > 0)
    def _():
        pltpu.sync_copy(rest_hbm.at[:rows], rest_ref)
        sums_ref[...] += dot(rest_ref[...], table)


def hop_kernel(
    flag_ref,
    part_ref,
    ghost_ref,
    rest_hbm,
    table_ref,
    rows_ref,
    old_ref,
    labels_ref,
    start_ref,
    out_ref,
    side_ref,
    sums_ref,
    rest_ref,
    turn_ref,
    pick_ref,
):
    width = start_ref.shape[1]
    table = table_ref[...].reshape(-1, width)
    aggregate(flag_ref, part_ref[...], ghost_ref[...], rest_hbm, table, sums_ref, rest_ref)
    start = normalize(sums_ref[...])
    start_ref[...] = start
    send(start, rows_ref, out_ref, turn_ref, pick_ref)
    train = labels_ref.shape[1]
    side_ref[:train, :] = old_ref[...]
    side_ref[train : 2 * train, :] = start[:train]
    turn_ref[:1, :train] = labels_ref[...]
    side_ref[2 * train :, :128] = turn_ref[:16, :].astype(f32).astype(bf16)


def own_kernel(
    flag_ref, own_hbm, rest_hbm, noise_hbm, start_ref, part_ref, own_ref, noise_ref, rest_ref, sems
):
    copies = fetch(((own_hbm, own_ref), (noise_hbm.at[1, 0, 0], noise_ref)), sems)
    for copy in copies:
        copy.wait()
    start = start_ref[...]
    noise = noise_ref[...].astype(f32)
    aggregate(flag_ref, noise, own_ref[...], rest_hbm, start, part_ref, rest_ref)


def train_kernel(flag_ref, place_ref, part_ref, ghost_ref, rest_hbm, table_ref, *refs):
    *piece_refs, out_ref, side_ref, sums_ref, rest_ref, turn_ref = refs
    train, width = sums_ref.shape
    table = table_ref[...].reshape(-1, width)
    aggregate(
        flag_ref, part_ref[:train], ghost_ref[:train], rest_hbm, table, sums_ref, rest_ref
    )
    spread(normalize(sums_ref[...]), out_ref)
    length = piece_refs[0].shape[0] - 16
    groups = len(piece_refs)
    if groups > 1:
        for shift, ref in enumerate(piece_refs):
            group = lax.rem(place_ref[1] + shift, groups)
            at = pl.multiple_of(group * length, length)
            side_ref[pl.ds(at, length), :] = ref[:length, :]
            turn_ref[pl.ds(group, 1), :] = ref[length:, :128].astype(f32)[:1]
        side_ref[groups * length :, :128] = turn_ref[:16, :].astype(bf16)


def last_kernel(
    flag_ref,
    token_ref,
    part_ref,
    ghost_ref,
    rest_hbm,
    table_ref,
    start_ref,
    out_ref,
    sums_ref,
    rest_ref,
):
    table = table_ref[...].reshape(-1, out_ref.shape[-1])
    aggregate(flag_ref, part_ref[...], ghost_ref[...], rest_hbm, table, sums_ref, rest_ref)
    out_ref[0, 0, 0] = start_ref[...]
    out_ref[1, 0, 0] = normalize(sums_ref[...])


def shares(ref, first, share):
    if share % 128 == 0:
        return ref[:, pl.ds(pl.multiple_of(first, 128), share)].astype(f32)
    length = ref.shape[1]
    rows = lax.broadcasted_iota(jnp.int32, (length, share), 0)
    cols = lax.broadcasted_iota(jnp.int32, (length, share), 1)
    return dot(ref[...], jnp.where(rows == cols + first, 1.0, 0.0).astype(bf16))


def lanes_sum(values):
    total = None
    for piece in range(values.shape[1] // 128):
        part = values[:, piece * 128 : (piece + 1) * 128].astype(f32)
        total = part * part if total is None else total + part * part
    return total


def classify_kernel(
    many,
    place_ref,
    label_ref,
    zero_ref,
    one_ref,
    two_ref,
    side_refs,
    w_first_hbm,
    w_second_hbm,
    w_third_hbm,
    n_first_hbm,
    n_second_hbm,
    n_third_hbm,
    g_first_ref,
    g_second_ref,
    g_third_ref,
    w_first_ref,
    w_second_ref,
    w_third_ref,
    n_first_ref,
    n_second_ref,
    n_third_ref,
    in_ref,
    w_third_pad_ref,
    turn_ref,
    column_ref,
    h_one_ref,
    h_two_ref,
    slope_one_ref,
    slope_two_ref,
    d_one_ref,
    d_two_ref,
    sems,
):
    classes = w_third_ref.shape[0]
    hid = w_second_ref.shape[0]
    width = two_ref.shape[2]
    wide = w_third_pad_ref.shape[0]
    train = two_ref.shape[1]
    scale = noise_mult * clip_bound
    place = place_ref[0]
    pairs = (
        (w_first_hbm, w_first_ref),
        (w_second_hbm, w_second_ref),
        (w_third_hbm, w_third_ref),
        (n_first_hbm, n_first_ref),
        (n_second_hbm, n_second_ref),
        (n_third_hbm, n_third_ref),
    )

    def set_noise():
        g_first_ref[...] = scale * n_first_ref[...]
        g_second_ref[...] = scale * n_second_ref[...]
        g_third_ref[...] = scale * n_third_ref[...]

    def pad():
        w_third_pad_ref[...] = jnp.zeros_like(w_third_pad_ref)
        w_third_pad_ref[:classes, :] = w_third_ref[...]

    def column(row, turned, lane):
        column_ref[row : row + train, :] = jnp.broadcast_to(
            turned[:train, lane : lane + 1], (train, 128)
        ).astype(jnp.int32)

    if many:

        @pl.when(pl.program_id(0) == 0)
        def _():
            for copy in fetch(pairs, sems):
                copy.wait()
            set_noise()
            pad()

        groups = label_ref.shape[0]
        turn_ref[:groups, :train] = label_ref[...].astype(f32)
        turned = turn_ref[...].T
        for group in range(groups):
            column(group * train, turned, group)
        for hop, ref in enumerate((zero_ref, one_ref)):
            in_ref[:, hop * width : (hop + 1) * width] = ref[...].reshape(-1, width)
    else:
        copies = fetch(pairs[:1], sems)
        parts = len(side_refs)
        groups = two_ref.shape[0] // parts
        rows = groups * train
        chips = parts // 2
        for at, ref in enumerate(side_refs):
            core = place % 2 if at < chips else 1 - place % 2
            part = 2 * lax.rem(place // 2 - at % chips + chips, chips) + core
            at = pl.multiple_of(part * rows, rows)
            for group in range(groups):
                for hop in range(2):
                    first = (2 * group + hop) * train
                    in_ref[pl.ds(at + group * train, train), hop * width : (hop + 1) * width] = ref[
                        first : first + train, :
                    ]
            turn_ref[pl.ds(pl.multiple_of(part * 16, 16), 16), :] = ref[2 * rows :, :128].astype(f32)
        turned = turn_ref[...].T
        for part in range(parts):
            for group in range(groups):
                column((part * groups + group) * train, turned, part * 16 + group)
    in_ref[:, 2 * width :] = two_ref[...].reshape(-1, width)
    if not many:
        copies[0].wait()
        copies = fetch(pairs[1:], sems)

    def activate(values, h_ref, slope_ref, cols):
        sigma = 0.5 + 0.5 * jnp.tanh(0.5 * values)
        out = values * sigma
        slope_ref[:, cols] = sigma + out * (1.0 - sigma)
        rounded = out.astype(bf16)
        h_ref[:, cols] = rounded
        return lanes_sum(rounded)

    step = 512
    cuts = [slice(at, at + step) for at in range(0, hid, step)]
    sq_in = lanes_sum(in_ref[...])
    sq_one = sum(
        activate(dot(in_ref[...], w_first_ref[:, cut]), h_one_ref, slope_one_ref, cut)
        for cut in cuts
    )
    if not many:
        copies[0].wait()
    sq_two = sum(
        activate(dot(h_one_ref[...], w_second_ref[:, cut]), h_two_ref, slope_two_ref, cut)
        for cut in cuts
    )
    if not many:
        copies[1].wait()
        pad()
    logits = dot_nt(h_two_ref[...], w_third_pad_ref[...])
    ids = lax.broadcasted_iota(jnp.int32, (logits.shape[0], wide), 1)
    expo = jnp.where(ids < classes, jnp.exp(logits), 0.0)
    probs = expo / jnp.sum(expo, -1, keepdims=True)
    label = column_ref[:, :1]
    d_three = (probs - jnp.where(ids == label, 1.0, 0.0)).astype(bf16)
    sq_dthree = lanes_sum(d_three)

    def back(values, slope_ref, d_ref, cut):
        rounded = (values * slope_ref[:, cut]).astype(bf16)
        d_ref[:, cut] = rounded
        return lanes_sum(rounded)

    sq_dtwo = sum(
        back(dot(d_three, w_third_pad_ref[:, cut]), slope_two_ref, d_two_ref, cut)
        for cut in cuts
    )
    sq_done = sum(
        back(dot_nt(d_two_ref[...], w_second_ref[cut, :]), slope_one_ref, d_one_ref, cut)
        for cut in cuts
    )

    def total(values):
        return jnp.sum(values, -1, keepdims=True)

    norm = jnp.sqrt(
        total(sq_in) * total(sq_done)
        + total(sq_one) * total(sq_dtwo)
        + total(sq_two) * total(sq_dthree)
    )
    factor = clip_bound / jnp.maximum(norm, clip_bound)

    def left(ref, share):
        return (shares(ref, place * share, share) * factor).astype(bf16)

    if not many:
        for copy in copies[2:]:
            copy.wait()
        set_noise()
    share = g_second_ref.shape[0]
    g_first_ref[...] += dot_tn(left(in_ref, g_first_ref.shape[0]), d_one_ref[...])
    g_second_ref[...] += dot_tn(left(h_one_ref, share), d_two_ref[...])
    g_third_ref[...] += dot_tn(d_three, left(h_two_ref, share))[:classes, :]


def call(kernel, mib, outs, ins, scratch):
    def shape_of(shape, dtype, space):
        if space is None or space is HBM:
            return (space or VMEM)(shape, dtype)
        return jax.ShapeDtypeStruct(shape, dtype)

    def block(space):
        return pl.BlockSpec(memory_space=VMEM if space is None else space)

    def held(value, space):
        if space is None or space is HBM:
            return pltpu.with_memory_space_constraint(value, space or VMEM)
        return value

    return pl.pallas_call(
        kernel,
        out_shape=[shape_of(*out) for out in outs],
        in_specs=[block(space) for _, space in ins],
        out_specs=[block(space) for _, _, space in outs],
        scratch_shapes=scratch,
        compiler_params=params(mib),
    )(*[held(value, space) for value, space in ins])


def local(
    feats,
    hop_noise,
    send_rows,
    tile_block,
    tile_src,
    tile_dst,
    tile_count,
    labels,
    w_first,
    w_second,
    w_third,
    noise_first,
    noise_second,
    noise_third,
):
    nodes, width = feats.shape[2:]
    parts, each = send_rows.shape[2:]
    ghosts = parts * each
    tiles = tile_src.shape[2]
    slots = tile_src.shape[3]
    train = labels.shape[2]
    classes = w_third.shape[1]
    hid = w_second.shape[0]
    d_in = w_first.shape[0]
    cols = nodes + ghosts
    rows = send_rows.reshape(parts, each)
    turn = VMEM((128, 128), jnp.int32)
    pick = VMEM((ghosts, nodes), bf16)
    axes = ("dom", "grp")
    members = lax.axis_size(axes)
    few = members <= FEW and parts <= 8 and parts % 2 == 0
    copies = members if few else 1

    def every(value, *names):
        for name in names:
            value = lax.all_gather(value, name, axis=0, tiled=True)
        return value

    start0, out0, own0 = call(
        first_kernel,
        16,
        [
            ((nodes, width), bf16, None),
            ((parts, each, width), bf16, None),
            ((train, width), bf16, None),
        ],
        [(feats, HBM), (send_rows, HBM)],
        [VMEM((nodes, width), bf16), VMEM((parts, each), jnp.int32), turn, pick, DMA((2,))],
    )
    table0 = lax.all_to_all(out0, "dom", split_axis=0, concat_axis=0, tiled=True)
    own, ghost, part1, flag, own_rest, ghost_rest = call(
        build_kernel,
        28,
        [
            ((nodes, nodes), bf16, HBM),
            ((nodes, ghosts), bf16, None),
            ((nodes, width), f32, None),
            ((1,), jnp.int32, SMEM),
            ((nodes, nodes), bf16, HBM),
            ((nodes, ghosts), bf16, HBM),
        ],
        [
            (tile_block, SMEM),
            (tile_count, SMEM),
            (tile_src, HBM),
            (tile_dst, HBM),
            (hop_noise, HBM),
            (start0, None),
        ],
        [
            VMEM((tiles, slots), jnp.int32),
            VMEM((tiles, slots), jnp.int32),
            VMEM((nodes, width), bf16),
            VMEM((tiles, slots, 128), bf16),
            VMEM((tiles * 16, slots), bf16),
            VMEM((tiles * 16, slots), bf16),
            VMEM((nodes, cols), f32),
            VMEM((nodes, max(nodes, ghosts)), bf16),
            VMEM((nodes, nodes), bf16),
            DMA((4,)),
        ],
    )
    start1, out1, side = call(
        hop_kernel,
        16,
        [
            ((nodes, width), bf16, None),
            ((parts, each, width), bf16, None),
            ((2 * train + 16, width), bf16, None),
        ],
        [
            (flag, SMEM),
            (part1, None),
            (ghost, None),
            (ghost_rest, HBM),
            (table0, None),
            (rows, VMEM),
            (own0, None),
            (labels.reshape(1, train), VMEM),
        ],
        [VMEM((nodes, width), f32), VMEM((nodes, ghosts), bf16), turn, pick],
    )
    table1 = lax.all_to_all(out1, "dom", split_axis=0, concat_axis=0, tiled=True)
    (part2,) = call(
        own_kernel,
        16,
        [((nodes, width), f32, None)],
        [(flag, SMEM), (own, HBM), (own_rest, HBM), (hop_noise, HBM), (start1, None)],
        [
            VMEM((nodes, nodes), bf16),
            VMEM((nodes, width), bf16),
            VMEM((nodes, nodes), bf16),
            DMA((2,)),
        ],
    )
    place = jnp.stack([lax.axis_index("dom"), lax.axis_index("grp")]).astype(jnp.int32)
    grp = lax.axis_size("grp")

    def shifted(value, name, size, step):
        return [
            lax.ppermute(value, name, [((at + step * shift) % size, at) for at in range(size)])
            for shift in range(1, size)
        ]

    sides = [side] + (shifted(side, "grp", grp, 1) if few else [])
    last, side = call(
        train_kernel,
        12,
        [
            ((copies, train, width), bf16, None),
            ((len(sides) * 2 * train + 16, width), bf16, None),
        ],
        [
            (flag, SMEM),
            (place, SMEM),
            (part2, None),
            (ghost, None),
            (ghost_rest, HBM),
            (table1, None),
        ]
        + [(value, None) for value in sides],
        [VMEM((train, width), f32), VMEM((train, ghosts), bf16), VMEM((128, 128), f32)],
    )
    if few:
        every2 = lax.all_to_all(last, axes, split_axis=0, concat_axis=0, tiled=True)
        chips = parts // 2
        sides = [side]
        for shift in range(1, chips):
            pairs = [
                (2 * ((chip - shift) % chips) + core, 2 * chip + core)
                for chip in range(chips)
                for core in range(2)
            ]
            sides.append(lax.ppermute(side, "dom", pairs))
        swap = [(at, at ^ 1) for at in range(parts)]
        sides += [lax.ppermute(value, "dom", swap) for value in sides]
    else:
        every0, every1, every2 = (
            every(value, axes) for value in (own0[None], start1[None, :train], last)
        )
        every_label = every(labels.reshape(1, train), axes)
    (hop_feats,) = call(
        last_kernel,
        12,
        [((2, 1, 1, nodes, width), bf16, VMEM)],
        [
            (flag, SMEM),
            (side, None),
            (part2, None),
            (ghost, None),
            (ghost_rest, HBM),
            (table1, None),
            (start1, None),
        ],
        [VMEM((nodes, width), f32), VMEM((nodes, ghosts), bf16)],
    )
    chunk = train * min(members, 32)
    groups = chunk // train
    wide = (classes + 255) // 256 * 256
    fixed = (w_first, w_second, w_third.T, noise_first, noise_second, noise_third.T)
    scratch = [VMEM(value.shape, value.dtype) for value in fixed]
    scratch += [
        VMEM((chunk, d_in), bf16),
        VMEM((wide, hid), bf16),
        VMEM((128, 128), f32),
        VMEM((chunk, 128), jnp.int32),
        VMEM((chunk, hid), bf16),
        VMEM((chunk, hid), bf16),
        VMEM((chunk, hid), f32),
        VMEM((chunk, hid), f32),
        VMEM((chunk, hid), bf16),
        VMEM((chunk, hid), bf16),
        DMA((6,)),
    ]
    if few:

        def classify(place_ref, *refs):
            sides_in, rest = refs[:parts], refs[parts:]
            classify_kernel(False, place_ref, None, None, None, rest[0], sides_in, *rest[1:])

        first, second, third = call(
            classify,
            44,
            [(value.shape, f32, VMEM) for value in fixed[3:]],
            [(place, SMEM)]
            + [(value, None) for value in sides]
            + [(every2, None)]
            + [(value, HBM) for value in fixed],
            scratch,
        )
    else:

        ins = (every_label, every0, every1, every2)

        def classify(place_ref, label_ref, zero_ref, one_ref, two_ref, *rest):
            classify_kernel(
                True, place_ref, label_ref, zero_ref, one_ref, two_ref, None, *rest
            )

        def whole(value):
            return pl.BlockSpec(value.shape, lambda i: (0, 0))

        def piece(value):
            return pl.BlockSpec(
                (groups,) + value.shape[1:], lambda i: (i,) + (0,) * (value.ndim - 1)
            )

        first, second, third = pl.pallas_call(
            classify,
            grid=(members // groups,),
            out_shape=[jax.ShapeDtypeStruct(value.shape, f32) for value in fixed[3:]],
            in_specs=[pl.BlockSpec(memory_space=SMEM)]
            + [piece(value) for value in ins]
            + [pl.BlockSpec(memory_space=HBM) for value in fixed],
            out_specs=[whole(value) for value in fixed[3:]],
            scratch_shapes=scratch,
            compiler_params=params(56),
        )(place, *ins, *fixed)
    return (hop_feats, first, second, third.T)


def solution(mesh):
    in_specs = (
        P("dom", "grp", None, None),
        P(None, "dom", "grp", None, None),
        P("dom", "grp", None, None),
        P("dom", "grp", None),
        P("dom", "grp", None, None),
        P("dom", "grp", None, None),
        P("dom", "grp"),
        P("dom", "grp", None),
        P(),
        P(),
        P(),
        P("dom", None),
        P("dom", None),
        P("dom", None),
    )
    out_specs = (P(None, "dom", "grp", None, None), P("dom", None), P("dom", None), P("dom", None))
    return jax.shard_map(local, mesh=mesh, in_specs=in_specs, out_specs=out_specs, check_vma=False)
```

```python
import functools

import jax
import jax.numpy as jnp
from jax import lax
from jax.experimental import pallas as pl
from jax.experimental.pallas import tpu as pltpu
from jax.sharding import PartitionSpec as P

BLOCK = 128
LOW = 256
GROUP = 4
clip_bound = 4.0
noise_mult = 1.0

f32 = jnp.float32
bf16 = jnp.bfloat16
VMEM = pltpu.VMEM
SMEM = pltpu.SMEM
HBM = pltpu.HBM
DMA = pltpu.SemaphoreType.DMA


FEW = 32


def params(mib):
    return pltpu.CompilerParams(vmem_limit_bytes=mib * 1024 * 1024)


def fetch(pairs, sems):
    copies = [pltpu.make_async_copy(*pair, sems.at[at]) for at, pair in enumerate(pairs)]
    for copy in copies:
        copy.start()
    return copies


def normalize(values):
    return (values * lax.rsqrt(jnp.sum(values * values, -1, keepdims=True) + 1e-06)).astype(bf16)


def dot(left, right):
    return jnp.dot(left, right, preferred_element_type=f32)


def dot_nt(left, right):
    return lax.dot_general(left, right, (((1,), (1,)), ((), ())), preferred_element_type=f32)


def dot_tn(left, right):
    return lax.dot_general(left, right, (((0,), (0,)), ((), ())), preferred_element_type=f32)


def send(start, rows_ref, out_ref, turn_ref, pick_ref):
    parts, each = rows_ref.shape
    nodes = start.shape[0]
    turn_ref[:parts, :each] = rows_ref[...]
    columns = turn_ref[...].T
    spots = lax.broadcasted_iota(jnp.int32, (each, nodes), 1)
    for part in range(parts):
        wanted = columns[:each, part : part + 1]
        pick_ref[part * each : (part + 1) * each, :] = jnp.where(wanted == spots, 1.0, 0.0).astype(
            bf16
        )
    out = dot(pick_ref[...], start).astype(bf16)
    out_ref[...] = out.reshape(out_ref.shape)


def spread(rows, out_ref):
    out_ref[...] = jnp.broadcast_to(rows[None], out_ref.shape)


def first_kernel(
    feats_hbm,
    rows_hbm,
    start_ref,
    out_ref,
    own_ref,
    feats_ref,
    rows_ref,
    turn_ref,
    pick_ref,
    sems,
):
    copies = fetch(
        ((feats_hbm.at[0, 0], feats_ref), (rows_hbm.at[0, 0], rows_ref)), sems
    )
    for copy in copies:
        copy.wait()
    start = normalize(feats_ref[...].astype(f32))
    start_ref[...] = start
    own_ref[...] = start[: own_ref.shape[0]]
    send(start, rows_ref, out_ref, turn_ref, pick_ref)


def build_kernel(
    blocks_hbm,
    count_ref,
    src_hbm,
    dst_hbm,
    noise_hbm,
    start_ref,
    own_hbm,
    ghost_ref,
    part_ref,
    flag_ref,
    own_rest_ref,
    ghost_rest_ref,
    src_ref,
    dst_ref,
    noise_ref,
    low_ref,
    high_ref,
    spot_ref,
    sums_ref,
    rest_ref,
    own_ref,
    blocks_ref,
    sems,
):
    copies = fetch(
        (
            (blocks_hbm, blocks_ref),
            (src_hbm.at[0, 0], src_ref),
            (dst_hbm.at[0, 0], dst_ref),
            (noise_hbm.at[0, 0, 0], noise_ref),
        ),
        sems,
    )
    nodes, cols = sums_ref.shape
    pieces = -(-cols // LOW)
    tiles, slots = src_ref.shape
    count = count_ref[0, 0]
    own_ref[...] = jnp.zeros_like(own_ref)
    ghost_ref[...] = jnp.zeros_like(ghost_ref)
    for copy in copies:
        copy.wait()

    def sixteen(values):
        wide = jnp.broadcast_to(values.astype(f32)[:, None, :], (tiles, 16, slots))
        return wide.reshape(tiles * 16, slots).astype(bf16)

    src = src_ref[...]
    dst = dst_ref[...]
    tile_ids = lax.broadcasted_iota(jnp.int32, (tiles, slots), 0)
    high_ref[...] = sixteen(src // LOW)
    spot_ref[...] = sixteen(jnp.where((dst < BLOCK) & (tile_ids < count), dst, -1))
    low = (src % LOW - LOW // 2).astype(f32).T
    for tile in range(tiles):
        low_ref[tile] = jnp.broadcast_to(low[:, tile : tile + 1], (slots, 128)).astype(bf16)
    ids = lax.broadcasted_iota(jnp.int32, (BLOCK, slots), 0).astype(f32).astype(bf16)
    lanes = lax.broadcasted_iota(jnp.int32, (slots, 128), 1).astype(f32)
    lanes = [(lanes + first).astype(bf16) for first in range(-LOW // 2, LOW // 2, 128)]
    one = jnp.ones((), bf16)
    zero = jnp.zeros((), bf16)

    def counts(tile):
        rows = pl.ds(pl.multiple_of(tile * 16, 16), 16)
        high, spot = high_ref[rows, :], spot_ref[rows, :]
        spots = []
        for piece in range(pieces):
            wanted = jnp.where(high == piece, spot, -one)
            tall = jnp.concatenate([wanted] * (BLOCK // 16), 0)
            spots.append(jnp.where(ids == tall, one, zero))
        low = low_ref[tile]
        low_hot = jnp.concatenate([jnp.where(low == ids, one, zero) for ids in lanes], 1)
        return dot(jnp.concatenate(spots, 0), low_hot)

    def turn(add, step, carry):
        first = step * GROUP
        outs = [counts(first + inner) for inner in range(GROUP)]
        for inner, out in enumerate(outs):
            base = pl.multiple_of(blocks_ref[0, 0, first + inner] * BLOCK, BLOCK)
            for piece in range(pieces):
                add(pl.ds(base, BLOCK), piece * LOW, out[piece * BLOCK : (piece + 1) * BLOCK])
        return carry

    def add_short(rows, at, values):
        ref, at = (own_ref, at) if at < nodes else (ghost_ref, at - nodes)
        size = min(LOW, ref.shape[1] - at)
        ref[rows, at : at + size] += values[:, :size].astype(bf16)

    def add_long(rows, at, values):
        size = min(LOW, cols - at)
        sums_ref[rows, at : at + size] += values[:, :size]

    steps = (count + GROUP - 1) // GROUP
    lax.fori_loop(0, steps, functools.partial(turn, add_short), 0)
    top = ghost_ref[:BLOCK, :256]
    for first in range(0, nodes, BLOCK):
        for ref in (own_ref, ghost_ref):
            for at in range(0, ref.shape[1], 256):
                top = jnp.maximum(top, ref[first : first + BLOCK, at : at + 256])
    big = jnp.max(top.astype(f32)) >= 256.0
    flag_ref[0] = big.astype(jnp.int32)

    @pl.when(big)
    def _():
        sums_ref[...] = jnp.zeros_like(sums_ref)
        lax.fori_loop(0, steps, functools.partial(turn, add_long), 0)
        own_ref[...] = sums_ref[:, :nodes].astype(bf16)
        ghost_ref[...] = sums_ref[:, nodes:].astype(bf16)

    own_copy = pltpu.make_async_copy(own_ref, own_hbm, sems.at[4])
    own_copy.start()
    part_ref[...] = dot(own_ref[...], start_ref[...]) + noise_ref[...].astype(f32)

    @pl.when(big)
    def _():
        own_rest = (sums_ref[:, :nodes] - own_ref[...].astype(f32)).astype(bf16)
        part_ref[...] += dot(own_rest, start_ref[...])
        rest_ref[:, :nodes] = own_rest
        pltpu.sync_copy(rest_ref.at[:, :nodes], own_rest_ref)
        rest_ref[:, : cols - nodes] = (sums_ref[:, nodes:] - ghost_ref[...].astype(f32)).astype(bf16)
        pltpu.sync_copy(rest_ref.at[:, : cols - nodes], ghost_rest_ref)

    own_copy.wait()


def aggregate(flag_ref, part_ref, count_ref, rest_hbm, table, sums_ref, rest_ref):
    rows = sums_ref.shape[0]
    sums_ref[...] = part_ref.astype(f32) + dot(count_ref, table)

    @pl.when(flag_ref[0] > 0)
    def _():
        pltpu.sync_copy(rest_hbm.at[:rows], rest_ref)
        sums_ref[...] += dot(rest_ref[...], table)


def hop_kernel(
    flag_ref,
    part_ref,
    ghost_ref,
    rest_hbm,
    table_ref,
    rows_ref,
    old_ref,
    labels_ref,
    start_ref,
    out_ref,
    side_ref,
    sums_ref,
    rest_ref,
    turn_ref,
    pick_ref,
):
    width = start_ref.shape[1]
    table = table_ref[...].reshape(-1, width)
    aggregate(flag_ref, part_ref[...], ghost_ref[...], rest_hbm, table, sums_ref, rest_ref)
    start = normalize(sums_ref[...])
    start_ref[...] = start
    send(start, rows_ref, out_ref, turn_ref, pick_ref)
    train = labels_ref.shape[1]
    side_ref[:train, :] = old_ref[...]
    side_ref[train : 2 * train, :] = start[:train]
    turn_ref[:1, :train] = labels_ref[...]
    side_ref[2 * train :, :128] = turn_ref[:16, :].astype(f32).astype(bf16)


def own_kernel(
    flag_ref, own_hbm, rest_hbm, noise_hbm, start_ref, part_ref, own_ref, noise_ref, rest_ref, sems
):
    copies = fetch(((own_hbm, own_ref), (noise_hbm.at[1, 0, 0], noise_ref)), sems)
    for copy in copies:
        copy.wait()
    start = start_ref[...]
    noise = noise_ref[...].astype(f32)
    aggregate(flag_ref, noise, own_ref[...], rest_hbm, start, part_ref, rest_ref)


def train_kernel(flag_ref, place_ref, part_ref, ghost_ref, rest_hbm, table_ref, *refs):
    *piece_refs, out_ref, side_ref, sums_ref, rest_ref, turn_ref = refs
    train, width = sums_ref.shape
    table = table_ref[...].reshape(-1, width)
    aggregate(
        flag_ref, part_ref[:train], ghost_ref[:train], rest_hbm, table, sums_ref, rest_ref
    )
    spread(normalize(sums_ref[...]), out_ref)
    length = piece_refs[0].shape[0] - 16
    groups = len(piece_refs)
    if groups > 1:
        for shift, ref in enumerate(piece_refs):
            group = lax.rem(place_ref[1] + shift, groups)
            at = pl.multiple_of(group * length, length)
            side_ref[pl.ds(at, length), :] = ref[:length, :]
            turn_ref[pl.ds(group, 1), :] = ref[length:, :128].astype(f32)[:1]
        side_ref[groups * length :, :128] = turn_ref[:16, :].astype(bf16)


def last_kernel(
    flag_ref,
    token_ref,
    part_ref,
    ghost_ref,
    rest_hbm,
    table_ref,
    start_ref,
    out_ref,
    again_ref,
    sums_ref,
    rest_ref,
):
    again_ref[...] = token_ref[...]
    table = table_ref[...].reshape(-1, out_ref.shape[-1])
    aggregate(flag_ref, part_ref[...], ghost_ref[...], rest_hbm, table, sums_ref, rest_ref)
    out_ref[0, 0, 0] = start_ref[...]
    out_ref[1, 0, 0] = normalize(sums_ref[...])


def shares(ref, first, share):
    if share % 128 == 0:
        return ref[:, pl.ds(pl.multiple_of(first, 128), share)].astype(f32)
    length = ref.shape[1]
    rows = lax.broadcasted_iota(jnp.int32, (length, share), 0)
    cols = lax.broadcasted_iota(jnp.int32, (length, share), 1)
    return dot(ref[...], jnp.where(rows == cols + first, 1.0, 0.0).astype(bf16))


def lanes_sum(values):
    total = None
    for piece in range(values.shape[1] // 128):
        part = values[:, piece * 128 : (piece + 1) * 128].astype(f32)
        total = part * part if total is None else total + part * part
    return total


def classify_kernel(
    many,
    place_ref,
    label_ref,
    zero_ref,
    one_ref,
    two_ref,
    sides_hbm,
    w_first_hbm,
    w_second_hbm,
    w_third_hbm,
    n_first_hbm,
    n_second_hbm,
    n_third_hbm,
    g_first_ref,
    g_second_ref,
    g_third_ref,
    side_refs,
    w_first_ref,
    w_second_ref,
    w_third_ref,
    n_first_ref,
    n_second_ref,
    n_third_ref,
    in_ref,
    w_third_pad_ref,
    turn_ref,
    column_ref,
    h_one_ref,
    h_two_ref,
    slope_one_ref,
    slope_two_ref,
    d_one_ref,
    d_two_ref,
    d_three_ref,
    sems,
):
    classes = w_third_ref.shape[0]
    hid = w_second_ref.shape[0]
    width = two_ref.shape[2]
    wide = w_third_pad_ref.shape[0]
    train = two_ref.shape[1]
    scale = noise_mult * clip_bound
    place = place_ref[0]
    pairs = (
        (w_first_hbm, w_first_ref),
        (w_second_hbm, w_second_ref),
        (w_third_hbm, w_third_ref),
        (n_first_hbm, n_first_ref),
        (n_second_hbm, n_second_ref),
        (n_third_hbm, n_third_ref),
    )

    def set_noise():
        g_first_ref[...] = scale * n_first_ref[...]
        g_second_ref[...] = scale * n_second_ref[...]
        g_third_ref[...] = scale * n_third_ref[...]

    def pad():
        w_third_pad_ref[...] = jnp.zeros_like(w_third_pad_ref)
        w_third_pad_ref[:classes, :] = w_third_ref[...]

    def column(row, turned, lane):
        column_ref[row : row + train, :] = jnp.broadcast_to(
            turned[:train, lane : lane + 1], (train, 128)
        ).astype(jnp.int32)

    if many:

        @pl.when(pl.program_id(0) == 0)
        def _():
            for copy in fetch(pairs, sems):
                copy.wait()
            set_noise()
            pad()

        groups = label_ref.shape[0]
        turn_ref[:groups, :train] = label_ref[...].astype(f32)
        turned = turn_ref[...].T
        for group in range(groups):
            column(group * train, turned, group)
        for hop, ref in enumerate((zero_ref, one_ref)):
            in_ref[:, hop * width : (hop + 1) * width] = ref[...].reshape(-1, width)
    else:
        parts = len(side_refs)
        copies = fetch(tuple(zip(sides_hbm, side_refs)) + pairs[:1], sems)
        for copy in copies[:parts]:
            copy.wait()
        groups = two_ref.shape[0] // parts
        rows = groups * train
        chips = parts // 2
        for at, ref in enumerate(side_refs):
            core = place % 2 if at < chips else 1 - place % 2
            part = 2 * lax.rem(place // 2 - at % chips + chips, chips) + core
            at = pl.multiple_of(part * rows, rows)
            for group in range(groups):
                for hop in range(2):
                    first = (2 * group + hop) * train
                    in_ref[pl.ds(at + group * train, train), hop * width : (hop + 1) * width] = ref[
                        first : first + train, :
                    ]
            turn_ref[pl.ds(pl.multiple_of(part * 16, 16), 16), :] = ref[2 * rows :, :128].astype(f32)
        turned = turn_ref[...].T
        for part in range(parts):
            for group in range(groups):
                column((part * groups + group) * train, turned, part * 16 + group)
    in_ref[:, 2 * width :] = two_ref[...].reshape(-1, width)
    if not many:
        copies[parts].wait()
        copies = fetch(pairs[1:], sems)

    def activate(values, h_ref, slope_ref, rows):
        sigma = 0.5 + 0.5 * jnp.tanh(0.5 * values)
        out = values * sigma
        slope_ref[rows, :] = sigma + out * (1.0 - sigma)
        h_ref[rows, :] = out.astype(bf16)
        return lanes_sum(out)

    def back(values, slope_ref, d_ref, rows):
        out = values * slope_ref[rows, :]
        d_ref[rows, :] = out.astype(bf16)
        return lanes_sum(out)

    def layer(product, finish, *refs):
        sums = []
        values = product(cuts[0])
        for at, cut in enumerate(cuts):
            ahead = product(cuts[at + 1]) if at + 1 < len(cuts) else None
            sums.append(finish(values, *refs, cut))
            values = ahead
        return jnp.concatenate(sums, 0)

    step = 256
    cuts = [slice(at, at + step) for at in range(0, in_ref.shape[0], step)]
    sq_in = lanes_sum(in_ref[...])
    sq_one = layer(
        lambda cut: dot(in_ref[cut, :], w_first_ref[...]), activate, h_one_ref, slope_one_ref
    )
    if not many:
        copies[0].wait()
    sq_two = layer(
        lambda cut: dot(h_one_ref[cut, :], w_second_ref[...]), activate, h_two_ref, slope_two_ref
    )
    if not many:
        copies[1].wait()
        pad()
    logits = dot_nt(h_two_ref[...], w_third_pad_ref[...])
    ids = lax.broadcasted_iota(jnp.int32, (logits.shape[0], wide), 1)
    expo = jnp.where(ids < classes, jnp.exp(logits), 0.0)
    probs = expo / jnp.sum(expo, -1, keepdims=True)
    label = column_ref[:, :1]
    d_three = (probs - jnp.where(ids == label, 1.0, 0.0)).astype(bf16)
    sq_dthree = lanes_sum(d_three)
    d_three_ref[...] = d_three
    sq_dtwo = layer(
        lambda cut: dot(d_three_ref[cut, :], w_third_pad_ref[...]), back, slope_two_ref, d_two_ref
    )
    sq_done = layer(
        lambda cut: dot_nt(d_two_ref[cut, :], w_second_ref[...]), back, slope_one_ref, d_one_ref
    )

    def total(values):
        return jnp.sum(values, -1, keepdims=True)

    norm = jnp.sqrt(
        total(sq_in) * total(sq_done)
        + total(sq_one) * total(sq_dtwo)
        + total(sq_two) * total(sq_dthree)
    )
    factor = clip_bound / jnp.maximum(norm, clip_bound)

    def left(ref, share):
        return (shares(ref, place * share, share) * factor).astype(bf16)

    if not many:
        for copy in copies[2:]:
            copy.wait()
        set_noise()
    share = g_second_ref.shape[0]
    g_first_ref[...] += dot_tn(left(in_ref, g_first_ref.shape[0]), d_one_ref[...])
    g_second_ref[...] += dot_tn(left(h_one_ref, share), d_two_ref[...])
    g_third_ref[...] += dot_tn(d_three, left(h_two_ref, share))[:classes, :]


def call(kernel, mib, outs, ins, scratch):
    def shape_of(shape, dtype, space):
        if space is None or space is HBM:
            return (space or VMEM)(shape, dtype)
        return jax.ShapeDtypeStruct(shape, dtype)

    def block(space):
        return pl.BlockSpec(memory_space=VMEM if space is None else space)

    def held(value, space):
        if space is None or space is HBM:
            return pltpu.with_memory_space_constraint(value, space or VMEM)
        return value

    return pl.pallas_call(
        kernel,
        out_shape=[shape_of(*out) for out in outs],
        in_specs=[block(space) for _, space in ins],
        out_specs=[block(space) for _, _, space in outs],
        scratch_shapes=scratch,
        compiler_params=params(mib),
    )(*[held(value, space) for value, space in ins])


def local(
    feats,
    hop_noise,
    send_rows,
    tile_block,
    tile_src,
    tile_dst,
    tile_count,
    labels,
    w_first,
    w_second,
    w_third,
    noise_first,
    noise_second,
    noise_third,
):
    nodes, width = feats.shape[2:]
    parts, each = send_rows.shape[2:]
    ghosts = parts * each
    tiles = tile_src.shape[2]
    slots = tile_src.shape[3]
    train = labels.shape[2]
    classes = w_third.shape[1]
    hid = w_second.shape[0]
    d_in = w_first.shape[0]
    cols = nodes + ghosts
    rows = send_rows.reshape(parts, each)
    turn = VMEM((128, 128), jnp.int32)
    pick = VMEM((ghosts, nodes), bf16)
    axes = ("dom", "grp")
    members = lax.axis_size(axes)
    few = members <= FEW and parts <= 8 and parts % 2 == 0
    copies = members if few else 1

    def every(value, *names):
        for name in names:
            value = lax.all_gather(value, name, axis=0, tiled=True)
        return value

    start0, out0, own0 = call(
        first_kernel,
        16,
        [
            ((nodes, width), bf16, None),
            ((parts, each, width), bf16, None),
            ((train, width), bf16, None),
        ],
        [(feats, HBM), (send_rows, HBM)],
        [VMEM((nodes, width), bf16), VMEM((parts, each), jnp.int32), turn, pick, DMA((2,))],
    )
    table0 = lax.all_to_all(out0, "dom", split_axis=0, concat_axis=0, tiled=True)
    own, ghost, part1, flag, own_rest, ghost_rest = call(
        build_kernel,
        28,
        [
            ((nodes, nodes), bf16, HBM),
            ((nodes, ghosts), bf16, None),
            ((nodes, width), f32, None),
            ((1,), jnp.int32, SMEM),
            ((nodes, nodes), bf16, HBM),
            ((nodes, ghosts), bf16, HBM),
        ],
        [
            (tile_block, HBM),
            (tile_count, SMEM),
            (tile_src, HBM),
            (tile_dst, HBM),
            (hop_noise, HBM),
            (start0, None),
        ],
        [
            VMEM((tiles, slots), jnp.int32),
            VMEM((tiles, slots), jnp.int32),
            VMEM((nodes, width), bf16),
            VMEM((tiles, slots, 128), bf16),
            VMEM((tiles * 16, slots), bf16),
            VMEM((tiles * 16, slots), bf16),
            VMEM((nodes, cols), f32),
            VMEM((nodes, max(nodes, ghosts)), bf16),
            VMEM((nodes, nodes), bf16),
            SMEM(tile_block.shape, jnp.int32),
            DMA((5,)),
        ],
    )
    start1, out1, side = call(
        hop_kernel,
        16,
        [
            ((nodes, width), bf16, None),
            ((parts, each, width), bf16, None),
            ((2 * train + 16, width), bf16, None),
        ],
        [
            (flag, SMEM),
            (part1, None),
            (ghost, None),
            (ghost_rest, HBM),
            (table0, None),
            (rows, VMEM),
            (own0, None),
            (labels.reshape(1, train), VMEM),
        ],
        [VMEM((nodes, width), f32), VMEM((nodes, ghosts), bf16), turn, pick],
    )
    table1 = lax.all_to_all(out1, "dom", split_axis=0, concat_axis=0, tiled=True)
    (part2,) = call(
        own_kernel,
        16,
        [((nodes, width), f32, None)],
        [(flag, SMEM), (own, HBM), (own_rest, HBM), (hop_noise, HBM), (start1, None)],
        [
            VMEM((nodes, nodes), bf16),
            VMEM((nodes, width), bf16),
            VMEM((nodes, nodes), bf16),
            DMA((2,)),
        ],
    )
    place = jnp.stack([lax.axis_index("dom"), lax.axis_index("grp")]).astype(jnp.int32)
    grp = lax.axis_size("grp")

    def shifted(value, name, size, step):
        return [
            lax.ppermute(value, name, [((at + step * shift) % size, at) for at in range(size)])
            for shift in range(1, size)
        ]

    sides = [side] + (shifted(side, "grp", grp, 1) if few else [])
    last, side = call(
        train_kernel,
        12,
        [
            ((copies, train, width), bf16, None),
            ((len(sides) * 2 * train + 16, width), bf16, None),
        ],
        [
            (flag, SMEM),
            (place, SMEM),
            (part2, None),
            (ghost, None),
            (ghost_rest, HBM),
            (table1, None),
        ]
        + [(value, None) for value in sides],
        [VMEM((train, width), f32), VMEM((train, ghosts), bf16), VMEM((128, 128), f32)],
    )
    if few:
        every2 = lax.all_to_all(last, axes, split_axis=0, concat_axis=0, tiled=True)
        chips = parts // 2
        sides = [side]
        for shift in range(1, chips):
            pairs = [
                (2 * ((chip - shift) % chips) + core, 2 * chip + core)
                for chip in range(chips)
                for core in range(2)
            ]
            sides.append(lax.ppermute(side, "dom", pairs))
    else:
        every0, every1, every2 = (
            every(value, axes) for value in (own0[None], start1[None, :train], last)
        )
        every_label = every(labels.reshape(1, train), axes)
    hop_feats, again = call(
        last_kernel,
        12,
        [((2, 1, 1, nodes, width), bf16, VMEM), (side.shape, bf16, None)],
        [
            (flag, SMEM),
            (side, None),
            (part2, None),
            (ghost, None),
            (ghost_rest, HBM),
            (table1, None),
            (start1, None),
        ],
        [VMEM((nodes, width), f32), VMEM((nodes, ghosts), bf16)],
    )
    if few:
        swap = [(at, at ^ 1) for at in range(parts)]
        sides += [lax.ppermute(value, "dom", swap) for value in [again] + sides[1:]]
    chunk = train * min(members, 32)
    groups = chunk // train
    wide = (classes + 255) // 256 * 256
    fixed = (w_first, w_second, w_third.T, noise_first, noise_second, noise_third.T)
    scratch = [VMEM(value.shape, value.dtype) for value in fixed]
    scratch += [
        VMEM((chunk, d_in), bf16),
        VMEM((wide, hid), bf16),
        VMEM((128, 128), f32),
        VMEM((chunk, 128), jnp.int32),
        VMEM((chunk, hid), bf16),
        VMEM((chunk, hid), bf16),
        VMEM((chunk, hid), f32),
        VMEM((chunk, hid), f32),
        VMEM((chunk, hid), bf16),
        VMEM((chunk, hid), bf16),
        VMEM((chunk, wide), bf16),
        DMA((16,)),
    ]
    if few:

        def classify(place_ref, *refs):
            sides_in, rest = refs[:parts], refs[parts:]
            outs, rest, held = rest[:10], rest[10 + parts :], rest[10 : 10 + parts]
            classify_kernel(
                False, place_ref, None, None, None, outs[0], sides_in, *outs[1:], held, *rest
            )

        first, second, third = call(
            classify,
            44,
            [(value.shape, f32, VMEM) for value in fixed[3:]],
            [(place, SMEM)]
            + [(value, HBM) for value in sides]
            + [(every2, None)]
            + [(value, HBM) for value in fixed],
            [VMEM(value.shape, bf16) for value in sides] + scratch,
        )
    else:

        ins = (every_label, every0, every1, every2)

        def classify(place_ref, label_ref, zero_ref, one_ref, two_ref, *rest):
            classify_kernel(
                True,
                place_ref,
                label_ref,
                zero_ref,
                one_ref,
                two_ref,
                None,
                *rest[:9],
                None,
                *rest[9:],
            )

        def whole(value):
            return pl.BlockSpec(value.shape, lambda i: (0, 0))

        def piece(value):
            return pl.BlockSpec(
                (groups,) + value.shape[1:], lambda i: (i,) + (0,) * (value.ndim - 1)
            )

        first, second, third = pl.pallas_call(
            classify,
            grid=(members // groups,),
            out_shape=[jax.ShapeDtypeStruct(value.shape, f32) for value in fixed[3:]],
            in_specs=[pl.BlockSpec(memory_space=SMEM)]
            + [piece(value) for value in ins]
            + [pl.BlockSpec(memory_space=HBM) for value in fixed],
            out_specs=[whole(value) for value in fixed[3:]],
            scratch_shapes=scratch,
            compiler_params=params(56),
        )(place, *ins, *fixed)
    return (hop_feats, first, second, third.T)


def solution(mesh):
    in_specs = (
        P("dom", "grp", None, None),
        P(None, "dom", "grp", None, None),
        P("dom", "grp", None, None),
        P("dom", "grp", None),
        P("dom", "grp", None, None),
        P("dom", "grp", None, None),
        P("dom", "grp"),
        P("dom", "grp", None),
        P(),
        P(),
        P(),
        P("dom", None),
        P("dom", None),
        P("dom", None),
    )
    out_specs = (P(None, "dom", "grp", None, None), P("dom", None), P("dom", None), P("dom", None))
    return jax.shard_map(local, mesh=mesh, in_specs=in_specs, out_specs=out_specs, check_vma=False)
```

```python
import functools

import jax
import jax.numpy as jnp
from jax import lax
from jax.experimental import pallas as pl
from jax.experimental.pallas import tpu as pltpu
from jax.sharding import PartitionSpec as P

BLOCK = 128
LOW = 256
GROUP = 4
clip_bound = 4.0
noise_mult = 1.0

f32 = jnp.float32
bf16 = jnp.bfloat16
VMEM = pltpu.VMEM
SMEM = pltpu.SMEM
HBM = pltpu.HBM
DMA = pltpu.SemaphoreType.DMA


FEW = 32


def params(mib):
    return pltpu.CompilerParams(vmem_limit_bytes=mib * 1024 * 1024)


def fetch(pairs, sems):
    copies = [pltpu.make_async_copy(*pair, sems.at[at]) for at, pair in enumerate(pairs)]
    for copy in copies:
        copy.start()
    return copies


def normalize(values):
    return (values * lax.rsqrt(jnp.sum(values * values, -1, keepdims=True) + 1e-06)).astype(bf16)


def dot(left, right):
    return jnp.dot(left, right, preferred_element_type=f32)


def dot_nt(left, right):
    return lax.dot_general(left, right, (((1,), (1,)), ((), ())), preferred_element_type=f32)


def dot_tn(left, right):
    return lax.dot_general(left, right, (((0,), (0,)), ((), ())), preferred_element_type=f32)


def send(start, rows_ref, out_ref, turn_ref, pick_ref):
    parts, each = rows_ref.shape
    nodes = start.shape[0]
    turn_ref[:parts, :each] = rows_ref[...]
    columns = turn_ref[...].T
    spots = lax.broadcasted_iota(jnp.int32, (each, nodes), 1)
    for part in range(parts):
        wanted = columns[:each, part : part + 1]
        pick_ref[part * each : (part + 1) * each, :] = jnp.where(wanted == spots, 1.0, 0.0).astype(
            bf16
        )
    out = dot(pick_ref[...], start).astype(bf16)
    out_ref[...] = out.reshape(out_ref.shape)


def spread(rows, out_ref):
    out_ref[...] = jnp.broadcast_to(rows[None], out_ref.shape)


def first_kernel(
    feats_hbm,
    rows_hbm,
    start_ref,
    out_ref,
    own_ref,
    feats_ref,
    rows_ref,
    turn_ref,
    pick_ref,
    sems,
):
    copies = fetch(
        ((feats_hbm.at[0, 0], feats_ref), (rows_hbm.at[0, 0], rows_ref)), sems
    )
    for copy in copies:
        copy.wait()
    start = normalize(feats_ref[...].astype(f32))
    start_ref[...] = start
    own_ref[...] = start[: own_ref.shape[0]]
    send(start, rows_ref, out_ref, turn_ref, pick_ref)


def build_kernel(
    blocks_hbm,
    count_ref,
    src_hbm,
    dst_hbm,
    noise_hbm,
    start_ref,
    own_hbm,
    ghost_ref,
    part_ref,
    flag_ref,
    own_rest_ref,
    ghost_rest_ref,
    src_ref,
    dst_ref,
    noise_ref,
    low_ref,
    high_ref,
    spot_ref,
    sums_ref,
    rest_ref,
    own_ref,
    blocks_ref,
    sems,
):
    copies = fetch(
        (
            (blocks_hbm, blocks_ref),
            (src_hbm.at[0, 0], src_ref),
            (dst_hbm.at[0, 0], dst_ref),
            (noise_hbm.at[0, 0, 0], noise_ref),
        ),
        sems,
    )
    nodes, cols = sums_ref.shape
    pieces = -(-cols // LOW)
    tiles, slots = src_ref.shape
    count = count_ref[0, 0]
    own_ref[...] = jnp.zeros_like(own_ref)
    ghost_ref[...] = jnp.zeros_like(ghost_ref)
    for copy in copies:
        copy.wait()

    def sixteen(values):
        wide = jnp.broadcast_to(values.astype(f32)[:, None, :], (tiles, 16, slots))
        return wide.reshape(tiles * 16, slots).astype(bf16)

    src = src_ref[...]
    dst = dst_ref[...]
    tile_ids = lax.broadcasted_iota(jnp.int32, (tiles, slots), 0)
    high_ref[...] = sixteen(src // LOW)
    spot_ref[...] = sixteen(jnp.where((dst < BLOCK) & (tile_ids < count), dst, -1))
    low = (src % LOW - LOW // 2).astype(f32).T
    for tile in range(tiles):
        low_ref[tile] = jnp.broadcast_to(low[:, tile : tile + 1], (slots, 128)).astype(bf16)
    ids = lax.broadcasted_iota(jnp.int32, (BLOCK, slots), 0).astype(f32).astype(bf16)
    lanes = lax.broadcasted_iota(jnp.int32, (slots, 128), 1).astype(f32)
    lanes = [(lanes + first).astype(bf16) for first in range(-LOW // 2, LOW // 2, 128)]
    one = jnp.ones((), bf16)
    zero = jnp.zeros((), bf16)

    def counts(tile):
        rows = pl.ds(pl.multiple_of(tile * 16, 16), 16)
        high, spot = high_ref[rows, :], spot_ref[rows, :]
        spots = []
        for piece in range(pieces):
            wanted = jnp.where(high == piece, spot, -one)
            tall = jnp.concatenate([wanted] * (BLOCK // 16), 0)
            spots.append(jnp.where(ids == tall, one, zero))
        low = low_ref[tile]
        low_hot = jnp.concatenate([jnp.where(low == ids, one, zero) for ids in lanes], 1)
        spot_hot = jnp.concatenate(spots, 0)
        return dot(spot_hot.astype(jnp.float8_e4m3fn), low_hot.astype(jnp.float8_e4m3fn))

    def turn(add, step, carry):
        first = step * GROUP
        outs = [counts(first + inner) for inner in range(GROUP)]
        for inner, out in enumerate(outs):
            base = pl.multiple_of(blocks_ref[0, 0, first + inner] * BLOCK, BLOCK)
            for piece in range(pieces):
                add(pl.ds(base, BLOCK), piece * LOW, out[piece * BLOCK : (piece + 1) * BLOCK])
        return carry

    def add_short(rows, at, values):
        ref, at = (own_ref, at) if at < nodes else (ghost_ref, at - nodes)
        size = min(LOW, ref.shape[1] - at)
        ref[rows, at : at + size] += values[:, :size].astype(bf16)

    def add_long(rows, at, values):
        size = min(LOW, cols - at)
        sums_ref[rows, at : at + size] += values[:, :size]

    steps = (count + GROUP - 1) // GROUP
    lax.fori_loop(0, steps, functools.partial(turn, add_short), 0)
    top = ghost_ref[:BLOCK, :256]
    for first in range(0, nodes, BLOCK):
        for ref in (own_ref, ghost_ref):
            for at in range(0, ref.shape[1], 256):
                top = jnp.maximum(top, ref[first : first + BLOCK, at : at + 256])
    big = jnp.max(top.astype(f32)) >= 256.0
    flag_ref[0] = big.astype(jnp.int32)

    @pl.when(big)
    def _():
        sums_ref[...] = jnp.zeros_like(sums_ref)
        lax.fori_loop(0, steps, functools.partial(turn, add_long), 0)
        own_ref[...] = sums_ref[:, :nodes].astype(bf16)
        ghost_ref[...] = sums_ref[:, nodes:].astype(bf16)

    own_copy = pltpu.make_async_copy(own_ref, own_hbm, sems.at[4])
    own_copy.start()
    part_ref[...] = dot(own_ref[...], start_ref[...]) + noise_ref[...].astype(f32)

    @pl.when(big)
    def _():
        own_rest = (sums_ref[:, :nodes] - own_ref[...].astype(f32)).astype(bf16)
        part_ref[...] += dot(own_rest, start_ref[...])
        rest_ref[:, :nodes] = own_rest
        pltpu.sync_copy(rest_ref.at[:, :nodes], own_rest_ref)
        rest_ref[:, : cols - nodes] = (sums_ref[:, nodes:] - ghost_ref[...].astype(f32)).astype(bf16)
        pltpu.sync_copy(rest_ref.at[:, : cols - nodes], ghost_rest_ref)

    own_copy.wait()


def aggregate(flag_ref, part_ref, count_ref, rest_hbm, table, sums_ref, rest_ref):
    rows = sums_ref.shape[0]
    sums_ref[...] = part_ref.astype(f32) + dot(count_ref, table)

    @pl.when(flag_ref[0] > 0)
    def _():
        pltpu.sync_copy(rest_hbm.at[:rows], rest_ref)
        sums_ref[...] += dot(rest_ref[...], table)


def hop_kernel(
    flag_ref,
    part_ref,
    ghost_ref,
    rest_hbm,
    table_ref,
    rows_ref,
    old_ref,
    labels_ref,
    start_ref,
    out_ref,
    side_ref,
    sums_ref,
    rest_ref,
    turn_ref,
    pick_ref,
):
    width = start_ref.shape[1]
    table = table_ref[...].reshape(-1, width)
    aggregate(flag_ref, part_ref[...], ghost_ref[...], rest_hbm, table, sums_ref, rest_ref)
    start = normalize(sums_ref[...])
    start_ref[...] = start
    send(start, rows_ref, out_ref, turn_ref, pick_ref)
    train = labels_ref.shape[1]
    side_ref[:train, :] = old_ref[...]
    side_ref[train : 2 * train, :] = start[:train]
    turn_ref[:1, :train] = labels_ref[...]
    side_ref[2 * train :, :128] = turn_ref[:16, :].astype(f32).astype(bf16)


def own_kernel(
    flag_ref, own_hbm, rest_hbm, noise_hbm, start_ref, part_ref, own_ref, noise_ref, rest_ref, sems
):
    copies = fetch(((own_hbm, own_ref), (noise_hbm.at[1, 0, 0], noise_ref)), sems)
    for copy in copies:
        copy.wait()
    start = start_ref[...]
    noise = noise_ref[...].astype(f32)
    aggregate(flag_ref, noise, own_ref[...], rest_hbm, start, part_ref, rest_ref)


def train_kernel(flag_ref, place_ref, part_ref, ghost_ref, rest_hbm, table_ref, *refs):
    *piece_refs, out_ref, side_ref, sums_ref, rest_ref, turn_ref = refs
    train, width = sums_ref.shape
    table = table_ref[...].reshape(-1, width)
    aggregate(
        flag_ref, part_ref[:train], ghost_ref[:train], rest_hbm, table, sums_ref, rest_ref
    )
    spread(normalize(sums_ref[...]), out_ref)
    length = piece_refs[0].shape[0] - 16
    groups = len(piece_refs)
    if groups > 1:
        for shift, ref in enumerate(piece_refs):
            group = lax.rem(place_ref[1] + shift, groups)
            at = pl.multiple_of(group * length, length)
            side_ref[pl.ds(at, length), :] = ref[:length, :]
            turn_ref[pl.ds(group, 1), :] = ref[length:, :128].astype(f32)[:1]
        side_ref[groups * length :, :128] = turn_ref[:16, :].astype(bf16)


def last_kernel(
    flag_ref,
    token_ref,
    part_ref,
    ghost_ref,
    rest_hbm,
    table_ref,
    start_ref,
    out_ref,
    sums_ref,
    rest_ref,
):
    table = table_ref[...].reshape(-1, out_ref.shape[-1])
    aggregate(flag_ref, part_ref[...], ghost_ref[...], rest_hbm, table, sums_ref, rest_ref)
    out_ref[0, 0, 0] = start_ref[...]
    out_ref[1, 0, 0] = normalize(sums_ref[...])


def shares(ref, first, share):
    if share % 128 == 0:
        return ref[:, pl.ds(pl.multiple_of(first, 128), share)].astype(f32)
    length = ref.shape[1]
    rows = lax.broadcasted_iota(jnp.int32, (length, share), 0)
    cols = lax.broadcasted_iota(jnp.int32, (length, share), 1)
    return dot(ref[...], jnp.where(rows == cols + first, 1.0, 0.0).astype(bf16))


def lanes_sum(values):
    total = None
    for piece in range(values.shape[1] // 128):
        part = values[:, piece * 128 : (piece + 1) * 128].astype(f32)
        total = part * part if total is None else total + part * part
    return total


def classify_kernel(
    many,
    place_ref,
    label_ref,
    zero_ref,
    one_ref,
    two_ref,
    sides_hbm,
    w_first_hbm,
    w_second_hbm,
    w_third_hbm,
    n_first_hbm,
    n_second_hbm,
    n_third_hbm,
    g_first_ref,
    g_second_ref,
    g_third_ref,
    send_ref,
    side_refs,
    w_first_ref,
    w_second_ref,
    w_third_ref,
    n_first_ref,
    n_second_ref,
    n_third_ref,
    in_ref,
    w_third_pad_ref,
    turn_ref,
    column_ref,
    h_one_ref,
    h_two_ref,
    slope_one_ref,
    slope_two_ref,
    d_one_ref,
    d_two_ref,
    d_three_ref,
    sems,
):
    classes = w_third_ref.shape[0]
    hid = w_second_ref.shape[0]
    width = two_ref.shape[2]
    wide = w_third_pad_ref.shape[0]
    train = two_ref.shape[1]
    scale = noise_mult * clip_bound
    place = place_ref[0]
    pairs = (
        (w_first_hbm, w_first_ref),
        (w_second_hbm, w_second_ref),
        (w_third_hbm, w_third_ref),
        (n_first_hbm, n_first_ref),
        (n_second_hbm, n_second_ref),
        (n_third_hbm, n_third_ref),
    )

    def set_noise():
        g_first_ref[...] = scale * n_first_ref[...]
        g_second_ref[...] = scale * n_second_ref[...]
        g_third_ref[...] = scale * n_third_ref[...]

    def pad():
        w_third_pad_ref[...] = jnp.zeros_like(w_third_pad_ref)
        w_third_pad_ref[:classes, :] = w_third_ref[...]

    def column(row, turned, lane):
        column_ref[row : row + train, :] = jnp.broadcast_to(
            turned[:train, lane : lane + 1], (train, 128)
        ).astype(jnp.int32)

    if many:

        @pl.when(pl.program_id(0) == 0)
        def _():
            for copy in fetch(pairs, sems):
                copy.wait()
            set_noise()
            pad()

        groups = label_ref.shape[0]
        turn_ref[:groups, :train] = label_ref[...].astype(f32)
        turned = turn_ref[...].T
        for group in range(groups):
            column(group * train, turned, group)
        for hop, ref in enumerate((zero_ref, one_ref)):
            in_ref[:, hop * width : (hop + 1) * width] = ref[...].reshape(-1, width)
    else:
        chips = len(side_refs)
        copies = fetch(tuple(zip(sides_hbm, side_refs)) + pairs[:1], sems)
        for copy in copies[:chips]:
            copy.wait()
        groups = two_ref.shape[0] // chips
        rows = groups * train
        for shift, ref in enumerate(side_refs):
            part = lax.rem(place // 2 - shift + chips, chips)
            at = pl.multiple_of(part * rows, rows)
            for group in range(groups):
                for hop in range(2):
                    first = (2 * group + hop) * train
                    in_ref[pl.ds(at + group * train, train), hop * width : (hop + 1) * width] = ref[
                        first : first + train, :
                    ]
            turn_ref[pl.ds(pl.multiple_of(part * 16, 16), 16), :] = ref[2 * rows :, :128].astype(f32)
        turned = turn_ref[...].T
        for part in range(chips):
            for group in range(groups):
                column((part * groups + group) * train, turned, part * 16 + group)
    in_ref[:, 2 * width :] = two_ref[...].reshape(-1, width)
    if not many:
        copies[chips].wait()
        copies = fetch(pairs[1:], sems)

    def activate(values, h_ref, slope_ref, rows):
        sigma = 0.5 + 0.5 * jnp.tanh(0.5 * values)
        out = values * sigma
        slope_ref[rows, :] = sigma + out * (1.0 - sigma)
        h_ref[rows, :] = out.astype(bf16)
        return lanes_sum(out)

    def back(values, slope_ref, d_ref, rows):
        out = values * slope_ref[rows, :]
        d_ref[rows, :] = out.astype(bf16)
        return lanes_sum(out)

    def layer(product, finish, *refs):
        sums = []
        values = product(cuts[0])
        for at, cut in enumerate(cuts):
            ahead = product(cuts[at + 1]) if at + 1 < len(cuts) else None
            sums.append(finish(values, *refs, cut))
            values = ahead
        return jnp.concatenate(sums, 0)

    step = 256
    cuts = [slice(at, at + step) for at in range(0, in_ref.shape[0], step)]
    sq_in = lanes_sum(in_ref[...])
    sq_one = layer(
        lambda cut: dot(in_ref[cut, :], w_first_ref[...]), activate, h_one_ref, slope_one_ref
    )
    if not many:
        copies[0].wait()
    sq_two = layer(
        lambda cut: dot(h_one_ref[cut, :], w_second_ref[...]), activate, h_two_ref, slope_two_ref
    )
    if not many:
        copies[1].wait()
        pad()
    logits = dot_nt(h_two_ref[...], w_third_pad_ref[...])
    ids = lax.broadcasted_iota(jnp.int32, (logits.shape[0], wide), 1)
    expo = jnp.where(ids < classes, jnp.exp(logits), 0.0)
    probs = expo / jnp.sum(expo, -1, keepdims=True)
    label = column_ref[:, :1]
    d_three = (probs - jnp.where(ids == label, 1.0, 0.0)).astype(bf16)
    sq_dthree = lanes_sum(d_three)
    d_three_ref[...] = d_three
    sq_dtwo = layer(
        lambda cut: dot(d_three_ref[cut, :], w_third_pad_ref[...]), back, slope_two_ref, d_two_ref
    )
    sq_done = layer(
        lambda cut: dot_nt(d_two_ref[cut, :], w_second_ref[...]), back, slope_one_ref, d_one_ref
    )

    def total(values):
        return jnp.sum(values, -1, keepdims=True)

    norm = jnp.sqrt(
        total(sq_in) * total(sq_done)
        + total(sq_one) * total(sq_dtwo)
        + total(sq_two) * total(sq_dthree)
    )
    factor = clip_bound / jnp.maximum(norm, clip_bound)

    if not many:
        for copy in copies[2:]:
            copy.wait()
        set_noise()
    share_one, share = g_first_ref.shape[0], g_second_ref.shape[0]
    places = [place] if many else [place, place + 1 - 2 * (place % 2)]

    def left(ref, share):
        picked = [shares(ref, at * share, share) for at in places]
        return (jnp.concatenate(picked, 1) * factor).astype(bf16)

    sum_one = dot_tn(left(in_ref, share_one), d_one_ref[...])
    sum_two = dot_tn(left(h_one_ref, share), d_two_ref[...])
    sum_three = dot_tn(d_three, left(h_two_ref, share))
    g_first_ref[...] += sum_one[:share_one]
    g_second_ref[...] += sum_two[:share]
    g_third_ref[...] += sum_three[:classes, :share]
    if not many:
        send_ref[:share_one, :] = sum_one[share_one:].astype(bf16)
        send_ref[share_one : share_one + share, :] = sum_two[share:].astype(bf16)
        first = share_one + share
        for at in range(0, classes, 32):
            cols = slice(at // 32 * share, (at // 32 + 1) * share)
            send_ref[first : first + 32, cols] = sum_three[at : at + 32, share:].astype(bf16)


def finish_kernel(got_ref, one_ref, two_ref, three_ref, g_first_ref, g_second_ref, g_third_ref):
    share_one, share = one_ref.shape[0], two_ref.shape[0]
    g_first_ref[...] = one_ref[...] + got_ref[:share_one, :].astype(f32)
    g_second_ref[...] = two_ref[...] + got_ref[share_one : share_one + share, :].astype(f32)
    first = share_one + share
    classes = three_ref.shape[0]
    for at in range(0, classes, 32):
        size = min(32, classes - at)
        cols = slice(at // 32 * share, (at // 32 + 1) * share)
        got = got_ref[first : first + 32, cols].astype(f32)
        g_third_ref[at : at + size, :] = three_ref[at : at + size, :] + got[:size]


def call(kernel, mib, outs, ins, scratch):
    def shape_of(shape, dtype, space):
        if space is None or space is HBM:
            return (space or VMEM)(shape, dtype)
        return jax.ShapeDtypeStruct(shape, dtype)

    def block(space):
        return pl.BlockSpec(memory_space=VMEM if space is None else space)

    def held(value, space):
        if space is None or space is HBM:
            return pltpu.with_memory_space_constraint(value, space or VMEM)
        return value

    return pl.pallas_call(
        kernel,
        out_shape=[shape_of(*out) for out in outs],
        in_specs=[block(space) for _, space in ins],
        out_specs=[block(space) for _, _, space in outs],
        scratch_shapes=scratch,
        compiler_params=params(mib),
    )(*[held(value, space) for value, space in ins])


def local(
    axes,
    feats,
    hop_noise,
    send_rows,
    tile_block,
    tile_src,
    tile_dst,
    tile_count,
    labels,
    w_first,
    w_second,
    w_third,
    noise_first,
    noise_second,
    noise_third,
):
    nodes, width = feats.shape[2:]
    parts, each = send_rows.shape[2:]
    ghosts = parts * each
    tiles = tile_src.shape[2]
    slots = tile_src.shape[3]
    train = labels.shape[2]
    classes = w_third.shape[1]
    hid = w_second.shape[0]
    d_in = w_first.shape[0]
    cols = nodes + ghosts
    rows = send_rows.reshape(parts, each)
    turn = VMEM((128, 128), jnp.int32)
    pick = VMEM((ghosts, nodes), bf16)
    dom = axes[:-1]
    members = lax.axis_size(axes)
    few = len(axes) == 3
    copies = members // 2 if few else 1

    def every(value, *names):
        for name in names:
            value = lax.all_gather(value, name, axis=0, tiled=True)
        return value

    start0, out0, own0 = call(
        first_kernel,
        16,
        [
            ((nodes, width), bf16, None),
            ((parts, each, width), bf16, None),
            ((train, width), bf16, None),
        ],
        [(feats, HBM), (send_rows, HBM)],
        [VMEM((nodes, width), bf16), VMEM((parts, each), jnp.int32), turn, pick, DMA((2,))],
    )
    table0 = lax.all_to_all(out0, dom, split_axis=0, concat_axis=0, tiled=True)
    own, ghost, part1, flag, own_rest, ghost_rest = call(
        build_kernel,
        28,
        [
            ((nodes, nodes), bf16, HBM),
            ((nodes, ghosts), bf16, None),
            ((nodes, width), f32, None),
            ((1,), jnp.int32, SMEM),
            ((nodes, nodes), bf16, HBM),
            ((nodes, ghosts), bf16, HBM),
        ],
        [
            (tile_block, HBM),
            (tile_count, SMEM),
            (tile_src, HBM),
            (tile_dst, HBM),
            (hop_noise, HBM),
            (start0, None),
        ],
        [
            VMEM((tiles, slots), jnp.int32),
            VMEM((tiles, slots), jnp.int32),
            VMEM((nodes, width), bf16),
            VMEM((tiles, slots, 128), bf16),
            VMEM((tiles * 16, slots), bf16),
            VMEM((tiles * 16, slots), bf16),
            VMEM((nodes, cols), f32),
            VMEM((nodes, max(nodes, ghosts)), bf16),
            VMEM((nodes, nodes), bf16),
            SMEM(tile_block.shape, jnp.int32),
            DMA((5,)),
        ],
    )
    start1, out1, side = call(
        hop_kernel,
        16,
        [
            ((nodes, width), bf16, None),
            ((parts, each, width), bf16, None),
            ((2 * train + 16, width), bf16, None),
        ],
        [
            (flag, SMEM),
            (part1, None),
            (ghost, None),
            (ghost_rest, HBM),
            (table0, None),
            (rows, VMEM),
            (own0, None),
            (labels.reshape(1, train), VMEM),
        ],
        [VMEM((nodes, width), f32), VMEM((nodes, ghosts), bf16), turn, pick],
    )
    table1 = lax.all_to_all(out1, dom, split_axis=0, concat_axis=0, tiled=True)
    (part2,) = call(
        own_kernel,
        16,
        [((nodes, width), f32, None)],
        [(flag, SMEM), (own, HBM), (own_rest, HBM), (hop_noise, HBM), (start1, None)],
        [
            VMEM((nodes, nodes), bf16),
            VMEM((nodes, width), bf16),
            VMEM((nodes, nodes), bf16),
            DMA((2,)),
        ],
    )
    place = jnp.stack([lax.axis_index(dom), lax.axis_index("grp")]).astype(jnp.int32)
    grp = lax.axis_size("grp")

    def shifted(value, name, size, step):
        return [
            lax.ppermute(value, name, [((at + step * shift) % size, at) for at in range(size)])
            for shift in range(1, size)
        ]

    sides = [side] + (shifted(side, "grp", grp, 1) if few else [])
    last, side = call(
        train_kernel,
        12,
        [
            ((copies, train, width), bf16, None),
            ((len(sides) * 2 * train + 16, width), bf16, None),
        ],
        [
            (flag, SMEM),
            (place, SMEM),
            (part2, None),
            (ghost, None),
            (ghost_rest, HBM),
            (table1, None),
        ]
        + [(value, None) for value in sides],
        [VMEM((train, width), f32), VMEM((train, ghosts), bf16), VMEM((128, 128), f32)],
    )
    if few:
        every2 = lax.all_to_all(last, ("chip", "grp"), split_axis=0, concat_axis=0, tiled=True)
        sides = [side] + shifted(side, "chip", parts // 2, -1)
    else:
        every0, every1, every2 = (
            every(value, axes) for value in (own0[None], start1[None, :train], last)
        )
        every_label = every(labels.reshape(1, train), axes)
    (hop_feats,) = call(
        last_kernel,
        12,
        [((2, 1, 1, nodes, width), bf16, VMEM)],
        [
            (flag, SMEM),
            (side, None),
            (part2, None),
            (ghost, None),
            (ghost_rest, HBM),
            (table1, None),
            (start1, None),
        ],
        [VMEM((nodes, width), f32), VMEM((nodes, ghosts), bf16)],
    )
    chunk = train * (copies if few else min(members, 32))
    groups = chunk // train
    wide = (classes + 255) // 256 * 256
    fixed = (w_first, w_second, w_third.T, noise_first, noise_second, noise_third.T)
    scratch = [VMEM(value.shape, value.dtype) for value in fixed]
    scratch += [
        VMEM((chunk, d_in), bf16),
        VMEM((wide, hid), bf16),
        VMEM((128, 128), f32),
        VMEM((chunk, 128), jnp.int32),
        VMEM((chunk, hid), bf16),
        VMEM((chunk, hid), bf16),
        VMEM((chunk, hid), f32),
        VMEM((chunk, hid), f32),
        VMEM((chunk, hid), bf16),
        VMEM((chunk, hid), bf16),
        VMEM((chunk, wide), bf16),
        DMA((16,)),
    ]
    if few:
        chips = parts // 2

        def classify(place_ref, *refs):
            sides_in, rest = refs[:chips], refs[chips:]
            outs, held, rest = rest[:11], rest[11 : 11 + chips], rest[11 + chips :]
            classify_kernel(
                False, place_ref, None, None, None, outs[0], sides_in, *outs[1:], held, *rest
            )

        rows = noise_first.shape[0] + noise_second.shape[0] + 32
        *own_sums, other = call(
            classify,
            44,
            [(value.shape, f32, None) for value in fixed[3:]] + [((rows, hid), bf16, None)],
            [(place, SMEM)]
            + [(value, HBM) for value in sides]
            + [(every2, None)]
            + [(value, HBM) for value in fixed],
            [VMEM(value.shape, bf16) for value in sides] + scratch,
        )
        got = lax.ppermute(other, "core", [(0, 1), (1, 0)])
        first, second, third = call(
            finish_kernel,
            16,
            [(value.shape, f32, VMEM) for value in fixed[3:]],
            [(got, None)] + [(value, None) for value in own_sums],
            [],
        )
    else:

        ins = (every_label, every0, every1, every2)

        def classify(place_ref, label_ref, zero_ref, one_ref, two_ref, *rest):
            classify_kernel(
                True,
                place_ref,
                label_ref,
                zero_ref,
                one_ref,
                two_ref,
                None,
                *rest[:9],
                None,
                None,
                *rest[9:],
            )

        def whole(value):
            return pl.BlockSpec(value.shape, lambda i: (0, 0))

        def piece(value):
            return pl.BlockSpec(
                (groups,) + value.shape[1:], lambda i: (i,) + (0,) * (value.ndim - 1)
            )

        first, second, third = pl.pallas_call(
            classify,
            grid=(members // groups,),
            out_shape=[jax.ShapeDtypeStruct(value.shape, f32) for value in fixed[3:]],
            in_specs=[pl.BlockSpec(memory_space=SMEM)]
            + [piece(value) for value in ins]
            + [pl.BlockSpec(memory_space=HBM) for value in fixed],
            out_specs=[whole(value) for value in fixed[3:]],
            scratch_shapes=scratch,
            compiler_params=params(56),
        )(place, *ins, *fixed)
    return (hop_feats, first, second, third.T)


def solution(mesh):
    dom, grp = mesh.shape["dom"], mesh.shape["grp"]
    names = ("dom", "grp")
    if dom * grp <= FEW and dom <= 8 and dom % 2 == 0:
        names = ("chip", "core", "grp")
        mesh = jax.sharding.Mesh(mesh.devices.reshape(dom // 2, 2, grp), names)
    doms, grps = names[:-1], "grp"
    in_specs = (
        P(doms, grps, None, None),
        P(None, doms, grps, None, None),
        P(doms, grps, None, None),
        P(doms, grps, None),
        P(doms, grps, None, None),
        P(doms, grps, None, None),
        P(doms, grps),
        P(doms, grps, None),
        P(),
        P(),
        P(),
        P(doms, None),
        P(doms, None),
        P(doms, None),
    )
    out_specs = (P(None, doms, grps, None, None), P(doms, None), P(doms, None), P(doms, None))
    return jax.shard_map(
        functools.partial(local, names),
        mesh=mesh,
        in_specs=in_specs,
        out_specs=out_specs,
        check_vma=False,
    )
```

```python
import functools
import math

import jax
import jax.numpy as jnp
from jax import lax
from jax.experimental import pallas as pl
from jax.experimental.pallas import tpu as pltpu
from jax.sharding import PartitionSpec as P

BLOCK = 128
LOW = 256
GROUP = 4
clip_bound = 4.0
noise_mult = 1.0

f32 = jnp.float32
bf16 = jnp.bfloat16
VMEM = pltpu.VMEM
SMEM = pltpu.SMEM
HBM = pltpu.HBM
DMA = pltpu.SemaphoreType.DMA


FEW = 32


def params(mib):
    return pltpu.CompilerParams(vmem_limit_bytes=mib * 1024 * 1024)


def fetch(pairs, sems):
    copies = [pltpu.make_async_copy(*pair, sems.at[at]) for at, pair in enumerate(pairs)]
    for copy in copies:
        copy.start()
    return copies


def normalize(values):
    return (values * lax.rsqrt(jnp.sum(values * values, -1, keepdims=True) + 1e-06)).astype(bf16)


def dot(left, right):
    return jnp.dot(left, right, preferred_element_type=f32)


def dot_nt(left, right):
    return lax.dot_general(left, right, (((1,), (1,)), ((), ())), preferred_element_type=f32)


def dot_tn(left, right):
    return lax.dot_general(left, right, (((0,), (0,)), ((), ())), preferred_element_type=f32)


def send(start, rows_ref, out_ref, turn_ref, pick_ref):
    parts, each = rows_ref.shape
    nodes = start.shape[0]
    turn_ref[:parts, :each] = rows_ref[...]
    columns = turn_ref[...].T
    spots = lax.broadcasted_iota(jnp.int32, (each, nodes), 1)
    for part in range(parts):
        wanted = columns[:each, part : part + 1]
        pick_ref[part * each : (part + 1) * each, :] = jnp.where(wanted == spots, 1.0, 0.0).astype(
            bf16
        )
    out = dot(pick_ref[...], start).astype(bf16)
    out_ref[...] = out.reshape(out_ref.shape)


def spread(rows, out_ref):
    out_ref[...] = jnp.broadcast_to(rows[None], out_ref.shape)


def first_kernel(
    feats_hbm,
    rows_hbm,
    start_ref,
    out_ref,
    own_ref,
    feats_ref,
    rows_ref,
    turn_ref,
    pick_ref,
    sems,
):
    copies = fetch(
        ((feats_hbm.at[0, 0], feats_ref), (rows_hbm.at[0, 0], rows_ref)), sems
    )
    for copy in copies:
        copy.wait()
    start = normalize(feats_ref[...].astype(f32))
    start_ref[...] = start
    own_ref[...] = start[: own_ref.shape[0]]
    send(start, rows_ref, out_ref, turn_ref, pick_ref)


def build_kernel(
    blocks_hbm,
    count_ref,
    src_hbm,
    dst_hbm,
    noise_hbm,
    start_ref,
    own_hbm,
    ghost_ref,
    own_train_ref,
    noise_train_ref,
    part_ref,
    flag_ref,
    own_rest_ref,
    ghost_rest_ref,
    src_ref,
    dst_ref,
    noise_ref,
    low_ref,
    high_ref,
    spot_ref,
    sums_ref,
    rest_ref,
    own_ref,
    blocks_ref,
    sems,
):
    train = own_train_ref.shape[0]
    copies = fetch(
        (
            (blocks_hbm, blocks_ref),
            (src_hbm.at[0, 0], src_ref),
            (dst_hbm.at[0, 0], dst_ref),
            (noise_hbm.at[0, 0, 0], noise_ref),
            (noise_hbm.at[1, 0, 0, :train], noise_train_ref),
        ),
        sems,
    )
    nodes, cols = sums_ref.shape
    pieces = -(-cols // LOW)
    tiles, slots = src_ref.shape
    own_ref[...] = jnp.zeros_like(own_ref)
    ghost_ref[...] = jnp.zeros_like(ghost_ref)
    for copy in copies:
        copy.wait()
    count = count_ref[0, 0]

    def sixteen(values):
        wide = jnp.broadcast_to(values.astype(f32)[:, None, :], (tiles, 16, slots))
        return wide.reshape(tiles * 16, slots).astype(bf16)

    src = src_ref[...]
    dst = dst_ref[...]
    tile_ids = lax.broadcasted_iota(jnp.int32, (tiles, slots), 0)
    high_ref[...] = sixteen(src // LOW)
    spot_ref[...] = sixteen(jnp.where((dst < BLOCK) & (tile_ids < count), dst, -1))
    low = (src % LOW - LOW // 2).astype(f32).T
    for tile in range(tiles):
        low_ref[tile] = jnp.broadcast_to(low[:, tile : tile + 1], (slots, 128)).astype(bf16)
    ids = lax.broadcasted_iota(jnp.int32, (BLOCK, slots), 0).astype(f32).astype(bf16)
    lanes = lax.broadcasted_iota(jnp.int32, (slots, 128), 1).astype(f32)
    lanes = [(lanes + first).astype(bf16) for first in range(-LOW // 2, LOW // 2, 128)]
    one = jnp.ones((), bf16)
    zero = jnp.zeros((), bf16)

    def counts(tile):
        rows = pl.ds(pl.multiple_of(tile * 16, 16), 16)
        high, spot = high_ref[rows, :], spot_ref[rows, :]
        spots = []
        for piece in range(pieces):
            wanted = jnp.where(high == piece, spot, -one)
            tall = jnp.concatenate([wanted] * (BLOCK // 16), 0)
            spots.append(jnp.where(ids == tall, one, zero))
        low = low_ref[tile]
        low_hot = jnp.concatenate([jnp.where(low == ids, one, zero) for ids in lanes], 1)
        spot_hot = jnp.concatenate(spots, 0)
        return dot(spot_hot.astype(jnp.float8_e4m3fn), low_hot.astype(jnp.float8_e4m3fn))

    def turn(add, step, carry):
        first = step * GROUP
        outs = [counts(first + inner) for inner in range(GROUP)]
        for inner, out in enumerate(outs):
            base = pl.multiple_of(blocks_ref[0, 0, first + inner] * BLOCK, BLOCK)
            for piece in range(pieces):
                add(pl.ds(base, BLOCK), piece * LOW, out[piece * BLOCK : (piece + 1) * BLOCK])
        return carry

    def add_short(rows, at, values):
        ref, at = (own_ref, at) if at < nodes else (ghost_ref, at - nodes)
        size = min(LOW, ref.shape[1] - at)
        ref[rows, at : at + size] += values[:, :size].astype(bf16)

    def add_long(rows, at, values):
        size = min(LOW, cols - at)
        sums_ref[rows, at : at + size] += values[:, :size]

    steps = (count + GROUP - 1) // GROUP
    lax.fori_loop(0, steps, functools.partial(turn, add_short), 0)
    top = ghost_ref[:BLOCK, :256]
    for first in range(0, nodes, BLOCK):
        for ref in (own_ref, ghost_ref):
            for at in range(0, ref.shape[1], 256):
                top = jnp.maximum(top, ref[first : first + BLOCK, at : at + 256])
    big = jnp.max(top.astype(f32)) >= 256.0
    flag_ref[0] = big.astype(jnp.int32)

    @pl.when(big)
    def _():
        sums_ref[...] = jnp.zeros_like(sums_ref)
        lax.fori_loop(0, steps, functools.partial(turn, add_long), 0)
        own_ref[...] = sums_ref[:, :nodes].astype(bf16)
        ghost_ref[...] = sums_ref[:, nodes:].astype(bf16)

    own_copy = pltpu.make_async_copy(own_ref, own_hbm, sems.at[5])
    own_copy.start()
    own_train_ref[...] = own_ref[:train, :]
    part_ref[...] = dot(own_ref[...], start_ref[...]) + noise_ref[...].astype(f32)

    @pl.when(big)
    def _():
        own_rest = (sums_ref[:, :nodes] - own_ref[...].astype(f32)).astype(bf16)
        part_ref[...] += dot(own_rest, start_ref[...])
        rest_ref[:, :nodes] = own_rest
        pltpu.sync_copy(rest_ref.at[:, :nodes], own_rest_ref)
        rest_ref[:, : cols - nodes] = (sums_ref[:, nodes:] - ghost_ref[...].astype(f32)).astype(bf16)
        pltpu.sync_copy(rest_ref.at[:, : cols - nodes], ghost_rest_ref)

    own_copy.wait()


def aggregate(flag_ref, start, parts, sums_ref, rest_ref):
    rows = sums_ref.shape[0]
    total = start
    for count, _, table in parts:
        total += dot(count, table)
    sums_ref[...] = total

    @pl.when(flag_ref[0] > 0)
    def _():
        for count, rest_hbm, table in parts:
            held = rest_ref.at[:, : count.shape[1]]
            pltpu.sync_copy(rest_hbm.at[:rows], held)
            sums_ref[...] += dot(held[...], table)


def hop_kernel(
    flag_ref,
    part_ref,
    ghost_ref,
    rest_hbm,
    table_ref,
    rows_ref,
    old_ref,
    labels_ref,
    start_ref,
    out_ref,
    side_ref,
    sums_ref,
    rest_ref,
    turn_ref,
    pick_ref,
):
    width = start_ref.shape[1]
    table = table_ref[...].reshape(-1, width)
    parts = ((ghost_ref[...], rest_hbm, table),)
    aggregate(flag_ref, part_ref[...], parts, sums_ref, rest_ref)
    start = normalize(sums_ref[...])
    start_ref[...] = start
    send(start, rows_ref, out_ref, turn_ref, pick_ref)
    train = labels_ref.shape[1]
    side_ref[:train, :] = old_ref[...]
    side_ref[train : 2 * train, :] = start[:train]
    turn_ref[:1, :train] = labels_ref[...]
    side_ref[2 * train :, :128] = turn_ref[:16, :].astype(f32).astype(bf16)


def train_kernel(
    flag_ref,
    place_ref,
    own_ref,
    ghost_ref,
    own_rest_hbm,
    ghost_rest_hbm,
    noise_ref,
    start_ref,
    table_ref,
    *refs,
):
    *piece_refs, out_ref, side_ref, sums_ref, rest_ref, turn_ref = refs
    train, width = sums_ref.shape
    table = table_ref[...].reshape(-1, width)
    parts = (
        (own_ref[...], own_rest_hbm, start_ref[...]),
        (ghost_ref[:train], ghost_rest_hbm, table),
    )
    aggregate(flag_ref, noise_ref[...].astype(f32), parts, sums_ref, rest_ref)
    spread(normalize(sums_ref[...]), out_ref)
    length = piece_refs[0].shape[0] - 16
    groups = len(piece_refs)
    if groups > 1:
        for shift, ref in enumerate(piece_refs):
            group = lax.rem(place_ref[1] + shift, groups)
            at = pl.multiple_of(group * length, length)
            side_ref[pl.ds(at, length), :] = ref[:length, :]
            turn_ref[pl.ds(group, 1), :] = ref[length:, :128].astype(f32)[:1]
        side_ref[groups * length :, :128] = turn_ref[:16, :].astype(bf16)


def last_kernel(
    flag_ref,
    token_ref,
    own_hbm,
    own_rest_hbm,
    ghost_rest_hbm,
    noise_hbm,
    weight_hbm,
    ghost_ref,
    table_ref,
    start_ref,
    out_ref,
    weight_ref,
    own_ref,
    noise_ref,
    sums_ref,
    rest_ref,
    sems,
):
    copies = fetch(
        ((own_hbm, own_ref), (noise_hbm.at[1, 0, 0], noise_ref), (weight_hbm, weight_ref)), sems
    )
    table = table_ref[...].reshape(-1, out_ref.shape[-1])
    out_ref[0, 0, 0] = start_ref[...]
    copies[0].wait()
    copies[1].wait()
    parts = (
        (own_ref[...], own_rest_hbm, start_ref[...]),
        (ghost_ref[...], ghost_rest_hbm, table),
    )
    aggregate(flag_ref, noise_ref[...].astype(f32), parts, sums_ref, rest_ref)
    out_ref[1, 0, 0] = normalize(sums_ref[...])
    copies[2].wait()


def shares(ref, first, share):
    return ref[:, pl.ds(pl.multiple_of(first, 128), share)].astype(f32)


def lanes_sum(values):
    total = None
    for piece in range(values.shape[1] // 128):
        part = values[:, piece * 128 : (piece + 1) * 128].astype(f32)
        total = part * part if total is None else total + part * part
    return total


def classify_kernel(
    many,
    place_ref,
    label_ref,
    zero_ref,
    one_ref,
    two_ref,
    sides_hbm,
    w_first_hbm,
    w_second_hbm,
    w_third_hbm,
    n_first_hbm,
    n_second_hbm,
    n_third_hbm,
    g_first_ref,
    g_second_ref,
    g_third_ref,
    send_ref,
    side_refs,
    w_first_ref,
    w_second_ref,
    w_third_ref,
    n_first_ref,
    n_second_ref,
    n_third_ref,
    in_ref,
    w_third_pad_ref,
    turn_ref,
    column_ref,
    h_one_ref,
    h_two_ref,
    slope_one_ref,
    slope_two_ref,
    d_one_ref,
    d_two_ref,
    d_three_ref,
    sems,
):
    classes = w_third_ref.shape[0]
    hid = w_second_ref.shape[0]
    width = two_ref.shape[2]
    wide = w_third_pad_ref.shape[0]
    train = two_ref.shape[1]
    scale = noise_mult * clip_bound
    place = place_ref[0]
    pairs = (
        (w_first_hbm, w_first_ref),
        (w_second_hbm, w_second_ref),
        (w_third_hbm, w_third_ref),
        (n_first_hbm, n_first_ref),
        (n_second_hbm, n_second_ref),
        (n_third_hbm, n_third_ref),
    )

    def set_noise():
        g_first_ref[...] = scale * n_first_ref[...]
        g_second_ref[...] = scale * n_second_ref[...]
        g_third_ref[...] = scale * n_third_ref[...]

    def pad():
        w_third_pad_ref[...] = jnp.zeros_like(w_third_pad_ref)
        w_third_pad_ref[:classes, :] = w_third_ref[...]

    def column(row, turned, lane):
        column_ref[row : row + train, :] = jnp.broadcast_to(
            turned[:train, lane : lane + 1], (train, 128)
        ).astype(jnp.int32)

    if many:

        @pl.when(pl.program_id(0) == 0)
        def _():
            for copy in fetch(pairs, sems):
                copy.wait()
            set_noise()
            pad()

        groups = label_ref.shape[0]
        turn_ref[:groups, :train] = label_ref[...].astype(f32)
        turned = turn_ref[...].T
        for group in range(groups):
            column(group * train, turned, group)
        for hop, ref in enumerate((zero_ref, one_ref)):
            in_ref[:, hop * width : (hop + 1) * width] = ref[...].reshape(-1, width)
    else:
        chips = len(side_refs)
        copies = fetch(tuple(zip(sides_hbm, side_refs)) + pairs[1:], sems)
        for copy in copies[:chips]:
            copy.wait()
        groups = two_ref.shape[0] // chips
        rows = groups * train
        for shift, ref in enumerate(side_refs):
            part = lax.rem(place // 2 - shift + chips, chips)
            at = pl.multiple_of(part * rows, rows)
            for group in range(groups):
                for hop in range(2):
                    first = (2 * group + hop) * train
                    in_ref[pl.ds(at + group * train, train), hop * width : (hop + 1) * width] = ref[
                        first : first + train, :
                    ]
            turn_ref[pl.ds(pl.multiple_of(part * 16, 16), 16), :] = ref[2 * rows :, :128].astype(f32)
        turned = turn_ref[...].T
        for part in range(chips):
            for group in range(groups):
                column((part * groups + group) * train, turned, part * 16 + group)
    in_ref[:, 2 * width :] = two_ref[...].reshape(-1, width)
    if not many:
        copies = copies[chips:]

    def activate(values, h_ref, slope_ref, rows):
        sigma = 0.5 + 0.5 * jnp.tanh(0.5 * values)
        out = values * sigma
        slope_ref[rows, :] = sigma + out * (1.0 - sigma)
        h_ref[rows, :] = out.astype(bf16)
        return lanes_sum(out)

    def back(values, slope_ref, d_ref, rows):
        out = values * slope_ref[rows, :]
        d_ref[rows, :] = out.astype(bf16)
        return lanes_sum(out)

    def layer(product, finish, *refs):
        sums = []
        values = product(cuts[0])
        for at, cut in enumerate(cuts):
            ahead = product(cuts[at + 1]) if at + 1 < len(cuts) else None
            sums.append(finish(values, *refs, cut))
            values = ahead
        return jnp.concatenate(sums, 0)

    step = 256
    cuts = [slice(at, at + step) for at in range(0, in_ref.shape[0], step)]
    sq_in = lanes_sum(in_ref[...])
    sq_one = layer(
        lambda cut: dot(in_ref[cut, :], w_first_ref[...]), activate, h_one_ref, slope_one_ref
    )
    if not many:
        copies[0].wait()
    sq_two = layer(
        lambda cut: dot(h_one_ref[cut, :], w_second_ref[...]), activate, h_two_ref, slope_two_ref
    )
    if not many:
        copies[1].wait()
        pad()
    logits = dot_nt(h_two_ref[...], w_third_pad_ref[...])
    ids = lax.broadcasted_iota(jnp.int32, (logits.shape[0], wide), 1)
    expo = jnp.where(ids < classes, jnp.exp(logits), 0.0)
    probs = expo / jnp.sum(expo, -1, keepdims=True)
    label = column_ref[:, :1]
    d_three = (probs - jnp.where(ids == label, 1.0, 0.0)).astype(bf16)
    sq_dthree = lanes_sum(d_three)
    d_three_ref[...] = d_three
    sq_dtwo = layer(
        lambda cut: dot(d_three_ref[cut, :], w_third_pad_ref[...]), back, slope_two_ref, d_two_ref
    )
    sq_done = layer(
        lambda cut: dot_nt(d_two_ref[cut, :], w_second_ref[...]), back, slope_one_ref, d_one_ref
    )

    def total(values):
        return jnp.sum(values, -1, keepdims=True)

    norm = jnp.sqrt(
        total(sq_in) * total(sq_done)
        + total(sq_one) * total(sq_dtwo)
        + total(sq_two) * total(sq_dthree)
    )
    factor = clip_bound / jnp.maximum(norm, clip_bound)

    if not many:
        for copy in copies[2:]:
            copy.wait()
        set_noise()
    share_one, share = g_first_ref.shape[0], g_second_ref.shape[0]
    places = [place] if many else [place, place + 1 - 2 * (place % 2)]

    def left(ref, share):
        if share % 128 == 0:
            picked = [shares(ref, at * share, share) for at in places]
            return (jnp.concatenate(picked, 1) * factor).astype(bf16)
        length, count = ref.shape[1], share * len(places)
        most = 128 - math.gcd(count, 128)
        size = min(length, -(-(count + most) // 128) * 128)
        first = [at * share for at in places]
        least = functools.reduce(jnp.minimum, first)
        start = jnp.minimum(least // 128 * 128, length - size)
        rows = lax.broadcasted_iota(jnp.int32, (size, count), 0)
        cols = lax.broadcasted_iota(jnp.int32, (size, count), 1)
        wanted = cols + (first[0] - start)
        for at, other in enumerate(first[1:], 1):
            wanted = jnp.where(cols >= at * share, cols - at * share + (other - start), wanted)
        window = ref[:, pl.ds(pl.multiple_of(start, 128), size)]
        picked = dot(window, jnp.where(rows == wanted, 1.0, 0.0).astype(bf16))
        return (picked * factor).astype(bf16)

    sum_one = dot_tn(left(in_ref, share_one), d_one_ref[...])
    sum_two = dot_tn(left(h_one_ref, share), d_two_ref[...])
    sum_three = dot_tn(d_three, left(h_two_ref, share))
    g_first_ref[...] += sum_one[:share_one]
    g_second_ref[...] += sum_two[:share]
    g_third_ref[...] += sum_three[:classes, :share]
    if not many:
        send_ref[:share_one, :] = sum_one[share_one:].astype(bf16)
        send_ref[share_one : share_one + share, :] = sum_two[share:].astype(bf16)
        first = share_one + share
        for at in range(0, classes, 32):
            cols = slice(at // 32 * share, (at // 32 + 1) * share)
            send_ref[first : first + 32, cols] = sum_three[at : at + 32, share:].astype(bf16)


def finish_kernel(got_ref, one_ref, two_ref, three_ref, g_first_ref, g_second_ref, g_third_ref):
    share_one, share = one_ref.shape[0], two_ref.shape[0]
    g_first_ref[...] = one_ref[...] + got_ref[:share_one, :].astype(f32)
    g_second_ref[...] = two_ref[...] + got_ref[share_one : share_one + share, :].astype(f32)
    first = share_one + share
    classes = three_ref.shape[0]
    for at in range(0, classes, 32):
        size = min(32, classes - at)
        cols = slice(at // 32 * share, (at // 32 + 1) * share)
        got = got_ref[first : first + 32, cols].astype(f32)
        g_third_ref[at : at + size, :] = three_ref[at : at + size, :] + got[:size]


def call(kernel, mib, outs, ins, scratch):
    def shape_of(shape, dtype, space):
        if space is None or space is HBM:
            return (space or VMEM)(shape, dtype)
        return jax.ShapeDtypeStruct(shape, dtype)

    def block(space):
        return pl.BlockSpec(memory_space=VMEM if space is None else space)

    def held(value, space):
        if space is None or space is HBM:
            return pltpu.with_memory_space_constraint(value, space or VMEM)
        return value

    return pl.pallas_call(
        kernel,
        out_shape=[shape_of(*out) for out in outs],
        in_specs=[block(space) for _, space in ins],
        out_specs=[block(space) for _, _, space in outs],
        scratch_shapes=scratch,
        compiler_params=params(mib),
    )(*[held(value, space) for value, space in ins])


def local(
    axes,
    feats,
    hop_noise,
    send_rows,
    tile_block,
    tile_src,
    tile_dst,
    tile_count,
    labels,
    w_first,
    w_second,
    w_third,
    noise_first,
    noise_second,
    noise_third,
):
    nodes, width = feats.shape[2:]
    parts, each = send_rows.shape[2:]
    ghosts = parts * each
    tiles = tile_src.shape[2]
    slots = tile_src.shape[3]
    train = labels.shape[2]
    classes = w_third.shape[1]
    hid = w_second.shape[0]
    d_in = w_first.shape[0]
    cols = nodes + ghosts
    rows = send_rows.reshape(parts, each)
    turn = VMEM((128, 128), jnp.int32)
    pick = VMEM((ghosts, nodes), bf16)
    dom = axes[:-1]
    members = lax.axis_size(axes)
    few = len(axes) == 3
    copies = members // 2 if few else 1

    def every(value, *names):
        for name in names:
            value = lax.all_gather(value, name, axis=0, tiled=True)
        return value

    start0, out0, own0 = call(
        first_kernel,
        16,
        [
            ((nodes, width), bf16, None),
            ((parts, each, width), bf16, None),
            ((train, width), bf16, None),
        ],
        [(feats, HBM), (send_rows, HBM)],
        [VMEM((nodes, width), bf16), VMEM((parts, each), jnp.int32), turn, pick, DMA((2,))],
    )
    table0 = lax.all_to_all(out0, dom, split_axis=0, concat_axis=0, tiled=True)
    own, ghost, own_train, noise_train, part1, flag, own_rest, ghost_rest = call(
        build_kernel,
        28,
        [
            ((nodes, nodes), bf16, HBM),
            ((nodes, ghosts), bf16, None),
            ((train, nodes), bf16, None),
            ((train, width), bf16, None),
            ((nodes, width), f32, None),
            ((1,), jnp.int32, SMEM),
            ((nodes, nodes), bf16, HBM),
            ((nodes, ghosts), bf16, HBM),
        ],
        [
            (tile_block, HBM),
            (tile_count, SMEM),
            (tile_src, HBM),
            (tile_dst, HBM),
            (hop_noise, HBM),
            (start0, None),
        ],
        [
            VMEM((tiles, slots), jnp.int32),
            VMEM((tiles, slots), jnp.int32),
            VMEM((nodes, width), bf16),
            VMEM((tiles, slots, 128), bf16),
            VMEM((tiles * 16, slots), bf16),
            VMEM((tiles * 16, slots), bf16),
            VMEM((nodes, cols), f32),
            VMEM((nodes, max(nodes, ghosts)), bf16),
            VMEM((nodes, nodes), bf16),
            SMEM(tile_block.shape, jnp.int32),
            DMA((6,)),
        ],
    )
    start1, out1, side = call(
        hop_kernel,
        16,
        [
            ((nodes, width), bf16, None),
            ((parts, each, width), bf16, None),
            ((2 * train + 16, width), bf16, None),
        ],
        [
            (flag, SMEM),
            (part1, None),
            (ghost, None),
            (ghost_rest, HBM),
            (table0, None),
            (rows, VMEM),
            (own0, None),
            (labels.reshape(1, train), VMEM),
        ],
        [VMEM((nodes, width), f32), VMEM((nodes, ghosts), bf16), turn, pick],
    )
    table1 = lax.all_to_all(out1, dom, split_axis=0, concat_axis=0, tiled=True)
    place = jnp.stack([lax.axis_index(dom), lax.axis_index("grp")]).astype(jnp.int32)
    grp = lax.axis_size("grp")

    def shifted(value, name, size, step):
        return [
            lax.ppermute(value, name, [((at + step * shift) % size, at) for at in range(size)])
            for shift in range(1, size)
        ]

    sides = [side] + (shifted(side, "grp", grp, 1) if few else [])
    last, side = call(
        train_kernel,
        12,
        [
            ((copies, train, width), bf16, None),
            ((len(sides) * 2 * train + 16, width), bf16, None),
        ],
        [
            (flag, SMEM),
            (place, SMEM),
            (own_train, None),
            (ghost, None),
            (own_rest, HBM),
            (ghost_rest, HBM),
            (noise_train, None),
            (start1, None),
            (table1, None),
        ]
        + [(value, None) for value in sides],
        [
            VMEM((train, width), f32),
            VMEM((train, max(nodes, ghosts)), bf16),
            VMEM((128, 128), f32),
        ],
    )
    if few:
        every2 = lax.all_to_all(last, ("chip", "grp"), split_axis=0, concat_axis=0, tiled=True)
        sides = [side] + shifted(side, "chip", parts // 2, -1)
    else:
        every0, every1, every2 = (
            every(value, axes) for value in (own0[None], start1[None, :train], last)
        )
        every_label = every(labels.reshape(1, train), axes)
    hop_feats, held_first = call(
        last_kernel,
        16,
        [((2, 1, 1, nodes, width), bf16, VMEM), (w_first.shape, bf16, None)],
        [
            (flag, SMEM),
            (side, None),
            (own, HBM),
            (own_rest, HBM),
            (ghost_rest, HBM),
            (hop_noise, HBM),
            (w_first, HBM),
            (ghost, None),
            (table1, None),
            (start1, None),
        ],
        [
            VMEM((nodes, nodes), bf16),
            VMEM((nodes, width), bf16),
            VMEM((nodes, width), f32),
            VMEM((nodes, max(nodes, ghosts)), bf16),
            DMA((3,)),
        ],
    )
    chunk = train * (copies if few else min(members, 32))
    groups = chunk // train
    wide = (classes + 255) // 256 * 256
    fixed = (w_first, w_second, w_third.T, noise_first, noise_second, noise_third.T)
    scratch = [VMEM(value.shape, value.dtype) for value in fixed]
    scratch += [
        VMEM((chunk, d_in), bf16),
        VMEM((wide, hid), bf16),
        VMEM((128, 128), f32),
        VMEM((chunk, 128), jnp.int32),
        VMEM((chunk, hid), bf16),
        VMEM((chunk, hid), bf16),
        VMEM((chunk, hid), f32),
        VMEM((chunk, hid), f32),
        VMEM((chunk, hid), bf16),
        VMEM((chunk, hid), bf16),
        VMEM((chunk, wide), bf16),
        DMA((16,)),
    ]
    if few:
        chips = parts // 2

        def classify(place_ref, *refs):
            sides_in, rest = refs[:chips], refs[chips:]
            two_ref, first_ref, *outs = rest[:11]
            held, rest = rest[11 : 11 + chips], rest[11 + chips :]
            classify_kernel(
                False,
                place_ref,
                None,
                None,
                None,
                two_ref,
                sides_in,
                first_ref,
                *outs,
                held,
                first_ref,
                *rest,
            )

        rows = noise_first.shape[0] + noise_second.shape[0] + 32
        *own_sums, other = call(
            classify,
            44,
            [(value.shape, f32, None) for value in fixed[3:]] + [((rows, hid), bf16, None)],
            [(place, SMEM)]
            + [(value, HBM) for value in sides]
            + [(every2, None), (held_first, None)]
            + [(value, HBM) for value in fixed[1:]],
            [VMEM(value.shape, bf16) for value in sides] + scratch[1:],
        )
        got = lax.ppermute(other, "core", [(0, 1), (1, 0)])
        first, second, third = call(
            finish_kernel,
            16,
            [(value.shape, f32, VMEM) for value in fixed[3:]],
            [(got, None)] + [(value, None) for value in own_sums],
            [],
        )
    else:

        ins = (every_label, every0, every1, every2)

        def classify(place_ref, label_ref, zero_ref, one_ref, two_ref, *rest):
            classify_kernel(
                True,
                place_ref,
                label_ref,
                zero_ref,
                one_ref,
                two_ref,
                None,
                *rest[:9],
                None,
                None,
                *rest[9:],
            )

        def whole(value):
            return pl.BlockSpec(value.shape, lambda i: (0, 0))

        def piece(value):
            return pl.BlockSpec(
                (groups,) + value.shape[1:], lambda i: (i,) + (0,) * (value.ndim - 1)
            )

        first, second, third = pl.pallas_call(
            classify,
            grid=(members // groups,),
            out_shape=[jax.ShapeDtypeStruct(value.shape, f32) for value in fixed[3:]],
            in_specs=[pl.BlockSpec(memory_space=SMEM)]
            + [piece(value) for value in ins]
            + [pl.BlockSpec(memory_space=HBM) for value in fixed],
            out_specs=[whole(value) for value in fixed[3:]],
            scratch_shapes=scratch,
            compiler_params=params(56),
        )(place, *ins, *fixed)
    return (hop_feats, first, second, third.T)


def solution(mesh):
    dom, grp = mesh.shape["dom"], mesh.shape["grp"]
    names = ("dom", "grp")
    if dom * grp <= FEW and dom <= 8 and dom % 2 == 0:
        names = ("chip", "core", "grp")
        mesh = jax.sharding.Mesh(mesh.devices.reshape(dom // 2, 2, grp), names)
    doms, grps = names[:-1], "grp"
    in_specs = (
        P(doms, grps, None, None),
        P(None, doms, grps, None, None),
        P(doms, grps, None, None),
        P(doms, grps, None),
        P(doms, grps, None, None),
        P(doms, grps, None, None),
        P(doms, grps),
        P(doms, grps, None),
        P(),
        P(),
        P(),
        P(doms, None),
        P(doms, None),
        P(doms, None),
    )
    out_specs = (P(None, doms, grps, None, None), P(doms, None), P(doms, None), P(doms, None))
    return jax.shard_map(
        functools.partial(local, names),
        mesh=mesh,
        in_specs=in_specs,
        out_specs=out_specs,
        check_vma=False,
    )
```

```python
import functools
import math

import jax
import jax.numpy as jnp
from jax import lax
from jax.experimental import pallas as pl
from jax.experimental.pallas import tpu as pltpu
from jax.sharding import PartitionSpec as P

BLOCK = 128
LOW = 256
GROUP = 8
clip_bound = 4.0
noise_mult = 1.0

f32 = jnp.float32
bf16 = jnp.bfloat16
VMEM = pltpu.VMEM
SMEM = pltpu.SMEM
HBM = pltpu.HBM
DMA = pltpu.SemaphoreType.DMA


FEW = 32


def params(mib):
    return pltpu.CompilerParams(vmem_limit_bytes=mib * 1024 * 1024)


def fetch(pairs, sems):
    copies = [pltpu.make_async_copy(*pair, sems.at[at]) for at, pair in enumerate(pairs)]
    for copy in copies:
        copy.start()
    return copies


def normalize(values):
    return (values * lax.rsqrt(jnp.sum(values * values, -1, keepdims=True) + 1e-06)).astype(bf16)


def dot(left, right):
    return jnp.dot(left, right, preferred_element_type=f32)


def dot_nt(left, right):
    return lax.dot_general(left, right, (((1,), (1,)), ((), ())), preferred_element_type=f32)


def dot_tn(left, right):
    return lax.dot_general(left, right, (((0,), (0,)), ((), ())), preferred_element_type=f32)


def choose(rows_ref, turn_ref, pick_ref):
    parts, each = rows_ref.shape
    turn_ref[:parts, :each] = rows_ref[...]
    columns = turn_ref[...].T
    spots = lax.broadcasted_iota(jnp.int32, (each, pick_ref.shape[1]), 1)
    for part in range(parts):
        wanted = columns[:each, part : part + 1]
        pick_ref[part * each : (part + 1) * each, :] = jnp.where(wanted == spots, 1.0, 0.0).astype(
            bf16
        )


def post(rows, staged_ref, out_hbm, sem):
    staged_ref[...] = rows.reshape(staged_ref.shape)
    copy = pltpu.make_async_copy(staged_ref, out_hbm, sem)
    copy.start()
    return copy


def first_kernel(
    feats_hbm,
    rows_hbm,
    src_hbm,
    dst_hbm,
    start_ref,
    out_hbm,
    own_ref,
    src_ref,
    dst_ref,
    feats_ref,
    rows_ref,
    turn_ref,
    pick_ref,
    staged_ref,
    sems,
):
    copies = fetch(
        (
            (rows_hbm.at[0, 0], rows_ref),
            (feats_hbm.at[0, 0], feats_ref),
            (src_hbm.at[0, 0], src_ref),
            (dst_hbm.at[0, 0], dst_ref),
        ),
        sems,
    )
    copies[0].wait()
    choose(rows_ref, turn_ref, pick_ref)
    copies[1].wait()
    sent = normalize(dot(pick_ref[...], feats_ref[...]))
    out_copy = post(sent, staged_ref, out_hbm, sems.at[4])
    start = normalize(feats_ref[...].astype(f32))
    start_ref[...] = start
    own_ref[...] = start[: own_ref.shape[0]]
    copies[2].wait()
    copies[3].wait()
    out_copy.wait()


def build_kernel(
    blocks_hbm,
    count_ref,
    src_ref,
    dst_ref,
    noise_hbm,
    start_ref,
    own_hbm,
    ghost_ref,
    own_train_ref,
    noise_train_ref,
    part_ref,
    flag_ref,
    own_rest_ref,
    ghost_rest_ref,
    noise_ref,
    low_ref,
    high_ref,
    spot_ref,
    sums_ref,
    rest_ref,
    own_ref,
    blocks_ref,
    sems,
):
    train = own_train_ref.shape[0]
    copies = fetch(
        (
            (blocks_hbm, blocks_ref),
            (noise_hbm.at[0, 0, 0], noise_ref),
            (noise_hbm.at[1, 0, 0, :train], noise_train_ref),
        ),
        sems,
    )
    nodes, cols = sums_ref.shape
    pieces = -(-cols // LOW)
    tiles, slots = src_ref.shape
    own_ref[...] = jnp.zeros_like(own_ref)
    ghost_ref[...] = jnp.zeros_like(ghost_ref)
    copies[0].wait()
    count = count_ref[0, 0]

    def sixteen(values):
        wide = jnp.broadcast_to(values.astype(f32)[:, None, :], (tiles, 16, slots))
        return wide.reshape(tiles * 16, slots).astype(bf16)

    src = src_ref[...]
    dst = dst_ref[...]
    tile_ids = lax.broadcasted_iota(jnp.int32, (tiles, slots), 0)
    high_ref[...] = sixteen(src // LOW)
    spot_ref[...] = sixteen(jnp.where((dst < BLOCK) & (tile_ids < count), dst, -1))
    low = (src % LOW - LOW // 2).astype(f32).T
    for tile in range(tiles):
        low_ref[tile] = jnp.broadcast_to(low[:, tile : tile + 1], (slots, 128)).astype(bf16)
    ids = lax.broadcasted_iota(jnp.int32, (BLOCK, slots), 0).astype(f32).astype(bf16)
    lanes = lax.broadcasted_iota(jnp.int32, (slots, 128), 1).astype(f32)
    lanes = [(lanes + first).astype(bf16) for first in range(-LOW // 2, LOW // 2, 128)]
    one = jnp.ones((), bf16)
    zero = jnp.zeros((), bf16)

    def counts(tile):
        rows = pl.ds(pl.multiple_of(tile * 16, 16), 16)
        high, spot = high_ref[rows, :], spot_ref[rows, :]
        spots = []
        for piece in range(pieces):
            wanted = jnp.where(high == piece, spot, -one)
            tall = jnp.concatenate([wanted] * (BLOCK // 16), 0)
            spots.append(jnp.where(ids == tall, one, zero))
        low = low_ref[tile]
        low_hot = jnp.concatenate([jnp.where(low == ids, one, zero) for ids in lanes], 1)
        spot_hot = jnp.concatenate(spots, 0)
        return dot(spot_hot.astype(jnp.float8_e4m3fn), low_hot.astype(jnp.float8_e4m3fn))

    def turn(add, step, carry):
        first = step * GROUP
        outs = [counts(first + inner) for inner in range(GROUP)]
        for inner, out in enumerate(outs):
            base = pl.multiple_of(blocks_ref[0, 0, first + inner] * BLOCK, BLOCK)
            for piece in range(pieces):
                add(pl.ds(base, BLOCK), piece * LOW, out[piece * BLOCK : (piece + 1) * BLOCK])
        return carry

    def add_short(rows, at, values):
        ref, at = (own_ref, at) if at < nodes else (ghost_ref, at - nodes)
        size = min(LOW, ref.shape[1] - at)
        ref[rows, at : at + size] += values[:, :size].astype(bf16)

    def add_long(rows, at, values):
        size = min(LOW, cols - at)
        sums_ref[rows, at : at + size] += values[:, :size]

    steps = (count + GROUP - 1) // GROUP
    lax.fori_loop(0, steps, functools.partial(turn, add_short), 0)
    top = ghost_ref[:BLOCK, :256]
    for first in range(0, nodes, BLOCK):
        for ref in (own_ref, ghost_ref):
            for at in range(0, ref.shape[1], 256):
                top = jnp.maximum(top, ref[first : first + BLOCK, at : at + 256])
    big = jnp.max(top.astype(f32)) >= 256.0
    flag_ref[0] = big.astype(jnp.int32)

    @pl.when(big)
    def _():
        sums_ref[...] = jnp.zeros_like(sums_ref)
        lax.fori_loop(0, steps, functools.partial(turn, add_long), 0)
        own_ref[...] = sums_ref[:, :nodes].astype(bf16)
        ghost_ref[...] = sums_ref[:, nodes:].astype(bf16)

    own_copy = pltpu.make_async_copy(own_ref, own_hbm, sems.at[3])
    own_copy.start()
    own_train_ref[...] = own_ref[:train, :]
    for copy in copies[1:]:
        copy.wait()
    part_ref[...] = dot(own_ref[...], start_ref[...]) + noise_ref[...].astype(f32)

    @pl.when(big)
    def _():
        own_rest = (sums_ref[:, :nodes] - own_ref[...].astype(f32)).astype(bf16)
        part_ref[...] += dot(own_rest, start_ref[...])
        rest_ref[:, :nodes] = own_rest
        pltpu.sync_copy(rest_ref.at[:, :nodes], own_rest_ref)
        rest_ref[:, : cols - nodes] = (sums_ref[:, nodes:] - ghost_ref[...].astype(f32)).astype(bf16)
        pltpu.sync_copy(rest_ref.at[:, : cols - nodes], ghost_rest_ref)

    own_copy.wait()


def aggregate(flag_ref, start, parts, sums_ref, rest_ref):
    rows = sums_ref.shape[0]
    total = start
    for count, _, table in parts:
        total += dot(count, table)
    sums_ref[...] = total

    @pl.when(flag_ref[0] > 0)
    def _():
        for count, rest_hbm, table in parts:
            held = rest_ref.at[:, : count.shape[1]]
            pltpu.sync_copy(rest_hbm.at[:rows], held)
            sums_ref[...] += dot(held[...], table)


def hop_kernel(
    flag_ref,
    part_ref,
    ghost_ref,
    rest_hbm,
    table_ref,
    rows_ref,
    old_ref,
    labels_ref,
    start_ref,
    out_hbm,
    side_ref,
    sums_ref,
    rest_ref,
    turn_ref,
    pick_ref,
    staged_ref,
    sem,
):
    width = start_ref.shape[1]
    table = table_ref[...].reshape(-1, width)
    parts = ((ghost_ref[...], rest_hbm, table),)
    aggregate(flag_ref, part_ref[...], parts, sums_ref, rest_ref)
    choose(rows_ref, turn_ref, pick_ref)
    start = normalize(sums_ref[...])
    start_ref[...] = start
    out_copy = post(dot(pick_ref[...], start).astype(bf16), staged_ref, out_hbm, sem)
    train = labels_ref.shape[1]
    side_ref[:train, :] = old_ref[...]
    side_ref[train : 2 * train, :] = start[:train]
    turn_ref[:1, :train] = labels_ref[...]
    side_ref[2 * train :, :128] = turn_ref[:16, :].astype(f32).astype(bf16)
    out_copy.wait()


def train_kernel(
    flag_ref,
    place_ref,
    own_ref,
    ghost_ref,
    own_rest_hbm,
    ghost_rest_hbm,
    noise_ref,
    start_ref,
    table_ref,
    *refs,
):
    *piece_refs, out_hbm, side_ref, sums_ref, rest_ref, turn_ref, staged_ref, sem = refs
    train, width = sums_ref.shape
    table = table_ref[...].reshape(-1, width)
    parts = (
        (own_ref[...], own_rest_hbm, start_ref[...]),
        (ghost_ref[:train], ghost_rest_hbm, table),
    )
    aggregate(flag_ref, noise_ref[...].astype(f32), parts, sums_ref, rest_ref)
    last = jnp.broadcast_to(normalize(sums_ref[...])[None], staged_ref.shape)
    out_copy = post(last, staged_ref, out_hbm, sem)
    length = piece_refs[0].shape[0] - 16
    groups = len(piece_refs)
    if groups > 1:
        for shift, ref in enumerate(piece_refs):
            group = lax.rem(place_ref[1] + shift, groups)
            at = pl.multiple_of(group * length, length)
            side_ref[pl.ds(at, length), :] = ref[:length, :]
            turn_ref[pl.ds(group, 1), :] = ref[length:, :128].astype(f32)[:1]
        side_ref[groups * length :, :128] = turn_ref[:16, :].astype(bf16)
    out_copy.wait()


def last_kernel(
    flag_ref,
    token_ref,
    own_hbm,
    own_rest_hbm,
    ghost_rest_hbm,
    noise_hbm,
    weight_hbm,
    ghost_ref,
    table_ref,
    start_ref,
    out_ref,
    weight_ref,
    own_ref,
    noise_ref,
    sums_ref,
    rest_ref,
    sems,
):
    copies = fetch(
        ((own_hbm, own_ref), (noise_hbm.at[1, 0, 0], noise_ref), (weight_hbm, weight_ref)), sems
    )
    table = table_ref[...].reshape(-1, out_ref.shape[-1])
    out_ref[0, 0, 0] = start_ref[...]
    copies[0].wait()
    copies[1].wait()
    parts = (
        (own_ref[...], own_rest_hbm, start_ref[...]),
        (ghost_ref[...], ghost_rest_hbm, table),
    )
    aggregate(flag_ref, noise_ref[...].astype(f32), parts, sums_ref, rest_ref)
    out_ref[1, 0, 0] = normalize(sums_ref[...])
    copies[2].wait()


def shares(ref, first, share):
    return ref[:, pl.ds(pl.multiple_of(first, 128), share)].astype(f32)


def lanes_sum(values):
    total = None
    for piece in range(values.shape[1] // 128):
        part = values[:, piece * 128 : (piece + 1) * 128].astype(f32)
        total = part * part if total is None else total + part * part
    return total


def classify_kernel(
    many,
    place_ref,
    label_ref,
    zero_ref,
    one_ref,
    two_ref,
    side_refs,
    w_first_hbm,
    w_second_hbm,
    w_third_hbm,
    n_first_hbm,
    n_second_hbm,
    n_third_hbm,
    g_first_ref,
    g_second_ref,
    g_third_ref,
    send_ref,
    w_first_ref,
    w_second_ref,
    w_third_ref,
    n_first_ref,
    n_second_ref,
    n_third_ref,
    in_ref,
    w_third_pad_ref,
    turn_ref,
    column_ref,
    h_one_ref,
    h_two_ref,
    slope_one_ref,
    slope_two_ref,
    d_one_ref,
    d_two_ref,
    d_three_ref,
    sems,
):
    classes = w_third_ref.shape[0]
    hid = w_second_ref.shape[0]
    width = two_ref.shape[2]
    wide = w_third_pad_ref.shape[0]
    train = two_ref.shape[1]
    scale = noise_mult * clip_bound
    place = place_ref[0]
    pairs = (
        (w_first_hbm, w_first_ref),
        (w_second_hbm, w_second_ref),
        (w_third_hbm, w_third_ref),
        (n_first_hbm, n_first_ref),
        (n_second_hbm, n_second_ref),
        (n_third_hbm, n_third_ref),
    )

    def set_noise():
        g_first_ref[...] = scale * n_first_ref[...]
        g_second_ref[...] = scale * n_second_ref[...]
        g_third_ref[...] = scale * n_third_ref[...]

    def pad():
        w_third_pad_ref[...] = jnp.zeros_like(w_third_pad_ref)
        w_third_pad_ref[:classes, :] = w_third_ref[...]

    def column(row, turned, lane):
        column_ref[row : row + train, :] = jnp.broadcast_to(
            turned[:train, lane : lane + 1], (train, 128)
        ).astype(jnp.int32)

    if many:

        @pl.when(pl.program_id(0) == 0)
        def _():
            for copy in fetch(pairs, sems):
                copy.wait()
            set_noise()
            pad()

        groups = label_ref.shape[0]
        turn_ref[:groups, :train] = label_ref[...].astype(f32)
        turned = turn_ref[...].T
        for group in range(groups):
            column(group * train, turned, group)
        for hop, ref in enumerate((zero_ref, one_ref)):
            in_ref[:, hop * width : (hop + 1) * width] = ref[...].reshape(-1, width)
    else:
        chips = len(side_refs)
        copies = fetch(pairs[1:], sems)
        groups = two_ref.shape[0] // chips
        rows = groups * train
        for shift, ref in enumerate(side_refs):
            part = lax.rem(place // 2 - shift + chips, chips)
            at = pl.multiple_of(part * rows, rows)
            for group in range(groups):
                for hop in range(2):
                    first = (2 * group + hop) * train
                    in_ref[pl.ds(at + group * train, train), hop * width : (hop + 1) * width] = ref[
                        first : first + train, :
                    ]
            turn_ref[pl.ds(pl.multiple_of(part * 16, 16), 16), :] = ref[2 * rows :, :128].astype(f32)
        turned = turn_ref[...].T
        for part in range(chips):
            for group in range(groups):
                column((part * groups + group) * train, turned, part * 16 + group)
    in_ref[:, 2 * width :] = two_ref[...].reshape(-1, width)

    def activate(values, h_ref, slope_ref, rows):
        sigma = 0.5 + 0.5 * jnp.tanh(0.5 * values)
        out = values * sigma
        slope_ref[rows, :] = sigma + out * (1.0 - sigma)
        h_ref[rows, :] = out.astype(bf16)
        return lanes_sum(out)

    def back(values, slope_ref, d_ref, rows):
        out = values * slope_ref[rows, :]
        d_ref[rows, :] = out.astype(bf16)
        return lanes_sum(out)

    def layer(product, finish, *refs):
        sums = []
        values = product(cuts[0])
        for at, cut in enumerate(cuts):
            ahead = product(cuts[at + 1]) if at + 1 < len(cuts) else None
            sums.append(finish(values, *refs, cut))
            values = ahead
        return jnp.concatenate(sums, 0)

    step = min(512, in_ref.shape[0])
    cuts = [slice(at, at + step) for at in range(0, in_ref.shape[0], step)]
    sq_in = lanes_sum(in_ref[...])
    sq_one = layer(
        lambda cut: dot(in_ref[cut, :], w_first_ref[...]), activate, h_one_ref, slope_one_ref
    )
    if not many:
        copies[0].wait()
    sq_two = layer(
        lambda cut: dot(h_one_ref[cut, :], w_second_ref[...]), activate, h_two_ref, slope_two_ref
    )
    if not many:
        copies[1].wait()
        pad()
    logits = dot_nt(h_two_ref[...], w_third_pad_ref[...])
    ids = lax.broadcasted_iota(jnp.int32, (logits.shape[0], wide), 1)
    expo = jnp.where(ids < classes, jnp.exp(logits), 0.0)
    probs = expo / jnp.sum(expo, -1, keepdims=True)
    label = column_ref[:, :1]
    d_three = (probs - jnp.where(ids == label, 1.0, 0.0)).astype(bf16)
    sq_dthree = lanes_sum(d_three)
    d_three_ref[...] = d_three
    sq_dtwo = layer(
        lambda cut: dot(d_three_ref[cut, :], w_third_pad_ref[...]), back, slope_two_ref, d_two_ref
    )
    sq_done = layer(
        lambda cut: dot_nt(d_two_ref[cut, :], w_second_ref[...]), back, slope_one_ref, d_one_ref
    )

    def total(values):
        return jnp.sum(values, -1, keepdims=True)

    norm = jnp.sqrt(
        total(sq_in) * total(sq_done)
        + total(sq_one) * total(sq_dtwo)
        + total(sq_two) * total(sq_dthree)
    )
    factor = clip_bound / jnp.maximum(norm, clip_bound)

    if not many:
        for copy in copies[2:]:
            copy.wait()
        set_noise()
    share_one, share = g_first_ref.shape[0], g_second_ref.shape[0]
    places = [place] if many else [place, place + 1 - 2 * (place % 2)]

    def left(ref, share):
        if share % 128 == 0:
            picked = [shares(ref, at * share, share) for at in places]
            return (jnp.concatenate(picked, 1) * factor).astype(bf16)
        length, count = ref.shape[1], share * len(places)
        most = 128 - math.gcd(count, 128)
        size = min(length, -(-(count + most) // 128) * 128)
        first = [at * share for at in places]
        least = functools.reduce(jnp.minimum, first)
        start = jnp.minimum(least // 128 * 128, length - size)
        rows = lax.broadcasted_iota(jnp.int32, (size, count), 0)
        cols = lax.broadcasted_iota(jnp.int32, (size, count), 1)
        wanted = cols + (first[0] - start)
        for at, other in enumerate(first[1:], 1):
            wanted = jnp.where(cols >= at * share, cols - at * share + (other - start), wanted)
        window = ref[:, pl.ds(pl.multiple_of(start, 128), size)]
        picked = dot(window, jnp.where(rows == wanted, 1.0, 0.0).astype(bf16))
        return (picked * factor).astype(bf16)

    sum_one = dot_tn(left(in_ref, share_one), d_one_ref[...])
    sum_two = dot_tn(left(h_one_ref, share), d_two_ref[...])
    sum_three = dot_tn(d_three, left(h_two_ref, share))
    g_first_ref[...] += sum_one[:share_one]
    g_second_ref[...] += sum_two[:share]
    g_third_ref[...] += sum_three[:classes, :share]
    if not many:
        send_ref[:share_one, :] = sum_one[share_one:].astype(bf16)
        send_ref[share_one : share_one + share, :] = sum_two[share:].astype(bf16)
        first = share_one + share
        for at in range(0, classes, 32):
            cols = slice(at // 32 * share, (at // 32 + 1) * share)
            send_ref[first : first + 32, cols] = sum_three[at : at + 32, share:].astype(bf16)


def finish_kernel(got_ref, one_ref, two_ref, three_ref, g_first_ref, g_second_ref, g_third_ref):
    share_one, share = one_ref.shape[0], two_ref.shape[0]
    g_first_ref[...] = one_ref[...] + got_ref[:share_one, :].astype(f32)
    g_second_ref[...] = two_ref[...] + got_ref[share_one : share_one + share, :].astype(f32)
    first = share_one + share
    classes = three_ref.shape[0]
    for at in range(0, classes, 32):
        size = min(32, classes - at)
        cols = slice(at // 32 * share, (at // 32 + 1) * share)
        got = got_ref[first : first + 32, cols].astype(f32)
        g_third_ref[at : at + size, :] = three_ref[at : at + size, :] + got[:size]


def call(kernel, mib, outs, ins, scratch):
    def shape_of(shape, dtype, space):
        if space is None or space is HBM:
            return (space or VMEM)(shape, dtype)
        return jax.ShapeDtypeStruct(shape, dtype)

    def block(space):
        return pl.BlockSpec(memory_space=VMEM if space is None else space)

    def held(value, space):
        if space is None or space is HBM:
            return pltpu.with_memory_space_constraint(value, space or VMEM)
        return value

    return pl.pallas_call(
        kernel,
        out_shape=[shape_of(*out) for out in outs],
        in_specs=[block(space) for _, space in ins],
        out_specs=[block(space) for _, _, space in outs],
        scratch_shapes=scratch,
        compiler_params=params(mib),
    )(*[held(value, space) for value, space in ins])


def local(
    axes,
    feats,
    hop_noise,
    send_rows,
    tile_block,
    tile_src,
    tile_dst,
    tile_count,
    labels,
    w_first,
    w_second,
    w_third,
    noise_first,
    noise_second,
    noise_third,
):
    nodes, width = feats.shape[2:]
    parts, each = send_rows.shape[2:]
    ghosts = parts * each
    tiles = tile_src.shape[2]
    slots = tile_src.shape[3]
    train = labels.shape[2]
    classes = w_third.shape[1]
    hid = w_second.shape[0]
    d_in = w_first.shape[0]
    cols = nodes + ghosts
    rows = send_rows.reshape(parts, each)
    turn = VMEM((128, 128), jnp.int32)
    pick = VMEM((ghosts, nodes), bf16)
    dom = axes[:-1]
    members = lax.axis_size(axes)
    few = len(axes) == 3
    copies = members // 2 if few else 1

    def every(value, *names):
        for name in names:
            value = lax.all_gather(value, name, axis=0, tiled=True)
        return value

    staged = VMEM((parts, each, width), bf16)
    start0, out0, own0, src, dst = call(
        first_kernel,
        16,
        [
            ((nodes, width), bf16, None),
            ((parts, each, width), bf16, HBM),
            ((train, width), bf16, None),
            ((tiles, slots), jnp.int32, None),
            ((tiles, slots), jnp.int32, None),
        ],
        [(feats, HBM), (send_rows, HBM), (tile_src, HBM), (tile_dst, HBM)],
        [
            VMEM((nodes, width), bf16),
            VMEM((parts, each), jnp.int32),
            turn,
            pick,
            staged,
            DMA((5,)),
        ],
    )
    table0 = lax.all_to_all(out0, dom, split_axis=0, concat_axis=0, tiled=True)
    own, ghost, own_train, noise_train, part1, flag, own_rest, ghost_rest = call(
        build_kernel,
        28,
        [
            ((nodes, nodes), bf16, HBM),
            ((nodes, ghosts), bf16, None),
            ((train, nodes), bf16, None),
            ((train, width), bf16, None),
            ((nodes, width), f32, None),
            ((1,), jnp.int32, SMEM),
            ((nodes, nodes), bf16, HBM),
            ((nodes, ghosts), bf16, HBM),
        ],
        [
            (tile_block, HBM),
            (tile_count, SMEM),
            (src, None),
            (dst, None),
            (hop_noise, HBM),
            (start0, None),
        ],
        [
            VMEM((nodes, width), bf16),
            VMEM((tiles, slots, 128), bf16),
            VMEM((tiles * 16, slots), bf16),
            VMEM((tiles * 16, slots), bf16),
            VMEM((nodes, cols), f32),
            VMEM((nodes, max(nodes, ghosts)), bf16),
            VMEM((nodes, nodes), bf16),
            SMEM(tile_block.shape, jnp.int32),
            DMA((4,)),
        ],
    )
    start1, out1, side = call(
        hop_kernel,
        16,
        [
            ((nodes, width), bf16, None),
            ((parts, each, width), bf16, HBM),
            ((2 * train + 16, width), bf16, None),
        ],
        [
            (flag, SMEM),
            (part1, None),
            (ghost, None),
            (ghost_rest, HBM),
            (table0, None),
            (rows, VMEM),
            (own0, None),
            (labels.reshape(1, train), VMEM),
        ],
        [VMEM((nodes, width), f32), VMEM((nodes, ghosts), bf16), turn, pick, staged, DMA(())],
    )
    table1 = lax.all_to_all(out1, dom, split_axis=0, concat_axis=0, tiled=True)
    place = jnp.stack([lax.axis_index(dom), lax.axis_index("grp")]).astype(jnp.int32)
    grp = lax.axis_size("grp")

    def shifted(value, name, size, step):
        return [
            lax.ppermute(value, name, [((at + step * shift) % size, at) for at in range(size)])
            for shift in range(1, size)
        ]

    sides = [side] + (shifted(side, "grp", grp, 1) if few else [])
    last, side = call(
        train_kernel,
        12,
        [
            ((copies, train, width), bf16, HBM),
            ((len(sides) * 2 * train + 16, width), bf16, None),
        ],
        [
            (flag, SMEM),
            (place, SMEM),
            (own_train, None),
            (ghost, None),
            (own_rest, HBM),
            (ghost_rest, HBM),
            (noise_train, None),
            (start1, None),
            (table1, None),
        ]
        + [(value, None) for value in sides],
        [
            VMEM((train, width), f32),
            VMEM((train, max(nodes, ghosts)), bf16),
            VMEM((128, 128), f32),
            VMEM((copies, train, width), bf16),
            DMA(()),
        ],
    )
    if few:
        every2 = lax.all_to_all(last, ("chip", "grp"), split_axis=0, concat_axis=0, tiled=True)
        sides = [side] + shifted(side, "chip", parts // 2, -1)
    else:
        every0, every1, every2 = (
            every(value, axes) for value in (own0[None], start1[None, :train], last)
        )
        every_label = every(labels.reshape(1, train), axes)
    hop_feats, held_first = call(
        last_kernel,
        16,
        [((2, 1, 1, nodes, width), bf16, VMEM), (w_first.shape, bf16, None)],
        [
            (flag, SMEM),
            (side, None),
            (own, HBM),
            (own_rest, HBM),
            (ghost_rest, HBM),
            (hop_noise, HBM),
            (w_first, HBM),
            (ghost, None),
            (table1, None),
            (start1, None),
        ],
        [
            VMEM((nodes, nodes), bf16),
            VMEM((nodes, width), bf16),
            VMEM((nodes, width), f32),
            VMEM((nodes, max(nodes, ghosts)), bf16),
            DMA((3,)),
        ],
    )
    chunk = train * (copies if few else min(members, 32))
    groups = chunk // train
    wide = (classes + 255) // 256 * 256
    fixed = (w_first, w_second, w_third.T, noise_first, noise_second, noise_third.T)
    scratch = [VMEM(value.shape, value.dtype) for value in fixed]
    scratch += [
        VMEM((chunk, d_in), bf16),
        VMEM((wide, hid), bf16),
        VMEM((128, 128), f32),
        VMEM((chunk, 128), jnp.int32),
        VMEM((chunk, hid), bf16),
        VMEM((chunk, hid), bf16),
        VMEM((chunk, hid), f32),
        VMEM((chunk, hid), f32),
        VMEM((chunk, hid), bf16),
        VMEM((chunk, hid), bf16),
        VMEM((chunk, wide), bf16),
        DMA((16,)),
    ]
    if few:
        chips = parts // 2

        def classify(place_ref, *refs):
            sides_in, rest = refs[:chips], refs[chips:]
            two_ref, first_ref, *outs = rest[:11]
            rest = rest[11:]
            classify_kernel(
                False,
                place_ref,
                None,
                None,
                None,
                two_ref,
                sides_in,
                first_ref,
                *outs,
                first_ref,
                *rest,
            )

        rows = noise_first.shape[0] + noise_second.shape[0] + 32
        *own_sums, other = call(
            classify,
            44,
            [(value.shape, f32, None) for value in fixed[3:]] + [((rows, hid), bf16, None)],
            [(place, SMEM)]
            + [(value, None) for value in sides]
            + [(every2, None), (held_first, None)]
            + [(value, HBM) for value in fixed[1:]],
            scratch[1:],
        )
        got = lax.ppermute(other, "core", [(0, 1), (1, 0)])
        first, second, third = call(
            finish_kernel,
            16,
            [(value.shape, f32, VMEM) for value in fixed[3:]],
            [(got, None)] + [(value, None) for value in own_sums],
            [],
        )
    else:

        ins = (every_label, every0, every1, every2)

        def classify(place_ref, label_ref, zero_ref, one_ref, two_ref, *rest):
            classify_kernel(
                True,
                place_ref,
                label_ref,
                zero_ref,
                one_ref,
                two_ref,
                None,
                *rest[:9],
                None,
                *rest[9:],
            )

        def whole(value):
            return pl.BlockSpec(value.shape, lambda i: (0, 0))

        def piece(value):
            return pl.BlockSpec(
                (groups,) + value.shape[1:], lambda i: (i,) + (0,) * (value.ndim - 1)
            )

        first, second, third = pl.pallas_call(
            classify,
            grid=(members // groups,),
            out_shape=[jax.ShapeDtypeStruct(value.shape, f32) for value in fixed[3:]],
            in_specs=[pl.BlockSpec(memory_space=SMEM)]
            + [piece(value) for value in ins]
            + [pl.BlockSpec(memory_space=HBM) for value in fixed],
            out_specs=[whole(value) for value in fixed[3:]],
            scratch_shapes=scratch,
            compiler_params=params(56),
        )(place, *ins, *fixed)
    return (hop_feats, first, second, third.T)


def solution(mesh):
    dom, grp = mesh.shape["dom"], mesh.shape["grp"]
    names = ("dom", "grp")
    if dom * grp <= FEW and dom <= 8 and dom % 2 == 0:
        names = ("chip", "core", "grp")
        mesh = jax.sharding.Mesh(mesh.devices.reshape(dom // 2, 2, grp), names)
    doms, grps = names[:-1], "grp"
    in_specs = (
        P(doms, grps, None, None),
        P(None, doms, grps, None, None),
        P(doms, grps, None, None),
        P(doms, grps, None),
        P(doms, grps, None, None),
        P(doms, grps, None, None),
        P(doms, grps),
        P(doms, grps, None),
        P(),
        P(),
        P(),
        P(doms, None),
        P(doms, None),
        P(doms, None),
    )
    out_specs = (P(None, doms, grps, None, None), P(doms, None), P(doms, None), P(doms, None))
    return jax.shard_map(
        functools.partial(local, names),
        mesh=mesh,
        in_specs=in_specs,
        out_specs=out_specs,
        check_vma=False,
    )
```

```python
import functools
import math

import jax
import jax.numpy as jnp
from jax import lax
from jax.experimental import pallas as pl
from jax.experimental.pallas import tpu as pltpu
from jax.sharding import PartitionSpec as P

BLOCK = 128
LOW = 512
GROUP = 8
clip_bound = 4.0
noise_mult = 1.0

f32 = jnp.float32
bf16 = jnp.bfloat16
VMEM = pltpu.VMEM
SMEM = pltpu.SMEM
HBM = pltpu.HBM
DMA = pltpu.SemaphoreType.DMA


FEW = 32


def params(mib):
    return pltpu.CompilerParams(vmem_limit_bytes=mib * 1024 * 1024)


def fetch(pairs, sems):
    copies = [pltpu.make_async_copy(*pair, sems.at[at]) for at, pair in enumerate(pairs)]
    for copy in copies:
        copy.start()
    return copies


def normalize(values):
    return (values * lax.rsqrt(jnp.sum(values * values, -1, keepdims=True) + 1e-06)).astype(bf16)


def dot(left, right):
    return jnp.dot(left, right, preferred_element_type=f32)


def dot_nt(left, right):
    return lax.dot_general(left, right, (((1,), (1,)), ((), ())), preferred_element_type=f32)


def dot_tn(left, right):
    return lax.dot_general(left, right, (((0,), (0,)), ((), ())), preferred_element_type=f32)


def choose(rows_ref, turn_ref, pick_ref):
    parts, each = rows_ref.shape
    turn_ref[:parts, :each] = rows_ref[...]
    columns = turn_ref[...].T
    spots = lax.broadcasted_iota(jnp.int32, (each, pick_ref.shape[1]), 1)
    for part in range(parts):
        wanted = columns[:each, part : part + 1]
        pick_ref[part * each : (part + 1) * each, :] = jnp.where(wanted == spots, 1.0, 0.0).astype(
            bf16
        )


def post(rows, staged_ref, out_hbm, sem):
    staged_ref[...] = rows.reshape(staged_ref.shape)
    copy = pltpu.make_async_copy(staged_ref, out_hbm, sem)
    copy.start()
    return copy


def first_kernel(
    feats_hbm,
    rows_hbm,
    src_hbm,
    dst_hbm,
    start_ref,
    out_hbm,
    own_ref,
    src_ref,
    dst_ref,
    feats_ref,
    rows_ref,
    turn_ref,
    pick_ref,
    staged_ref,
    sems,
):
    copies = fetch(
        (
            (rows_hbm.at[0, 0], rows_ref),
            (feats_hbm.at[0, 0], feats_ref),
            (src_hbm.at[0, 0], src_ref),
            (dst_hbm.at[0, 0], dst_ref),
        ),
        sems,
    )
    copies[0].wait()
    choose(rows_ref, turn_ref, pick_ref)
    copies[1].wait()
    sent = normalize(dot(pick_ref[...], feats_ref[...]))
    out_copy = post(sent, staged_ref, out_hbm, sems.at[4])
    start = normalize(feats_ref[...].astype(f32))
    start_ref[...] = start
    own_ref[...] = start[: own_ref.shape[0]]
    copies[2].wait()
    copies[3].wait()
    out_copy.wait()


def build_kernel(
    blocks_hbm,
    count_ref,
    src_ref,
    dst_ref,
    noise_hbm,
    start_ref,
    own_hbm,
    ghost_ref,
    own_train_ref,
    noise_train_ref,
    part_ref,
    flag_ref,
    own_rest_ref,
    ghost_rest_ref,
    noise_ref,
    low_ref,
    high_ref,
    spot_ref,
    sums_ref,
    rest_ref,
    own_ref,
    blocks_ref,
    sems,
):
    train = own_train_ref.shape[0]
    copies = fetch(
        (
            (blocks_hbm, blocks_ref),
            (noise_hbm.at[0, 0, 0], noise_ref),
            (noise_hbm.at[1, 0, 0, :train], noise_train_ref),
        ),
        sems,
    )
    nodes, cols = sums_ref.shape
    pieces = -(-cols // LOW)
    tiles, slots = src_ref.shape
    own_ref[...] = jnp.zeros_like(own_ref)
    ghost_ref[...] = jnp.zeros_like(ghost_ref)
    copies[0].wait()
    count = count_ref[0, 0]

    def sixteen(values):
        wide = jnp.broadcast_to(values.astype(f32)[:, None, :], (tiles, 16, slots))
        return wide.reshape(tiles * 16, slots).astype(bf16)

    src = src_ref[...]
    dst = dst_ref[...]
    tile_ids = lax.broadcasted_iota(jnp.int32, (tiles, slots), 0)
    high_ref[...] = sixteen(src // LOW)
    spot_ref[...] = sixteen(jnp.where((dst < BLOCK) & (tile_ids < count), dst, -1))
    low = (src % LOW - LOW // 2).astype(f32).T
    for tile in range(tiles):
        low_ref[tile] = jnp.broadcast_to(low[:, tile : tile + 1], (slots, 128)).astype(bf16)
    ids = lax.broadcasted_iota(jnp.int32, (BLOCK, slots), 0).astype(f32).astype(bf16)
    lanes = lax.broadcasted_iota(jnp.int32, (slots, 128), 1).astype(f32)
    lanes = [(lanes + first).astype(bf16) for first in range(-LOW // 2, LOW // 2, 128)]
    one = jnp.ones((), bf16)
    zero = jnp.zeros((), bf16)

    def counts(tile):
        rows = pl.ds(pl.multiple_of(tile * 16, 16), 16)
        high, spot = high_ref[rows, :], spot_ref[rows, :]
        spots = []
        for piece in range(pieces):
            wanted = jnp.where(high == piece, spot, -one)
            tall = jnp.concatenate([wanted] * (BLOCK // 16), 0)
            spots.append(jnp.where(ids == tall, one, zero))
        low = low_ref[tile]
        low_hot = jnp.concatenate([jnp.where(low == ids, one, zero) for ids in lanes], 1)
        spot_hot = jnp.concatenate(spots, 0)
        return dot(spot_hot.astype(jnp.float8_e4m3fn), low_hot.astype(jnp.float8_e4m3fn))

    def turn(add, step, carry):
        first = step * GROUP
        outs = [counts(first + inner) for inner in range(GROUP)]
        for inner, out in enumerate(outs):
            base = pl.multiple_of(blocks_ref[0, 0, first + inner] * BLOCK, BLOCK)
            for piece in range(pieces):
                add(pl.ds(base, BLOCK), piece * LOW, out[piece * BLOCK : (piece + 1) * BLOCK])
        return carry

    def add_short(rows, at, values):
        ref, at = (own_ref, at) if at < nodes else (ghost_ref, at - nodes)
        size = min(LOW, ref.shape[1] - at)
        ref[rows, at : at + size] += values[:, :size].astype(bf16)

    def add_long(rows, at, values):
        size = min(LOW, cols - at)
        sums_ref[rows, at : at + size] += values[:, :size]

    steps = (count + GROUP - 1) // GROUP
    lax.fori_loop(0, steps, functools.partial(turn, add_short), 0)
    top = ghost_ref[:BLOCK, :256]
    for first in range(0, nodes, BLOCK):
        for ref in (own_ref, ghost_ref):
            for at in range(0, ref.shape[1], 256):
                top = jnp.maximum(top, ref[first : first + BLOCK, at : at + 256])
    big = jnp.max(top.astype(f32)) >= 256.0
    flag_ref[0] = big.astype(jnp.int32)

    @pl.when(big)
    def _():
        sums_ref[...] = jnp.zeros_like(sums_ref)
        lax.fori_loop(0, steps, functools.partial(turn, add_long), 0)
        own_ref[...] = sums_ref[:, :nodes].astype(bf16)
        ghost_ref[...] = sums_ref[:, nodes:].astype(bf16)

    own_copy = pltpu.make_async_copy(own_ref, own_hbm, sems.at[3])
    own_copy.start()
    own_train_ref[...] = own_ref[:train, :]
    for copy in copies[1:]:
        copy.wait()
    part_ref[...] = dot(own_ref[...], start_ref[...]) + noise_ref[...].astype(f32)

    @pl.when(big)
    def _():
        own_rest = (sums_ref[:, :nodes] - own_ref[...].astype(f32)).astype(bf16)
        part_ref[...] += dot(own_rest, start_ref[...])
        rest_ref[:, :nodes] = own_rest
        pltpu.sync_copy(rest_ref.at[:, :nodes], own_rest_ref)
        rest_ref[:, : cols - nodes] = (sums_ref[:, nodes:] - ghost_ref[...].astype(f32)).astype(bf16)
        pltpu.sync_copy(rest_ref.at[:, : cols - nodes], ghost_rest_ref)

    own_copy.wait()


def aggregate(flag_ref, start, parts, sums_ref, rest_ref):
    rows = sums_ref.shape[0]
    total = start
    for count, _, table in parts:
        total += dot(count, table)
    sums_ref[...] = total

    @pl.when(flag_ref[0] > 0)
    def _():
        for count, rest_hbm, table in parts:
            held = rest_ref.at[:, : count.shape[1]]
            pltpu.sync_copy(rest_hbm.at[:rows], held)
            sums_ref[...] += dot(held[...], table)


def hop_kernel(
    flag_ref,
    part_ref,
    ghost_ref,
    rest_hbm,
    table_ref,
    rows_ref,
    old_ref,
    labels_ref,
    start_ref,
    out_hbm,
    side_ref,
    sums_ref,
    rest_ref,
    turn_ref,
    pick_ref,
    staged_ref,
    sem,
):
    width = start_ref.shape[1]
    table = table_ref[...].reshape(-1, width)
    parts = ((ghost_ref[...], rest_hbm, table),)
    aggregate(flag_ref, part_ref[...], parts, sums_ref, rest_ref)
    choose(rows_ref, turn_ref, pick_ref)
    start = normalize(sums_ref[...])
    start_ref[...] = start
    out_copy = post(dot(pick_ref[...], start).astype(bf16), staged_ref, out_hbm, sem)
    train = labels_ref.shape[1]
    side_ref[:train, :] = old_ref[...]
    side_ref[train : 2 * train, :] = start[:train]
    turn_ref[:1, :train] = labels_ref[...]
    side_ref[2 * train :, :128] = turn_ref[:16, :].astype(f32).astype(bf16)
    out_copy.wait()


def train_kernel(
    flag_ref,
    place_ref,
    own_ref,
    ghost_ref,
    own_rest_hbm,
    ghost_rest_hbm,
    noise_ref,
    start_ref,
    table_ref,
    *refs,
):
    *piece_refs, out_hbm, side_hbm, sums_ref, rest_ref, turn_ref, staged_ref, side_ref, sems = refs
    train, width = sums_ref.shape
    table = table_ref[...].reshape(-1, width)
    parts = (
        (own_ref[...], own_rest_hbm, start_ref[...]),
        (ghost_ref[:train], ghost_rest_hbm, table),
    )
    aggregate(flag_ref, noise_ref[...].astype(f32), parts, sums_ref, rest_ref)
    last = jnp.broadcast_to(normalize(sums_ref[...])[None], staged_ref.shape)
    out_copy = post(last, staged_ref, out_hbm, sems.at[0])
    length = piece_refs[0].shape[0] - 16
    groups = len(piece_refs)
    if groups > 1:
        for shift, ref in enumerate(piece_refs):
            group = lax.rem(place_ref[1] + shift, groups)
            at = pl.multiple_of(group * length, length)
            side_ref[pl.ds(at, length), :] = ref[:length, :]
            turn_ref[pl.ds(group, 1), :] = ref[length:, :128].astype(f32)[:1]
        side_ref[groups * length :, :128] = turn_ref[:16, :].astype(bf16)
        side_copy = pltpu.make_async_copy(side_ref, side_hbm, sems.at[1])
        side_copy.start()
        side_copy.wait()
    out_copy.wait()


def last_kernel(
    flag_ref,
    token_ref,
    own_hbm,
    own_rest_hbm,
    ghost_rest_hbm,
    noise_hbm,
    weight_hbm,
    ghost_ref,
    table_ref,
    start_ref,
    out_ref,
    weight_ref,
    own_ref,
    noise_ref,
    sums_ref,
    rest_ref,
    sems,
):
    copies = fetch(
        ((own_hbm, own_ref), (noise_hbm.at[1, 0, 0], noise_ref), (weight_hbm, weight_ref)), sems
    )
    table = table_ref[...].reshape(-1, out_ref.shape[-1])
    out_ref[0, 0, 0] = start_ref[...]
    copies[0].wait()
    copies[1].wait()
    parts = (
        (own_ref[...], own_rest_hbm, start_ref[...]),
        (ghost_ref[...], ghost_rest_hbm, table),
    )
    aggregate(flag_ref, noise_ref[...].astype(f32), parts, sums_ref, rest_ref)
    out_ref[1, 0, 0] = normalize(sums_ref[...])
    copies[2].wait()


def shares(ref, first, share):
    return ref[:, pl.ds(pl.multiple_of(first, 128), share)].astype(f32)


def lanes_sum(values):
    total = None
    for piece in range(values.shape[1] // 128):
        part = values[:, piece * 128 : (piece + 1) * 128].astype(f32)
        total = part * part if total is None else total + part * part
    return total


def classify_kernel(
    many,
    place_ref,
    label_ref,
    zero_ref,
    one_ref,
    two_ref,
    side_refs,
    w_first_hbm,
    w_second_hbm,
    w_third_hbm,
    n_first_hbm,
    n_second_hbm,
    n_third_hbm,
    g_first_ref,
    g_second_ref,
    g_third_ref,
    send_ref,
    side_hbm,
    w_first_ref,
    w_second_ref,
    w_third_ref,
    n_first_ref,
    n_second_ref,
    n_third_ref,
    in_ref,
    w_third_pad_ref,
    turn_ref,
    column_ref,
    h_one_ref,
    h_two_ref,
    slope_one_ref,
    slope_two_ref,
    d_one_ref,
    d_two_ref,
    d_three_ref,
    sems,
):
    classes = w_third_ref.shape[0]
    hid = w_second_ref.shape[0]
    width = two_ref.shape[2]
    wide = w_third_pad_ref.shape[0]
    train = two_ref.shape[1]
    scale = noise_mult * clip_bound
    place = place_ref[0]
    pairs = (
        (w_first_hbm, w_first_ref),
        (w_second_hbm, w_second_ref),
        (w_third_hbm, w_third_ref),
        (n_first_hbm, n_first_ref),
        (n_second_hbm, n_second_ref),
        (n_third_hbm, n_third_ref),
    )

    def set_noise():
        g_first_ref[...] = scale * n_first_ref[...]
        g_second_ref[...] = scale * n_second_ref[...]
        g_third_ref[...] = scale * n_third_ref[...]

    def pad():
        w_third_pad_ref[...] = jnp.zeros_like(w_third_pad_ref)
        w_third_pad_ref[:classes, :] = w_third_ref[...]

    def column(row, turned, lane):
        column_ref[row : row + train, :] = jnp.broadcast_to(
            turned[:train, lane : lane + 1], (train, 128)
        ).astype(jnp.int32)

    if many:

        @pl.when(pl.program_id(0) == 0)
        def _():
            for copy in fetch(pairs, sems):
                copy.wait()
            set_noise()
            pad()

        groups = label_ref.shape[0]
        turn_ref[:groups, :train] = label_ref[...].astype(f32)
        turned = turn_ref[...].T
        for group in range(groups):
            column(group * train, turned, group)
        for hop, ref in enumerate((zero_ref, one_ref)):
            in_ref[:, hop * width : (hop + 1) * width] = ref[...].reshape(-1, width)
    else:
        chips = len(side_refs)
        copies = fetch(((side_hbm, side_refs[0]),) + pairs[1:], sems)
        groups = two_ref.shape[0] // chips
        rows = groups * train
        for shift, ref in [*enumerate(side_refs)][::-1]:
            if shift == 0:
                copies[0].wait()
            part = lax.rem(place // 2 - shift + chips, chips)
            at = pl.multiple_of(part * rows, rows)
            for group in range(groups):
                for hop in range(2):
                    first = (2 * group + hop) * train
                    in_ref[pl.ds(at + group * train, train), hop * width : (hop + 1) * width] = ref[
                        first : first + train, :
                    ]
            turn_ref[pl.ds(pl.multiple_of(part * 16, 16), 16), :] = ref[2 * rows :, :128].astype(f32)
        turned = turn_ref[...].T
        for part in range(chips):
            for group in range(groups):
                column((part * groups + group) * train, turned, part * 16 + group)
    in_ref[:, 2 * width :] = two_ref[...].reshape(-1, width)

    def activate(values, h_ref, slope_ref, rows):
        sigma = 0.5 + 0.5 * jnp.tanh(0.5 * values)
        out = values * sigma
        slope_ref[rows, :] = sigma + out * (1.0 - sigma)
        h_ref[rows, :] = out.astype(bf16)
        return lanes_sum(out)

    def back(values, slope_ref, d_ref, rows):
        out = values * slope_ref[rows, :]
        d_ref[rows, :] = out.astype(bf16)
        return lanes_sum(out)

    def layer(product, finish, *refs):
        sums = []
        values = product(cuts[0])
        for at, cut in enumerate(cuts):
            ahead = product(cuts[at + 1]) if at + 1 < len(cuts) else None
            sums.append(finish(values, *refs, cut))
            values = ahead
        return jnp.concatenate(sums, 0)

    step = min(512, in_ref.shape[0])
    cuts = [slice(at, at + step) for at in range(0, in_ref.shape[0], step)]
    sq_in = lanes_sum(in_ref[...])
    sq_one = layer(
        lambda cut: dot(in_ref[cut, :], w_first_ref[...]), activate, h_one_ref, slope_one_ref
    )
    if not many:
        copies[1].wait()
    sq_two = layer(
        lambda cut: dot(h_one_ref[cut, :], w_second_ref[...]), activate, h_two_ref, slope_two_ref
    )
    if not many:
        copies[2].wait()
        pad()
    logits = dot_nt(h_two_ref[...], w_third_pad_ref[...])
    ids = lax.broadcasted_iota(jnp.int32, (logits.shape[0], wide), 1)
    expo = jnp.where(ids < classes, jnp.exp(logits), 0.0)
    probs = expo / jnp.sum(expo, -1, keepdims=True)
    label = column_ref[:, :1]
    d_three = (probs - jnp.where(ids == label, 1.0, 0.0)).astype(bf16)
    sq_dthree = lanes_sum(d_three)
    d_three_ref[...] = d_three
    sq_dtwo = layer(
        lambda cut: dot(d_three_ref[cut, :], w_third_pad_ref[...]), back, slope_two_ref, d_two_ref
    )
    sq_done = layer(
        lambda cut: dot_nt(d_two_ref[cut, :], w_second_ref[...]), back, slope_one_ref, d_one_ref
    )

    def total(values):
        return jnp.sum(values, -1, keepdims=True)

    norm = jnp.sqrt(
        total(sq_in) * total(sq_done)
        + total(sq_one) * total(sq_dtwo)
        + total(sq_two) * total(sq_dthree)
    )
    factor = clip_bound / jnp.maximum(norm, clip_bound)

    if not many:
        for copy in copies[3:]:
            copy.wait()
        set_noise()
    share_one, share = g_first_ref.shape[0], g_second_ref.shape[0]
    places = [place] if many else [place, place + 1 - 2 * (place % 2)]

    def left(ref, share):
        if share % 128 == 0:
            picked = [shares(ref, at * share, share) for at in places]
            return (jnp.concatenate(picked, 1) * factor).astype(bf16)
        length, count = ref.shape[1], share * len(places)
        most = 128 - math.gcd(count, 128)
        size = min(length, -(-(count + most) // 128) * 128)
        first = [at * share for at in places]
        least = functools.reduce(jnp.minimum, first)
        start = jnp.minimum(least // 128 * 128, length - size)
        rows = lax.broadcasted_iota(jnp.int32, (size, count), 0)
        cols = lax.broadcasted_iota(jnp.int32, (size, count), 1)
        wanted = cols + (first[0] - start)
        for at, other in enumerate(first[1:], 1):
            wanted = jnp.where(cols >= at * share, cols - at * share + (other - start), wanted)
        window = ref[:, pl.ds(pl.multiple_of(start, 128), size)]
        picked = dot(window, jnp.where(rows == wanted, 1.0, 0.0).astype(bf16))
        return (picked * factor).astype(bf16)

    sum_one = dot_tn(left(in_ref, share_one), d_one_ref[...])
    sum_two = dot_tn(left(h_one_ref, share), d_two_ref[...])
    sum_three = dot_tn(d_three, left(h_two_ref, share))
    g_first_ref[...] += sum_one[:share_one]
    g_second_ref[...] += sum_two[:share]
    g_third_ref[...] += sum_three[:classes, :share]
    if not many:
        send_ref[:share_one, :] = sum_one[share_one:].astype(bf16)
        send_ref[share_one : share_one + share, :] = sum_two[share:].astype(bf16)
        first = share_one + share
        for at in range(0, classes, 32):
            cols = slice(at // 32 * share, (at // 32 + 1) * share)
            send_ref[first : first + 32, cols] = sum_three[at : at + 32, share:].astype(bf16)


def finish_kernel(got_ref, one_ref, two_ref, three_ref, g_first_ref, g_second_ref, g_third_ref):
    share_one, share = one_ref.shape[0], two_ref.shape[0]
    g_first_ref[...] = one_ref[...] + got_ref[:share_one, :].astype(f32)
    g_second_ref[...] = two_ref[...] + got_ref[share_one : share_one + share, :].astype(f32)
    first = share_one + share
    classes = three_ref.shape[0]
    for at in range(0, classes, 32):
        size = min(32, classes - at)
        cols = slice(at // 32 * share, (at // 32 + 1) * share)
        got = got_ref[first : first + 32, cols].astype(f32)
        g_third_ref[at : at + size, :] = three_ref[at : at + size, :] + got[:size]


def call(kernel, mib, outs, ins, scratch):
    def shape_of(shape, dtype, space):
        if space is None or space is HBM:
            return (space or VMEM)(shape, dtype)
        return jax.ShapeDtypeStruct(shape, dtype)

    def block(space):
        return pl.BlockSpec(memory_space=VMEM if space is None else space)

    def held(value, space):
        if space is None or space is HBM:
            return pltpu.with_memory_space_constraint(value, space or VMEM)
        return value

    return pl.pallas_call(
        kernel,
        out_shape=[shape_of(*out) for out in outs],
        in_specs=[block(space) for _, space in ins],
        out_specs=[block(space) for _, _, space in outs],
        scratch_shapes=scratch,
        compiler_params=params(mib),
    )(*[held(value, space) for value, space in ins])


def local(
    axes,
    feats,
    hop_noise,
    send_rows,
    tile_block,
    tile_src,
    tile_dst,
    tile_count,
    labels,
    w_first,
    w_second,
    w_third,
    noise_first,
    noise_second,
    noise_third,
):
    nodes, width = feats.shape[2:]
    parts, each = send_rows.shape[2:]
    ghosts = parts * each
    tiles = tile_src.shape[2]
    slots = tile_src.shape[3]
    train = labels.shape[2]
    classes = w_third.shape[1]
    hid = w_second.shape[0]
    d_in = w_first.shape[0]
    cols = nodes + ghosts
    rows = send_rows.reshape(parts, each)
    turn = VMEM((128, 128), jnp.int32)
    pick = VMEM((ghosts, nodes), bf16)
    dom = axes[:-1]
    members = lax.axis_size(axes)
    few = len(axes) == 3
    copies = members // 2 if few else 1

    def every(value, *names):
        for name in names:
            value = lax.all_gather(value, name, axis=0, tiled=True)
        return value

    staged = VMEM((parts, each, width), bf16)
    start0, out0, own0, src, dst = call(
        first_kernel,
        16,
        [
            ((nodes, width), bf16, None),
            ((parts, each, width), bf16, HBM),
            ((train, width), bf16, None),
            ((tiles, slots), jnp.int32, None),
            ((tiles, slots), jnp.int32, None),
        ],
        [(feats, HBM), (send_rows, HBM), (tile_src, HBM), (tile_dst, HBM)],
        [
            VMEM((nodes, width), bf16),
            VMEM((parts, each), jnp.int32),
            turn,
            pick,
            staged,
            DMA((5,)),
        ],
    )
    table0 = lax.all_to_all(out0, dom, split_axis=0, concat_axis=0, tiled=True)
    own, ghost, own_train, noise_train, part1, flag, own_rest, ghost_rest = call(
        build_kernel,
        28,
        [
            ((nodes, nodes), bf16, HBM),
            ((nodes, ghosts), bf16, None),
            ((train, nodes), bf16, None),
            ((train, width), bf16, None),
            ((nodes, width), f32, None),
            ((1,), jnp.int32, SMEM),
            ((nodes, nodes), bf16, HBM),
            ((nodes, ghosts), bf16, HBM),
        ],
        [
            (tile_block, HBM),
            (tile_count, SMEM),
            (src, None),
            (dst, None),
            (hop_noise, HBM),
            (start0, None),
        ],
        [
            VMEM((nodes, width), bf16),
            VMEM((tiles, slots, 128), bf16),
            VMEM((tiles * 16, slots), bf16),
            VMEM((tiles * 16, slots), bf16),
            VMEM((nodes, cols), f32),
            VMEM((nodes, max(nodes, ghosts)), bf16),
            VMEM((nodes, nodes), bf16),
            SMEM(tile_block.shape, jnp.int32),
            DMA((4,)),
        ],
    )
    start1, out1, side = call(
        hop_kernel,
        16,
        [
            ((nodes, width), bf16, None),
            ((parts, each, width), bf16, HBM),
            ((2 * train + 16, width), bf16, None),
        ],
        [
            (flag, SMEM),
            (part1, None),
            (ghost, None),
            (ghost_rest, HBM),
            (table0, None),
            (rows, VMEM),
            (own0, None),
            (labels.reshape(1, train), VMEM),
        ],
        [VMEM((nodes, width), f32), VMEM((nodes, ghosts), bf16), turn, pick, staged, DMA(())],
    )
    table1 = lax.all_to_all(out1, dom, split_axis=0, concat_axis=0, tiled=True)
    place = jnp.stack([lax.axis_index(dom), lax.axis_index("grp")]).astype(jnp.int32)
    grp = lax.axis_size("grp")

    def shifted(value, name, size, step):
        return [
            lax.ppermute(value, name, [((at + step * shift) % size, at) for at in range(size)])
            for shift in range(1, size)
        ]

    sides = [side] + (shifted(side, "grp", grp, 1) if few else [])
    side_shape = (len(sides) * 2 * train + 16, width)
    last, side = call(
        train_kernel,
        12,
        [
            ((copies, train, width), bf16, HBM),
            (side_shape, bf16, HBM),
        ],
        [
            (flag, SMEM),
            (place, SMEM),
            (own_train, None),
            (ghost, None),
            (own_rest, HBM),
            (ghost_rest, HBM),
            (noise_train, None),
            (start1, None),
            (table1, None),
        ]
        + [(value, None) for value in sides],
        [
            VMEM((train, width), f32),
            VMEM((train, max(nodes, ghosts)), bf16),
            VMEM((128, 128), f32),
            VMEM((copies, train, width), bf16),
            VMEM(side_shape, bf16),
            DMA((2,)),
        ],
    )
    if few:
        every2 = lax.all_to_all(last, ("chip", "grp"), split_axis=0, concat_axis=0, tiled=True)
        sides = [side] + shifted(side, "chip", parts // 2, -1)
    else:
        every0, every1, every2 = (
            every(value, axes) for value in (own0[None], start1[None, :train], last)
        )
        every_label = every(labels.reshape(1, train), axes)
    hop_feats, held_first = call(
        last_kernel,
        16,
        [((2, 1, 1, nodes, width), bf16, VMEM), (w_first.shape, bf16, None)],
        [
            (flag, SMEM),
            (side, HBM),
            (own, HBM),
            (own_rest, HBM),
            (ghost_rest, HBM),
            (hop_noise, HBM),
            (w_first, HBM),
            (ghost, None),
            (table1, None),
            (start1, None),
        ],
        [
            VMEM((nodes, nodes), bf16),
            VMEM((nodes, width), bf16),
            VMEM((nodes, width), f32),
            VMEM((nodes, max(nodes, ghosts)), bf16),
            DMA((3,)),
        ],
    )
    chunk = train * (copies if few else min(members, 32))
    groups = chunk // train
    wide = (classes + 255) // 256 * 256
    fixed = (w_first, w_second, w_third.T, noise_first, noise_second, noise_third.T)
    scratch = [VMEM(value.shape, value.dtype) for value in fixed]
    scratch += [
        VMEM((chunk, d_in), bf16),
        VMEM((wide, hid), bf16),
        VMEM((128, 128), f32),
        VMEM((chunk, 128), jnp.int32),
        VMEM((chunk, hid), bf16),
        VMEM((chunk, hid), bf16),
        VMEM((chunk, hid), f32),
        VMEM((chunk, hid), f32),
        VMEM((chunk, hid), bf16),
        VMEM((chunk, hid), bf16),
        VMEM((chunk, wide), bf16),
        DMA((16,)),
    ]
    if few:
        chips = parts // 2

        def classify(place_ref, *refs):
            sides_in, rest = refs[:chips], refs[chips:]
            two_ref, first_ref, *outs = rest[:11]
            held, *rest = rest[11:]
            classify_kernel(
                False,
                place_ref,
                None,
                None,
                None,
                two_ref,
                (held,) + sides_in[1:],
                first_ref,
                *outs,
                sides_in[0],
                first_ref,
                *rest,
            )

        rows = noise_first.shape[0] + noise_second.shape[0] + 32
        *own_sums, other = call(
            classify,
            44,
            [(value.shape, f32, None) for value in fixed[3:]] + [((rows, hid), bf16, None)],
            [(place, SMEM)]
            + [(side, HBM)]
            + [(value, None) for value in sides[1:]]
            + [(every2, None), (held_first, None)]
            + [(value, HBM) for value in fixed[1:]],
            [VMEM(side_shape, bf16)] + scratch[1:],
        )
        got = lax.ppermute(other, "core", [(0, 1), (1, 0)])
        first, second, third = call(
            finish_kernel,
            16,
            [(value.shape, f32, VMEM) for value in fixed[3:]],
            [(got, None)] + [(value, None) for value in own_sums],
            [],
        )
    else:

        ins = (every_label, every0, every1, every2)

        def classify(place_ref, label_ref, zero_ref, one_ref, two_ref, *rest):
            classify_kernel(
                True,
                place_ref,
                label_ref,
                zero_ref,
                one_ref,
                two_ref,
                None,
                *rest[:9],
                None,
                None,
                *rest[9:],
            )

        def whole(value):
            return pl.BlockSpec(value.shape, lambda i: (0, 0))

        def piece(value):
            return pl.BlockSpec(
                (groups,) + value.shape[1:], lambda i: (i,) + (0,) * (value.ndim - 1)
            )

        first, second, third = pl.pallas_call(
            classify,
            grid=(members // groups,),
            out_shape=[jax.ShapeDtypeStruct(value.shape, f32) for value in fixed[3:]],
            in_specs=[pl.BlockSpec(memory_space=SMEM)]
            + [piece(value) for value in ins]
            + [pl.BlockSpec(memory_space=HBM) for value in fixed],
            out_specs=[whole(value) for value in fixed[3:]],
            scratch_shapes=scratch,
            compiler_params=params(56),
        )(place, *ins, *fixed)
    return (hop_feats, first, second, third.T)


def solution(mesh):
    dom, grp = mesh.shape["dom"], mesh.shape["grp"]
    names = ("dom", "grp")
    if dom * grp <= FEW and dom <= 8 and dom % 2 == 0:
        names = ("chip", "core", "grp")
        mesh = jax.sharding.Mesh(mesh.devices.reshape(dom // 2, 2, grp), names)
    doms, grps = names[:-1], "grp"
    in_specs = (
        P(doms, grps, None, None),
        P(None, doms, grps, None, None),
        P(doms, grps, None, None),
        P(doms, grps, None),
        P(doms, grps, None, None),
        P(doms, grps, None, None),
        P(doms, grps),
        P(doms, grps, None),
        P(),
        P(),
        P(),
        P(doms, None),
        P(doms, None),
        P(doms, None),
    )
    out_specs = (P(None, doms, grps, None, None), P(doms, None), P(doms, None), P(doms, None))
    return jax.shard_map(
        functools.partial(local, names),
        mesh=mesh,
        in_specs=in_specs,
        out_specs=out_specs,
        check_vma=False,
    )
```

```python
import functools
import math

import jax
import jax.numpy as jnp
from jax import lax
from jax.experimental import pallas as pl
from jax.experimental.pallas import tpu as pltpu
from jax.sharding import PartitionSpec as P

BLOCK = 128
LOW = 256
GROUP = 8
clip_bound = 4.0
noise_mult = 1.0

f32 = jnp.float32
bf16 = jnp.bfloat16
VMEM = pltpu.VMEM
SMEM = pltpu.SMEM
HBM = pltpu.HBM
DMA = pltpu.SemaphoreType.DMA


FEW = 32


def params(mib):
    return pltpu.CompilerParams(vmem_limit_bytes=mib * 1024 * 1024)


def fetch(pairs, sems):
    copies = [pltpu.make_async_copy(*pair, sems.at[at]) for at, pair in enumerate(pairs)]
    for copy in copies:
        copy.start()
    return copies


def normalize(values):
    return (values * lax.rsqrt(jnp.sum(values * values, -1, keepdims=True) + 1e-06)).astype(bf16)


def dot(left, right):
    return jnp.dot(left, right, preferred_element_type=f32)


def dot_nt(left, right):
    return lax.dot_general(left, right, (((1,), (1,)), ((), ())), preferred_element_type=f32)


def dot_tn(left, right):
    return lax.dot_general(left, right, (((0,), (0,)), ((), ())), preferred_element_type=f32)


def choose(rows_ref, turn_ref, pick_ref):
    parts, each = rows_ref.shape
    turn_ref[:parts, :each] = rows_ref[...]
    columns = turn_ref[...].T
    spots = lax.broadcasted_iota(jnp.int32, (each, pick_ref.shape[1]), 1)
    for part in range(parts):
        wanted = columns[:each, part : part + 1]
        pick_ref[part * each : (part + 1) * each, :] = jnp.where(wanted == spots, 1.0, 0.0).astype(
            bf16
        )


def post(rows, staged_ref, out_hbm, sem):
    staged_ref[...] = rows.reshape(staged_ref.shape)
    copy = pltpu.make_async_copy(staged_ref, out_hbm, sem)
    copy.start()
    return copy


def first_kernel(
    feats_hbm,
    rows_hbm,
    src_hbm,
    dst_hbm,
    start_ref,
    out_hbm,
    own_ref,
    src_ref,
    dst_ref,
    feats_ref,
    rows_ref,
    turn_ref,
    pick_ref,
    staged_ref,
    sems,
):
    copies = fetch(
        (
            (rows_hbm.at[0, 0], rows_ref),
            (feats_hbm.at[0, 0], feats_ref),
            (src_hbm.at[0, 0], src_ref),
            (dst_hbm.at[0, 0], dst_ref),
        ),
        sems,
    )
    copies[0].wait()
    choose(rows_ref, turn_ref, pick_ref)
    copies[1].wait()
    sent = normalize(dot(pick_ref[...], feats_ref[...]))
    out_copy = post(sent, staged_ref, out_hbm, sems.at[4])
    start = normalize(feats_ref[...].astype(f32))
    start_ref[...] = start
    own_ref[...] = start[: own_ref.shape[0]]
    copies[2].wait()
    copies[3].wait()
    out_copy.wait()


def build_kernel(
    blocks_hbm,
    count_any,
    src_ref,
    dst_ref,
    noise_hbm,
    start_ref,
    own_hbm,
    ghost_ref,
    own_train_ref,
    noise_train_ref,
    part_ref,
    flag_ref,
    own_rest_ref,
    ghost_rest_ref,
    noise_ref,
    low_ref,
    high_ref,
    spot_ref,
    sums_ref,
    rest_ref,
    own_ref,
    blocks_ref,
    count_ref,
    sems,
):
    train = own_train_ref.shape[0]
    copies = fetch(
        (
            (count_any, count_ref),
            (blocks_hbm, blocks_ref),
            (noise_hbm.at[0, 0, 0], noise_ref),
            (noise_hbm.at[1, 0, 0, :train], noise_train_ref),
        ),
        sems,
    )
    nodes, cols = sums_ref.shape
    pieces = -(-cols // LOW)
    tiles, slots = src_ref.shape
    own_ref[...] = jnp.zeros_like(own_ref)
    ghost_ref[...] = jnp.zeros_like(ghost_ref)
    copies[0].wait()
    count = count_ref[0, 0]

    def sixteen(values):
        wide = jnp.broadcast_to(values.astype(f32)[:, None, :], (tiles, 16, slots))
        return wide.reshape(tiles * 16, slots).astype(bf16)

    src = src_ref[...]
    dst = dst_ref[...]
    tile_ids = lax.broadcasted_iota(jnp.int32, (tiles, slots), 0)
    high_ref[...] = sixteen(src // LOW)
    spot_ref[...] = sixteen(jnp.where((dst < BLOCK) & (tile_ids < count), dst, -1))
    low = (src % LOW - LOW // 2).astype(f32).T
    for tile in range(tiles):
        low_ref[tile] = jnp.broadcast_to(low[:, tile : tile + 1], (slots, 128)).astype(bf16)
    ids = lax.broadcasted_iota(jnp.int32, (BLOCK, slots), 0).astype(f32).astype(bf16)
    lanes = lax.broadcasted_iota(jnp.int32, (slots, 128), 1).astype(f32)
    lanes = [(lanes + first).astype(bf16) for first in range(-LOW // 2, LOW // 2, 128)]
    one = jnp.ones((), bf16)
    zero = jnp.zeros((), bf16)

    def counts(tile):
        rows = pl.ds(pl.multiple_of(tile * 16, 16), 16)
        high, spot = high_ref[rows, :], spot_ref[rows, :]
        spots = []
        for piece in range(pieces):
            wanted = jnp.where(high == piece, spot, -one)
            tall = jnp.concatenate([wanted] * (BLOCK // 16), 0)
            spots.append(jnp.where(ids == tall, one, zero))
        low = low_ref[tile]
        low_hot = jnp.concatenate([jnp.where(low == ids, one, zero) for ids in lanes], 1)
        spot_hot = jnp.concatenate(spots, 0)
        return dot(spot_hot.astype(jnp.float8_e4m3fn), low_hot.astype(jnp.float8_e4m3fn))

    def turn(add, step, carry):
        first = step * GROUP
        for inner in range(GROUP):
            out = counts(first + inner)
            base = pl.multiple_of(blocks_ref[0, 0, first + inner] * BLOCK, BLOCK)
            for piece in range(pieces):
                add(pl.ds(base, BLOCK), piece * LOW, out[piece * BLOCK : (piece + 1) * BLOCK])
        return carry

    def add_short(rows, at, values):
        ref, at = (own_ref, at) if at < nodes else (ghost_ref, at - nodes)
        size = min(LOW, ref.shape[1] - at)
        ref[rows, at : at + size] += values[:, :size].astype(bf16)

    def add_long(rows, at, values):
        size = min(LOW, cols - at)
        sums_ref[rows, at : at + size] += values[:, :size]

    steps = (count + GROUP - 1) // GROUP
    copies[1].wait()
    lax.fori_loop(0, steps, functools.partial(turn, add_short), 0)
    top = ghost_ref[:BLOCK, :256]
    for first in range(0, nodes, BLOCK):
        for ref in (own_ref, ghost_ref):
            for at in range(0, ref.shape[1], 256):
                top = jnp.maximum(top, ref[first : first + BLOCK, at : at + 256])
    big = jnp.max(top.astype(f32)) >= 256.0
    flag_ref[0] = big.astype(jnp.int32)

    @pl.when(big)
    def _():
        sums_ref[...] = jnp.zeros_like(sums_ref)
        lax.fori_loop(0, steps, functools.partial(turn, add_long), 0)
        own_ref[...] = sums_ref[:, :nodes].astype(bf16)
        ghost_ref[...] = sums_ref[:, nodes:].astype(bf16)

    own_copy = pltpu.make_async_copy(own_ref, own_hbm, sems.at[4])
    own_copy.start()
    own_train_ref[...] = own_ref[:train, :]
    for copy in copies[2:]:
        copy.wait()
    part_ref[...] = dot(own_ref[...], start_ref[...]) + noise_ref[...].astype(f32)

    @pl.when(big)
    def _():
        own_rest = (sums_ref[:, :nodes] - own_ref[...].astype(f32)).astype(bf16)
        part_ref[...] += dot(own_rest, start_ref[...])
        rest_ref[:, :nodes] = own_rest
        pltpu.sync_copy(rest_ref.at[:, :nodes], own_rest_ref)
        rest_ref[:, : cols - nodes] = (sums_ref[:, nodes:] - ghost_ref[...].astype(f32)).astype(bf16)
        pltpu.sync_copy(rest_ref.at[:, : cols - nodes], ghost_rest_ref)

    own_copy.wait()


def aggregate(flag_ref, start, parts, sums_ref, rest_ref):
    rows = sums_ref.shape[0]
    total = start
    for count, _, table in parts:
        total += dot(count, table)
    sums_ref[...] = total

    @pl.when(flag_ref[0] > 0)
    def _():
        for count, rest_hbm, table in parts:
            held = rest_ref.at[:, : count.shape[1]]
            pltpu.sync_copy(rest_hbm.at[:rows], held)
            sums_ref[...] += dot(held[...], table)


def hop_kernel(
    flag_ref,
    part_ref,
    ghost_ref,
    rest_hbm,
    table_ref,
    rows_ref,
    old_ref,
    labels_ref,
    start_ref,
    out_hbm,
    side_ref,
    sums_ref,
    rest_ref,
    turn_ref,
    pick_ref,
    staged_ref,
    sem,
):
    width = start_ref.shape[1]
    table = table_ref[...].reshape(-1, width)
    parts = ((ghost_ref[...], rest_hbm, table),)
    aggregate(flag_ref, part_ref[...], parts, sums_ref, rest_ref)
    choose(rows_ref, turn_ref, pick_ref)
    start = normalize(sums_ref[...])
    start_ref[...] = start
    out_copy = post(dot(pick_ref[...], start).astype(bf16), staged_ref, out_hbm, sem)
    train = labels_ref.shape[1]
    side_ref[:train, :] = old_ref[...]
    side_ref[train : 2 * train, :] = start[:train]
    turn_ref[:1, :train] = labels_ref[...]
    side_ref[2 * train :, :128] = turn_ref[:16, :].astype(f32).astype(bf16)
    out_copy.wait()


def train_kernel(
    flag_ref,
    place_ref,
    own_ref,
    ghost_ref,
    own_rest_hbm,
    ghost_rest_hbm,
    noise_ref,
    start_ref,
    table_ref,
    *refs,
):
    *piece_refs, out_hbm, side_hbm, sums_ref, rest_ref, turn_ref, staged_ref, side_ref, sems = refs
    train, width = sums_ref.shape
    table = table_ref[...].reshape(-1, width)
    parts = (
        (own_ref[...], own_rest_hbm, start_ref[...]),
        (ghost_ref[:train], ghost_rest_hbm, table),
    )
    aggregate(flag_ref, noise_ref[...].astype(f32), parts, sums_ref, rest_ref)
    last = jnp.broadcast_to(normalize(sums_ref[...])[None], staged_ref.shape)
    out_copy = post(last, staged_ref, out_hbm, sems.at[0])
    length = piece_refs[0].shape[0] - 16
    groups = len(piece_refs)
    if groups > 1:
        for shift, ref in enumerate(piece_refs):
            group = lax.rem(place_ref[1] + shift, groups)
            at = pl.multiple_of(group * length, length)
            side_ref[pl.ds(at, length), :] = ref[:length, :]
            turn_ref[pl.ds(group, 1), :] = ref[length:, :128].astype(f32)[:1]
        side_ref[groups * length :, :128] = turn_ref[:16, :].astype(bf16)
        side_copy = pltpu.make_async_copy(side_ref, side_hbm, sems.at[1])
        side_copy.start()
        side_copy.wait()
    out_copy.wait()


def last_kernel(
    flag_ref,
    token_ref,
    own_hbm,
    own_rest_hbm,
    ghost_rest_hbm,
    noise_hbm,
    weight_hbm,
    ghost_ref,
    table_ref,
    start_ref,
    out_ref,
    weight_ref,
    own_ref,
    noise_ref,
    sums_ref,
    rest_ref,
    sems,
):
    copies = fetch(
        ((own_hbm, own_ref), (noise_hbm.at[1, 0, 0], noise_ref), (weight_hbm, weight_ref)), sems
    )
    table = table_ref[...].reshape(-1, out_ref.shape[-1])
    out_ref[0, 0, 0] = start_ref[...]
    copies[0].wait()
    copies[1].wait()
    parts = (
        (own_ref[...], own_rest_hbm, start_ref[...]),
        (ghost_ref[...], ghost_rest_hbm, table),
    )
    aggregate(flag_ref, noise_ref[...].astype(f32), parts, sums_ref, rest_ref)
    out_ref[1, 0, 0] = normalize(sums_ref[...])
    copies[2].wait()


def shares(ref, first, share):
    return ref[:, pl.ds(pl.multiple_of(first, 128), share)].astype(f32)


def lanes_sum(values):
    total = None
    for piece in range(values.shape[1] // 128):
        part = values[:, piece * 128 : (piece + 1) * 128].astype(f32)
        total = part * part if total is None else total + part * part
    return total


def classify_kernel(
    many,
    place_ref,
    label_ref,
    zero_ref,
    one_ref,
    two_ref,
    side_refs,
    w_first_hbm,
    w_second_hbm,
    w_third_hbm,
    n_first_hbm,
    n_second_hbm,
    n_third_hbm,
    g_first_ref,
    g_second_ref,
    g_third_ref,
    send_ref,
    side_hbm,
    w_first_ref,
    w_second_ref,
    w_third_ref,
    n_first_ref,
    n_second_ref,
    n_third_ref,
    in_ref,
    w_third_pad_ref,
    turn_ref,
    column_ref,
    h_one_ref,
    h_two_ref,
    slope_one_ref,
    slope_two_ref,
    d_one_ref,
    d_two_ref,
    d_three_ref,
    sems,
):
    classes = w_third_ref.shape[0]
    hid = w_second_ref.shape[0]
    width = two_ref.shape[2]
    wide = w_third_pad_ref.shape[0]
    train = two_ref.shape[1]
    scale = noise_mult * clip_bound
    place = place_ref[0]
    pairs = (
        (w_first_hbm, w_first_ref),
        (w_second_hbm, w_second_ref),
        (w_third_hbm, w_third_ref),
        (n_first_hbm, n_first_ref),
        (n_second_hbm, n_second_ref),
        (n_third_hbm, n_third_ref),
    )

    def set_noise():
        g_first_ref[...] = scale * n_first_ref[...]
        g_second_ref[...] = scale * n_second_ref[...]
        g_third_ref[...] = scale * n_third_ref[...]

    def pad():
        w_third_pad_ref[...] = jnp.zeros_like(w_third_pad_ref)
        w_third_pad_ref[:classes, :] = w_third_ref[...]

    def column(row, turned, lane):
        column_ref[row : row + train, :] = jnp.broadcast_to(
            turned[:train, lane : lane + 1], (train, 128)
        ).astype(jnp.int32)

    if many:

        @pl.when(pl.program_id(0) == 0)
        def _():
            for copy in fetch(pairs, sems):
                copy.wait()
            set_noise()
            pad()

        groups = label_ref.shape[0]
        turn_ref[:groups, :train] = label_ref[...].astype(f32)
        turned = turn_ref[...].T
        for group in range(groups):
            column(group * train, turned, group)
        for hop, ref in enumerate((zero_ref, one_ref)):
            in_ref[:, hop * width : (hop + 1) * width] = ref[...].reshape(-1, width)
    else:
        chips = len(side_refs)
        copies = fetch(((side_hbm, side_refs[0]),) + pairs[1:], sems)
        groups = two_ref.shape[0] // chips
        rows = groups * train
        for shift, ref in [*enumerate(side_refs)][::-1]:
            if shift == 0:
                copies[0].wait()
            part = lax.rem(place // 2 - shift + chips, chips)
            at = pl.multiple_of(part * rows, rows)
            for group in range(groups):
                for hop in range(2):
                    first = (2 * group + hop) * train
                    in_ref[pl.ds(at + group * train, train), hop * width : (hop + 1) * width] = ref[
                        first : first + train, :
                    ]
            turn_ref[pl.ds(pl.multiple_of(part * 16, 16), 16), :] = ref[2 * rows :, :128].astype(f32)
        turned = turn_ref[...].T
        for part in range(chips):
            for group in range(groups):
                column((part * groups + group) * train, turned, part * 16 + group)
    in_ref[:, 2 * width :] = two_ref[...].reshape(-1, width)

    def activate(values, h_ref, slope_ref, rows):
        sigma = 0.5 + 0.5 * jnp.tanh(0.5 * values)
        out = values * sigma
        slope_ref[rows, :] = sigma + out * (1.0 - sigma)
        h_ref[rows, :] = out.astype(bf16)
        return lanes_sum(out)

    def back(values, slope_ref, d_ref, rows):
        out = values * slope_ref[rows, :]
        d_ref[rows, :] = out.astype(bf16)
        return lanes_sum(out)

    def layer(product, finish, *refs):
        sums = []
        values = product(cuts[0])
        for at, cut in enumerate(cuts):
            ahead = product(cuts[at + 1]) if at + 1 < len(cuts) else None
            sums.append(finish(values, *refs, cut))
            values = ahead
        return jnp.concatenate(sums, 0)

    step = min(512, in_ref.shape[0])
    cuts = [slice(at, at + step) for at in range(0, in_ref.shape[0], step)]
    sq_in = lanes_sum(in_ref[...])
    sq_one = layer(
        lambda cut: dot(in_ref[cut, :], w_first_ref[...]), activate, h_one_ref, slope_one_ref
    )
    if not many:
        copies[1].wait()
    sq_two = layer(
        lambda cut: dot(h_one_ref[cut, :], w_second_ref[...]), activate, h_two_ref, slope_two_ref
    )
    if not many:
        copies[2].wait()
        pad()
    logits = dot_nt(h_two_ref[...], w_third_pad_ref[...])
    ids = lax.broadcasted_iota(jnp.int32, (logits.shape[0], wide), 1)
    expo = jnp.where(ids < classes, jnp.exp(logits), 0.0)
    probs = expo / jnp.sum(expo, -1, keepdims=True)
    label = column_ref[:, :1]
    d_three = (probs - jnp.where(ids == label, 1.0, 0.0)).astype(bf16)
    sq_dthree = lanes_sum(d_three)
    d_three_ref[...] = d_three
    sq_dtwo = layer(
        lambda cut: dot(d_three_ref[cut, :], w_third_pad_ref[...]), back, slope_two_ref, d_two_ref
    )
    sq_done = layer(
        lambda cut: dot_nt(d_two_ref[cut, :], w_second_ref[...]), back, slope_one_ref, d_one_ref
    )

    def total(values):
        return jnp.sum(values, -1, keepdims=True)

    norm = jnp.sqrt(
        total(sq_in) * total(sq_done)
        + total(sq_one) * total(sq_dtwo)
        + total(sq_two) * total(sq_dthree)
    )
    factor = clip_bound / jnp.maximum(norm, clip_bound)

    if not many:
        for copy in copies[3:]:
            copy.wait()
        set_noise()
    share_one, share = g_first_ref.shape[0], g_second_ref.shape[0]
    places = [place] if many else [place, place + 1 - 2 * (place % 2)]

    def left(ref, share):
        if share % 128 == 0:
            picked = [shares(ref, at * share, share) for at in places]
            return (jnp.concatenate(picked, 1) * factor).astype(bf16)
        length, count = ref.shape[1], share * len(places)
        most = 128 - math.gcd(count, 128)
        size = min(length, -(-(count + most) // 128) * 128)
        first = [at * share for at in places]
        least = functools.reduce(jnp.minimum, first)
        start = jnp.minimum(least // 128 * 128, length - size)
        rows = lax.broadcasted_iota(jnp.int32, (size, count), 0)
        cols = lax.broadcasted_iota(jnp.int32, (size, count), 1)
        wanted = cols + (first[0] - start)
        for at, other in enumerate(first[1:], 1):
            wanted = jnp.where(cols >= at * share, cols - at * share + (other - start), wanted)
        window = ref[:, pl.ds(pl.multiple_of(start, 128), size)]
        picked = dot(window, jnp.where(rows == wanted, 1.0, 0.0).astype(bf16))
        return (picked * factor).astype(bf16)

    sum_one = dot_tn(left(in_ref, share_one), d_one_ref[...])
    sum_two = dot_tn(left(h_one_ref, share), d_two_ref[...])
    sum_three = dot_tn(d_three, left(h_two_ref, share))
    g_first_ref[...] += sum_one[:share_one]
    g_second_ref[...] += sum_two[:share]
    g_third_ref[...] += sum_three[:classes, :share]
    if not many:
        send_ref[:share_one, :] = sum_one[share_one:].astype(bf16)
        send_ref[share_one : share_one + share, :] = sum_two[share:].astype(bf16)
        first = share_one + share
        for at in range(0, classes, 32):
            cols = slice(at // 32 * share, (at // 32 + 1) * share)
            send_ref[first : first + 32, cols] = sum_three[at : at + 32, share:].astype(bf16)


def finish_kernel(got_ref, one_ref, two_ref, three_ref, g_first_ref, g_second_ref, g_third_ref):
    share_one, share = one_ref.shape[0], two_ref.shape[0]
    g_first_ref[...] = one_ref[...] + got_ref[:share_one, :].astype(f32)
    g_second_ref[...] = two_ref[...] + got_ref[share_one : share_one + share, :].astype(f32)
    first = share_one + share
    classes = three_ref.shape[0]
    for at in range(0, classes, 32):
        size = min(32, classes - at)
        cols = slice(at // 32 * share, (at // 32 + 1) * share)
        got = got_ref[first : first + 32, cols].astype(f32)
        g_third_ref[at : at + size, :] = three_ref[at : at + size, :] + got[:size]


def call(kernel, mib, outs, ins, scratch):
    def shape_of(shape, dtype, space):
        if space is None or space is HBM:
            return (space or VMEM)(shape, dtype)
        return jax.ShapeDtypeStruct(shape, dtype)

    def block(space):
        return pl.BlockSpec(memory_space=VMEM if space is None else space)

    def held(value, space):
        if space is None or space is HBM:
            return pltpu.with_memory_space_constraint(value, space or VMEM)
        return value

    return pl.pallas_call(
        kernel,
        out_shape=[shape_of(*out) for out in outs],
        in_specs=[block(space) for _, space in ins],
        out_specs=[block(space) for _, _, space in outs],
        scratch_shapes=scratch,
        compiler_params=params(mib),
    )(*[held(value, space) for value, space in ins])


def local(
    axes,
    feats,
    hop_noise,
    send_rows,
    tile_block,
    tile_src,
    tile_dst,
    tile_count,
    labels,
    w_first,
    w_second,
    w_third,
    noise_first,
    noise_second,
    noise_third,
):
    nodes, width = feats.shape[2:]
    parts, each = send_rows.shape[2:]
    ghosts = parts * each
    tiles = tile_src.shape[2]
    slots = tile_src.shape[3]
    train = labels.shape[2]
    classes = w_third.shape[1]
    hid = w_second.shape[0]
    d_in = w_first.shape[0]
    cols = nodes + ghosts
    rows = send_rows.reshape(parts, each)
    turn = VMEM((128, 128), jnp.int32)
    pick = VMEM((ghosts, nodes), bf16)
    dom = axes[:-1]
    members = lax.axis_size(axes)
    few = len(axes) == 3
    copies = members // 2 if few else 1

    def every(value, *names):
        for name in names:
            value = lax.all_gather(value, name, axis=0, tiled=True)
        return value

    staged = VMEM((parts, each, width), bf16)
    start0, out0, own0, src, dst = call(
        first_kernel,
        16,
        [
            ((nodes, width), bf16, None),
            ((parts, each, width), bf16, HBM),
            ((train, width), bf16, None),
            ((tiles, slots), jnp.int32, None),
            ((tiles, slots), jnp.int32, None),
        ],
        [(feats, HBM), (send_rows, HBM), (tile_src, HBM), (tile_dst, HBM)],
        [
            VMEM((nodes, width), bf16),
            VMEM((parts, each), jnp.int32),
            turn,
            pick,
            staged,
            DMA((5,)),
        ],
    )
    table0 = lax.all_to_all(out0, dom, split_axis=0, concat_axis=0, tiled=True)
    own, ghost, own_train, noise_train, part1, flag, own_rest, ghost_rest = call(
        build_kernel,
        28,
        [
            ((nodes, nodes), bf16, HBM),
            ((nodes, ghosts), bf16, None),
            ((train, nodes), bf16, None),
            ((train, width), bf16, None),
            ((nodes, width), f32, None),
            ((1,), jnp.int32, SMEM),
            ((nodes, nodes), bf16, HBM),
            ((nodes, ghosts), bf16, HBM),
        ],
        [
            (tile_block, HBM),
            (tile_count, pl.ANY),
            (src, None),
            (dst, None),
            (hop_noise, HBM),
            (start0, None),
        ],
        [
            VMEM((nodes, width), bf16),
            VMEM((tiles, slots, 128), bf16),
            VMEM((tiles * 16, slots), bf16),
            VMEM((tiles * 16, slots), bf16),
            VMEM((nodes, cols), f32),
            VMEM((nodes, max(nodes, ghosts)), bf16),
            VMEM((nodes, nodes), bf16),
            SMEM(tile_block.shape, jnp.int32),
            SMEM(tile_count.shape, jnp.int32),
            DMA((5,)),
        ],
    )
    start1, out1, side = call(
        hop_kernel,
        16,
        [
            ((nodes, width), bf16, None),
            ((parts, each, width), bf16, HBM),
            ((2 * train + 16, width), bf16, None),
        ],
        [
            (flag, SMEM),
            (part1, None),
            (ghost, None),
            (ghost_rest, HBM),
            (table0, None),
            (rows, VMEM),
            (own0, None),
            (labels.reshape(1, train), VMEM),
        ],
        [VMEM((nodes, width), f32), VMEM((nodes, ghosts), bf16), turn, pick, staged, DMA(())],
    )
    table1 = lax.all_to_all(out1, dom, split_axis=0, concat_axis=0, tiled=True)
    place = jnp.stack([lax.axis_index(dom), lax.axis_index("grp")]).astype(jnp.int32)
    grp = lax.axis_size("grp")

    def shifted(value, name, size, step):
        return [
            lax.ppermute(value, name, [((at + step * shift) % size, at) for at in range(size)])
            for shift in range(1, size)
        ]

    sides = [side] + (shifted(side, "grp", grp, 1) if few else [])
    side_shape = (len(sides) * 2 * train + 16, width)
    last, side = call(
        train_kernel,
        12,
        [
            ((copies, train, width), bf16, HBM),
            (side_shape, bf16, HBM),
        ],
        [
            (flag, SMEM),
            (place, SMEM),
            (own_train, None),
            (ghost, None),
            (own_rest, HBM),
            (ghost_rest, HBM),
            (noise_train, None),
            (start1, None),
            (table1, None),
        ]
        + [(value, None) for value in sides],
        [
            VMEM((train, width), f32),
            VMEM((train, max(nodes, ghosts)), bf16),
            VMEM((128, 128), f32),
            VMEM((copies, train, width), bf16),
            VMEM(side_shape, bf16),
            DMA((2,)),
        ],
    )
    if few:
        every2 = lax.all_to_all(last, ("chip", "grp"), split_axis=0, concat_axis=0, tiled=True)
        sides = [side] + shifted(side, "chip", parts // 2, -1)
    else:
        every0, every1, every2 = (
            every(value, axes) for value in (own0[None], start1[None, :train], last)
        )
        every_label = every(labels.reshape(1, train), axes)
    hop_feats, held_first = call(
        last_kernel,
        16,
        [((2, 1, 1, nodes, width), bf16, VMEM), (w_first.shape, bf16, None)],
        [
            (flag, SMEM),
            (side, HBM),
            (own, HBM),
            (own_rest, HBM),
            (ghost_rest, HBM),
            (hop_noise, HBM),
            (w_first, HBM),
            (ghost, None),
            (table1, None),
            (start1, None),
        ],
        [
            VMEM((nodes, nodes), bf16),
            VMEM((nodes, width), bf16),
            VMEM((nodes, width), f32),
            VMEM((nodes, max(nodes, ghosts)), bf16),
            DMA((3,)),
        ],
    )
    chunk = train * (copies if few else min(members, 32))
    groups = chunk // train
    wide = (classes + 255) // 256 * 256
    fixed = (w_first, w_second, w_third.T, noise_first, noise_second, noise_third.T)
    scratch = [VMEM(value.shape, value.dtype) for value in fixed]
    scratch += [
        VMEM((chunk, d_in), bf16),
        VMEM((wide, hid), bf16),
        VMEM((128, 128), f32),
        VMEM((chunk, 128), jnp.int32),
        VMEM((chunk, hid), bf16),
        VMEM((chunk, hid), bf16),
        VMEM((chunk, hid), f32),
        VMEM((chunk, hid), f32),
        VMEM((chunk, hid), bf16),
        VMEM((chunk, hid), bf16),
        VMEM((chunk, wide), bf16),
        DMA((16,)),
    ]
    if few:
        chips = parts // 2

        def classify(place_ref, *refs):
            sides_in, rest = refs[:chips], refs[chips:]
            two_ref, first_ref, *outs = rest[:11]
            held, *rest = rest[11:]
            classify_kernel(
                False,
                place_ref,
                None,
                None,
                None,
                two_ref,
                (held,) + sides_in[1:],
                first_ref,
                *outs,
                sides_in[0],
                first_ref,
                *rest,
            )

        rows = noise_first.shape[0] + noise_second.shape[0] + 32
        *own_sums, other = call(
            classify,
            44,
            [(value.shape, f32, None) for value in fixed[3:]] + [((rows, hid), bf16, None)],
            [(place, SMEM)]
            + [(side, HBM)]
            + [(value, None) for value in sides[1:]]
            + [(every2, None), (held_first, None)]
            + [(value, HBM) for value in fixed[1:]],
            [VMEM(side_shape, bf16)] + scratch[1:],
        )
        got = lax.ppermute(other, "core", [(0, 1), (1, 0)])
        first, second, third = call(
            finish_kernel,
            16,
            [(value.shape, f32, VMEM) for value in fixed[3:]],
            [(got, None)] + [(value, None) for value in own_sums],
            [],
        )
    else:

        ins = (every_label, every0, every1, every2)

        def classify(place_ref, label_ref, zero_ref, one_ref, two_ref, *rest):
            classify_kernel(
                True,
                place_ref,
                label_ref,
                zero_ref,
                one_ref,
                two_ref,
                None,
                *rest[:9],
                None,
                None,
                *rest[9:],
            )

        def whole(value):
            return pl.BlockSpec(value.shape, lambda i: (0, 0))

        def piece(value):
            return pl.BlockSpec(
                (groups,) + value.shape[1:], lambda i: (i,) + (0,) * (value.ndim - 1)
            )

        first, second, third = pl.pallas_call(
            classify,
            grid=(members // groups,),
            out_shape=[jax.ShapeDtypeStruct(value.shape, f32) for value in fixed[3:]],
            in_specs=[pl.BlockSpec(memory_space=SMEM)]
            + [piece(value) for value in ins]
            + [pl.BlockSpec(memory_space=HBM) for value in fixed],
            out_specs=[whole(value) for value in fixed[3:]],
            scratch_shapes=scratch,
            compiler_params=params(56),
        )(place, *ins, *fixed)
    return (hop_feats, first, second, third.T)


def solution(mesh):
    dom, grp = mesh.shape["dom"], mesh.shape["grp"]
    names = ("dom", "grp")
    if dom * grp <= FEW and dom <= 8 and dom % 2 == 0:
        names = ("chip", "core", "grp")
        mesh = jax.sharding.Mesh(mesh.devices.reshape(dom // 2, 2, grp), names)
    doms, grps = names[:-1], "grp"
    in_specs = (
        P(doms, grps, None, None),
        P(None, doms, grps, None, None),
        P(doms, grps, None, None),
        P(doms, grps, None),
        P(doms, grps, None, None),
        P(doms, grps, None, None),
        P(doms, grps),
        P(doms, grps, None),
        P(),
        P(),
        P(),
        P(doms, None),
        P(doms, None),
        P(doms, None),
    )
    out_specs = (P(None, doms, grps, None, None), P(doms, None), P(doms, None), P(doms, None))
    return jax.shard_map(
        functools.partial(local, names),
        mesh=mesh,
        in_specs=in_specs,
        out_specs=out_specs,
        check_vma=False,
    )
```

```python
import functools
import math

import jax
import jax.numpy as jnp
from jax import lax
from jax.experimental import pallas as pl
from jax.experimental.pallas import tpu as pltpu
from jax.sharding import PartitionSpec as P

BLOCK = 128
LOW = 256
GROUP = 8
clip_bound = 4.0
noise_mult = 1.0

f32 = jnp.float32
bf16 = jnp.bfloat16
VMEM = pltpu.VMEM
SMEM = pltpu.SMEM
HBM = pltpu.HBM
DMA = pltpu.SemaphoreType.DMA


FEW = 32


def params(mib):
    return pltpu.CompilerParams(vmem_limit_bytes=mib * 1024 * 1024)


def fetch(pairs, sems):
    copies = [pltpu.make_async_copy(*pair, sems.at[at]) for at, pair in enumerate(pairs)]
    for copy in copies:
        copy.start()
    return copies


def normalize(values):
    return (values * lax.rsqrt(jnp.sum(values * values, -1, keepdims=True) + 1e-06)).astype(bf16)


def dot(left, right):
    return jnp.dot(left, right, preferred_element_type=f32)


def dot_tn(left, right):
    return lax.dot_general(left, right, (((0,), (0,)), ((), ())), preferred_element_type=f32)


def choose(rows_ref, turn_ref, pick_ref):
    parts, each = rows_ref.shape
    turn_ref[:parts, :each] = rows_ref[...]
    columns = turn_ref[...].T
    spots = lax.broadcasted_iota(jnp.int32, (each, pick_ref.shape[1]), 1)
    for part in range(parts):
        wanted = columns[:each, part : part + 1]
        pick_ref[part * each : (part + 1) * each, :] = jnp.where(wanted == spots, 1.0, 0.0).astype(
            bf16
        )


def post(rows, staged_ref, out_hbm, sem):
    staged_ref[...] = rows.reshape(staged_ref.shape)
    copy = pltpu.make_async_copy(staged_ref, out_hbm, sem)
    copy.start()
    return copy


def first_kernel(
    feats_hbm,
    rows_hbm,
    src_hbm,
    dst_hbm,
    start_ref,
    out_hbm,
    own_ref,
    src_ref,
    dst_ref,
    feats_ref,
    rows_ref,
    turn_ref,
    pick_ref,
    staged_ref,
    sems,
):
    copies = fetch(
        (
            (rows_hbm.at[0, 0], rows_ref),
            (feats_hbm.at[0, 0], feats_ref),
            (src_hbm.at[0, 0], src_ref),
            (dst_hbm.at[0, 0], dst_ref),
        ),
        sems,
    )
    copies[0].wait()
    choose(rows_ref, turn_ref, pick_ref)
    copies[1].wait()
    sent = normalize(dot(pick_ref[...], feats_ref[...]))
    out_copy = post(sent, staged_ref, out_hbm, sems.at[4])
    start = normalize(feats_ref[...].astype(f32))
    start_ref[...] = start
    own_ref[...] = start[: own_ref.shape[0]]
    copies[2].wait()
    copies[3].wait()
    out_copy.wait()


def build_kernel(
    blocks_hbm,
    count_ref,
    src_ref,
    dst_ref,
    noise_hbm,
    start_ref,
    own_hbm,
    ghost_ref,
    own_train_ref,
    noise_train_ref,
    part_ref,
    flag_ref,
    own_rest_ref,
    ghost_rest_ref,
    noise_ref,
    low_ref,
    high_ref,
    spot_ref,
    sums_ref,
    rest_ref,
    own_ref,
    blocks_ref,
    sems,
):
    train = own_train_ref.shape[0]
    copies = fetch(
        (
            (blocks_hbm, blocks_ref),
            (noise_hbm.at[0, 0, 0], noise_ref),
            (noise_hbm.at[1, 0, 0, :train], noise_train_ref),
        ),
        sems,
    )
    nodes, cols = sums_ref.shape
    pieces = -(-cols // LOW)
    tiles, slots = src_ref.shape
    own_ref[...] = jnp.zeros_like(own_ref)
    ghost_ref[...] = jnp.zeros_like(ghost_ref)
    count = count_ref[0, 0]

    def sixteen(values):
        wide = jnp.broadcast_to(values.astype(f32)[:, None, :], (tiles, 16, slots))
        return wide.reshape(tiles * 16, slots).astype(bf16)

    src = src_ref[...]
    dst = dst_ref[...]
    tile_ids = lax.broadcasted_iota(jnp.int32, (tiles, slots), 0)
    high_ref[...] = sixteen(src // LOW)
    spot_ref[...] = sixteen(jnp.where((dst < BLOCK) & (tile_ids < count), dst, -1))
    low = (src % LOW - LOW // 2).astype(f32).T
    for tile in range(tiles):
        low_ref[tile] = jnp.broadcast_to(low[:, tile : tile + 1], (slots, 128)).astype(bf16)
    ids = lax.broadcasted_iota(jnp.int32, (BLOCK, slots), 0).astype(f32).astype(bf16)
    lanes = lax.broadcasted_iota(jnp.int32, (slots, 128), 1).astype(f32)
    lanes = [(lanes + first).astype(bf16) for first in range(-LOW // 2, LOW // 2, 128)]
    one = jnp.ones((), bf16)
    zero = jnp.zeros((), bf16)

    def counts(tile):
        rows = pl.ds(pl.multiple_of(tile * 16, 16), 16)
        high, spot = high_ref[rows, :], spot_ref[rows, :]
        tall = jnp.concatenate([spot] * (BLOCK // 16), 0)
        spot_one = jnp.where(ids == tall, one, zero)
        spots = []
        for piece in range(pieces):
            here = jnp.where(high == piece, one, zero)
            spots.append(spot_one * jnp.concatenate([here] * (BLOCK // 16), 0))
        low = low_ref[tile]
        low_hot = jnp.concatenate([jnp.where(low == ids, one, zero) for ids in lanes], 1)
        spot_hot = jnp.concatenate(spots, 0)
        return dot(spot_hot.astype(jnp.float8_e4m3fn), low_hot.astype(jnp.float8_e4m3fn))

    def turn(add, step, carry):
        first = step * GROUP
        outs = [counts(first + inner) for inner in range(GROUP)]
        for inner, out in enumerate(outs):
            base = pl.multiple_of(blocks_ref[0, 0, first + inner] * BLOCK, BLOCK)
            for piece in range(pieces):
                add(pl.ds(base, BLOCK), piece * LOW, out[piece * BLOCK : (piece + 1) * BLOCK])
        return carry

    def add_short(rows, at, values):
        ref, at = (own_ref, at) if at < nodes else (ghost_ref, at - nodes)
        size = min(LOW, ref.shape[1] - at)
        ref[rows, at : at + size] += values[:, :size].astype(bf16)

    def add_long(rows, at, values):
        size = min(LOW, cols - at)
        sums_ref[rows, at : at + size] += values[:, :size]

    steps = (count + GROUP - 1) // GROUP
    copies[0].wait()
    lax.fori_loop(0, steps, functools.partial(turn, add_short), 0)
    top = ghost_ref[:BLOCK, :256]
    for first in range(0, nodes, BLOCK):
        for ref in (own_ref, ghost_ref):
            for at in range(0, ref.shape[1], 256):
                top = jnp.maximum(top, ref[first : first + BLOCK, at : at + 256])
    big = jnp.max(top.astype(f32)) >= 256.0
    flag_ref[0] = big.astype(jnp.int32)

    @pl.when(big)
    def _():
        sums_ref[...] = jnp.zeros_like(sums_ref)
        lax.fori_loop(0, steps, functools.partial(turn, add_long), 0)
        own_ref[...] = sums_ref[:, :nodes].astype(bf16)
        ghost_ref[...] = sums_ref[:, nodes:].astype(bf16)

    own_copy = pltpu.make_async_copy(own_ref, own_hbm, sems.at[3])
    own_copy.start()
    own_train_ref[...] = own_ref[:train, :]
    for copy in copies[1:]:
        copy.wait()
    part_ref[...] = dot(own_ref[...], start_ref[...]) + noise_ref[...].astype(f32)

    @pl.when(big)
    def _():
        own_rest = (sums_ref[:, :nodes] - own_ref[...].astype(f32)).astype(bf16)
        part_ref[...] += dot(own_rest, start_ref[...])
        rest_ref[:, :nodes] = own_rest
        pltpu.sync_copy(rest_ref.at[:, :nodes], own_rest_ref)
        rest_ref[:, : cols - nodes] = (sums_ref[:, nodes:] - ghost_ref[...].astype(f32)).astype(bf16)
        pltpu.sync_copy(rest_ref.at[:, : cols - nodes], ghost_rest_ref)

    own_copy.wait()


def aggregate(flag_ref, start, parts, sums_ref, rest_ref):
    rows = sums_ref.shape[0]
    total = start
    for count, _, table in parts:
        total += dot(count, table)
    sums_ref[...] = total

    @pl.when(flag_ref[0] > 0)
    def _():
        for count, rest_hbm, table in parts:
            held = rest_ref.at[:, : count.shape[1]]
            pltpu.sync_copy(rest_hbm.at[:rows], held)
            sums_ref[...] += dot(held[...], table)


def hop_kernel(
    flag_ref,
    part_ref,
    ghost_ref,
    rest_hbm,
    table_ref,
    rows_ref,
    old_ref,
    labels_ref,
    start_ref,
    out_hbm,
    side_ref,
    sums_ref,
    rest_ref,
    turn_ref,
    pick_ref,
    staged_ref,
    sem,
):
    width = start_ref.shape[1]
    table = table_ref[...].reshape(-1, width)
    parts = ((ghost_ref[...], rest_hbm, table),)
    aggregate(flag_ref, part_ref[...], parts, sums_ref, rest_ref)
    choose(rows_ref, turn_ref, pick_ref)
    start = normalize(sums_ref[...])
    start_ref[...] = start
    out_copy = post(dot(pick_ref[...], start).astype(bf16), staged_ref, out_hbm, sem)
    train = labels_ref.shape[1]
    side_ref[:train, :] = old_ref[...]
    side_ref[train : 2 * train, :] = start[:train]
    turn_ref[:1, :train] = labels_ref[...]
    side_ref[2 * train :, :128] = turn_ref[:16, :].astype(f32).astype(bf16)
    out_copy.wait()


def train_kernel(
    flag_ref,
    place_ref,
    own_ref,
    ghost_ref,
    own_rest_hbm,
    ghost_rest_hbm,
    noise_ref,
    start_ref,
    table_ref,
    *refs,
):
    *piece_refs, out_hbm, side_hbm, sums_ref, rest_ref, turn_ref, staged_ref, side_ref, sems = refs
    train, width = sums_ref.shape
    table = table_ref[...].reshape(-1, width)
    parts = (
        (own_ref[...], own_rest_hbm, start_ref[...]),
        (ghost_ref[:train], ghost_rest_hbm, table),
    )
    aggregate(flag_ref, noise_ref[...].astype(f32), parts, sums_ref, rest_ref)
    last = jnp.broadcast_to(normalize(sums_ref[...])[None], staged_ref.shape)
    out_copy = post(last, staged_ref, out_hbm, sems.at[0])
    length = piece_refs[0].shape[0] - 16
    groups = len(piece_refs)
    if groups > 1:
        for shift, ref in enumerate(piece_refs):
            group = lax.rem(place_ref[1] + shift, groups)
            at = pl.multiple_of(group * length, length)
            side_ref[pl.ds(at, length), :] = ref[:length, :]
            turn_ref[pl.ds(group, 1), :] = ref[length:, :128].astype(f32)[:1]
        side_ref[groups * length :, :128] = turn_ref[:16, :].astype(bf16)
        side_copy = pltpu.make_async_copy(side_ref, side_hbm, sems.at[1])
        side_copy.start()
        side_copy.wait()
    out_copy.wait()


def last_kernel(
    flag_ref,
    token_ref,
    own_hbm,
    own_rest_hbm,
    ghost_rest_hbm,
    noise_hbm,
    weight_hbm,
    second_hbm,
    third_hbm,
    ghost_ref,
    table_ref,
    start_ref,
    out_hbm,
    weight_ref,
    second_t_hbm,
    third_t_hbm,
    own_ref,
    noise_ref,
    sums_ref,
    rest_ref,
    out_ref,
    second_ref,
    third_ref,
    second_t_ref,
    third_t_ref,
    sems,
):
    copies = fetch(
        (
            (own_hbm, own_ref),
            (noise_hbm.at[1, 0, 0], noise_ref),
            (second_hbm, second_ref),
            (third_hbm, third_ref),
            (weight_hbm, weight_ref),
        ),
        sems,
    )
    table = table_ref[...].reshape(-1, out_ref.shape[-1])
    out_ref[0, 0, 0] = start_ref[...]
    copies[0].wait()
    copies[1].wait()
    parts = (
        (own_ref[...], own_rest_hbm, start_ref[...]),
        (ghost_ref[...], ghost_rest_hbm, table),
    )
    aggregate(flag_ref, noise_ref[...].astype(f32), parts, sums_ref, rest_ref)
    out_ref[1, 0, 0] = normalize(sums_ref[...])
    out_copy = pltpu.make_async_copy(out_ref, out_hbm, sems.at[5])
    out_copy.start()
    copies[3].wait()
    classes = third_ref.shape[0]
    third_t_ref[:, 128:] = jnp.zeros((third_t_ref.shape[0], third_t_ref.shape[1] - 128), bf16)
    third_t_ref[:, :128] = third_ref[:128, :].T
    third_t_ref[:, 128:classes] = third_ref[128:, :].T
    third_copy = pltpu.make_async_copy(third_t_ref, third_t_hbm, sems.at[6])
    third_copy.start()
    copies[2].wait()
    hid = second_ref.shape[0]
    for at in range(0, hid, 256):
        second_t_ref[at : at + 256, :] = second_ref[:, at : at + 256].T
    second_copy = pltpu.make_async_copy(second_t_ref, second_t_hbm, sems.at[7])
    second_copy.start()
    for copy in (copies[4], out_copy, third_copy, second_copy):
        copy.wait()


def shares(ref, first, share):
    return ref[:, pl.ds(pl.multiple_of(first, 128), share)].astype(f32)


def lanes_sum(values):
    total = None
    for piece in range(values.shape[1] // 128):
        part = values[:, piece * 128 : (piece + 1) * 128].astype(f32)
        total = part * part if total is None else total + part * part
    return total


def classify_kernel(
    many,
    place_ref,
    label_ref,
    zero_ref,
    one_ref,
    two_ref,
    side_refs,
    w_first_hbm,
    w_second_hbm,
    w_third_t_hbm,
    w_third_hbm,
    w_second_t_hbm,
    n_first_hbm,
    n_second_hbm,
    n_third_hbm,
    g_first_ref,
    g_second_ref,
    g_third_ref,
    send_ref,
    side_hbm,
    w_first_ref,
    w_second_ref,
    w_third_t_ref,
    w_third_ref,
    w_second_t_ref,
    n_first_ref,
    n_second_ref,
    n_third_ref,
    in_ref,
    w_third_pad_ref,
    turn_ref,
    column_ref,
    h_one_ref,
    h_two_ref,
    slope_one_ref,
    slope_two_ref,
    d_one_ref,
    d_two_ref,
    d_three_ref,
    sems,
):
    classes = w_third_ref.shape[0]
    hid = w_second_ref.shape[0]
    width = two_ref.shape[2]
    wide = w_third_pad_ref.shape[0]
    train = two_ref.shape[1]
    scale = noise_mult * clip_bound
    place = place_ref[0]
    pairs = (
        (w_first_hbm, w_first_ref),
        (w_second_hbm, w_second_ref),
        (w_third_t_hbm, w_third_t_ref),
        (w_third_hbm, w_third_ref),
        (w_second_t_hbm, w_second_t_ref),
        (n_first_hbm, n_first_ref),
        (n_second_hbm, n_second_ref),
        (n_third_hbm, n_third_ref),
    )

    def set_noise():
        g_first_ref[...] = scale * n_first_ref[...]
        g_second_ref[...] = scale * n_second_ref[...]
        g_third_ref[...] = scale * n_third_ref[...]

    def pad():
        w_third_pad_ref[...] = jnp.zeros_like(w_third_pad_ref)
        w_third_pad_ref[:classes, :] = w_third_ref[...]

    def column(row, turned, lane):
        column_ref[row : row + train, :] = jnp.broadcast_to(
            turned[:train, lane : lane + 1], (train, 128)
        ).astype(jnp.int32)

    if many:

        @pl.when(pl.program_id(0) == 0)
        def _():
            for copy in fetch(pairs, sems):
                copy.wait()
            set_noise()
            pad()

        groups = label_ref.shape[0]
        turn_ref[:groups, :train] = label_ref[...].astype(f32)
        turned = turn_ref[...].T
        for group in range(groups):
            column(group * train, turned, group)
        for hop, ref in enumerate((zero_ref, one_ref)):
            in_ref[:, hop * width : (hop + 1) * width] = ref[...].reshape(-1, width)
    else:
        chips = len(side_refs)
        copies = fetch(((side_hbm, side_refs[0]),) + pairs[1:], sems)
        groups = two_ref.shape[0] // chips
        rows = groups * train
        for shift, ref in [*enumerate(side_refs)][::-1]:
            if shift == 0:
                copies[0].wait()
            part = lax.rem(place // 2 - shift + chips, chips)
            at = pl.multiple_of(part * rows, rows)
            for group in range(groups):
                for hop in range(2):
                    first = (2 * group + hop) * train
                    in_ref[pl.ds(at + group * train, train), hop * width : (hop + 1) * width] = ref[
                        first : first + train, :
                    ]
            turn_ref[pl.ds(pl.multiple_of(part * 16, 16), 16), :] = ref[2 * rows :, :128].astype(f32)
        turned = turn_ref[...].T
        for part in range(chips):
            for group in range(groups):
                column((part * groups + group) * train, turned, part * 16 + group)
    in_ref[:, 2 * width :] = two_ref[...].reshape(-1, width)

    def activate(values, h_ref, slope_ref, rows):
        sigma = 0.5 + 0.5 * jnp.tanh(0.5 * values)
        out = values * sigma
        slope_ref[rows, :] = sigma + out * (1.0 - sigma)
        h_ref[rows, :] = out.astype(bf16)
        return lanes_sum(out)

    def back(values, slope_ref, d_ref, rows):
        out = values * slope_ref[rows, :]
        d_ref[rows, :] = out.astype(bf16)
        return lanes_sum(out)

    def layer(product, finish, *refs):
        sums = []
        values = product(cuts[0])
        for at, cut in enumerate(cuts):
            ahead = product(cuts[at + 1]) if at + 1 < len(cuts) else None
            sums.append(finish(values, *refs, cut))
            values = ahead
        return jnp.concatenate(sums, 0)

    step = min(512, in_ref.shape[0])
    cuts = [slice(at, at + step) for at in range(0, in_ref.shape[0], step)]
    sq_in = lanes_sum(in_ref[...])
    sq_one = layer(
        lambda cut: dot(in_ref[cut, :], w_first_ref[...]), activate, h_one_ref, slope_one_ref
    )
    if not many:
        copies[1].wait()
    sq_two = layer(
        lambda cut: dot(h_one_ref[cut, :], w_second_ref[...]), activate, h_two_ref, slope_two_ref
    )
    if not many:
        copies[2].wait()
    logits = dot(h_two_ref[...], w_third_t_ref[...])
    ids = lax.broadcasted_iota(jnp.int32, (logits.shape[0], wide), 1)
    expo = jnp.where(ids < classes, jnp.exp(logits), 0.0)
    probs = expo / jnp.sum(expo, -1, keepdims=True)
    label = column_ref[:, :1]
    d_three = (probs - jnp.where(ids == label, 1.0, 0.0)).astype(bf16)
    sq_dthree = lanes_sum(d_three)
    d_three_ref[...] = d_three
    if not many:
        copies[3].wait()
        copies[4].wait()
        pad()
    sq_dtwo = layer(
        lambda cut: dot(d_three_ref[cut, :], w_third_pad_ref[...]), back, slope_two_ref, d_two_ref
    )
    sq_done = layer(
        lambda cut: dot(d_two_ref[cut, :], w_second_t_ref[...]), back, slope_one_ref, d_one_ref
    )

    def total(values):
        return jnp.sum(values, -1, keepdims=True)

    norm = jnp.sqrt(
        total(sq_in) * total(sq_done)
        + total(sq_one) * total(sq_dtwo)
        + total(sq_two) * total(sq_dthree)
    )
    factor = clip_bound / jnp.maximum(norm, clip_bound)

    if not many:
        for copy in copies[5:]:
            copy.wait()
        set_noise()
    share_one, share = g_first_ref.shape[0], g_second_ref.shape[0]
    places = [place] if many else [place, place + 1 - 2 * (place % 2)]

    def left(ref, share):
        if share % 128 == 0:
            picked = [shares(ref, at * share, share) for at in places]
            return (jnp.concatenate(picked, 1) * factor).astype(bf16)
        length, count = ref.shape[1], share * len(places)
        most = 128 - math.gcd(count, 128)
        size = min(length, -(-(count + most) // 128) * 128)
        first = [at * share for at in places]
        least = functools.reduce(jnp.minimum, first)
        start = jnp.minimum(least // 128 * 128, length - size)
        rows = lax.broadcasted_iota(jnp.int32, (size, count), 0)
        cols = lax.broadcasted_iota(jnp.int32, (size, count), 1)
        wanted = cols + (first[0] - start)
        for at, other in enumerate(first[1:], 1):
            wanted = jnp.where(cols >= at * share, cols - at * share + (other - start), wanted)
        window = ref[:, pl.ds(pl.multiple_of(start, 128), size)]
        picked = dot(window, jnp.where(rows == wanted, 1.0, 0.0).astype(bf16))
        return (picked * factor).astype(bf16)

    sum_one = dot_tn(left(in_ref, share_one), d_one_ref[...])
    sum_two = dot_tn(left(h_one_ref, share), d_two_ref[...])
    sum_three = dot_tn(d_three, left(h_two_ref, share))
    g_first_ref[...] += sum_one[:share_one]
    g_second_ref[...] += sum_two[:share]
    g_third_ref[...] += sum_three[:classes, :share]
    if not many:
        send_ref[:share_one, :] = sum_one[share_one:].astype(bf16)
        send_ref[share_one : share_one + share, :] = sum_two[share:].astype(bf16)
        first = share_one + share
        for at in range(0, classes, 32):
            cols = slice(at // 32 * share, (at // 32 + 1) * share)
            send_ref[first : first + 32, cols] = sum_three[at : at + 32, share:].astype(bf16)


def finish_kernel(got_ref, one_ref, two_ref, three_ref, g_first_ref, g_second_ref, g_third_ref):
    share_one, share = one_ref.shape[0], two_ref.shape[0]
    g_first_ref[...] = one_ref[...] + got_ref[:share_one, :].astype(f32)
    g_second_ref[...] = two_ref[...] + got_ref[share_one : share_one + share, :].astype(f32)
    first = share_one + share
    classes = three_ref.shape[0]
    for at in range(0, classes, 32):
        size = min(32, classes - at)
        cols = slice(at // 32 * share, (at // 32 + 1) * share)
        got = got_ref[first : first + 32, cols].astype(f32)
        g_third_ref[at : at + size, :] = three_ref[at : at + size, :] + got[:size]


def call(kernel, mib, outs, ins, scratch):
    def shape_of(shape, dtype, space):
        if space is None or space is HBM:
            return (space or VMEM)(shape, dtype)
        return jax.ShapeDtypeStruct(shape, dtype)

    def block(space):
        return pl.BlockSpec(memory_space=VMEM if space is None else space)

    def held(value, space):
        if space is None or space is HBM:
            return pltpu.with_memory_space_constraint(value, space or VMEM)
        return value

    return pl.pallas_call(
        kernel,
        out_shape=[shape_of(*out) for out in outs],
        in_specs=[block(space) for _, space in ins],
        out_specs=[block(space) for _, _, space in outs],
        scratch_shapes=scratch,
        compiler_params=params(mib),
    )(*[held(value, space) for value, space in ins])


def local(
    axes,
    feats,
    hop_noise,
    send_rows,
    tile_block,
    tile_src,
    tile_dst,
    tile_count,
    labels,
    w_first,
    w_second,
    w_third,
    noise_first,
    noise_second,
    noise_third,
):
    nodes, width = feats.shape[2:]
    parts, each = send_rows.shape[2:]
    ghosts = parts * each
    tiles = tile_src.shape[2]
    slots = tile_src.shape[3]
    train = labels.shape[2]
    classes = w_third.shape[1]
    hid = w_second.shape[0]
    d_in = w_first.shape[0]
    cols = nodes + ghosts
    rows = send_rows.reshape(parts, each)
    turn = VMEM((128, 128), jnp.int32)
    pick = VMEM((ghosts, nodes), bf16)
    dom = axes[:-1]
    members = lax.axis_size(axes)
    few = len(axes) == 3
    copies = members // 2 if few else 1

    def every(value, *names):
        for name in names:
            value = lax.all_gather(value, name, axis=0, tiled=True)
        return value

    staged = VMEM((parts, each, width), bf16)
    start0, out0, own0, src, dst = call(
        first_kernel,
        16,
        [
            ((nodes, width), bf16, None),
            ((parts, each, width), bf16, HBM),
            ((train, width), bf16, None),
            ((tiles, slots), jnp.int32, None),
            ((tiles, slots), jnp.int32, None),
        ],
        [(feats, HBM), (send_rows, HBM), (tile_src, HBM), (tile_dst, HBM)],
        [
            VMEM((nodes, width), bf16),
            VMEM((parts, each), jnp.int32),
            turn,
            pick,
            staged,
            DMA((5,)),
        ],
    )
    table0 = lax.all_to_all(out0, dom, split_axis=0, concat_axis=0, tiled=True)
    own, ghost, own_train, noise_train, part1, flag, own_rest, ghost_rest = call(
        build_kernel,
        28,
        [
            ((nodes, nodes), bf16, HBM),
            ((nodes, ghosts), bf16, None),
            ((train, nodes), bf16, None),
            ((train, width), bf16, None),
            ((nodes, width), f32, None),
            ((1,), jnp.int32, SMEM),
            ((nodes, nodes), bf16, HBM),
            ((nodes, ghosts), bf16, HBM),
        ],
        [
            (tile_block, HBM),
            (tile_count, SMEM),
            (src, None),
            (dst, None),
            (hop_noise, HBM),
            (start0, None),
        ],
        [
            VMEM((nodes, width), bf16),
            VMEM((tiles, slots, 128), bf16),
            VMEM((tiles * 16, slots), bf16),
            VMEM((tiles * 16, slots), bf16),
            VMEM((nodes, cols), f32),
            VMEM((nodes, max(nodes, ghosts)), bf16),
            VMEM((nodes, nodes), bf16),
            SMEM(tile_block.shape, jnp.int32),
            DMA((4,)),
        ],
    )
    start1, out1, side = call(
        hop_kernel,
        16,
        [
            ((nodes, width), bf16, None),
            ((parts, each, width), bf16, HBM),
            ((2 * train + 16, width), bf16, None),
        ],
        [
            (flag, SMEM),
            (part1, None),
            (ghost, None),
            (ghost_rest, HBM),
            (table0, None),
            (rows, VMEM),
            (own0, None),
            (labels.reshape(1, train), VMEM),
        ],
        [VMEM((nodes, width), f32), VMEM((nodes, ghosts), bf16), turn, pick, staged, DMA(())],
    )
    table1 = lax.all_to_all(out1, dom, split_axis=0, concat_axis=0, tiled=True)
    place = jnp.stack([lax.axis_index(dom), lax.axis_index("grp")]).astype(jnp.int32)
    grp = lax.axis_size("grp")

    def shifted(value, name, size, step):
        return [
            lax.ppermute(value, name, [((at + step * shift) % size, at) for at in range(size)])
            for shift in range(1, size)
        ]

    sides = [side] + (shifted(side, "grp", grp, 1) if few else [])
    side_shape = (len(sides) * 2 * train + 16, width)
    last, side = call(
        train_kernel,
        12,
        [
            ((copies, train, width), bf16, HBM),
            (side_shape, bf16, HBM),
        ],
        [
            (flag, SMEM),
            (place, SMEM),
            (own_train, None),
            (ghost, None),
            (own_rest, HBM),
            (ghost_rest, HBM),
            (noise_train, None),
            (start1, None),
            (table1, None),
        ]
        + [(value, None) for value in sides],
        [
            VMEM((train, width), f32),
            VMEM((train, max(nodes, ghosts)), bf16),
            VMEM((128, 128), f32),
            VMEM((copies, train, width), bf16),
            VMEM(side_shape, bf16),
            DMA((2,)),
        ],
    )
    if few:
        every2 = lax.all_to_all(last, ("chip", "grp"), split_axis=0, concat_axis=0, tiled=True)
        sides = [side] + shifted(side, "chip", parts // 2, -1)
    else:
        every0, every1, every2 = (
            every(value, axes) for value in (own0[None], start1[None, :train], last)
        )
        every_label = every(labels.reshape(1, train), axes)
    wide = (classes + 255) // 256 * 256
    hop_feats, held_first, second_t, third_t = call(
        last_kernel,
        28,
        [
            ((2, 1, 1, nodes, width), bf16, HBM),
            (w_first.shape, bf16, None),
            ((hid, hid), bf16, HBM),
            ((hid, wide), bf16, HBM),
        ],
        [
            (flag, SMEM),
            (side, HBM),
            (own, HBM),
            (own_rest, HBM),
            (ghost_rest, HBM),
            (hop_noise, HBM),
            (w_first, HBM),
            (w_second, HBM),
            (w_third.T, HBM),
            (ghost, None),
            (table1, None),
            (start1, None),
        ],
        [
            VMEM((nodes, nodes), bf16),
            VMEM((nodes, width), bf16),
            VMEM((nodes, width), f32),
            VMEM((nodes, max(nodes, ghosts)), bf16),
            VMEM((2, 1, 1, nodes, width), bf16),
            VMEM((hid, hid), bf16),
            VMEM((classes, hid), bf16),
            VMEM((hid, hid), bf16),
            VMEM((hid, wide), bf16),
            DMA((8,)),
        ],
    )
    chunk = train * (copies if few else min(members, 32))
    groups = chunk // train
    noises = (noise_first, noise_second, noise_third.T)
    fixed = (w_first, w_second, third_t, w_third.T, second_t) + noises
    scratch = [VMEM(value.shape, value.dtype) for value in fixed]
    scratch += [
        VMEM((chunk, d_in), bf16),
        VMEM((wide, hid), bf16),
        VMEM((128, 128), f32),
        VMEM((chunk, 128), jnp.int32),
        VMEM((chunk, hid), bf16),
        VMEM((chunk, hid), bf16),
        VMEM((chunk, hid), f32),
        VMEM((chunk, hid), f32),
        VMEM((chunk, hid), bf16),
        VMEM((chunk, hid), bf16),
        VMEM((chunk, wide), bf16),
        DMA((16,)),
    ]
    if few:
        chips = parts // 2

        def classify(place_ref, *refs):
            sides_in, rest = refs[:chips], refs[chips:]
            two_ref, first_ref, *outs = rest[:13]
            held, *rest = rest[13:]
            classify_kernel(
                False,
                place_ref,
                None,
                None,
                None,
                two_ref,
                (held,) + sides_in[1:],
                first_ref,
                *outs,
                sides_in[0],
                first_ref,
                *rest,
            )

        rows = noise_first.shape[0] + noise_second.shape[0] + 32
        *own_sums, other = call(
            classify,
            44,
            [(value.shape, f32, None) for value in noises] + [((rows, hid), bf16, None)],
            [(place, SMEM)]
            + [(side, HBM)]
            + [(value, None) for value in sides[1:]]
            + [(every2, None), (held_first, None)]
            + [(value, HBM) for value in fixed[1:]],
            [VMEM(side_shape, bf16)] + scratch[1:],
        )
        got = lax.ppermute(other, "core", [(0, 1), (1, 0)])
        first, second, third = call(
            finish_kernel,
            16,
            [(value.shape, f32, VMEM) for value in noises],
            [(got, None)] + [(value, None) for value in own_sums],
            [],
        )
    else:

        ins = (every_label, every0, every1, every2)

        def classify(place_ref, label_ref, zero_ref, one_ref, two_ref, *rest):
            classify_kernel(
                True,
                place_ref,
                label_ref,
                zero_ref,
                one_ref,
                two_ref,
                None,
                *rest[:11],
                None,
                None,
                *rest[11:],
            )

        def whole(value):
            return pl.BlockSpec(value.shape, lambda i: (0, 0))

        def piece(value):
            return pl.BlockSpec(
                (groups,) + value.shape[1:], lambda i: (i,) + (0,) * (value.ndim - 1)
            )

        first, second, third = pl.pallas_call(
            classify,
            grid=(members // groups,),
            out_shape=[jax.ShapeDtypeStruct(value.shape, f32) for value in noises],
            in_specs=[pl.BlockSpec(memory_space=SMEM)]
            + [piece(value) for value in ins]
            + [pl.BlockSpec(memory_space=HBM) for value in fixed],
            out_specs=[whole(value) for value in noises],
            scratch_shapes=scratch,
            compiler_params=params(56),
        )(place, *ins, *fixed)
    return (hop_feats, first, second, third.T)


def solution(mesh):
    dom, grp = mesh.shape["dom"], mesh.shape["grp"]
    names = ("dom", "grp")
    if dom * grp <= FEW and dom <= 8 and dom % 2 == 0:
        names = ("chip", "core", "grp")
        mesh = jax.sharding.Mesh(mesh.devices.reshape(dom // 2, 2, grp), names)
    doms, grps = names[:-1], "grp"
    in_specs = (
        P(doms, grps, None, None),
        P(None, doms, grps, None, None),
        P(doms, grps, None, None),
        P(doms, grps, None),
        P(doms, grps, None, None),
        P(doms, grps, None, None),
        P(doms, grps),
        P(doms, grps, None),
        P(),
        P(),
        P(),
        P(doms, None),
        P(doms, None),
        P(doms, None),
    )
    out_specs = (P(None, doms, grps, None, None), P(doms, None), P(doms, None), P(doms, None))
    return jax.shard_map(
        functools.partial(local, names),
        mesh=mesh,
        in_specs=in_specs,
        out_specs=out_specs,
        check_vma=False,
    )
```

```python
import functools
import math

import jax
import jax.numpy as jnp
from jax import lax
from jax.experimental import pallas as pl
from jax.experimental.pallas import tpu as pltpu
from jax.sharding import PartitionSpec as P

BLOCK = 128
LOW = 256
GROUP = 8
clip_bound = 4.0
noise_mult = 1.0

f32 = jnp.float32
bf16 = jnp.bfloat16
f8 = jnp.float8_e4m3fn
VMEM = pltpu.VMEM
SMEM = pltpu.SMEM
HBM = pltpu.HBM
DMA = pltpu.SemaphoreType.DMA


FEW = 32


def params(mib):
    return pltpu.CompilerParams(vmem_limit_bytes=mib * 1024 * 1024)


def fetch(pairs, sems):
    copies = [pltpu.make_async_copy(*pair, sems.at[at]) for at, pair in enumerate(pairs)]
    for copy in copies:
        copy.start()
    return copies


def normalize(values):
    return (values * lax.rsqrt(jnp.sum(values * values, -1, keepdims=True) + 1e-06)).astype(bf16)


def blocks_of(length, step):
    return [slice(at, min(at + step, length)) for at in range(0, length, step)]


def dot(left, right):
    return jnp.dot(left, right, preferred_element_type=f32)


def dot_tn(left, right):
    return lax.dot_general(left, right, (((0,), (0,)), ((), ())), preferred_element_type=f32)


def choose(rows_ref, turn_ref, pick_ref):
    parts, each = rows_ref.shape
    turn_ref[:parts, :each] = rows_ref[...]
    columns = turn_ref[...].T
    spots = lax.broadcasted_iota(jnp.int32, (each, pick_ref.shape[1]), 1)
    for part in range(parts):
        wanted = columns[:each, part : part + 1]
        pick_ref[part * each : (part + 1) * each, :] = jnp.where(wanted == spots, 1.0, 0.0).astype(
            bf16
        )


def post(rows, staged_ref, out_hbm, sem):
    staged_ref[...] = rows.reshape(staged_ref.shape)
    copy = pltpu.make_async_copy(staged_ref, out_hbm, sem)
    copy.start()
    return copy


def first_kernel(
    feats_hbm,
    rows_hbm,
    src_hbm,
    dst_hbm,
    start_ref,
    out_hbm,
    own_ref,
    src_ref,
    dst_ref,
    feats_ref,
    rows_ref,
    turn_ref,
    pick_ref,
    staged_ref,
    sems,
):
    copies = fetch(
        (
            (rows_hbm.at[0, 0], rows_ref),
            (feats_hbm.at[0, 0], feats_ref),
            (src_hbm.at[0, 0], src_ref),
            (dst_hbm.at[0, 0], dst_ref),
        ),
        sems,
    )
    copies[0].wait()
    choose(rows_ref, turn_ref, pick_ref)
    copies[1].wait()
    picked = dot(pick_ref[...], feats_ref[...])
    each = staged_ref.shape[1]
    for part in range(staged_ref.shape[0]):
        staged_ref[part] = normalize(picked[part * each : (part + 1) * each])
    out_copy = pltpu.make_async_copy(staged_ref, out_hbm, sems.at[4])
    out_copy.start()
    for cut in blocks_of(start_ref.shape[0], 32):
        start_ref[cut, :] = normalize(feats_ref[cut, :].astype(f32))
    own_ref[...] = start_ref[: own_ref.shape[0], :]
    copies[2].wait()
    copies[3].wait()
    out_copy.wait()


def build_kernel(
    blocks_hbm,
    count_ref,
    src_ref,
    dst_ref,
    noise_hbm,
    start_ref,
    own_hbm,
    ghost_ref,
    own_train_ref,
    noise_train_ref,
    part_ref,
    flag_ref,
    own_rest_ref,
    ghost_rest_ref,
    noise_ref,
    low_ref,
    high_ref,
    spot_ref,
    sums_ref,
    rest_ref,
    own_ref,
    blocks_ref,
    sems,
):
    train = own_train_ref.shape[0]
    copies = fetch(
        (
            (blocks_hbm, blocks_ref),
            (noise_hbm.at[0, 0, 0], noise_ref),
            (noise_hbm.at[1, 0, 0, :train], noise_train_ref),
        ),
        sems,
    )
    nodes, cols = sums_ref.shape
    pieces = -(-cols // LOW)
    tiles, slots = src_ref.shape
    own_ref[...] = jnp.zeros_like(own_ref)
    ghost_ref[...] = jnp.zeros_like(ghost_ref)
    count = count_ref[0, 0]

    def sixteen(values):
        wide = jnp.broadcast_to(values.astype(f32)[:, None, :], (tiles, 16, slots))
        return wide.reshape(tiles * 16, slots).astype(bf16)

    src = src_ref[...]
    dst = dst_ref[...]
    tile_ids = lax.broadcasted_iota(jnp.int32, (tiles, slots), 0)
    high_ref[...] = sixteen(src // LOW)
    spot_ref[...] = sixteen(jnp.where((dst < BLOCK) & (tile_ids < count), dst, -1))
    low = (src % LOW - LOW // 2).astype(f32).T
    for tile in range(tiles):
        low_ref[tile] = jnp.broadcast_to(low[:, tile : tile + 1], (slots, 128)).astype(bf16)
    ids = lax.broadcasted_iota(jnp.int32, (BLOCK, slots), 0).astype(f32).astype(bf16)
    lanes = lax.broadcasted_iota(jnp.int32, (slots, 128), 1).astype(f32)
    lanes = [(lanes + first).astype(bf16) for first in range(-LOW // 2, LOW // 2, 128)]
    one = jnp.ones((), bf16)
    zero = jnp.zeros((), bf16)

    def counts(tile):
        rows = pl.ds(pl.multiple_of(tile * 16, 16), 16)
        high, spot = high_ref[rows, :], spot_ref[rows, :]
        tall = jnp.concatenate([spot] * (BLOCK // 16), 0)
        spot_one = jnp.where(ids == tall, one, zero)
        spots = []
        for piece in range(pieces):
            here = jnp.where(high == piece, one, zero)
            hot = spot_one * jnp.concatenate([here] * (BLOCK // 16), 0)
            spots.append(hot.astype(f8))
        low = low_ref[tile]
        low_hot = [jnp.where(low == ids, one, zero).astype(f8) for ids in lanes]
        return dot(jnp.concatenate(spots, 0), jnp.concatenate(low_hot, 1))

    def turn(add, step, carry):
        first = step * GROUP
        outs = [counts(first + inner) for inner in range(GROUP)]
        for inner, out in enumerate(outs):
            base = pl.multiple_of(blocks_ref[0, 0, first + inner] * BLOCK, BLOCK)
            for piece in range(pieces):
                add(pl.ds(base, BLOCK), piece * LOW, out[piece * BLOCK : (piece + 1) * BLOCK])
        return carry

    def add_short(rows, at, values):
        ref, at = (own_ref, at) if at < nodes else (ghost_ref, at - nodes)
        size = min(LOW, ref.shape[1] - at)
        ref[rows, at : at + size] += values[:, :size].astype(bf16)

    def add_long(rows, at, values):
        size = min(LOW, cols - at)
        sums_ref[rows, at : at + size] += values[:, :size]

    steps = (count + GROUP - 1) // GROUP
    copies[0].wait()
    lax.fori_loop(0, steps, functools.partial(turn, add_short), 0)
    top = ghost_ref[:BLOCK, :256]
    for first in range(0, nodes, BLOCK):
        for ref in (own_ref, ghost_ref):
            for at in range(0, ref.shape[1], 256):
                top = jnp.maximum(top, ref[first : first + BLOCK, at : at + 256])
    big = jnp.max(top.astype(f32)) >= 256.0
    flag_ref[0] = big.astype(jnp.int32)

    @pl.when(big)
    def _():
        sums_ref[...] = jnp.zeros_like(sums_ref)
        lax.fori_loop(0, steps, functools.partial(turn, add_long), 0)
        own_ref[...] = sums_ref[:, :nodes].astype(bf16)
        ghost_ref[...] = sums_ref[:, nodes:].astype(bf16)

    own_copy = pltpu.make_async_copy(own_ref, own_hbm, sems.at[3])
    own_copy.start()
    own_train_ref[...] = own_ref[:train, :]
    for copy in copies[1:]:
        copy.wait()
    part_ref[...] = dot(own_ref[...], start_ref[...]) + noise_ref[...].astype(f32)

    @pl.when(big)
    def _():
        own_rest = (sums_ref[:, :nodes] - own_ref[...].astype(f32)).astype(bf16)
        part_ref[...] += dot(own_rest, start_ref[...])
        rest_ref[:, :nodes] = own_rest
        pltpu.sync_copy(rest_ref.at[:, :nodes], own_rest_ref)
        rest_ref[:, : cols - nodes] = (sums_ref[:, nodes:] - ghost_ref[...].astype(f32)).astype(bf16)
        pltpu.sync_copy(rest_ref.at[:, : cols - nodes], ghost_rest_ref)

    own_copy.wait()


def aggregate(flag_ref, first_ref, parts, sums_ref, rest_ref):
    rows = sums_ref.shape[0]
    for cut in blocks_of(rows, 256):
        total = sum(dot(count_ref[cut, :], table) for count_ref, _, table in parts)
        for inner in blocks_of(total.shape[0], 32):
            at = slice(cut.start + inner.start, cut.start + inner.stop)
            sums_ref[at, :] = first_ref[at, :].astype(f32) + total[inner]

    @pl.when(flag_ref[0] > 0)
    def _():
        for count_ref, rest_hbm, table in parts:
            held = rest_ref.at[:, : count_ref.shape[1]]
            pltpu.sync_copy(rest_hbm.at[:rows], held)
            sums_ref[...] += dot(held[...], table)


def hop_kernel(
    flag_ref,
    part_ref,
    ghost_ref,
    rest_hbm,
    table_ref,
    rows_ref,
    old_ref,
    labels_ref,
    start_ref,
    out_hbm,
    side_ref,
    sums_ref,
    rest_ref,
    turn_ref,
    pick_ref,
    staged_ref,
    sem,
):
    width = start_ref.shape[1]
    table = table_ref[...].reshape(-1, width)
    parts = ((ghost_ref, rest_hbm, table),)
    choose(rows_ref, turn_ref, pick_ref)
    aggregate(flag_ref, part_ref, parts, sums_ref, rest_ref)
    for cut in blocks_of(start_ref.shape[0], 32):
        start_ref[cut, :] = normalize(sums_ref[cut, :])
    out_copy = post(dot(pick_ref[...], start_ref[...]).astype(bf16), staged_ref, out_hbm, sem)
    train = labels_ref.shape[1]
    side_ref[:train, :] = old_ref[...]
    side_ref[train : 2 * train, :] = start_ref[:train, :]
    turn_ref[:1, :train] = labels_ref[...]
    side_ref[2 * train :, :128] = turn_ref[:16, :].astype(f32).astype(bf16)
    out_copy.wait()


def train_kernel(
    flag_ref,
    place_ref,
    own_ref,
    ghost_ref,
    own_rest_hbm,
    ghost_rest_hbm,
    noise_ref,
    start_ref,
    table_ref,
    *refs,
):
    *piece_refs, out_hbm, side_hbm, sums_ref, rest_ref, turn_ref, staged_ref, side_ref, sems = refs
    train, width = sums_ref.shape
    table = table_ref[...].reshape(-1, width)
    parts = (
        (own_ref, own_rest_hbm, start_ref[...]),
        (ghost_ref, ghost_rest_hbm, table),
    )
    aggregate(flag_ref, noise_ref, parts, sums_ref, rest_ref)
    last = jnp.broadcast_to(normalize(sums_ref[...])[None], staged_ref.shape)
    out_copy = post(last, staged_ref, out_hbm, sems.at[0])
    length = piece_refs[0].shape[0] - 16
    groups = len(piece_refs)
    if groups > 1:
        for shift, ref in enumerate(piece_refs):
            group = lax.rem(place_ref[1] + shift, groups)
            at = pl.multiple_of(group * length, length)
            side_ref[pl.ds(at, length), :] = ref[:length, :]
            turn_ref[pl.ds(group, 1), :] = ref[length:, :128].astype(f32)[:1]
        side_ref[groups * length :, :128] = turn_ref[:16, :].astype(bf16)
        side_copy = pltpu.make_async_copy(side_ref, side_hbm, sems.at[1])
        side_copy.start()
        side_copy.wait()
    out_copy.wait()


def last_kernel(
    flag_ref,
    token_ref,
    own_hbm,
    own_rest_hbm,
    ghost_rest_hbm,
    noise_hbm,
    weight_hbm,
    second_hbm,
    third_hbm,
    ghost_ref,
    table_ref,
    start_ref,
    out_hbm,
    weight_ref,
    second_t_hbm,
    third_t_hbm,
    own_ref,
    noise_ref,
    sums_ref,
    rest_ref,
    out_ref,
    second_ref,
    third_ref,
    second_t_ref,
    third_t_ref,
    sems,
):
    copies = fetch(
        (
            (own_hbm, own_ref),
            (noise_hbm.at[1, 0, 0], noise_ref),
            (second_hbm, second_ref),
            (third_hbm, third_ref),
            (weight_hbm, weight_ref),
        ),
        sems,
    )
    table = table_ref[...].reshape(-1, out_ref.shape[-1])
    out_ref[0, 0, 0] = start_ref[...]
    copies[0].wait()
    copies[1].wait()
    parts = (
        (own_ref, own_rest_hbm, start_ref[...]),
        (ghost_ref, ghost_rest_hbm, table),
    )
    aggregate(flag_ref, noise_ref, parts, sums_ref, rest_ref)
    for cut in blocks_of(sums_ref.shape[0], 32):
        out_ref[1, 0, 0, cut, :] = normalize(sums_ref[cut, :])
    out_copy = pltpu.make_async_copy(out_ref, out_hbm, sems.at[5])
    out_copy.start()
    copies[3].wait()
    classes = third_ref.shape[0]
    third_t_ref[:, 128:] = jnp.zeros((third_t_ref.shape[0], third_t_ref.shape[1] - 128), bf16)
    third_t_ref[:, :128] = third_ref[:128, :].T
    third_t_ref[:, 128:classes] = third_ref[128:, :].T
    third_copy = pltpu.make_async_copy(third_t_ref, third_t_hbm, sems.at[6])
    third_copy.start()
    copies[2].wait()
    hid = second_ref.shape[0]
    for at in range(0, hid, 256):
        second_t_ref[at : at + 256, :] = second_ref[:, at : at + 256].T
    second_copy = pltpu.make_async_copy(second_t_ref, second_t_hbm, sems.at[7])
    second_copy.start()
    for copy in (copies[4], out_copy, third_copy, second_copy):
        copy.wait()


def shares(ref, first, share):
    return ref[:, pl.ds(pl.multiple_of(first, 128), share)].astype(f32)


def lanes_sum(values):
    total = None
    for piece in range(values.shape[1] // 128):
        part = values[:, piece * 128 : (piece + 1) * 128].astype(f32)
        total = part * part if total is None else total + part * part
    return total


def classify_kernel(
    many,
    place_ref,
    label_ref,
    zero_ref,
    one_ref,
    two_ref,
    side_refs,
    w_first_hbm,
    w_second_hbm,
    w_third_t_hbm,
    w_third_hbm,
    w_second_t_hbm,
    n_first_hbm,
    n_second_hbm,
    n_third_hbm,
    g_first_ref,
    g_second_ref,
    g_third_ref,
    send_ref,
    side_hbm,
    w_first_ref,
    w_second_ref,
    w_third_t_ref,
    w_third_ref,
    w_second_t_ref,
    n_first_ref,
    n_second_ref,
    n_third_ref,
    in_ref,
    w_third_pad_ref,
    turn_ref,
    column_ref,
    h_one_ref,
    h_two_ref,
    slope_one_ref,
    slope_two_ref,
    d_one_ref,
    d_two_ref,
    d_three_ref,
    sems,
):
    classes = w_third_ref.shape[0]
    hid = w_second_ref.shape[0]
    width = two_ref.shape[2]
    wide = w_third_pad_ref.shape[0]
    train = two_ref.shape[1]
    scale = noise_mult * clip_bound
    place = place_ref[0]
    pairs = (
        (w_first_hbm, w_first_ref),
        (w_second_hbm, w_second_ref),
        (w_third_t_hbm, w_third_t_ref),
        (w_third_hbm, w_third_ref),
        (w_second_t_hbm, w_second_t_ref),
        (n_first_hbm, n_first_ref),
        (n_second_hbm, n_second_ref),
        (n_third_hbm, n_third_ref),
    )

    def set_noise():
        g_first_ref[...] = scale * n_first_ref[...]
        g_second_ref[...] = scale * n_second_ref[...]
        g_third_ref[...] = scale * n_third_ref[...]

    def pad():
        w_third_pad_ref[...] = jnp.zeros_like(w_third_pad_ref)
        w_third_pad_ref[:classes, :] = w_third_ref[...]

    def column(row, turned, lane):
        column_ref[row : row + train, :] = jnp.broadcast_to(
            turned[:train, lane : lane + 1], (train, 128)
        ).astype(jnp.int32)

    if many:

        @pl.when(pl.program_id(0) == 0)
        def _():
            for copy in fetch(pairs, sems):
                copy.wait()
            set_noise()
            pad()

        groups = label_ref.shape[0]
        turn_ref[:groups, :train] = label_ref[...].astype(f32)
        turned = turn_ref[...].T
        for group in range(groups):
            column(group * train, turned, group)
        for hop, ref in enumerate((zero_ref, one_ref)):
            in_ref[:, hop * width : (hop + 1) * width] = ref[...].reshape(-1, width)
    else:
        chips = len(side_refs)
        copies = fetch(((side_hbm, side_refs[0]),) + pairs[1:], sems)
        groups = two_ref.shape[0] // chips
        rows = groups * train
        for shift, ref in [*enumerate(side_refs)][::-1]:
            if shift == 0:
                copies[0].wait()
            part = lax.rem(place // 2 - shift + chips, chips)
            at = pl.multiple_of(part * rows, rows)
            for group in range(groups):
                for hop in range(2):
                    first = (2 * group + hop) * train
                    in_ref[pl.ds(at + group * train, train), hop * width : (hop + 1) * width] = ref[
                        first : first + train, :
                    ]
            turn_ref[pl.ds(pl.multiple_of(part * 16, 16), 16), :] = ref[2 * rows :, :128].astype(f32)
        turned = turn_ref[...].T
        for part in range(chips):
            for group in range(groups):
                column((part * groups + group) * train, turned, part * 16 + group)
    in_ref[:, 2 * width :] = two_ref[...].reshape(-1, width)

    def activate(values, at, cols, h_ref, slope_ref):
        sigma = 0.5 + 0.5 * jnp.tanh(0.5 * values)
        out = values * sigma
        slope_ref[at, cols] = sigma + out * (1.0 - sigma)
        h_ref[at, cols] = out.astype(bf16)
        return lanes_sum(out)

    def back(values, at, cols, slope_ref, d_ref):
        out = values * slope_ref[at, cols]
        d_ref[at, cols] = out.astype(bf16)
        return lanes_sum(out)

    def layer(product, finish, *refs):
        sums = []
        values = product(cuts[0])
        for at, cut in enumerate(cuts):
            ahead = product(cuts[at + 1]) if at + 1 < len(cuts) else None
            for rows in blocks_of(values.shape[0], 32):
                here = slice(cut.start + rows.start, cut.start + rows.stop)
                sums.append(
                    sum(
                        finish(values[rows, cols], here, cols, *refs)
                        for cols in blocks_of(values.shape[1], 256)
                    )
                )
            values = ahead
        return jnp.concatenate(sums, 0)

    step = min(512, in_ref.shape[0])
    cuts = [slice(at, at + step) for at in range(0, in_ref.shape[0], step)]
    sq_in = jnp.concatenate([lanes_sum(in_ref[at, :]) for at in blocks_of(in_ref.shape[0], 32)], 0)
    sq_one = layer(
        lambda cut: dot(in_ref[cut, :], w_first_ref[...]), activate, h_one_ref, slope_one_ref
    )
    if not many:
        copies[1].wait()
    sq_two = layer(
        lambda cut: dot(h_one_ref[cut, :], w_second_ref[...]), activate, h_two_ref, slope_two_ref
    )
    if not many:
        copies[2].wait()
    logits = dot(h_two_ref[...], w_third_t_ref[...])
    sums = []
    for at in blocks_of(logits.shape[0], 32):
        ids = lax.broadcasted_iota(jnp.int32, (at.stop - at.start, wide), 1)
        expo = jnp.where(ids < classes, jnp.exp(logits[at]), 0.0)
        probs = expo / jnp.sum(expo, -1, keepdims=True)
        label = column_ref[at, :1]
        d_three = (probs - jnp.where(ids == label, 1.0, 0.0)).astype(bf16)
        d_three_ref[at, :] = d_three
        sums.append(lanes_sum(d_three))
    sq_dthree = jnp.concatenate(sums, 0)
    if not many:
        copies[3].wait()
        copies[4].wait()
        pad()
    sq_dtwo = layer(
        lambda cut: dot(d_three_ref[cut, :], w_third_pad_ref[...]), back, slope_two_ref, d_two_ref
    )
    sq_done = layer(
        lambda cut: dot(d_two_ref[cut, :], w_second_t_ref[...]), back, slope_one_ref, d_one_ref
    )

    def total(values):
        return jnp.sum(values, -1, keepdims=True)

    norm = jnp.sqrt(
        total(sq_in) * total(sq_done)
        + total(sq_one) * total(sq_dtwo)
        + total(sq_two) * total(sq_dthree)
    )
    factor = clip_bound / jnp.maximum(norm, clip_bound)

    if not many:
        for copy in copies[5:]:
            copy.wait()
        set_noise()
    share_one, share = g_first_ref.shape[0], g_second_ref.shape[0]
    places = [place] if many else [place, place + 1 - 2 * (place % 2)]

    def left(ref, share):
        if share % 128 == 0:
            picked = [shares(ref, at * share, share) for at in places]
            return (jnp.concatenate(picked, 1) * factor).astype(bf16)
        length, count = ref.shape[1], share * len(places)
        most = 128 - math.gcd(count, 128)
        size = min(length, -(-(count + most) // 128) * 128)
        first = [at * share for at in places]
        least = functools.reduce(jnp.minimum, first)
        start = jnp.minimum(least // 128 * 128, length - size)
        rows = lax.broadcasted_iota(jnp.int32, (size, count), 0)
        cols = lax.broadcasted_iota(jnp.int32, (size, count), 1)
        wanted = cols + (first[0] - start)
        for at, other in enumerate(first[1:], 1):
            wanted = jnp.where(cols >= at * share, cols - at * share + (other - start), wanted)
        window = ref[:, pl.ds(pl.multiple_of(start, 128), size)]
        picked = dot(window, jnp.where(rows == wanted, 1.0, 0.0).astype(bf16))
        return (picked * factor).astype(bf16)

    sum_one = dot_tn(left(in_ref, share_one), d_one_ref[...])
    sum_two = dot_tn(left(h_one_ref, share), d_two_ref[...])
    sum_three = dot_tn(d_three_ref[...], left(h_two_ref, share))
    g_first_ref[...] += sum_one[:share_one]
    g_second_ref[...] += sum_two[:share]
    g_third_ref[...] += sum_three[:classes, :share]
    if not many:
        send_ref[:share_one, :] = sum_one[share_one:].astype(bf16)
        send_ref[share_one : share_one + share, :] = sum_two[share:].astype(bf16)
        first = share_one + share
        for at in range(0, classes, 32):
            cols = slice(at // 32 * share, (at // 32 + 1) * share)
            send_ref[first : first + 32, cols] = sum_three[at : at + 32, share:].astype(bf16)


def finish_kernel(got_ref, one_ref, two_ref, three_ref, g_first_ref, g_second_ref, g_third_ref):
    share_one, share = one_ref.shape[0], two_ref.shape[0]
    g_first_ref[...] = one_ref[...] + got_ref[:share_one, :].astype(f32)
    g_second_ref[...] = two_ref[...] + got_ref[share_one : share_one + share, :].astype(f32)
    first = share_one + share
    classes = three_ref.shape[0]
    for at in range(0, classes, 32):
        size = min(32, classes - at)
        cols = slice(at // 32 * share, (at // 32 + 1) * share)
        got = got_ref[first : first + 32, cols].astype(f32)
        g_third_ref[at : at + size, :] = three_ref[at : at + size, :] + got[:size]


def call(kernel, mib, outs, ins, scratch):
    def shape_of(shape, dtype, space):
        if space is None or space is HBM:
            return (space or VMEM)(shape, dtype)
        return jax.ShapeDtypeStruct(shape, dtype)

    def block(space):
        return pl.BlockSpec(memory_space=VMEM if space is None else space)

    def held(value, space):
        if space is None or space is HBM:
            return pltpu.with_memory_space_constraint(value, space or VMEM)
        return value

    return pl.pallas_call(
        kernel,
        out_shape=[shape_of(*out) for out in outs],
        in_specs=[block(space) for _, space in ins],
        out_specs=[block(space) for _, _, space in outs],
        scratch_shapes=scratch,
        compiler_params=params(mib),
    )(*[held(value, space) for value, space in ins])


def local(
    axes,
    feats,
    hop_noise,
    send_rows,
    tile_block,
    tile_src,
    tile_dst,
    tile_count,
    labels,
    w_first,
    w_second,
    w_third,
    noise_first,
    noise_second,
    noise_third,
):
    nodes, width = feats.shape[2:]
    parts, each = send_rows.shape[2:]
    ghosts = parts * each
    tiles = tile_src.shape[2]
    slots = tile_src.shape[3]
    train = labels.shape[2]
    classes = w_third.shape[1]
    hid = w_second.shape[0]
    d_in = w_first.shape[0]
    cols = nodes + ghosts
    rows = send_rows.reshape(parts, each)
    turn = VMEM((128, 128), jnp.int32)
    pick = VMEM((ghosts, nodes), bf16)
    dom = axes[:-1]
    members = lax.axis_size(axes)
    few = len(axes) == 3
    copies = members // 2 if few else 1

    def every(value, *names):
        for name in names:
            value = lax.all_gather(value, name, axis=0, tiled=True)
        return value

    staged = VMEM((parts, each, width), bf16)
    start0, out0, own0, src, dst = call(
        first_kernel,
        16,
        [
            ((nodes, width), bf16, None),
            ((parts, each, width), bf16, HBM),
            ((train, width), bf16, None),
            ((tiles, slots), jnp.int32, None),
            ((tiles, slots), jnp.int32, None),
        ],
        [(feats, HBM), (send_rows, HBM), (tile_src, HBM), (tile_dst, HBM)],
        [
            VMEM((nodes, width), bf16),
            VMEM((parts, each), jnp.int32),
            turn,
            pick,
            staged,
            DMA((5,)),
        ],
    )
    table0 = lax.all_to_all(out0, dom, split_axis=0, concat_axis=0, tiled=True)
    own, ghost, own_train, noise_train, part1, flag, own_rest, ghost_rest = call(
        build_kernel,
        28,
        [
            ((nodes, nodes), bf16, HBM),
            ((nodes, ghosts), bf16, None),
            ((train, nodes), bf16, None),
            ((train, width), bf16, None),
            ((nodes, width), f32, None),
            ((1,), jnp.int32, SMEM),
            ((nodes, nodes), bf16, HBM),
            ((nodes, ghosts), bf16, HBM),
        ],
        [
            (tile_block, HBM),
            (tile_count, SMEM),
            (src, None),
            (dst, None),
            (hop_noise, HBM),
            (start0, None),
        ],
        [
            VMEM((nodes, width), bf16),
            VMEM((tiles, slots, 128), bf16),
            VMEM((tiles * 16, slots), bf16),
            VMEM((tiles * 16, slots), bf16),
            VMEM((nodes, cols), f32),
            VMEM((nodes, max(nodes, ghosts)), bf16),
            VMEM((nodes, nodes), bf16),
            SMEM(tile_block.shape, jnp.int32),
            DMA((4,)),
        ],
    )
    start1, out1, side = call(
        hop_kernel,
        16,
        [
            ((nodes, width), bf16, None),
            ((parts, each, width), bf16, HBM),
            ((2 * train + 16, width), bf16, None),
        ],
        [
            (flag, SMEM),
            (part1, None),
            (ghost, None),
            (ghost_rest, HBM),
            (table0, None),
            (rows, VMEM),
            (own0, None),
            (labels.reshape(1, train), VMEM),
        ],
        [VMEM((nodes, width), f32), VMEM((nodes, ghosts), bf16), turn, pick, staged, DMA(())],
    )
    table1 = lax.all_to_all(out1, dom, split_axis=0, concat_axis=0, tiled=True)
    place = jnp.stack([lax.axis_index(dom), lax.axis_index("grp")]).astype(jnp.int32)
    grp = lax.axis_size("grp")

    def shifted(value, name, size, step):
        return [
            lax.ppermute(value, name, [((at + step * shift) % size, at) for at in range(size)])
            for shift in range(1, size)
        ]

    sides = [side] + (shifted(side, "grp", grp, 1) if few else [])
    side_shape = (len(sides) * 2 * train + 16, width)
    last, side = call(
        train_kernel,
        12,
        [
            ((copies, train, width), bf16, HBM),
            (side_shape, bf16, HBM),
        ],
        [
            (flag, SMEM),
            (place, SMEM),
            (own_train, None),
            (ghost, None),
            (own_rest, HBM),
            (ghost_rest, HBM),
            (noise_train, None),
            (start1, None),
            (table1, None),
        ]
        + [(value, None) for value in sides],
        [
            VMEM((train, width), f32),
            VMEM((train, max(nodes, ghosts)), bf16),
            VMEM((128, 128), f32),
            VMEM((copies, train, width), bf16),
            VMEM(side_shape, bf16),
            DMA((2,)),
        ],
    )
    if few:
        every2 = lax.all_to_all(last, ("chip", "grp"), split_axis=0, concat_axis=0, tiled=True)
        sides = [side] + shifted(side, "chip", parts // 2, -1)
    else:
        every0, every1, every2 = (
            every(value, axes) for value in (own0[None], start1[None, :train], last)
        )
        every_label = every(labels.reshape(1, train), axes)
    wide = (classes + 255) // 256 * 256
    hop_feats, held_first, second_t, third_t = call(
        last_kernel,
        28,
        [
            ((2, 1, 1, nodes, width), bf16, HBM),
            (w_first.shape, bf16, None),
            ((hid, hid), bf16, HBM),
            ((hid, wide), bf16, HBM),
        ],
        [
            (flag, SMEM),
            (side, HBM),
            (own, HBM),
            (own_rest, HBM),
            (ghost_rest, HBM),
            (hop_noise, HBM),
            (w_first, HBM),
            (w_second, HBM),
            (w_third.T, HBM),
            (ghost, None),
            (table1, None),
            (start1, None),
        ],
        [
            VMEM((nodes, nodes), bf16),
            VMEM((nodes, width), bf16),
            VMEM((nodes, width), f32),
            VMEM((nodes, max(nodes, ghosts)), bf16),
            VMEM((2, 1, 1, nodes, width), bf16),
            VMEM((hid, hid), bf16),
            VMEM((classes, hid), bf16),
            VMEM((hid, hid), bf16),
            VMEM((hid, wide), bf16),
            DMA((8,)),
        ],
    )
    chunk = train * (copies if few else min(members, 32))
    groups = chunk // train
    noises = (noise_first, noise_second, noise_third.T)
    fixed = (w_first, w_second, third_t, w_third.T, second_t) + noises
    scratch = [VMEM(value.shape, value.dtype) for value in fixed]
    scratch += [
        VMEM((chunk, d_in), bf16),
        VMEM((wide, hid), bf16),
        VMEM((128, 128), f32),
        VMEM((chunk, 128), jnp.int32),
        VMEM((chunk, hid), bf16),
        VMEM((chunk, hid), bf16),
        VMEM((chunk, hid), f32),
        VMEM((chunk, hid), f32),
        VMEM((chunk, hid), bf16),
        VMEM((chunk, hid), bf16),
        VMEM((chunk, wide), bf16),
        DMA((16,)),
    ]
    if few:
        chips = parts // 2

        def classify(place_ref, *refs):
            sides_in, rest = refs[:chips], refs[chips:]
            two_ref, first_ref, *outs = rest[:13]
            held, *rest = rest[13:]
            classify_kernel(
                False,
                place_ref,
                None,
                None,
                None,
                two_ref,
                (held,) + sides_in[1:],
                first_ref,
                *outs,
                sides_in[0],
                first_ref,
                *rest,
            )

        rows = noise_first.shape[0] + noise_second.shape[0] + 32
        *own_sums, other = call(
            classify,
            44,
            [(value.shape, f32, None) for value in noises] + [((rows, hid), bf16, None)],
            [(place, SMEM)]
            + [(side, HBM)]
            + [(value, None) for value in sides[1:]]
            + [(every2, None), (held_first, None)]
            + [(value, HBM) for value in fixed[1:]],
            [VMEM(side_shape, bf16)] + scratch[1:],
        )
        got = lax.ppermute(other, "core", [(0, 1), (1, 0)])
        first, second, third = call(
            finish_kernel,
            16,
            [(value.shape, f32, VMEM) for value in noises],
            [(got, None)] + [(value, None) for value in own_sums],
            [],
        )
    else:

        ins = (every_label, every0, every1, every2)

        def classify(place_ref, label_ref, zero_ref, one_ref, two_ref, *rest):
            classify_kernel(
                True,
                place_ref,
                label_ref,
                zero_ref,
                one_ref,
                two_ref,
                None,
                *rest[:11],
                None,
                None,
                *rest[11:],
            )

        def whole(value):
            return pl.BlockSpec(value.shape, lambda i: (0, 0))

        def piece(value):
            return pl.BlockSpec(
                (groups,) + value.shape[1:], lambda i: (i,) + (0,) * (value.ndim - 1)
            )

        first, second, third = pl.pallas_call(
            classify,
            grid=(members // groups,),
            out_shape=[jax.ShapeDtypeStruct(value.shape, f32) for value in noises],
            in_specs=[pl.BlockSpec(memory_space=SMEM)]
            + [piece(value) for value in ins]
            + [pl.BlockSpec(memory_space=HBM) for value in fixed],
            out_specs=[whole(value) for value in noises],
            scratch_shapes=scratch,
            compiler_params=params(56),
        )(place, *ins, *fixed)
    return (hop_feats, first, second, third.T)


def solution(mesh):
    dom, grp = mesh.shape["dom"], mesh.shape["grp"]
    names = ("dom", "grp")
    if dom * grp <= FEW and dom <= 8 and dom % 2 == 0:
        names = ("chip", "core", "grp")
        mesh = jax.sharding.Mesh(mesh.devices.reshape(dom // 2, 2, grp), names)
    doms, grps = names[:-1], "grp"
    in_specs = (
        P(doms, grps, None, None),
        P(None, doms, grps, None, None),
        P(doms, grps, None, None),
        P(doms, grps, None),
        P(doms, grps, None, None),
        P(doms, grps, None, None),
        P(doms, grps),
        P(doms, grps, None),
        P(),
        P(),
        P(),
        P(doms, None),
        P(doms, None),
        P(doms, None),
    )
    out_specs = (P(None, doms, grps, None, None), P(doms, None), P(doms, None), P(doms, None))
    return jax.shard_map(
        functools.partial(local, names),
        mesh=mesh,
        in_specs=in_specs,
        out_specs=out_specs,
        check_vma=False,
    )
```

```python
import functools
import math

import jax
import jax.numpy as jnp
from jax import lax
from jax.experimental import pallas as pl
from jax.experimental.pallas import tpu as pltpu
from jax.sharding import PartitionSpec as P

BLOCK = 128
LOW = 256
GROUP = 8
clip_bound = 4.0
noise_mult = 1.0

f32 = jnp.float32
bf16 = jnp.bfloat16
f8 = jnp.float8_e4m3fn
VMEM = pltpu.VMEM
SMEM = pltpu.SMEM
HBM = pltpu.HBM
DMA = pltpu.SemaphoreType.DMA


FEW = 32


def params(mib):
    return pltpu.CompilerParams(vmem_limit_bytes=mib * 1024 * 1024)


def fetch(pairs, sems):
    copies = [pltpu.make_async_copy(*pair, sems.at[at]) for at, pair in enumerate(pairs)]
    for copy in copies:
        copy.start()
    return copies


def normalize(values):
    return (values * lax.rsqrt(jnp.sum(values * values, -1, keepdims=True) + 1e-06)).astype(bf16)


def blocks_of(length, step):
    return [slice(at, min(at + step, length)) for at in range(0, length, step)]


def dot(left, right):
    return jnp.dot(left, right, preferred_element_type=f32)


def dot_nt(left, right):
    return lax.dot_general(left, right, (((1,), (1,)), ((), ())), preferred_element_type=f32)


def dot_tn(left, right):
    return lax.dot_general(left, right, (((0,), (0,)), ((), ())), preferred_element_type=f32)


def choose(rows_ref, turn_ref, pick_ref):
    parts, each = rows_ref.shape
    turn_ref[:parts, :each] = rows_ref[...]
    columns = turn_ref[...].T
    spots = lax.broadcasted_iota(jnp.int32, (each, pick_ref.shape[1]), 1)
    for part in range(parts):
        wanted = columns[:each, part : part + 1]
        pick_ref[part * each : (part + 1) * each, :] = jnp.where(wanted == spots, 1.0, 0.0).astype(
            bf16
        )


def post(rows, staged_ref, out_hbm, sem):
    staged_ref[...] = rows.reshape(staged_ref.shape)
    copy = pltpu.make_async_copy(staged_ref, out_hbm, sem)
    copy.start()
    return copy


def first_kernel(
    feats_hbm,
    rows_hbm,
    src_hbm,
    dst_hbm,
    start_ref,
    out_hbm,
    own_ref,
    src_ref,
    dst_ref,
    feats_ref,
    rows_ref,
    turn_ref,
    pick_ref,
    staged_ref,
    sems,
):
    copies = fetch(
        (
            (rows_hbm.at[0, 0], rows_ref),
            (feats_hbm.at[0, 0], feats_ref),
            (src_hbm.at[0, 0], src_ref),
            (dst_hbm.at[0, 0], dst_ref),
        ),
        sems,
    )
    copies[0].wait()
    choose(rows_ref, turn_ref, pick_ref)
    copies[1].wait()
    picked = dot(pick_ref[...], feats_ref[...])
    each = staged_ref.shape[1]
    train = own_ref.shape[0]
    each -= train
    own_ref[...] = normalize(feats_ref[:train, :].astype(f32))
    for part in range(staged_ref.shape[0]):
        staged_ref[part, :each] = normalize(picked[part * each : (part + 1) * each])
        staged_ref[part, each:] = own_ref[...]
    out_copy = pltpu.make_async_copy(staged_ref, out_hbm, sems.at[4])
    out_copy.start()
    for cut in blocks_of(start_ref.shape[0], 32):
        start_ref[cut, :] = normalize(feats_ref[cut, :].astype(f32))
    copies[2].wait()
    copies[3].wait()
    out_copy.wait()


def build_kernel(
    blocks_hbm,
    count_ref,
    src_ref,
    dst_ref,
    noise_hbm,
    start_ref,
    own_hbm,
    ghost_ref,
    own_train_ref,
    noise_train_ref,
    part_ref,
    flag_ref,
    own_rest_ref,
    ghost_rest_ref,
    noise_ref,
    low_ref,
    high_ref,
    spot_ref,
    sums_ref,
    rest_ref,
    own_ref,
    blocks_ref,
    sems,
):
    train = own_train_ref.shape[0]
    copies = fetch(
        (
            (blocks_hbm, blocks_ref),
            (noise_hbm.at[0, 0, 0], noise_ref),
            (noise_hbm.at[1, 0, 0, :train], noise_train_ref),
        ),
        sems,
    )
    nodes, cols = sums_ref.shape
    pieces = -(-cols // LOW)
    tiles, slots = src_ref.shape
    own_ref[...] = jnp.zeros_like(own_ref)
    ghost_ref[...] = jnp.zeros_like(ghost_ref)
    count = count_ref[0, 0]

    def sixteen(values):
        wide = jnp.broadcast_to(values.astype(f32)[:, None, :], (tiles, 16, slots))
        return wide.reshape(tiles * 16, slots).astype(bf16)

    src = src_ref[...]
    dst = dst_ref[...]
    tile_ids = lax.broadcasted_iota(jnp.int32, (tiles, slots), 0)
    high_ref[...] = sixteen(src // LOW)
    spot_ref[...] = sixteen(jnp.where((dst < BLOCK) & (tile_ids < count), dst, -1))
    low = (src % LOW - LOW // 2).astype(f32).T
    for tile in range(tiles):
        low_ref[tile] = jnp.broadcast_to(low[:, tile : tile + 1], (slots, 128)).astype(bf16)
    ids = lax.broadcasted_iota(jnp.int32, (BLOCK, slots), 0).astype(f32).astype(bf16)
    lanes = lax.broadcasted_iota(jnp.int32, (slots, 128), 1).astype(f32)
    lanes = [(lanes + first).astype(bf16) for first in range(-LOW // 2, LOW // 2, 128)]
    one = jnp.ones((), bf16)
    zero = jnp.zeros((), bf16)

    def counts(tile):
        rows = pl.ds(pl.multiple_of(tile * 16, 16), 16)
        high, spot = high_ref[rows, :], spot_ref[rows, :]
        tall = jnp.concatenate([spot] * (BLOCK // 16), 0)
        spot_one = jnp.where(ids == tall, one, zero)
        spots = []
        for piece in range(pieces):
            here = jnp.where(high == piece, one, zero)
            hot = spot_one * jnp.concatenate([here] * (BLOCK // 16), 0)
            spots.append(hot.astype(f8))
        low = low_ref[tile]
        low_hot = [jnp.where(low == ids, one, zero).astype(f8) for ids in lanes]
        return dot(jnp.concatenate(spots, 0), jnp.concatenate(low_hot, 1))

    def turn(add, step, carry):
        first = step * GROUP
        outs = [counts(first + inner) for inner in range(GROUP)]
        for inner, out in enumerate(outs):
            base = pl.multiple_of(blocks_ref[0, 0, first + inner] * BLOCK, BLOCK)
            for piece in range(pieces):
                add(pl.ds(base, BLOCK), piece * LOW, out[piece * BLOCK : (piece + 1) * BLOCK])
        return carry

    def add_short(rows, at, values):
        ref, at = (own_ref, at) if at < nodes else (ghost_ref, at - nodes)
        size = min(LOW, ref.shape[1] - at)
        ref[rows, at : at + size] += values[:, :size].astype(bf16)

    def add_long(rows, at, values):
        size = min(LOW, cols - at)
        sums_ref[rows, at : at + size] += values[:, :size]

    steps = (count + GROUP - 1) // GROUP
    copies[0].wait()
    lax.fori_loop(0, steps, functools.partial(turn, add_short), 0)
    top = ghost_ref[:BLOCK, :256]
    for first in range(0, nodes, BLOCK):
        for ref in (own_ref, ghost_ref):
            for at in range(0, ref.shape[1], 256):
                top = jnp.maximum(top, ref[first : first + BLOCK, at : at + 256])
    big = jnp.max(top.astype(f32)) >= 256.0
    flag_ref[0] = big.astype(jnp.int32)

    @pl.when(big)
    def _():
        sums_ref[...] = jnp.zeros_like(sums_ref)
        lax.fori_loop(0, steps, functools.partial(turn, add_long), 0)
        own_ref[...] = sums_ref[:, :nodes].astype(bf16)
        ghost_ref[...] = sums_ref[:, nodes:].astype(bf16)

    own_copy = pltpu.make_async_copy(own_ref, own_hbm, sems.at[3])
    own_copy.start()
    own_train_ref[...] = own_ref[:train, :]
    for copy in copies[1:]:
        copy.wait()
    part_ref[...] = dot(own_ref[...], start_ref[...]) + noise_ref[...].astype(f32)

    @pl.when(big)
    def _():
        own_rest = (sums_ref[:, :nodes] - own_ref[...].astype(f32)).astype(bf16)
        part_ref[...] += dot(own_rest, start_ref[...])
        rest_ref[:, :nodes] = own_rest
        pltpu.sync_copy(rest_ref.at[:, :nodes], own_rest_ref)
        rest_ref[:, : cols - nodes] = (sums_ref[:, nodes:] - ghost_ref[...].astype(f32)).astype(bf16)
        pltpu.sync_copy(rest_ref.at[:, : cols - nodes], ghost_rest_ref)

    own_copy.wait()


def aggregate(flag_ref, first_ref, parts, sums_ref, rest_ref):
    rows = sums_ref.shape[0]
    for cut in blocks_of(rows, 256):
        total = sum(dot(count_ref[cut, :], table) for count_ref, _, table in parts)
        for inner in blocks_of(total.shape[0], 32):
            at = slice(cut.start + inner.start, cut.start + inner.stop)
            sums_ref[at, :] = first_ref[at, :].astype(f32) + total[inner]

    @pl.when(flag_ref[0] > 0)
    def _():
        for count_ref, rest_hbm, table in parts:
            held = rest_ref.at[:, : count_ref.shape[1]]
            pltpu.sync_copy(rest_hbm.at[:rows], held)
            sums_ref[...] += dot(held[...], table)


def near_rows(place_ref, table_ref, each, near_ref, first):
    chips, _, width = near_ref.shape
    size = table_ref.shape[1] - each
    for chip in range(chips):
        member = 2 * chip + place_ref[0] % 2
        near_ref[chip, first : first + size, :] = table_ref[pl.ds(member, 1), each:, :].reshape(
            size, width
        )


def hop_kernel(
    flag_ref,
    place_ref,
    part_ref,
    ghost_ref,
    rest_hbm,
    table_ref,
    rows_ref,
    old_ref,
    labels_ref,
    start_ref,
    out_hbm,
    side_ref,
    near_ref,
    sums_ref,
    rest_ref,
    turn_ref,
    pick_ref,
    staged_ref,
    sem,
):
    width = start_ref.shape[1]
    parts, each = rows_ref.shape
    table = table_ref[:, :each, :].reshape(-1, width)
    choose(rows_ref, turn_ref, pick_ref)
    aggregate(flag_ref, part_ref, ((ghost_ref, rest_hbm, table),), sums_ref, rest_ref)
    for cut in blocks_of(start_ref.shape[0], 32):
        start_ref[cut, :] = normalize(sums_ref[cut, :])
    sent = dot(pick_ref[...], start_ref[...]).astype(bf16)
    train = labels_ref.shape[1]
    for part in range(parts):
        staged_ref[part, :each] = sent[part * each : (part + 1) * each]
        staged_ref[part, each:] = start_ref[:train, :]
    out_copy = pltpu.make_async_copy(staged_ref, out_hbm, sem)
    out_copy.start()
    near_rows(place_ref, table_ref, each, near_ref, 0)
    side_ref[:train, :] = old_ref[...]
    side_ref[train : 2 * train, :] = start_ref[:train, :]
    turn_ref[:1, :train] = labels_ref[...]
    side_ref[2 * train :, :128] = turn_ref[:16, :].astype(f32).astype(bf16)
    out_copy.wait()


def train_kernel(
    flag_ref,
    place_ref,
    own_ref,
    ghost_ref,
    own_rest_hbm,
    ghost_rest_hbm,
    noise_ref,
    start_ref,
    table_ref,
    *refs,
):
    near0_ref, *piece_refs = refs[: -10]
    out_hbm, side_hbm, near_hbm, sums_ref, rest_ref, turn_ref, staged_ref = refs[-10:-3]
    side_ref, near_ref, sems = refs[-3:]
    train, width = sums_ref.shape
    each = table_ref.shape[1] - train
    table = table_ref[:, :each, :].reshape(-1, width)
    parts = (
        (own_ref, own_rest_hbm, start_ref[...]),
        (ghost_ref, ghost_rest_hbm, table),
    )
    aggregate(flag_ref, noise_ref, parts, sums_ref, rest_ref)
    last = jnp.broadcast_to(normalize(sums_ref[...])[None], staged_ref.shape)
    out_copy = post(last, staged_ref, out_hbm, sems.at[0])
    length = piece_refs[0].shape[0] - 16
    groups = len(piece_refs)
    if groups > 1:
        near_ref[:, :train, :] = near0_ref[...]
        near_rows(place_ref, table_ref, each, near_ref, train)
        near_copy = pltpu.make_async_copy(near_ref, near_hbm, sems.at[2])
        near_copy.start()
        for shift, ref in enumerate(piece_refs):
            if shift:
                side_ref[(shift - 1) * length : shift * length, :] = ref[:length, :]
            group = lax.rem(place_ref[1] + shift, groups)
            turn_ref[pl.ds(group, 1), :] = ref[length:, :128].astype(f32)[:1]
        side_ref[(groups - 1) * length :, :128] = turn_ref[:16, :].astype(bf16)
        side_copy = pltpu.make_async_copy(side_ref, side_hbm, sems.at[1])
        side_copy.start()
        side_copy.wait()
        near_copy.wait()
    out_copy.wait()


def last_kernel(
    flag_ref,
    token_ref,
    own_hbm,
    own_rest_hbm,
    ghost_rest_hbm,
    noise_hbm,
    weight_hbm,
    ghost_ref,
    table_ref,
    start_ref,
    out_hbm,
    weight_ref,
    own_ref,
    noise_ref,
    sums_ref,
    rest_ref,
    out_ref,
    sems,
):
    copies = fetch(
        (
            (own_hbm, own_ref),
            (noise_hbm.at[1, 0, 0], noise_ref),
            (weight_hbm, weight_ref),
        ),
        sems,
    )
    width = out_ref.shape[-1]
    ghosts = ghost_ref.shape[1]
    table = table_ref[:, : ghosts // table_ref.shape[0], :].reshape(ghosts, width)
    out_ref[0, 0, 0] = start_ref[...]
    copies[0].wait()
    copies[1].wait()
    parts = (
        (own_ref, own_rest_hbm, start_ref[...]),
        (ghost_ref, ghost_rest_hbm, table),
    )
    aggregate(flag_ref, noise_ref, parts, sums_ref, rest_ref)
    for cut in blocks_of(sums_ref.shape[0], 32):
        out_ref[1, 0, 0, cut, :] = normalize(sums_ref[cut, :])
    out_copy = pltpu.make_async_copy(out_ref, out_hbm, sems.at[3])
    out_copy.start()
    copies[2].wait()
    out_copy.wait()


def shares(ref, first, share):
    return ref[:, pl.ds(pl.multiple_of(first, 128), share)].astype(f32)


def lanes_sum(values):
    total = None
    for piece in range(values.shape[1] // 128):
        part = values[:, piece * 128 : (piece + 1) * 128].astype(f32)
        total = part * part if total is None else total + part * part
    return total


def classify_kernel(
    many,
    place_ref,
    label_ref,
    zero_ref,
    one_ref,
    two_ref,
    side_refs,
    w_first_hbm,
    w_second_hbm,
    w_third_hbm,
    n_first_hbm,
    n_second_hbm,
    n_third_hbm,
    g_first_ref,
    g_second_ref,
    g_third_ref,
    send_ref,
    side_hbm,
    near_hbm,
    near_ref,
    w_first_ref,
    w_second_ref,
    w_third_ref,
    n_first_ref,
    n_second_ref,
    n_third_ref,
    in_ref,
    w_third_pad_ref,
    turn_ref,
    column_ref,
    h_one_ref,
    h_two_ref,
    slope_one_ref,
    slope_two_ref,
    d_one_ref,
    d_two_ref,
    d_three_ref,
    sems,
):
    classes = w_third_ref.shape[0]
    hid = w_second_ref.shape[0]
    width = two_ref.shape[2]
    wide = w_third_pad_ref.shape[0]
    train = two_ref.shape[1]
    scale = noise_mult * clip_bound
    place = place_ref[0]
    pairs = (
        (w_first_hbm, w_first_ref),
        (w_second_hbm, w_second_ref),
        (w_third_hbm, w_third_ref),
        (n_first_hbm, n_first_ref),
        (n_second_hbm, n_second_ref),
        (n_third_hbm, n_third_ref),
    )

    def set_noise():
        g_first_ref[...] = scale * n_first_ref[...]
        g_second_ref[...] = scale * n_second_ref[...]
        g_third_ref[...] = scale * n_third_ref[...]

    def pad():
        w_third_pad_ref[...] = jnp.zeros_like(w_third_pad_ref)
        w_third_pad_ref[:classes, :] = w_third_ref[...]

    def column(row, turned, lane):
        column_ref[row : row + train, :] = jnp.broadcast_to(
            turned[:train, lane : lane + 1], (train, 128)
        ).astype(jnp.int32)

    if many:

        @pl.when(pl.program_id(0) == 0)
        def _():
            for copy in fetch(pairs, sems):
                copy.wait()
            set_noise()
            pad()

        groups = label_ref.shape[0]
        turn_ref[:groups, :train] = label_ref[...].astype(f32)
        turned = turn_ref[...].T
        for group in range(groups):
            column(group * train, turned, group)
        for hop, ref in enumerate((zero_ref, one_ref)):
            in_ref[:, hop * width : (hop + 1) * width] = ref[...].reshape(-1, width)
    else:
        chips = len(side_refs)
        copies = fetch(((side_hbm, side_refs[0]), (near_hbm, near_ref)) + pairs[1:], sems)
        groups = two_ref.shape[0] // chips
        rows = groups * train
        for shift, ref in [*enumerate(side_refs)][::-1]:
            if shift == 0:
                copies[0].wait()
            part = lax.rem(place // 2 - shift + chips, chips)
            at = pl.multiple_of(part * rows, rows)
            for after in range(1, groups):
                row = at + lax.rem(place_ref[1] + after, groups) * train
                for hop in range(2):
                    first = (2 * (after - 1) + hop) * train
                    in_ref[
                        pl.ds(pl.multiple_of(row, train), train), hop * width : (hop + 1) * width
                    ] = ref[first : first + train, :]
            turn_ref[pl.ds(pl.multiple_of(part * 16, 16), 16), :] = ref[2 * (rows - train) :, :128].astype(f32)
        copies[1].wait()
        for chip in range(chips):
            row = pl.multiple_of(chip * rows + place_ref[1] * train, train)
            for hop in range(2):
                in_ref[pl.ds(row, train), hop * width : (hop + 1) * width] = near_ref[
                    chip, hop * train : (hop + 1) * train, :
                ]
        turned = turn_ref[...].T
        for part in range(chips):
            for group in range(groups):
                column((part * groups + group) * train, turned, part * 16 + group)
    in_ref[:, 2 * width :] = two_ref[...].reshape(-1, width)

    def activate(values, at, cols, h_ref, slope_ref):
        sigma = 0.5 + 0.5 * jnp.tanh(0.5 * values)
        out = values * sigma
        slope_ref[at, cols] = sigma + out * (1.0 - sigma)
        h_ref[at, cols] = out.astype(bf16)
        return lanes_sum(out)

    def back(values, at, cols, slope_ref, d_ref):
        out = values * slope_ref[at, cols]
        d_ref[at, cols] = out.astype(bf16)
        return lanes_sum(out)

    def layer(product, finish, *refs):
        sums = []
        values = product(cuts[0])
        for at, cut in enumerate(cuts):
            ahead = product(cuts[at + 1]) if at + 1 < len(cuts) else None
            for rows in blocks_of(values.shape[0], 32):
                here = slice(cut.start + rows.start, cut.start + rows.stop)
                sums.append(
                    sum(
                        finish(values[rows, cols], here, cols, *refs)
                        for cols in blocks_of(values.shape[1], 256)
                    )
                )
            values = ahead
        return jnp.concatenate(sums, 0)

    step = min(512, in_ref.shape[0])
    cuts = [slice(at, at + step) for at in range(0, in_ref.shape[0], step)]
    sq_in = jnp.concatenate([lanes_sum(in_ref[at, :]) for at in blocks_of(in_ref.shape[0], 32)], 0)
    sq_one = layer(
        lambda cut: dot(in_ref[cut, :], w_first_ref[...]), activate, h_one_ref, slope_one_ref
    )
    if not many:
        copies[2].wait()
    sq_two = layer(
        lambda cut: dot(h_one_ref[cut, :], w_second_ref[...]), activate, h_two_ref, slope_two_ref
    )
    if not many:
        copies[3].wait()
        pad()
    logits = dot_nt(h_two_ref[...], w_third_pad_ref[...])
    sums = []
    for at in blocks_of(logits.shape[0], 32):
        ids = lax.broadcasted_iota(jnp.int32, (at.stop - at.start, wide), 1)
        expo = jnp.where(ids < classes, jnp.exp(logits[at]), 0.0)
        probs = expo / jnp.sum(expo, -1, keepdims=True)
        label = column_ref[at, :1]
        d_three = (probs - jnp.where(ids == label, 1.0, 0.0)).astype(bf16)
        d_three_ref[at, :] = d_three
        sums.append(lanes_sum(d_three))
    sq_dthree = jnp.concatenate(sums, 0)
    sq_dtwo = layer(
        lambda cut: dot(d_three_ref[cut, :], w_third_pad_ref[...]), back, slope_two_ref, d_two_ref
    )
    sq_done = layer(
        lambda cut: dot_nt(d_two_ref[cut, :], w_second_ref[...]), back, slope_one_ref, d_one_ref
    )

    def total(values):
        return jnp.sum(values, -1, keepdims=True)

    norm = jnp.sqrt(
        total(sq_in) * total(sq_done)
        + total(sq_one) * total(sq_dtwo)
        + total(sq_two) * total(sq_dthree)
    )
    factor = clip_bound / jnp.maximum(norm, clip_bound)

    if not many:
        for copy in copies[4:]:
            copy.wait()
        set_noise()
    share_one, share = g_first_ref.shape[0], g_second_ref.shape[0]
    places = [place] if many else [place, place + 1 - 2 * (place % 2)]

    def left(ref, share):
        if share % 128 == 0:
            picked = [shares(ref, at * share, share) for at in places]
            return (jnp.concatenate(picked, 1) * factor).astype(bf16)
        length, count = ref.shape[1], share * len(places)
        most = 128 - math.gcd(count, 128)
        size = min(length, -(-(count + most) // 128) * 128)
        first = [at * share for at in places]
        least = functools.reduce(jnp.minimum, first)
        start = jnp.minimum(least // 128 * 128, length - size)
        rows = lax.broadcasted_iota(jnp.int32, (size, count), 0)
        cols = lax.broadcasted_iota(jnp.int32, (size, count), 1)
        wanted = cols + (first[0] - start)
        for at, other in enumerate(first[1:], 1):
            wanted = jnp.where(cols >= at * share, cols - at * share + (other - start), wanted)
        window = ref[:, pl.ds(pl.multiple_of(start, 128), size)]
        picked = dot(window, jnp.where(rows == wanted, 1.0, 0.0).astype(bf16))
        return (picked * factor).astype(bf16)

    sum_one = dot_tn(left(in_ref, share_one), d_one_ref[...])
    sum_two = dot_tn(left(h_one_ref, share), d_two_ref[...])
    sum_three = dot_tn(d_three_ref[...], left(h_two_ref, share))
    g_first_ref[...] += sum_one[:share_one]
    g_second_ref[...] += sum_two[:share]
    g_third_ref[...] += sum_three[:classes, :share]
    if not many:
        send_ref[:share_one, :] = sum_one[share_one:].astype(bf16)
        send_ref[share_one : share_one + share, :] = sum_two[share:].astype(bf16)
        first = share_one + share
        for at in range(0, classes, 32):
            cols = slice(at // 32 * share, (at // 32 + 1) * share)
            send_ref[first : first + 32, cols] = sum_three[at : at + 32, share:].astype(bf16)


def finish_kernel(got_ref, one_ref, two_ref, three_ref, g_first_ref, g_second_ref, g_third_ref):
    share_one, share = one_ref.shape[0], two_ref.shape[0]
    g_first_ref[...] = one_ref[...] + got_ref[:share_one, :].astype(f32)
    g_second_ref[...] = two_ref[...] + got_ref[share_one : share_one + share, :].astype(f32)
    first = share_one + share
    classes = three_ref.shape[0]
    for at in range(0, classes, 32):
        size = min(32, classes - at)
        cols = slice(at // 32 * share, (at // 32 + 1) * share)
        got = got_ref[first : first + 32, cols].astype(f32)
        g_third_ref[at : at + size, :] = three_ref[at : at + size, :] + got[:size]


def call(kernel, mib, outs, ins, scratch):
    def shape_of(shape, dtype, space):
        if space is None or space is HBM:
            return (space or VMEM)(shape, dtype)
        return jax.ShapeDtypeStruct(shape, dtype)

    def block(space):
        return pl.BlockSpec(memory_space=VMEM if space is None else space)

    def held(value, space):
        if space is None or space is HBM:
            return pltpu.with_memory_space_constraint(value, space or VMEM)
        return value

    return pl.pallas_call(
        kernel,
        out_shape=[shape_of(*out) for out in outs],
        in_specs=[block(space) for _, space in ins],
        out_specs=[block(space) for _, _, space in outs],
        scratch_shapes=scratch,
        compiler_params=params(mib),
    )(*[held(value, space) for value, space in ins])


def local(
    axes,
    feats,
    hop_noise,
    send_rows,
    tile_block,
    tile_src,
    tile_dst,
    tile_count,
    labels,
    w_first,
    w_second,
    w_third,
    noise_first,
    noise_second,
    noise_third,
):
    nodes, width = feats.shape[2:]
    parts, each = send_rows.shape[2:]
    ghosts = parts * each
    tiles = tile_src.shape[2]
    slots = tile_src.shape[3]
    train = labels.shape[2]
    classes = w_third.shape[1]
    hid = w_second.shape[0]
    d_in = w_first.shape[0]
    cols = nodes + ghosts
    rows = send_rows.reshape(parts, each)
    turn = VMEM((128, 128), jnp.int32)
    pick = VMEM((ghosts, nodes), bf16)
    dom = axes[:-1]
    members = lax.axis_size(axes)
    few = len(axes) == 3
    copies = members // 2 if few else 1

    def every(value, *names):
        for name in names:
            value = lax.all_gather(value, name, axis=0, tiled=True)
        return value

    staged = VMEM((parts, each + train, width), bf16)
    start0, out0, own0, src, dst = call(
        first_kernel,
        16,
        [
            ((nodes, width), bf16, None),
            ((parts, each + train, width), bf16, HBM),
            ((train, width), bf16, None),
            ((tiles, slots), jnp.int32, None),
            ((tiles, slots), jnp.int32, None),
        ],
        [(feats, HBM), (send_rows, HBM), (tile_src, HBM), (tile_dst, HBM)],
        [
            VMEM((nodes, width), bf16),
            VMEM((parts, each), jnp.int32),
            turn,
            pick,
            staged,
            DMA((5,)),
        ],
    )
    table0 = lax.all_to_all(out0, dom, split_axis=0, concat_axis=0, tiled=True)
    own, ghost, own_train, noise_train, part1, flag, own_rest, ghost_rest = call(
        build_kernel,
        28,
        [
            ((nodes, nodes), bf16, HBM),
            ((nodes, ghosts), bf16, None),
            ((train, nodes), bf16, None),
            ((train, width), bf16, None),
            ((nodes, width), f32, None),
            ((1,), jnp.int32, SMEM),
            ((nodes, nodes), bf16, HBM),
            ((nodes, ghosts), bf16, HBM),
        ],
        [
            (tile_block, HBM),
            (tile_count, SMEM),
            (src, None),
            (dst, None),
            (hop_noise, HBM),
            (start0, None),
        ],
        [
            VMEM((nodes, width), bf16),
            VMEM((tiles, slots, 128), bf16),
            VMEM((tiles * 16, slots), bf16),
            VMEM((tiles * 16, slots), bf16),
            VMEM((nodes, cols), f32),
            VMEM((nodes, max(nodes, ghosts)), bf16),
            VMEM((nodes, nodes), bf16),
            SMEM(tile_block.shape, jnp.int32),
            DMA((4,)),
        ],
    )
    place = jnp.stack([lax.axis_index(dom), lax.axis_index("grp")]).astype(jnp.int32)
    start1, out1, side, near0 = call(
        hop_kernel,
        16,
        [
            ((nodes, width), bf16, None),
            ((parts, each + train, width), bf16, HBM),
            ((2 * train + 16, width), bf16, None),
            ((parts // 2, train, width), bf16, None),
        ],
        [
            (flag, SMEM),
            (place, SMEM),
            (part1, None),
            (ghost, None),
            (ghost_rest, HBM),
            (table0, None),
            (rows, VMEM),
            (own0, None),
            (labels.reshape(1, train), VMEM),
        ],
        [VMEM((nodes, width), f32), VMEM((nodes, ghosts), bf16), turn, pick, staged, DMA(())],
    )
    table1 = lax.all_to_all(out1, dom, split_axis=0, concat_axis=0, tiled=True)
    grp = lax.axis_size("grp")

    def shifted(value, name, size, step):
        return [
            lax.ppermute(value, name, [((at + step * shift) % size, at) for at in range(size)])
            for shift in range(1, size)
        ]

    sides = [side] + (shifted(side, "grp", grp, 1) if few else [])
    side_shape = ((len(sides) - 1) * 2 * train + 16, width)
    near_shape = (parts // 2, 2 * train, width)
    last, side, near = call(
        train_kernel,
        12,
        [
            ((copies, train, width), bf16, HBM),
            (side_shape, bf16, HBM),
            (near_shape, bf16, HBM),
        ],
        [
            (flag, SMEM),
            (place, SMEM),
            (own_train, None),
            (ghost, None),
            (own_rest, HBM),
            (ghost_rest, HBM),
            (noise_train, None),
            (start1, None),
            (table1, None),
            (near0, None),
        ]
        + [(value, None) for value in sides],
        [
            VMEM((train, width), f32),
            VMEM((train, max(nodes, ghosts)), bf16),
            VMEM((128, 128), f32),
            VMEM((copies, train, width), bf16),
            VMEM(side_shape, bf16),
            VMEM(near_shape, bf16),
            DMA((3,)),
        ],
    )
    if few:
        every2 = lax.all_to_all(last, ("chip", "grp"), split_axis=0, concat_axis=0, tiled=True)
        sides = [side] + shifted(side, "chip", parts // 2, -1)
    else:
        every0, every1, every2 = (
            every(value, axes) for value in (own0[None], start1[None, :train], last)
        )
        every_label = every(labels.reshape(1, train), axes)
    wide = (classes + 255) // 256 * 256
    hop_feats, held_first = call(
        last_kernel,
        28,
        [
            ((2, 1, 1, nodes, width), bf16, HBM),
            (w_first.shape, bf16, None),
        ],
        [
            (flag, SMEM),
            (side, HBM),
            (own, HBM),
            (own_rest, HBM),
            (ghost_rest, HBM),
            (hop_noise, HBM),
            (w_first, HBM),
            (ghost, None),
            (table1, None),
            (start1, None),
        ],
        [
            VMEM((nodes, nodes), bf16),
            VMEM((nodes, width), bf16),
            VMEM((nodes, width), f32),
            VMEM((nodes, max(nodes, ghosts)), bf16),
            VMEM((2, 1, 1, nodes, width), bf16),
            DMA((4,)),
        ],
    )
    chunk = train * (copies if few else min(members, 32))
    groups = chunk // train
    noises = (noise_first, noise_second, noise_third.T)
    fixed = (w_first, w_second, w_third.T) + noises
    scratch = [VMEM(value.shape, value.dtype) for value in fixed]
    scratch += [
        VMEM((chunk, d_in), bf16),
        VMEM((wide, hid), bf16),
        VMEM((128, 128), f32),
        VMEM((chunk, 128), jnp.int32),
        VMEM((chunk, hid), bf16),
        VMEM((chunk, hid), bf16),
        VMEM((chunk, hid), f32),
        VMEM((chunk, hid), f32),
        VMEM((chunk, hid), bf16),
        VMEM((chunk, hid), bf16),
        VMEM((chunk, wide), bf16),
        DMA((16,)),
    ]
    if few:
        chips = parts // 2

        def classify(place_ref, *refs):
            sides_in, rest = refs[:chips], refs[chips:]
            near_hbm, two_ref, first_ref, *outs = rest[:12]
            held, near_ref, *rest = rest[12:]
            classify_kernel(
                False,
                place_ref,
                None,
                None,
                None,
                two_ref,
                (held,) + sides_in[1:],
                first_ref,
                *outs,
                sides_in[0],
                near_hbm,
                near_ref,
                first_ref,
                *rest,
            )

        rows = noise_first.shape[0] + noise_second.shape[0] + 32
        *own_sums, other = call(
            classify,
            44,
            [(value.shape, f32, None) for value in noises] + [((rows, hid), bf16, None)],
            [(place, SMEM)]
            + [(side, HBM)]
            + [(value, None) for value in sides[1:]]
            + [(near, HBM), (every2, None), (held_first, None)]
            + [(value, HBM) for value in fixed[1:]],
            [VMEM(side_shape, bf16), VMEM(near_shape, bf16)] + scratch[1:],
        )
        got = lax.ppermute(other, "core", [(0, 1), (1, 0)])
        first, second, third = call(
            finish_kernel,
            16,
            [(value.shape, f32, VMEM) for value in noises],
            [(got, None)] + [(value, None) for value in own_sums],
            [],
        )
    else:

        ins = (every_label, every0, every1, every2)

        def classify(place_ref, label_ref, zero_ref, one_ref, two_ref, *rest):
            classify_kernel(
                True,
                place_ref,
                label_ref,
                zero_ref,
                one_ref,
                two_ref,
                None,
                *rest[:9],
                None,
                None,
                None,
                None,
                *rest[9:],
            )

        def whole(value):
            return pl.BlockSpec(value.shape, lambda i: (0, 0))

        def piece(value):
            return pl.BlockSpec(
                (groups,) + value.shape[1:], lambda i: (i,) + (0,) * (value.ndim - 1)
            )

        first, second, third = pl.pallas_call(
            classify,
            grid=(members // groups,),
            out_shape=[jax.ShapeDtypeStruct(value.shape, f32) for value in noises],
            in_specs=[pl.BlockSpec(memory_space=SMEM)]
            + [piece(value) for value in ins]
            + [pl.BlockSpec(memory_space=HBM) for value in fixed],
            out_specs=[whole(value) for value in noises],
            scratch_shapes=scratch,
            compiler_params=params(56),
        )(place, *ins, *fixed)
    return (hop_feats, first, second, third.T)


def solution(mesh):
    dom, grp = mesh.shape["dom"], mesh.shape["grp"]
    names = ("dom", "grp")
    if dom * grp <= FEW and dom <= 8 and dom % 2 == 0:
        names = ("chip", "core", "grp")
        mesh = jax.sharding.Mesh(mesh.devices.reshape(dom // 2, 2, grp), names)
    doms, grps = names[:-1], "grp"
    in_specs = (
        P(doms, grps, None, None),
        P(None, doms, grps, None, None),
        P(doms, grps, None, None),
        P(doms, grps, None),
        P(doms, grps, None, None),
        P(doms, grps, None, None),
        P(doms, grps),
        P(doms, grps, None),
        P(),
        P(),
        P(),
        P(doms, None),
        P(doms, None),
        P(doms, None),
    )
    out_specs = (P(None, doms, grps, None, None), P(doms, None), P(doms, None), P(doms, None))
    return jax.shard_map(
        functools.partial(local, names),
        mesh=mesh,
        in_specs=in_specs,
        out_specs=out_specs,
        check_vma=False,
    )
```

```python
import functools
import math

import jax
import jax.numpy as jnp
from jax import lax
from jax.experimental import pallas as pl
from jax.experimental.pallas import tpu as pltpu
from jax.sharding import PartitionSpec as P

BLOCK = 128
LOW = 256
GROUP = 8
clip_bound = 4.0
noise_mult = 1.0

f32 = jnp.float32
bf16 = jnp.bfloat16
f8 = jnp.float8_e4m3fn
VMEM = pltpu.VMEM
SMEM = pltpu.SMEM
HBM = pltpu.HBM
DMA = pltpu.SemaphoreType.DMA


FEW = 32


def params(mib):
    return pltpu.CompilerParams(vmem_limit_bytes=mib * 1024 * 1024)


def fetch(pairs, sems):
    copies = [pltpu.make_async_copy(*pair, sems.at[at]) for at, pair in enumerate(pairs)]
    for copy in copies:
        copy.start()
    return copies


def normalize(values):
    return (values * lax.rsqrt(jnp.sum(values * values, -1, keepdims=True) + 1e-06)).astype(bf16)


def blocks_of(length, step):
    return [slice(at, min(at + step, length)) for at in range(0, length, step)]


def dot(left, right):
    return jnp.dot(left, right, preferred_element_type=f32)


def dot_nt(left, right):
    return lax.dot_general(left, right, (((1,), (1,)), ((), ())), preferred_element_type=f32)


def dot_tn(left, right):
    return lax.dot_general(left, right, (((0,), (0,)), ((), ())), preferred_element_type=f32)


def choose(rows_ref, turn_ref, pick_ref):
    parts, each = rows_ref.shape
    turn_ref[:parts, :each] = rows_ref[...]
    columns = turn_ref[...].T
    spots = lax.broadcasted_iota(jnp.int32, (each, pick_ref.shape[1]), 1)
    for part in range(parts):
        wanted = columns[:each, part : part + 1]
        pick_ref[part * each : (part + 1) * each, :] = jnp.where(wanted == spots, 1.0, 0.0).astype(
            bf16
        )


def post(rows, staged_ref, out_hbm, sem):
    staged_ref[...] = rows.reshape(staged_ref.shape)
    copy = pltpu.make_async_copy(staged_ref, out_hbm, sem)
    copy.start()
    return copy


def first_kernel(
    feats_hbm,
    rows_hbm,
    src_hbm,
    dst_hbm,
    start_ref,
    out_hbm,
    own_ref,
    src_ref,
    dst_ref,
    feats_ref,
    rows_ref,
    turn_ref,
    pick_ref,
    staged_ref,
    sems,
):
    copies = fetch(
        (
            (rows_hbm.at[0, 0], rows_ref),
            (feats_hbm.at[0, 0], feats_ref),
            (src_hbm.at[0, 0], src_ref),
            (dst_hbm.at[0, 0], dst_ref),
        ),
        sems,
    )
    copies[0].wait()
    choose(rows_ref, turn_ref, pick_ref)
    copies[1].wait()
    picked = dot(pick_ref[...], feats_ref[...])
    each = staged_ref.shape[1]
    train = own_ref.shape[0]
    each -= train
    own_ref[...] = normalize(feats_ref[:train, :].astype(f32))
    for part in range(staged_ref.shape[0]):
        staged_ref[part, :each] = normalize(picked[part * each : (part + 1) * each])
        staged_ref[part, each:] = own_ref[...]
    out_copy = pltpu.make_async_copy(staged_ref, out_hbm, sems.at[4])
    out_copy.start()
    for cut in blocks_of(start_ref.shape[0], 32):
        start_ref[cut, :] = normalize(feats_ref[cut, :].astype(f32))
    copies[2].wait()
    copies[3].wait()
    out_copy.wait()


def build_kernel(
    blocks_hbm,
    count_ref,
    src_ref,
    dst_ref,
    noise_hbm,
    start_ref,
    own_hbm,
    ghost_ref,
    own_train_ref,
    noise_train_ref,
    part_ref,
    flag_ref,
    own_rest_ref,
    ghost_rest_ref,
    noise_ref,
    low_ref,
    high_ref,
    spot_ref,
    sums_ref,
    rest_ref,
    own_ref,
    blocks_ref,
    sems,
):
    train = own_train_ref.shape[0]
    copies = fetch(
        (
            (blocks_hbm, blocks_ref),
            (noise_hbm.at[0, 0, 0], noise_ref),
            (noise_hbm.at[1, 0, 0, :train], noise_train_ref),
        ),
        sems,
    )
    nodes, cols = sums_ref.shape
    pieces = -(-cols // LOW)
    tiles, slots = src_ref.shape
    own_ref[...] = jnp.zeros_like(own_ref)
    ghost_ref[...] = jnp.zeros_like(ghost_ref)
    count = count_ref[0, 0]

    def sixteen(values):
        wide = jnp.broadcast_to(values.astype(f32)[:, None, :], (tiles, 16, slots))
        return wide.reshape(tiles * 16, slots).astype(bf16)

    src = src_ref[...]
    dst = dst_ref[...]
    tile_ids = lax.broadcasted_iota(jnp.int32, (tiles, slots), 0)
    high_ref[...] = sixteen(src // LOW)
    spot_ref[...] = sixteen(jnp.where((dst < BLOCK) & (tile_ids < count), dst, -1))
    low = (src % LOW - LOW // 2).astype(f32).T
    for tile in range(tiles):
        low_ref[tile] = jnp.broadcast_to(low[:, tile : tile + 1], (slots, 128)).astype(bf16)
    ids = lax.broadcasted_iota(jnp.int32, (BLOCK, slots), 0).astype(f32).astype(bf16)
    lanes = lax.broadcasted_iota(jnp.int32, (slots, 128), 1).astype(f32)
    lanes = [(lanes + first).astype(bf16) for first in range(-LOW // 2, LOW // 2, 128)]
    one = jnp.ones((), bf16)
    zero = jnp.zeros((), bf16)

    def counts(tile):
        rows = pl.ds(pl.multiple_of(tile * 16, 16), 16)
        high, spot = high_ref[rows, :], spot_ref[rows, :]
        tall = jnp.concatenate([spot] * (BLOCK // 16), 0)
        spot_one = jnp.where(ids == tall, one, zero)
        spots = []
        for piece in range(pieces):
            here = jnp.where(high == piece, one, zero)
            hot = spot_one * jnp.concatenate([here] * (BLOCK // 16), 0)
            spots.append(hot.astype(f8))
        low = low_ref[tile]
        low_hot = [jnp.where(low == ids, one, zero).astype(f8) for ids in lanes]
        return dot(jnp.concatenate(spots, 0), jnp.concatenate(low_hot, 1))

    def turn(add, step, carry):
        first = step * GROUP
        outs = [counts(first + inner) for inner in range(GROUP)]
        for inner, out in enumerate(outs):
            base = pl.multiple_of(blocks_ref[0, 0, first + inner] * BLOCK, BLOCK)
            for piece in range(pieces):
                add(pl.ds(base, BLOCK), piece * LOW, out[piece * BLOCK : (piece + 1) * BLOCK])
        return carry

    def add_short(rows, at, values):
        ref, at = (own_ref, at) if at < nodes else (ghost_ref, at - nodes)
        size = min(LOW, ref.shape[1] - at)
        ref[rows, at : at + size] += values[:, :size].astype(bf16)

    def add_long(rows, at, values):
        size = min(LOW, cols - at)
        sums_ref[rows, at : at + size] += values[:, :size]

    steps = (count + GROUP - 1) // GROUP
    copies[0].wait()
    lax.fori_loop(0, steps, functools.partial(turn, add_short), 0)
    top = ghost_ref[:BLOCK, :256]
    for first in range(0, nodes, BLOCK):
        for ref in (own_ref, ghost_ref):
            for at in range(0, ref.shape[1], 256):
                top = jnp.maximum(top, ref[first : first + BLOCK, at : at + 256])
    big = jnp.max(top.astype(f32)) >= 256.0
    flag_ref[0] = big.astype(jnp.int32)

    @pl.when(big)
    def _():
        sums_ref[...] = jnp.zeros_like(sums_ref)
        lax.fori_loop(0, steps, functools.partial(turn, add_long), 0)
        own_ref[...] = sums_ref[:, :nodes].astype(bf16)
        ghost_ref[...] = sums_ref[:, nodes:].astype(bf16)

    own_copy = pltpu.make_async_copy(own_ref, own_hbm, sems.at[3])
    own_copy.start()
    own_train_ref[...] = own_ref[:train, :]
    for copy in copies[1:]:
        copy.wait()
    for cut in blocks_of(nodes, 256):
        part_ref[cut, :] = dot(own_ref[cut, :], start_ref[...]) + noise_ref[cut, :].astype(f32)

    @pl.when(big)
    def _():
        own_rest = (sums_ref[:, :nodes] - own_ref[...].astype(f32)).astype(bf16)
        part_ref[...] += dot(own_rest, start_ref[...])
        rest_ref[:, :nodes] = own_rest
        pltpu.sync_copy(rest_ref.at[:, :nodes], own_rest_ref)
        rest_ref[:, : cols - nodes] = (sums_ref[:, nodes:] - ghost_ref[...].astype(f32)).astype(bf16)
        pltpu.sync_copy(rest_ref.at[:, : cols - nodes], ghost_rest_ref)

    own_copy.wait()


def aggregate(flag_ref, first_ref, parts, sums_ref, rest_ref):
    rows = sums_ref.shape[0]
    for cut in blocks_of(rows, 256):
        total = sum(dot(count_ref[cut, :], table) for count_ref, _, table in parts)
        for inner in blocks_of(total.shape[0], 32):
            at = slice(cut.start + inner.start, cut.start + inner.stop)
            sums_ref[at, :] = first_ref[at, :].astype(f32) + total[inner]

    @pl.when(flag_ref[0] > 0)
    def _():
        for count_ref, rest_hbm, table in parts:
            held = rest_ref.at[:, : count_ref.shape[1]]
            pltpu.sync_copy(rest_hbm.at[:rows], held)
            sums_ref[...] += dot(held[...], table)


def near_rows(place_ref, table_ref, each, near_ref, first):
    chips, _, width = near_ref.shape
    size = table_ref.shape[1] - each
    for chip in range(chips):
        member = 2 * chip + place_ref[0] % 2
        near_ref[chip, first : first + size, :] = table_ref[pl.ds(member, 1), each:, :].reshape(
            size, width
        )


def hop_kernel(
    flag_ref,
    place_ref,
    part_ref,
    ghost_ref,
    rest_hbm,
    table_ref,
    rows_ref,
    old_ref,
    labels_ref,
    start_ref,
    out_hbm,
    side_ref,
    near_ref,
    sums_ref,
    rest_ref,
    turn_ref,
    pick_ref,
    staged_ref,
    sems,
):
    width = start_ref.shape[1]
    parts, each = rows_ref.shape
    table = table_ref[:, :each, :].reshape(-1, width)
    choose(rows_ref, turn_ref, pick_ref)
    aggregate(flag_ref, part_ref, ((ghost_ref, rest_hbm, table),), sums_ref, rest_ref)
    for cut in blocks_of(start_ref.shape[0], 32):
        start_ref[cut, :] = normalize(sums_ref[cut, :])
    train = labels_ref.shape[1]
    copies = fetch(
        [(start_ref.at[:train], out_hbm.at[part, each:]) for part in range(parts)], sems
    )
    sent = dot(pick_ref[...], start_ref[...]).astype(bf16)
    staged_ref[...] = sent.reshape(staged_ref.shape)
    out_copy = pltpu.make_async_copy(staged_ref, out_hbm.at[:, :each], sems.at[parts])
    out_copy.start()
    near_rows(place_ref, table_ref, each, near_ref, 0)
    side_ref[:train, :] = old_ref[...]
    side_ref[train : 2 * train, :] = start_ref[:train, :]
    turn_ref[:1, :train] = labels_ref[...]
    side_ref[2 * train :, :128] = turn_ref[:16, :].astype(f32).astype(bf16)
    for copy in copies:
        copy.wait()
    out_copy.wait()


def train_kernel(
    flag_ref,
    place_ref,
    own_ref,
    ghost_ref,
    own_rest_hbm,
    ghost_rest_hbm,
    noise_ref,
    start_ref,
    table_ref,
    *refs,
):
    near0_ref, *piece_refs = refs[: -10]
    out_hbm, side_hbm, near_hbm, sums_ref, rest_ref, turn_ref, staged_ref = refs[-10:-3]
    side_ref, near_ref, sems = refs[-3:]
    train, width = sums_ref.shape
    each = table_ref.shape[1] - train
    table = table_ref[:, :each, :].reshape(-1, width)
    parts = (
        (own_ref, own_rest_hbm, start_ref[...]),
        (ghost_ref, ghost_rest_hbm, table),
    )
    aggregate(flag_ref, noise_ref, parts, sums_ref, rest_ref)
    last = jnp.broadcast_to(normalize(sums_ref[...])[None], staged_ref.shape)
    out_copy = post(last, staged_ref, out_hbm, sems.at[0])
    length = piece_refs[0].shape[0] - 16
    groups = len(piece_refs)
    if groups > 1:
        near_ref[:, :train, :] = near0_ref[...]
        near_rows(place_ref, table_ref, each, near_ref, train)
        near_copy = pltpu.make_async_copy(near_ref, near_hbm, sems.at[2])
        near_copy.start()
        for shift, ref in enumerate(piece_refs):
            if shift:
                side_ref[(shift - 1) * length : shift * length, :] = ref[:length, :]
            group = lax.rem(place_ref[1] + shift, groups)
            turn_ref[pl.ds(group, 1), :] = ref[length:, :128].astype(f32)[:1]
        side_ref[(groups - 1) * length :, :128] = turn_ref[:16, :].astype(bf16)
        side_copy = pltpu.make_async_copy(side_ref, side_hbm, sems.at[1])
        side_copy.start()
        side_copy.wait()
        near_copy.wait()
    out_copy.wait()


def last_kernel(
    flag_ref,
    token_ref,
    own_hbm,
    own_rest_hbm,
    ghost_rest_hbm,
    noise_hbm,
    weight_hbm,
    ghost_ref,
    table_ref,
    start_ref,
    out_hbm,
    weight_ref,
    own_ref,
    noise_ref,
    sums_ref,
    rest_ref,
    out_ref,
    sems,
):
    cuts = blocks_of(sums_ref.shape[0], 256)
    pairs = []
    for cut in cuts:
        pairs.append((own_hbm.at[cut], own_ref.at[cut]))
        pairs.append((noise_hbm.at[1, 0, 0, cut], noise_ref.at[cut]))
    pairs.append((weight_hbm, weight_ref))
    pairs.append((start_ref, out_hbm.at[0, 0, 0]))
    copies = fetch(pairs, sems)
    width = out_ref.shape[-1]
    ghosts = ghost_ref.shape[1]
    table = table_ref[:, : ghosts // table_ref.shape[0], :].reshape(ghosts, width)
    tables = ((own_ref, own_rest_hbm, start_ref[...]), (ghost_ref, ghost_rest_hbm, table))
    outs = []
    for at, cut in enumerate(cuts):
        copies[2 * at].wait()
        copies[2 * at + 1].wait()
        rows = cut.stop - cut.start
        sums = sums_ref.at[cut]
        aggregate(
            flag_ref,
            noise_ref.at[cut],
            [(ref.at[cut], rest.at[cut], table) for ref, rest, table in tables],
            sums,
            rest_ref.at[:rows],
        )
        for inner in blocks_of(rows, 32):
            row = slice(cut.start + inner.start, cut.start + inner.stop)
            out_ref[row, :] = normalize(sums_ref[row, :])
        outs.append(
            pltpu.make_async_copy(
                out_ref.at[cut], out_hbm.at[1, 0, 0, cut], sems.at[len(pairs) + at]
            )
        )
        outs[-1].start()
    for copy in copies[-2:] + outs:
        copy.wait()


def shares(ref, first, share):
    return ref[:, pl.ds(pl.multiple_of(first, 128), share)].astype(f32)


def lanes_sum(values):
    total = None
    for piece in range(values.shape[1] // 128):
        part = values[:, piece * 128 : (piece + 1) * 128].astype(f32)
        total = part * part if total is None else total + part * part
    return total


def classify_kernel(
    many,
    place_ref,
    label_ref,
    zero_ref,
    one_ref,
    two_ref,
    side_refs,
    w_first_hbm,
    w_second_hbm,
    w_third_hbm,
    n_first_hbm,
    n_second_hbm,
    n_third_hbm,
    g_first_ref,
    g_second_ref,
    g_third_ref,
    send_ref,
    side_hbm,
    near_hbm,
    near_ref,
    w_first_ref,
    w_second_ref,
    w_third_ref,
    n_first_ref,
    n_second_ref,
    n_third_ref,
    in_ref,
    w_third_pad_ref,
    turn_ref,
    column_ref,
    h_one_ref,
    h_two_ref,
    slope_one_ref,
    slope_two_ref,
    d_one_ref,
    d_two_ref,
    d_three_ref,
    sems,
):
    classes = w_third_ref.shape[0]
    hid = w_second_ref.shape[0]
    width = two_ref.shape[2]
    wide = w_third_pad_ref.shape[0]
    train = two_ref.shape[1]
    scale = noise_mult * clip_bound
    place = place_ref[0]
    pairs = (
        (w_first_hbm, w_first_ref),
        (w_second_hbm, w_second_ref),
        (w_third_hbm, w_third_ref),
        (n_first_hbm, n_first_ref),
        (n_second_hbm, n_second_ref),
        (n_third_hbm, n_third_ref),
    )

    def set_noise():
        g_first_ref[...] = scale * n_first_ref[...]
        g_second_ref[...] = scale * n_second_ref[...]
        g_third_ref[...] = scale * n_third_ref[...]

    def pad():
        w_third_pad_ref[...] = jnp.zeros_like(w_third_pad_ref)
        w_third_pad_ref[:classes, :] = w_third_ref[...]

    def column(row, turned, lane):
        column_ref[row : row + train, :] = jnp.broadcast_to(
            turned[:train, lane : lane + 1], (train, 128)
        ).astype(jnp.int32)

    if many:

        @pl.when(pl.program_id(0) == 0)
        def _():
            for copy in fetch(pairs, sems):
                copy.wait()
            set_noise()
            pad()

        groups = label_ref.shape[0]
        turn_ref[:groups, :train] = label_ref[...].astype(f32)
        turned = turn_ref[...].T
        for group in range(groups):
            column(group * train, turned, group)
        for hop, ref in enumerate((zero_ref, one_ref)):
            in_ref[:, hop * width : (hop + 1) * width] = ref[...].reshape(-1, width)
    else:
        chips = len(side_refs)
        copies = fetch(((side_hbm, side_refs[0]), (near_hbm, near_ref)) + pairs[1:], sems)
        groups = two_ref.shape[0] // chips
        rows = groups * train
        for shift, ref in [*enumerate(side_refs)][::-1]:
            if shift == 0:
                copies[0].wait()
            part = lax.rem(place // 2 - shift + chips, chips)
            at = pl.multiple_of(part * rows, rows)
            for after in range(1, groups):
                row = at + lax.rem(place_ref[1] + after, groups) * train
                for hop in range(2):
                    first = (2 * (after - 1) + hop) * train
                    in_ref[
                        pl.ds(pl.multiple_of(row, train), train), hop * width : (hop + 1) * width
                    ] = ref[first : first + train, :]
            turn_ref[pl.ds(pl.multiple_of(part * 16, 16), 16), :] = ref[2 * (rows - train) :, :128].astype(f32)
        copies[1].wait()
        for chip in range(chips):
            row = pl.multiple_of(chip * rows + place_ref[1] * train, train)
            for hop in range(2):
                in_ref[pl.ds(row, train), hop * width : (hop + 1) * width] = near_ref[
                    chip, hop * train : (hop + 1) * train, :
                ]
        turned = turn_ref[...].T
        for part in range(chips):
            for group in range(groups):
                column((part * groups + group) * train, turned, part * 16 + group)
    in_ref[:, 2 * width :] = two_ref[...].reshape(-1, width)

    def activate(values, at, cols, h_ref, slope_ref):
        sigma = 0.5 + 0.5 * jnp.tanh(0.5 * values)
        out = values * sigma
        slope_ref[at, cols] = sigma + out * (1.0 - sigma)
        h_ref[at, cols] = out.astype(bf16)
        return lanes_sum(out)

    def back(values, at, cols, slope_ref, d_ref):
        out = values * slope_ref[at, cols]
        d_ref[at, cols] = out.astype(bf16)
        return lanes_sum(out)

    def layer(product, finish, *refs):
        sums = []
        values = product(cuts[0])
        for at, cut in enumerate(cuts):
            ahead = product(cuts[at + 1]) if at + 1 < len(cuts) else None
            for rows in blocks_of(values.shape[0], 32):
                here = slice(cut.start + rows.start, cut.start + rows.stop)
                sums.append(
                    sum(
                        finish(values[rows, cols], here, cols, *refs)
                        for cols in blocks_of(values.shape[1], 256)
                    )
                )
            values = ahead
        return jnp.concatenate(sums, 0)

    step = min(512, in_ref.shape[0])
    cuts = [slice(at, at + step) for at in range(0, in_ref.shape[0], step)]
    sq_in = jnp.concatenate([lanes_sum(in_ref[at, :]) for at in blocks_of(in_ref.shape[0], 32)], 0)
    sq_one = layer(
        lambda cut: dot(in_ref[cut, :], w_first_ref[...]), activate, h_one_ref, slope_one_ref
    )
    if not many:
        copies[2].wait()
    sq_two = layer(
        lambda cut: dot(h_one_ref[cut, :], w_second_ref[...]), activate, h_two_ref, slope_two_ref
    )
    if not many:
        copies[3].wait()
        pad()
    logits = dot_nt(h_two_ref[...], w_third_pad_ref[...])
    sums = []
    for at in blocks_of(logits.shape[0], 32):
        ids = lax.broadcasted_iota(jnp.int32, (at.stop - at.start, wide), 1)
        expo = jnp.where(ids < classes, jnp.exp(logits[at]), 0.0)
        probs = expo / jnp.sum(expo, -1, keepdims=True)
        label = column_ref[at, :1]
        d_three = (probs - jnp.where(ids == label, 1.0, 0.0)).astype(bf16)
        d_three_ref[at, :] = d_three
        sums.append(lanes_sum(d_three))
    sq_dthree = jnp.concatenate(sums, 0)
    sq_dtwo = layer(
        lambda cut: dot(d_three_ref[cut, :], w_third_pad_ref[...]), back, slope_two_ref, d_two_ref
    )
    sq_done = layer(
        lambda cut: dot_nt(d_two_ref[cut, :], w_second_ref[...]), back, slope_one_ref, d_one_ref
    )

    def total(values):
        return jnp.sum(values, -1, keepdims=True)

    norm = jnp.sqrt(
        total(sq_in) * total(sq_done)
        + total(sq_one) * total(sq_dtwo)
        + total(sq_two) * total(sq_dthree)
    )
    factor = clip_bound / jnp.maximum(norm, clip_bound)

    if not many:
        for copy in copies[4:]:
            copy.wait()
        set_noise()
    share_one, share = g_first_ref.shape[0], g_second_ref.shape[0]
    places = [place] if many else [place, place + 1 - 2 * (place % 2)]

    def left(ref, share):
        if share % 128 == 0:
            picked = [shares(ref, at * share, share) for at in places]
            return (jnp.concatenate(picked, 1) * factor).astype(bf16)
        length, count = ref.shape[1], share * len(places)
        most = 128 - math.gcd(count, 128)
        size = min(length, -(-(count + most) // 128) * 128)
        first = [at * share for at in places]
        least = functools.reduce(jnp.minimum, first)
        start = jnp.minimum(least // 128 * 128, length - size)
        rows = lax.broadcasted_iota(jnp.int32, (size, count), 0)
        cols = lax.broadcasted_iota(jnp.int32, (size, count), 1)
        wanted = cols + (first[0] - start)
        for at, other in enumerate(first[1:], 1):
            wanted = jnp.where(cols >= at * share, cols - at * share + (other - start), wanted)
        window = ref[:, pl.ds(pl.multiple_of(start, 128), size)]
        picked = dot(window, jnp.where(rows == wanted, 1.0, 0.0).astype(bf16))
        return (picked * factor).astype(bf16)

    sum_one = dot_tn(left(in_ref, share_one), d_one_ref[...])
    sum_two = dot_tn(left(h_one_ref, share), d_two_ref[...])
    sum_three = dot_tn(d_three_ref[...], left(h_two_ref, share))
    g_first_ref[...] += sum_one[:share_one]
    g_second_ref[...] += sum_two[:share]
    g_third_ref[...] += sum_three[:classes, :share]
    if not many:
        send_ref[:share_one, :] = sum_one[share_one:].astype(bf16)
        send_ref[share_one : share_one + share, :] = sum_two[share:].astype(bf16)
        first = share_one + share
        for at in range(0, classes, 32):
            cols = slice(at // 32 * share, (at // 32 + 1) * share)
            send_ref[first : first + 32, cols] = sum_three[at : at + 32, share:].astype(bf16)


def finish_kernel(got_ref, one_ref, two_ref, three_ref, g_first_ref, g_second_ref, g_third_ref):
    share_one, share = one_ref.shape[0], two_ref.shape[0]
    g_first_ref[...] = one_ref[...] + got_ref[:share_one, :].astype(f32)
    g_second_ref[...] = two_ref[...] + got_ref[share_one : share_one + share, :].astype(f32)
    first = share_one + share
    classes = three_ref.shape[0]
    for at in range(0, classes, 32):
        size = min(32, classes - at)
        cols = slice(at // 32 * share, (at // 32 + 1) * share)
        got = got_ref[first : first + 32, cols].astype(f32)
        g_third_ref[at : at + size, :] = three_ref[at : at + size, :] + got[:size]


def call(kernel, mib, outs, ins, scratch):
    def shape_of(shape, dtype, space):
        if space is None or space is HBM:
            return (space or VMEM)(shape, dtype)
        return jax.ShapeDtypeStruct(shape, dtype)

    def block(space):
        return pl.BlockSpec(memory_space=VMEM if space is None else space)

    def held(value, space):
        if space is None or space is HBM:
            return pltpu.with_memory_space_constraint(value, space or VMEM)
        return value

    return pl.pallas_call(
        kernel,
        out_shape=[shape_of(*out) for out in outs],
        in_specs=[block(space) for _, space in ins],
        out_specs=[block(space) for _, _, space in outs],
        scratch_shapes=scratch,
        compiler_params=params(mib),
    )(*[held(value, space) for value, space in ins])


def local(
    axes,
    feats,
    hop_noise,
    send_rows,
    tile_block,
    tile_src,
    tile_dst,
    tile_count,
    labels,
    w_first,
    w_second,
    w_third,
    noise_first,
    noise_second,
    noise_third,
):
    nodes, width = feats.shape[2:]
    parts, each = send_rows.shape[2:]
    ghosts = parts * each
    tiles = tile_src.shape[2]
    slots = tile_src.shape[3]
    train = labels.shape[2]
    classes = w_third.shape[1]
    hid = w_second.shape[0]
    d_in = w_first.shape[0]
    cols = nodes + ghosts
    rows = send_rows.reshape(parts, each)
    turn = VMEM((128, 128), jnp.int32)
    pick = VMEM((ghosts, nodes), bf16)
    dom = axes[:-1]
    members = lax.axis_size(axes)
    few = len(axes) == 3
    copies = members // 2 if few else 1

    def every(value, *names):
        for name in names:
            value = lax.all_gather(value, name, axis=0, tiled=True)
        return value

    staged = VMEM((parts, each + train, width), bf16)
    start0, out0, own0, src, dst = call(
        first_kernel,
        16,
        [
            ((nodes, width), bf16, None),
            ((parts, each + train, width), bf16, HBM),
            ((train, width), bf16, None),
            ((tiles, slots), jnp.int32, None),
            ((tiles, slots), jnp.int32, None),
        ],
        [(feats, HBM), (send_rows, HBM), (tile_src, HBM), (tile_dst, HBM)],
        [
            VMEM((nodes, width), bf16),
            VMEM((parts, each), jnp.int32),
            turn,
            pick,
            staged,
            DMA((5,)),
        ],
    )
    table0 = lax.all_to_all(out0, dom, split_axis=0, concat_axis=0, tiled=True)
    own, ghost, own_train, noise_train, part1, flag, own_rest, ghost_rest = call(
        build_kernel,
        28,
        [
            ((nodes, nodes), bf16, HBM),
            ((nodes, ghosts), bf16, None),
            ((train, nodes), bf16, None),
            ((train, width), bf16, None),
            ((nodes, width), f32, None),
            ((1,), jnp.int32, SMEM),
            ((nodes, nodes), bf16, HBM),
            ((nodes, ghosts), bf16, HBM),
        ],
        [
            (tile_block, HBM),
            (tile_count, SMEM),
            (src, None),
            (dst, None),
            (hop_noise, HBM),
            (start0, None),
        ],
        [
            VMEM((nodes, width), bf16),
            VMEM((tiles, slots, 128), bf16),
            VMEM((tiles * 16, slots), bf16),
            VMEM((tiles * 16, slots), bf16),
            VMEM((nodes, cols), f32),
            VMEM((nodes, max(nodes, ghosts)), bf16),
            VMEM((nodes, nodes), bf16),
            SMEM(tile_block.shape, jnp.int32),
            DMA((4,)),
        ],
    )
    place = jnp.stack([lax.axis_index(dom), lax.axis_index("grp")]).astype(jnp.int32)
    start1, out1, side, near0 = call(
        hop_kernel,
        16,
        [
            ((nodes, width), bf16, None),
            ((parts, each + train, width), bf16, HBM),
            ((2 * train + 16, width), bf16, None),
            ((parts // 2, train, width), bf16, None),
        ],
        [
            (flag, SMEM),
            (place, SMEM),
            (part1, None),
            (ghost, None),
            (ghost_rest, HBM),
            (table0, None),
            (rows, VMEM),
            (own0, None),
            (labels.reshape(1, train), VMEM),
        ],
        [
            VMEM((nodes, width), f32),
            VMEM((nodes, ghosts), bf16),
            turn,
            pick,
            VMEM((parts, each, width), bf16),
            DMA((parts + 1,)),
        ],
    )
    table1 = lax.all_to_all(out1, dom, split_axis=0, concat_axis=0, tiled=True)
    grp = lax.axis_size("grp")

    def shifted(value, name, size, step):
        return [
            lax.ppermute(value, name, [((at + step * shift) % size, at) for at in range(size)])
            for shift in range(1, size)
        ]

    sides = [side] + (shifted(side, "grp", grp, 1) if few else [])
    side_shape = ((len(sides) - 1) * 2 * train + 16, width)
    near_shape = (parts // 2, 2 * train, width)
    last, side, near = call(
        train_kernel,
        12,
        [
            ((copies, train, width), bf16, HBM),
            (side_shape, bf16, HBM),
            (near_shape, bf16, HBM),
        ],
        [
            (flag, SMEM),
            (place, SMEM),
            (own_train, None),
            (ghost, None),
            (own_rest, HBM),
            (ghost_rest, HBM),
            (noise_train, None),
            (start1, None),
            (table1, None),
            (near0, None),
        ]
        + [(value, None) for value in sides],
        [
            VMEM((train, width), f32),
            VMEM((train, max(nodes, ghosts)), bf16),
            VMEM((128, 128), f32),
            VMEM((copies, train, width), bf16),
            VMEM(side_shape, bf16),
            VMEM(near_shape, bf16),
            DMA((3,)),
        ],
    )
    if few:
        every2 = lax.all_to_all(last, ("chip", "grp"), split_axis=0, concat_axis=0, tiled=True)
        sides = [side] + shifted(side, "chip", parts // 2, -1)
    else:
        every0, every1, every2 = (
            every(value, axes) for value in (own0[None], start1[None, :train], last)
        )
        every_label = every(labels.reshape(1, train), axes)
    wide = (classes + 255) // 256 * 256
    hop_feats, held_first = call(
        last_kernel,
        28,
        [
            ((2, 1, 1, nodes, width), bf16, HBM),
            (w_first.shape, bf16, None),
        ],
        [
            (flag, SMEM),
            (side, HBM),
            (own, HBM),
            (own_rest, HBM),
            (ghost_rest, HBM),
            (hop_noise, HBM),
            (w_first, HBM),
            (ghost, None),
            (table1, None),
            (start1, None),
        ],
        [
            VMEM((nodes, nodes), bf16),
            VMEM((nodes, width), bf16),
            VMEM((nodes, width), f32),
            VMEM((nodes, max(nodes, ghosts)), bf16),
            VMEM((nodes, width), bf16),
            DMA((3 * -(-nodes // 256) + 2,)),
        ],
    )
    chunk = train * (copies if few else min(members, 32))
    groups = chunk // train
    noises = (noise_first, noise_second, noise_third.T)
    fixed = (w_first, w_second, w_third.T) + noises
    scratch = [VMEM(value.shape, value.dtype) for value in fixed]
    scratch += [
        VMEM((chunk, d_in), bf16),
        VMEM((wide, hid), bf16),
        VMEM((128, 128), f32),
        VMEM((chunk, 128), jnp.int32),
        VMEM((chunk, hid), bf16),
        VMEM((chunk, hid), bf16),
        VMEM((chunk, hid), f32),
        VMEM((chunk, hid), f32),
        VMEM((chunk, hid), bf16),
        VMEM((chunk, hid), bf16),
        VMEM((chunk, wide), bf16),
        DMA((16,)),
    ]
    if few:
        chips = parts // 2

        def classify(place_ref, *refs):
            sides_in, rest = refs[:chips], refs[chips:]
            near_hbm, two_ref, first_ref, *outs = rest[:12]
            held, near_ref, *rest = rest[12:]
            classify_kernel(
                False,
                place_ref,
                None,
                None,
                None,
                two_ref,
                (held,) + sides_in[1:],
                first_ref,
                *outs,
                sides_in[0],
                near_hbm,
                near_ref,
                first_ref,
                *rest,
            )

        rows = noise_first.shape[0] + noise_second.shape[0] + 32
        *own_sums, other = call(
            classify,
            44,
            [(value.shape, f32, None) for value in noises] + [((rows, hid), bf16, None)],
            [(place, SMEM)]
            + [(side, HBM)]
            + [(value, None) for value in sides[1:]]
            + [(near, HBM), (every2, None), (held_first, None)]
            + [(value, HBM) for value in fixed[1:]],
            [VMEM(side_shape, bf16), VMEM(near_shape, bf16)] + scratch[1:],
        )
        got = lax.ppermute(other, "core", [(0, 1), (1, 0)])
        first, second, third = call(
            finish_kernel,
            16,
            [(value.shape, f32, VMEM) for value in noises],
            [(got, None)] + [(value, None) for value in own_sums],
            [],
        )
    else:

        ins = (every_label, every0, every1, every2)

        def classify(place_ref, label_ref, zero_ref, one_ref, two_ref, *rest):
            classify_kernel(
                True,
                place_ref,
                label_ref,
                zero_ref,
                one_ref,
                two_ref,
                None,
                *rest[:9],
                None,
                None,
                None,
                None,
                *rest[9:],
            )

        def whole(value):
            return pl.BlockSpec(value.shape, lambda i: (0, 0))

        def piece(value):
            return pl.BlockSpec(
                (groups,) + value.shape[1:], lambda i: (i,) + (0,) * (value.ndim - 1)
            )

        first, second, third = pl.pallas_call(
            classify,
            grid=(members // groups,),
            out_shape=[jax.ShapeDtypeStruct(value.shape, f32) for value in noises],
            in_specs=[pl.BlockSpec(memory_space=SMEM)]
            + [piece(value) for value in ins]
            + [pl.BlockSpec(memory_space=HBM) for value in fixed],
            out_specs=[whole(value) for value in noises],
            scratch_shapes=scratch,
            compiler_params=params(56),
        )(place, *ins, *fixed)
    return (hop_feats, first, second, third.T)


def solution(mesh):
    dom, grp = mesh.shape["dom"], mesh.shape["grp"]
    names = ("dom", "grp")
    if dom * grp <= FEW and dom <= 8 and dom % 2 == 0:
        names = ("chip", "core", "grp")
        mesh = jax.sharding.Mesh(mesh.devices.reshape(dom // 2, 2, grp), names)
    doms, grps = names[:-1], "grp"
    in_specs = (
        P(doms, grps, None, None),
        P(None, doms, grps, None, None),
        P(doms, grps, None, None),
        P(doms, grps, None),
        P(doms, grps, None, None),
        P(doms, grps, None, None),
        P(doms, grps),
        P(doms, grps, None),
        P(),
        P(),
        P(),
        P(doms, None),
        P(doms, None),
        P(doms, None),
    )
    out_specs = (P(None, doms, grps, None, None), P(doms, None), P(doms, None), P(doms, None))
    return jax.shard_map(
        functools.partial(local, names),
        mesh=mesh,
        in_specs=in_specs,
        out_specs=out_specs,
        check_vma=False,
    )
```

```python
import functools
import math

import jax
import jax.numpy as jnp
from jax import lax
from jax.experimental import pallas as pl
from jax.experimental.pallas import tpu as pltpu
from jax.sharding import PartitionSpec as P

BLOCK = 128
LOW = 256
GROUP = 8
clip_bound = 4.0
noise_mult = 1.0

f32 = jnp.float32
bf16 = jnp.bfloat16
f8 = jnp.float8_e4m3fn
VMEM = pltpu.VMEM
SMEM = pltpu.SMEM
HBM = pltpu.HBM
DMA = pltpu.SemaphoreType.DMA


FEW = 32


def params(mib):
    return pltpu.CompilerParams(vmem_limit_bytes=mib * 1024 * 1024)


def fetch(pairs, sems):
    copies = [pltpu.make_async_copy(*pair, sems.at[at]) for at, pair in enumerate(pairs)]
    for copy in copies:
        copy.start()
    return copies


def normalize(values):
    return (values * lax.rsqrt(jnp.sum(values * values, -1, keepdims=True) + 1e-06)).astype(bf16)


def blocks_of(length, step):
    return [slice(at, min(at + step, length)) for at in range(0, length, step)]


def dot(left, right):
    return jnp.dot(left, right, preferred_element_type=f32)


def dot_nt(left, right):
    return lax.dot_general(left, right, (((1,), (1,)), ((), ())), preferred_element_type=f32)


def dot_tn(left, right):
    return lax.dot_general(left, right, (((0,), (0,)), ((), ())), preferred_element_type=f32)


def choose(rows_ref, turn_ref, pick_ref):
    parts, each = rows_ref.shape
    turn_ref[:parts, :each] = rows_ref[...]
    columns = turn_ref[...].T
    spots = lax.broadcasted_iota(jnp.int32, (each, pick_ref.shape[1]), 1)
    for part in range(parts):
        wanted = columns[:each, part : part + 1]
        pick_ref[part * each : (part + 1) * each, :] = jnp.where(wanted == spots, 1.0, 0.0).astype(
            bf16
        )


def post(rows, staged_ref, out_hbm, sem):
    staged_ref[...] = rows.reshape(staged_ref.shape)
    copy = pltpu.make_async_copy(staged_ref, out_hbm, sem)
    copy.start()
    return copy


def first_kernel(
    feats_hbm,
    rows_hbm,
    src_hbm,
    dst_hbm,
    start_ref,
    out_hbm,
    own_ref,
    src_ref,
    dst_ref,
    feats_ref,
    rows_ref,
    turn_ref,
    pick_ref,
    staged_ref,
    sems,
):
    copies = fetch(
        (
            (rows_hbm.at[0, 0], rows_ref),
            (feats_hbm.at[0, 0], feats_ref),
            (src_hbm.at[0, 0], src_ref),
            (dst_hbm.at[0, 0], dst_ref),
        ),
        sems,
    )
    copies[0].wait()
    choose(rows_ref, turn_ref, pick_ref)
    copies[1].wait()
    picked = dot(pick_ref[...], feats_ref[...])
    each = staged_ref.shape[1]
    train = own_ref.shape[0]
    each -= train
    own_ref[...] = normalize(feats_ref[:train, :].astype(f32))
    for part in range(staged_ref.shape[0]):
        staged_ref[part, :each] = normalize(picked[part * each : (part + 1) * each])
        staged_ref[part, each:] = own_ref[...]
    out_copy = pltpu.make_async_copy(staged_ref, out_hbm, sems.at[4])
    out_copy.start()
    for cut in blocks_of(start_ref.shape[0], 32):
        start_ref[cut, :] = normalize(feats_ref[cut, :].astype(f32))
    copies[2].wait()
    copies[3].wait()
    out_copy.wait()


def build_kernel(
    blocks_hbm,
    count_ref,
    src_ref,
    dst_ref,
    noise_hbm,
    start_ref,
    own_hbm,
    ghost_ref,
    own_train_ref,
    noise_train_ref,
    part_ref,
    flag_ref,
    own_rest_ref,
    ghost_rest_ref,
    noise_ref,
    low_ref,
    high_ref,
    spot_ref,
    sums_ref,
    rest_ref,
    own_ref,
    blocks_ref,
    sems,
):
    train = own_train_ref.shape[0]
    copies = fetch(
        (
            (blocks_hbm, blocks_ref),
            (noise_hbm.at[0, 0, 0], noise_ref),
            (noise_hbm.at[1, 0, 0, :train], noise_train_ref),
        ),
        sems,
    )
    nodes, cols = sums_ref.shape
    pieces = -(-cols // LOW)
    tiles, slots = src_ref.shape
    own_ref[...] = jnp.zeros_like(own_ref)
    ghost_ref[...] = jnp.zeros_like(ghost_ref)
    count = count_ref[0, 0]

    def sixteen(values):
        wide = jnp.broadcast_to(values.astype(f32)[:, None, :], (tiles, 16, slots))
        return wide.reshape(tiles * 16, slots).astype(bf16)

    src = src_ref[...]
    dst = dst_ref[...]
    tile_ids = lax.broadcasted_iota(jnp.int32, (tiles, slots), 0)
    high_ref[...] = sixteen(src // LOW)
    spot_ref[...] = sixteen(jnp.where((dst < BLOCK) & (tile_ids < count), dst, -1))
    low = (src % LOW - LOW // 2).astype(f32).T
    for tile in range(tiles):
        low_ref[tile] = jnp.broadcast_to(low[:, tile : tile + 1], (slots, 128)).astype(bf16)
    ids = lax.broadcasted_iota(jnp.int32, (BLOCK, slots), 0).astype(f32).astype(bf16)
    lanes = lax.broadcasted_iota(jnp.int32, (slots, 128), 1).astype(f32)
    lanes = [(lanes + first).astype(bf16) for first in range(-LOW // 2, LOW // 2, 128)]
    one = jnp.ones((), bf16)
    zero = jnp.zeros((), bf16)

    def counts(tile):
        rows = pl.ds(pl.multiple_of(tile * 16, 16), 16)
        high, spot = high_ref[rows, :], spot_ref[rows, :]
        tall = jnp.concatenate([spot] * (BLOCK // 16), 0)
        spot_one = jnp.where(ids == tall, one, zero)
        spots = []
        for piece in range(pieces):
            here = jnp.where(high == piece, one, zero)
            hot = spot_one * jnp.concatenate([here] * (BLOCK // 16), 0)
            spots.append(hot.astype(f8))
        low = low_ref[tile]
        low_hot = [jnp.where(low == ids, one, zero).astype(f8) for ids in lanes]
        return dot(jnp.concatenate(spots, 0), jnp.concatenate(low_hot, 1))

    def turn(add, step, carry):
        first = step * GROUP
        outs = [counts(first + inner) for inner in range(GROUP)]
        for inner, out in enumerate(outs):
            base = pl.multiple_of(blocks_ref[0, 0, first + inner] * BLOCK, BLOCK)
            for piece in range(pieces):
                add(pl.ds(base, BLOCK), piece * LOW, out[piece * BLOCK : (piece + 1) * BLOCK])
        return carry

    def add_short(rows, at, values):
        ref, at = (own_ref, at) if at < nodes else (ghost_ref, at - nodes)
        size = min(LOW, ref.shape[1] - at)
        ref[rows, at : at + size] += values[:, :size].astype(bf16)

    def add_long(rows, at, values):
        size = min(LOW, cols - at)
        sums_ref[rows, at : at + size] += values[:, :size]

    steps = (count + GROUP - 1) // GROUP
    copies[0].wait()
    lax.fori_loop(0, steps, functools.partial(turn, add_short), 0)
    top = ghost_ref[:BLOCK, :256]
    for first in range(0, nodes, BLOCK):
        for ref in (own_ref, ghost_ref):
            for at in range(0, ref.shape[1], 256):
                top = jnp.maximum(top, ref[first : first + BLOCK, at : at + 256])
    big = jnp.max(top.astype(f32)) >= 256.0
    flag_ref[0] = big.astype(jnp.int32)

    @pl.when(big)
    def _():
        sums_ref[...] = jnp.zeros_like(sums_ref)
        lax.fori_loop(0, steps, functools.partial(turn, add_long), 0)
        own_ref[...] = sums_ref[:, :nodes].astype(bf16)
        ghost_ref[...] = sums_ref[:, nodes:].astype(bf16)

    own_copy = pltpu.make_async_copy(own_ref, own_hbm, sems.at[3])
    own_copy.start()
    own_train_ref[...] = own_ref[:train, :]
    for copy in copies[1:]:
        copy.wait()
    part_ref[...] = dot(own_ref[...], start_ref[...]) + noise_ref[...].astype(f32)

    @pl.when(big)
    def _():
        own_rest = (sums_ref[:, :nodes] - own_ref[...].astype(f32)).astype(bf16)
        part_ref[...] += dot(own_rest, start_ref[...])
        rest_ref[:, :nodes] = own_rest
        pltpu.sync_copy(rest_ref.at[:, :nodes], own_rest_ref)
        rest_ref[:, : cols - nodes] = (sums_ref[:, nodes:] - ghost_ref[...].astype(f32)).astype(bf16)
        pltpu.sync_copy(rest_ref.at[:, : cols - nodes], ghost_rest_ref)

    own_copy.wait()


def aggregate(flag_ref, first_ref, parts, sums_ref, rest_ref):
    rows = sums_ref.shape[0]
    for cut in blocks_of(rows, 256):
        total = sum(dot(count_ref[cut, :], table) for count_ref, _, table in parts)
        for inner in blocks_of(total.shape[0], 32):
            at = slice(cut.start + inner.start, cut.start + inner.stop)
            sums_ref[at, :] = first_ref[at, :].astype(f32) + total[inner]

    @pl.when(flag_ref[0] > 0)
    def _():
        for count_ref, rest_hbm, table in parts:
            held = rest_ref.at[:, : count_ref.shape[1]]
            pltpu.sync_copy(rest_hbm.at[:rows], held)
            sums_ref[...] += dot(held[...], table)


def near_rows(place_ref, table_ref, each, near_ref, first):
    chips, _, width = near_ref.shape
    size = table_ref.shape[1] - each
    for chip in range(chips):
        member = 2 * chip + place_ref[0] % 2
        near_ref[chip, first : first + size, :] = table_ref[pl.ds(member, 1), each:, :].reshape(
            size, width
        )


def hop_kernel(
    flag_ref,
    part_ref,
    ghost_ref,
    rest_hbm,
    table_ref,
    rows_ref,
    old_ref,
    labels_ref,
    start_ref,
    out_hbm,
    side_ref,
    near_ref,
    sums_ref,
    rest_ref,
    turn_ref,
    pick_ref,
    staged_ref,
    sem,
):
    width = start_ref.shape[1]
    parts, each = rows_ref.shape
    table = table_ref[:, :each, :].reshape(-1, width)
    choose(rows_ref, turn_ref, pick_ref)
    aggregate(flag_ref, part_ref, ((ghost_ref, rest_hbm, table),), sums_ref, rest_ref)
    for cut in blocks_of(start_ref.shape[0], 32):
        start_ref[cut, :] = normalize(sums_ref[cut, :])
    sent = dot(pick_ref[...], start_ref[...]).astype(bf16)
    train = labels_ref.shape[1]
    for part in range(parts):
        staged_ref[part, :each] = sent[part * each : (part + 1) * each]
        staged_ref[part, each:] = start_ref[:train, :]
    out_copy = pltpu.make_async_copy(staged_ref, out_hbm, sem)
    out_copy.start()
    near_ref[...] = table_ref[:, each:, :]
    side_ref[:train, :] = old_ref[...]
    side_ref[train : 2 * train, :] = start_ref[:train, :]
    turn_ref[:1, :train] = labels_ref[...]
    side_ref[2 * train :, :128] = turn_ref[:16, :].astype(f32).astype(bf16)
    out_copy.wait()


def train_kernel(
    flag_ref,
    place_ref,
    own_ref,
    ghost_ref,
    own_rest_hbm,
    ghost_rest_hbm,
    noise_ref,
    start_ref,
    table_ref,
    *refs,
):
    near0_ref, *piece_refs = refs[: -10]
    out_hbm, side_hbm, near_hbm, sums_ref, rest_ref, turn_ref, staged_ref = refs[-10:-3]
    side_ref, near_ref, sems = refs[-3:]
    train, width = sums_ref.shape
    each = table_ref.shape[1] - train
    table = table_ref[:, :each, :].reshape(-1, width)
    parts = (
        (own_ref, own_rest_hbm, start_ref[...]),
        (ghost_ref, ghost_rest_hbm, table),
    )
    aggregate(flag_ref, noise_ref, parts, sums_ref, rest_ref)
    last = jnp.broadcast_to(normalize(sums_ref[...])[None], staged_ref.shape)
    out_copy = post(last, staged_ref, out_hbm, sems.at[0])
    length = piece_refs[0].shape[0] - 16
    groups = len(piece_refs)
    if groups > 1:
        near_rows(place_ref, near0_ref, 0, near_ref, 0)
        near_rows(place_ref, table_ref, each, near_ref, train)
        near_copy = pltpu.make_async_copy(near_ref, near_hbm, sems.at[2])
        near_copy.start()
        for shift, ref in enumerate(piece_refs):
            if shift:
                side_ref[(shift - 1) * length : shift * length, :] = ref[:length, :]
            group = lax.rem(place_ref[1] + shift, groups)
            turn_ref[pl.ds(group, 1), :] = ref[length:, :128].astype(f32)[:1]
        side_ref[(groups - 1) * length :, :128] = turn_ref[:16, :].astype(bf16)
        side_copy = pltpu.make_async_copy(side_ref, side_hbm, sems.at[1])
        side_copy.start()
        side_copy.wait()
        near_copy.wait()
    out_copy.wait()


def last_kernel(
    flag_ref,
    token_ref,
    own_hbm,
    own_rest_hbm,
    ghost_rest_hbm,
    noise_hbm,
    weight_hbm,
    ghost_ref,
    table_ref,
    start_ref,
    out_hbm,
    weight_ref,
    own_ref,
    noise_ref,
    sums_ref,
    rest_ref,
    out_ref,
    sems,
):
    copies = fetch(
        (
            (own_hbm, own_ref),
            (noise_hbm.at[1, 0, 0], noise_ref),
            (weight_hbm, weight_ref),
        ),
        sems,
    )
    width = out_ref.shape[-1]
    ghosts = ghost_ref.shape[1]
    table = table_ref[:, : ghosts // table_ref.shape[0], :].reshape(ghosts, width)
    out_ref[0, 0, 0] = start_ref[...]
    copies[0].wait()
    copies[1].wait()
    parts = (
        (own_ref, own_rest_hbm, start_ref[...]),
        (ghost_ref, ghost_rest_hbm, table),
    )
    aggregate(flag_ref, noise_ref, parts, sums_ref, rest_ref)
    for cut in blocks_of(sums_ref.shape[0], 32):
        out_ref[1, 0, 0, cut, :] = normalize(sums_ref[cut, :])
    out_copy = pltpu.make_async_copy(out_ref, out_hbm, sems.at[3])
    out_copy.start()
    copies[2].wait()
    out_copy.wait()


def shares(ref, first, share):
    return ref[:, pl.ds(pl.multiple_of(first, 128), share)].astype(f32)


def lanes_sum(values):
    total = None
    for piece in range(values.shape[1] // 128):
        part = values[:, piece * 128 : (piece + 1) * 128].astype(f32)
        total = part * part if total is None else total + part * part
    return total


def classify_kernel(
    many,
    place_ref,
    label_ref,
    zero_ref,
    one_ref,
    two_ref,
    side_refs,
    w_first_hbm,
    w_second_hbm,
    w_third_hbm,
    n_first_hbm,
    n_second_hbm,
    n_third_hbm,
    g_first_ref,
    g_second_ref,
    g_third_ref,
    send_ref,
    side_hbm,
    near_hbm,
    near_ref,
    w_first_ref,
    w_second_ref,
    w_third_ref,
    n_first_ref,
    n_second_ref,
    n_third_ref,
    in_ref,
    w_third_pad_ref,
    turn_ref,
    column_ref,
    h_one_ref,
    h_two_ref,
    slope_one_ref,
    slope_two_ref,
    d_one_ref,
    d_two_ref,
    d_three_ref,
    sems,
):
    classes = w_third_ref.shape[0]
    hid = w_second_ref.shape[0]
    width = two_ref.shape[2]
    wide = w_third_pad_ref.shape[0]
    train = two_ref.shape[1]
    scale = noise_mult * clip_bound
    place = place_ref[0]
    pairs = (
        (w_first_hbm, w_first_ref),
        (w_second_hbm, w_second_ref),
        (w_third_hbm, w_third_ref),
        (n_first_hbm, n_first_ref),
        (n_second_hbm, n_second_ref),
        (n_third_hbm, n_third_ref),
    )

    def set_noise():
        g_first_ref[...] = scale * n_first_ref[...]
        g_second_ref[...] = scale * n_second_ref[...]
        g_third_ref[...] = scale * n_third_ref[...]

    def pad():
        w_third_pad_ref[...] = jnp.zeros_like(w_third_pad_ref)
        w_third_pad_ref[:classes, :] = w_third_ref[...]

    def column(row, turned, lane):
        column_ref[row : row + train, :] = jnp.broadcast_to(
            turned[:train, lane : lane + 1], (train, 128)
        ).astype(jnp.int32)

    if many:

        @pl.when(pl.program_id(0) == 0)
        def _():
            for copy in fetch(pairs, sems):
                copy.wait()
            set_noise()
            pad()

        groups = label_ref.shape[0]
        turn_ref[:groups, :train] = label_ref[...].astype(f32)
        turned = turn_ref[...].T
        for group in range(groups):
            column(group * train, turned, group)
        for hop, ref in enumerate((zero_ref, one_ref)):
            in_ref[:, hop * width : (hop + 1) * width] = ref[...].reshape(-1, width)
    else:
        chips = len(side_refs)
        copies = fetch(((side_hbm, side_refs[0]), (near_hbm, near_ref)) + pairs[1:], sems)
        groups = two_ref.shape[0] // chips
        rows = groups * train
        for shift, ref in [*enumerate(side_refs)][::-1]:
            if shift == 0:
                copies[0].wait()
            part = lax.rem(place // 2 - shift + chips, chips)
            at = pl.multiple_of(part * rows, rows)
            for after in range(1, groups):
                row = at + lax.rem(place_ref[1] + after, groups) * train
                for hop in range(2):
                    first = (2 * (after - 1) + hop) * train
                    in_ref[
                        pl.ds(pl.multiple_of(row, train), train), hop * width : (hop + 1) * width
                    ] = ref[first : first + train, :]
            turn_ref[pl.ds(pl.multiple_of(part * 16, 16), 16), :] = ref[2 * (rows - train) :, :128].astype(f32)
        copies[1].wait()
        for chip in range(chips):
            row = pl.multiple_of(chip * rows + place_ref[1] * train, train)
            for hop in range(2):
                in_ref[pl.ds(row, train), hop * width : (hop + 1) * width] = near_ref[
                    chip, hop * train : (hop + 1) * train, :
                ]
        turned = turn_ref[...].T
        for part in range(chips):
            for group in range(groups):
                column((part * groups + group) * train, turned, part * 16 + group)
    in_ref[:, 2 * width :] = two_ref[...].reshape(-1, width)

    def activate(values, at, cols, h_ref, slope_ref):
        sigma = 0.5 + 0.5 * jnp.tanh(0.5 * values)
        out = values * sigma
        slope_ref[at, cols] = sigma + out * (1.0 - sigma)
        h_ref[at, cols] = out.astype(bf16)
        return lanes_sum(out)

    def back(values, at, cols, slope_ref, d_ref):
        out = values * slope_ref[at, cols]
        d_ref[at, cols] = out.astype(bf16)
        return lanes_sum(out)

    def layer(product, finish, *refs):
        sums = []
        values = product(cuts[0])
        for at, cut in enumerate(cuts):
            ahead = product(cuts[at + 1]) if at + 1 < len(cuts) else None
            for rows in blocks_of(values.shape[0], 32):
                here = slice(cut.start + rows.start, cut.start + rows.stop)
                sums.append(
                    sum(
                        finish(values[rows, cols], here, cols, *refs)
                        for cols in blocks_of(values.shape[1], 256)
                    )
                )
            values = ahead
        return jnp.concatenate(sums, 0)

    step = min(512, in_ref.shape[0])
    cuts = [slice(at, at + step) for at in range(0, in_ref.shape[0], step)]
    sq_in = jnp.concatenate([lanes_sum(in_ref[at, :]) for at in blocks_of(in_ref.shape[0], 32)], 0)
    sq_one = layer(
        lambda cut: dot(in_ref[cut, :], w_first_ref[...]), activate, h_one_ref, slope_one_ref
    )
    if not many:
        copies[2].wait()
    sq_two = layer(
        lambda cut: dot(h_one_ref[cut, :], w_second_ref[...]), activate, h_two_ref, slope_two_ref
    )
    if not many:
        copies[3].wait()
        pad()
    logits = dot_nt(h_two_ref[...], w_third_pad_ref[...])
    sums = []
    for at in blocks_of(logits.shape[0], 32):
        ids = lax.broadcasted_iota(jnp.int32, (at.stop - at.start, wide), 1)
        expo = jnp.where(ids < classes, jnp.exp(logits[at]), 0.0)
        probs = expo / jnp.sum(expo, -1, keepdims=True)
        label = column_ref[at, :1]
        d_three = (probs - jnp.where(ids == label, 1.0, 0.0)).astype(bf16)
        d_three_ref[at, :] = d_three
        sums.append(lanes_sum(d_three))
    sq_dthree = jnp.concatenate(sums, 0)
    sq_dtwo = layer(
        lambda cut: dot(d_three_ref[cut, :], w_third_pad_ref[...]), back, slope_two_ref, d_two_ref
    )
    sq_done = layer(
        lambda cut: dot_nt(d_two_ref[cut, :], w_second_ref[...]), back, slope_one_ref, d_one_ref
    )

    def total(values):
        return jnp.sum(values, -1, keepdims=True)

    norm = jnp.sqrt(
        total(sq_in) * total(sq_done)
        + total(sq_one) * total(sq_dtwo)
        + total(sq_two) * total(sq_dthree)
    )
    factor = clip_bound / jnp.maximum(norm, clip_bound)

    if not many:
        for copy in copies[4:]:
            copy.wait()
        set_noise()
    share_one, share = g_first_ref.shape[0], g_second_ref.shape[0]
    places = [place] if many else [place, place + 1 - 2 * (place % 2)]

    def left(ref, share):
        if share % 128 == 0:
            picked = [shares(ref, at * share, share) for at in places]
            return (jnp.concatenate(picked, 1) * factor).astype(bf16)
        length, count = ref.shape[1], share * len(places)
        most = 128 - math.gcd(count, 128)
        size = min(length, -(-(count + most) // 128) * 128)
        first = [at * share for at in places]
        least = functools.reduce(jnp.minimum, first)
        start = jnp.minimum(least // 128 * 128, length - size)
        rows = lax.broadcasted_iota(jnp.int32, (size, count), 0)
        cols = lax.broadcasted_iota(jnp.int32, (size, count), 1)
        wanted = cols + (first[0] - start)
        for at, other in enumerate(first[1:], 1):
            wanted = jnp.where(cols >= at * share, cols - at * share + (other - start), wanted)
        window = ref[:, pl.ds(pl.multiple_of(start, 128), size)]
        picked = dot(window, jnp.where(rows == wanted, 1.0, 0.0).astype(bf16))
        return (picked * factor).astype(bf16)

    sum_one = dot_tn(left(in_ref, share_one), d_one_ref[...])
    sum_two = dot_tn(left(h_one_ref, share), d_two_ref[...])
    sum_three = dot_tn(d_three_ref[...], left(h_two_ref, share))
    g_first_ref[...] += sum_one[:share_one]
    g_second_ref[...] += sum_two[:share]
    g_third_ref[...] += sum_three[:classes, :share]
    if not many:
        send_ref[:share_one, :] = sum_one[share_one:].astype(bf16)
        send_ref[share_one : share_one + share, :] = sum_two[share:].astype(bf16)
        first = share_one + share
        for at in range(0, classes, 32):
            cols = slice(at // 32 * share, (at // 32 + 1) * share)
            send_ref[first : first + 32, cols] = sum_three[at : at + 32, share:].astype(bf16)


def finish_kernel(got_ref, one_ref, two_ref, three_ref, g_first_ref, g_second_ref, g_third_ref):
    share_one, share = one_ref.shape[0], two_ref.shape[0]
    g_first_ref[...] = one_ref[...] + got_ref[:share_one, :].astype(f32)
    g_second_ref[...] = two_ref[...] + got_ref[share_one : share_one + share, :].astype(f32)
    first = share_one + share
    classes = three_ref.shape[0]
    for at in range(0, classes, 32):
        size = min(32, classes - at)
        cols = slice(at // 32 * share, (at // 32 + 1) * share)
        got = got_ref[first : first + 32, cols].astype(f32)
        g_third_ref[at : at + size, :] = three_ref[at : at + size, :] + got[:size]


def call(kernel, mib, outs, ins, scratch):
    def shape_of(shape, dtype, space):
        if space is None or space is HBM:
            return (space or VMEM)(shape, dtype)
        return jax.ShapeDtypeStruct(shape, dtype)

    def block(space):
        return pl.BlockSpec(memory_space=VMEM if space is None else space)

    def held(value, space):
        if space is None or space is HBM:
            return pltpu.with_memory_space_constraint(value, space or VMEM)
        return value

    return pl.pallas_call(
        kernel,
        out_shape=[shape_of(*out) for out in outs],
        in_specs=[block(space) for _, space in ins],
        out_specs=[block(space) for _, _, space in outs],
        scratch_shapes=scratch,
        compiler_params=params(mib),
    )(*[held(value, space) for value, space in ins])


def local(
    axes,
    feats,
    hop_noise,
    send_rows,
    tile_block,
    tile_src,
    tile_dst,
    tile_count,
    labels,
    w_first,
    w_second,
    w_third,
    noise_first,
    noise_second,
    noise_third,
):
    nodes, width = feats.shape[2:]
    parts, each = send_rows.shape[2:]
    ghosts = parts * each
    tiles = tile_src.shape[2]
    slots = tile_src.shape[3]
    train = labels.shape[2]
    classes = w_third.shape[1]
    hid = w_second.shape[0]
    d_in = w_first.shape[0]
    cols = nodes + ghosts
    rows = send_rows.reshape(parts, each)
    turn = VMEM((128, 128), jnp.int32)
    pick = VMEM((ghosts, nodes), bf16)
    dom = axes[:-1]
    members = lax.axis_size(axes)
    few = len(axes) == 3
    copies = members // 2 if few else 1

    def every(value, *names):
        for name in names:
            value = lax.all_gather(value, name, axis=0, tiled=True)
        return value

    staged = VMEM((parts, each + train, width), bf16)
    start0, out0, own0, src, dst = call(
        first_kernel,
        16,
        [
            ((nodes, width), bf16, None),
            ((parts, each + train, width), bf16, HBM),
            ((train, width), bf16, None),
            ((tiles, slots), jnp.int32, None),
            ((tiles, slots), jnp.int32, None),
        ],
        [(feats, HBM), (send_rows, HBM), (tile_src, HBM), (tile_dst, HBM)],
        [
            VMEM((nodes, width), bf16),
            VMEM((parts, each), jnp.int32),
            turn,
            pick,
            staged,
            DMA((5,)),
        ],
    )
    table0 = lax.all_to_all(out0, dom, split_axis=0, concat_axis=0, tiled=True)
    own, ghost, own_train, noise_train, part1, flag, own_rest, ghost_rest = call(
        build_kernel,
        28,
        [
            ((nodes, nodes), bf16, HBM),
            ((nodes, ghosts), bf16, None),
            ((train, nodes), bf16, None),
            ((train, width), bf16, None),
            ((nodes, width), f32, None),
            ((1,), jnp.int32, SMEM),
            ((nodes, nodes), bf16, HBM),
            ((nodes, ghosts), bf16, HBM),
        ],
        [
            (tile_block, HBM),
            (tile_count, SMEM),
            (src, None),
            (dst, None),
            (hop_noise, HBM),
            (start0, None),
        ],
        [
            VMEM((nodes, width), bf16),
            VMEM((tiles, slots, 128), bf16),
            VMEM((tiles * 16, slots), bf16),
            VMEM((tiles * 16, slots), bf16),
            VMEM((nodes, cols), f32),
            VMEM((nodes, max(nodes, ghosts)), bf16),
            VMEM((nodes, nodes), bf16),
            SMEM(tile_block.shape, jnp.int32),
            DMA((4,)),
        ],
    )
    place = jnp.stack([lax.axis_index(dom), lax.axis_index("grp")]).astype(jnp.int32)
    start1, out1, side, near0 = call(
        hop_kernel,
        16,
        [
            ((nodes, width), bf16, None),
            ((parts, each + train, width), bf16, HBM),
            ((2 * train + 16, width), bf16, None),
            ((parts, train, width), bf16, None),
        ],
        [
            (flag, SMEM),
            (part1, None),
            (ghost, None),
            (ghost_rest, HBM),
            (table0, None),
            (rows, VMEM),
            (own0, None),
            (labels.reshape(1, train), VMEM),
        ],
        [VMEM((nodes, width), f32), VMEM((nodes, ghosts), bf16), turn, pick, staged, DMA(())],
    )
    table1 = lax.all_to_all(out1, dom, split_axis=0, concat_axis=0, tiled=True)
    grp = lax.axis_size("grp")

    def shifted(value, name, size, step):
        return [
            lax.ppermute(value, name, [((at + step * shift) % size, at) for at in range(size)])
            for shift in range(1, size)
        ]

    sides = [side] + (shifted(side, "grp", grp, 1) if few else [])
    side_shape = ((len(sides) - 1) * 2 * train + 16, width)
    near_shape = (parts // 2, 2 * train, width)
    last, side, near = call(
        train_kernel,
        12,
        [
            ((copies, train, width), bf16, HBM),
            (side_shape, bf16, HBM),
            (near_shape, bf16, HBM),
        ],
        [
            (flag, SMEM),
            (place, SMEM),
            (own_train, None),
            (ghost, None),
            (own_rest, HBM),
            (ghost_rest, HBM),
            (noise_train, None),
            (start1, None),
            (table1, None),
            (near0, None),
        ]
        + [(value, None) for value in sides],
        [
            VMEM((train, width), f32),
            VMEM((train, max(nodes, ghosts)), bf16),
            VMEM((128, 128), f32),
            VMEM((copies, train, width), bf16),
            VMEM(side_shape, bf16),
            VMEM(near_shape, bf16),
            DMA((3,)),
        ],
    )
    if few:
        every2 = lax.all_to_all(last, ("chip", "grp"), split_axis=0, concat_axis=0, tiled=True)
        sides = [side] + shifted(side, "chip", parts // 2, -1)
    else:
        every0, every1, every2 = (
            every(value, axes) for value in (own0[None], start1[None, :train], last)
        )
        every_label = every(labels.reshape(1, train), axes)
    wide = (classes + 255) // 256 * 256
    hop_feats, held_first = call(
        last_kernel,
        28,
        [
            ((2, 1, 1, nodes, width), bf16, HBM),
            (w_first.shape, bf16, None),
        ],
        [
            (flag, SMEM),
            (side, HBM),
            (own, HBM),
            (own_rest, HBM),
            (ghost_rest, HBM),
            (hop_noise, HBM),
            (w_first, HBM),
            (ghost, None),
            (table1, None),
            (start1, None),
        ],
        [
            VMEM((nodes, nodes), bf16),
            VMEM((nodes, width), bf16),
            VMEM((nodes, width), f32),
            VMEM((nodes, max(nodes, ghosts)), bf16),
            VMEM((2, 1, 1, nodes, width), bf16),
            DMA((4,)),
        ],
    )
    chunk = train * (copies if few else min(members, 32))
    groups = chunk // train
    noises = (noise_first, noise_second, noise_third.T)
    fixed = (w_first, w_second, w_third.T) + noises
    scratch = [VMEM(value.shape, value.dtype) for value in fixed]
    scratch += [
        VMEM((chunk, d_in), bf16),
        VMEM((wide, hid), bf16),
        VMEM((128, 128), f32),
        VMEM((chunk, 128), jnp.int32),
        VMEM((chunk, hid), bf16),
        VMEM((chunk, hid), bf16),
        VMEM((chunk, hid), f32),
        VMEM((chunk, hid), f32),
        VMEM((chunk, hid), bf16),
        VMEM((chunk, hid), bf16),
        VMEM((chunk, wide), bf16),
        DMA((16,)),
    ]
    if few:
        chips = parts // 2

        def classify(place_ref, *refs):
            sides_in, rest = refs[:chips], refs[chips:]
            near_hbm, two_ref, first_ref, *outs = rest[:12]
            held, near_ref, *rest = rest[12:]
            classify_kernel(
                False,
                place_ref,
                None,
                None,
                None,
                two_ref,
                (held,) + sides_in[1:],
                first_ref,
                *outs,
                sides_in[0],
                near_hbm,
                near_ref,
                first_ref,
                *rest,
            )

        rows = noise_first.shape[0] + noise_second.shape[0] + 32
        *own_sums, other = call(
            classify,
            44,
            [(value.shape, f32, None) for value in noises] + [((rows, hid), bf16, None)],
            [(place, SMEM)]
            + [(side, HBM)]
            + [(value, None) for value in sides[1:]]
            + [(near, HBM), (every2, None), (held_first, None)]
            + [(value, HBM) for value in fixed[1:]],
            [VMEM(side_shape, bf16), VMEM(near_shape, bf16)] + scratch[1:],
        )
        got = lax.ppermute(other, "core", [(0, 1), (1, 0)])
        first, second, third = call(
            finish_kernel,
            16,
            [(value.shape, f32, VMEM) for value in noises],
            [(got, None)] + [(value, None) for value in own_sums],
            [],
        )
    else:

        ins = (every_label, every0, every1, every2)

        def classify(place_ref, label_ref, zero_ref, one_ref, two_ref, *rest):
            classify_kernel(
                True,
                place_ref,
                label_ref,
                zero_ref,
                one_ref,
                two_ref,
                None,
                *rest[:9],
                None,
                None,
                None,
                None,
                *rest[9:],
            )

        def whole(value):
            return pl.BlockSpec(value.shape, lambda i: (0, 0))

        def piece(value):
            return pl.BlockSpec(
                (groups,) + value.shape[1:], lambda i: (i,) + (0,) * (value.ndim - 1)
            )

        first, second, third = pl.pallas_call(
            classify,
            grid=(members // groups,),
            out_shape=[jax.ShapeDtypeStruct(value.shape, f32) for value in noises],
            in_specs=[pl.BlockSpec(memory_space=SMEM)]
            + [piece(value) for value in ins]
            + [pl.BlockSpec(memory_space=HBM) for value in fixed],
            out_specs=[whole(value) for value in noises],
            scratch_shapes=scratch,
            compiler_params=params(56),
        )(place, *ins, *fixed)
    return (hop_feats, first, second, third.T)


def solution(mesh):
    dom, grp = mesh.shape["dom"], mesh.shape["grp"]
    names = ("dom", "grp")
    if dom * grp <= FEW and dom <= 8 and dom % 2 == 0:
        names = ("chip", "core", "grp")
        mesh = jax.sharding.Mesh(mesh.devices.reshape(dom // 2, 2, grp), names)
    doms, grps = names[:-1], "grp"
    in_specs = (
        P(doms, grps, None, None),
        P(None, doms, grps, None, None),
        P(doms, grps, None, None),
        P(doms, grps, None),
        P(doms, grps, None, None),
        P(doms, grps, None, None),
        P(doms, grps),
        P(doms, grps, None),
        P(),
        P(),
        P(),
        P(doms, None),
        P(doms, None),
        P(doms, None),
    )
    out_specs = (P(None, doms, grps, None, None), P(doms, None), P(doms, None), P(doms, None))
    return jax.shard_map(
        functools.partial(local, names),
        mesh=mesh,
        in_specs=in_specs,
        out_specs=out_specs,
        check_vma=False,
    )
```

```python
import functools
import math

import jax
import jax.numpy as jnp
from jax import lax
from jax.experimental import pallas as pl
from jax.experimental.pallas import tpu as pltpu
from jax.sharding import PartitionSpec as P

BLOCK = 128
LOW = 256
GROUP = 8
clip_bound = 4.0
noise_mult = 1.0

f32 = jnp.float32
bf16 = jnp.bfloat16
f8 = jnp.float8_e4m3fn
VMEM = pltpu.VMEM
SMEM = pltpu.SMEM
HBM = pltpu.HBM
DMA = pltpu.SemaphoreType.DMA


FEW = 32


def params(mib):
    return pltpu.CompilerParams(vmem_limit_bytes=mib * 1024 * 1024)


def fetch(pairs, sems):
    copies = [pltpu.make_async_copy(*pair, sems.at[at]) for at, pair in enumerate(pairs)]
    for copy in copies:
        copy.start()
    return copies


def normalize(values):
    return (values * lax.rsqrt(jnp.sum(values * values, -1, keepdims=True) + 1e-06)).astype(bf16)


def blocks_of(length, step):
    return [slice(at, min(at + step, length)) for at in range(0, length, step)]


def dot(left, right):
    return jnp.dot(left, right, preferred_element_type=f32)


def dot_nt(left, right):
    return lax.dot_general(left, right, (((1,), (1,)), ((), ())), preferred_element_type=f32)


def dot_tn(left, right):
    return lax.dot_general(left, right, (((0,), (0,)), ((), ())), preferred_element_type=f32)


def choose(rows_ref, turn_ref, pick_ref):
    parts, each = rows_ref.shape
    turn_ref[:parts, :each] = rows_ref[...]
    columns = turn_ref[...].T
    spots = lax.broadcasted_iota(jnp.int32, (each, pick_ref.shape[1]), 1)
    for part in range(parts):
        wanted = columns[:each, part : part + 1]
        pick_ref[part * each : (part + 1) * each, :] = jnp.where(wanted == spots, 1.0, 0.0).astype(
            bf16
        )


def post(rows, staged_ref, out_hbm, sem):
    staged_ref[...] = rows.reshape(staged_ref.shape)
    copy = pltpu.make_async_copy(staged_ref, out_hbm, sem)
    copy.start()
    return copy


def first_kernel(
    feats_hbm,
    rows_hbm,
    src_hbm,
    dst_hbm,
    start_ref,
    out_hbm,
    own_ref,
    src_ref,
    dst_ref,
    feats_ref,
    rows_ref,
    turn_ref,
    pick_ref,
    staged_ref,
    sems,
):
    copies = fetch(
        (
            (rows_hbm.at[0, 0], rows_ref),
            (feats_hbm.at[0, 0], feats_ref),
            (src_hbm.at[0, 0], src_ref),
            (dst_hbm.at[0, 0], dst_ref),
        ),
        sems,
    )
    copies[0].wait()
    choose(rows_ref, turn_ref, pick_ref)
    copies[1].wait()
    picked = dot(pick_ref[...], feats_ref[...])
    each = staged_ref.shape[1]
    train = own_ref.shape[0]
    each -= train
    own_ref[...] = normalize(feats_ref[:train, :].astype(f32))
    for part in range(staged_ref.shape[0]):
        staged_ref[part, :each] = normalize(picked[part * each : (part + 1) * each])
        staged_ref[part, each:] = own_ref[...]
    out_copy = pltpu.make_async_copy(staged_ref, out_hbm, sems.at[4])
    out_copy.start()
    for cut in blocks_of(start_ref.shape[0], 32):
        start_ref[cut, :] = normalize(feats_ref[cut, :].astype(f32))
    copies[2].wait()
    copies[3].wait()
    out_copy.wait()


def build_kernel(
    blocks_hbm,
    count_ref,
    src_ref,
    dst_ref,
    noise_hbm,
    start_ref,
    own_hbm,
    ghost_ref,
    own_train_ref,
    noise_train_ref,
    part_ref,
    flag_ref,
    own_rest_ref,
    ghost_rest_ref,
    noise_ref,
    low_ref,
    high_ref,
    spot_ref,
    sums_ref,
    rest_ref,
    own_ref,
    blocks_ref,
    sems,
):
    train = own_train_ref.shape[0]
    copies = fetch(
        (
            (blocks_hbm, blocks_ref),
            (noise_hbm.at[0, 0, 0], noise_ref),
            (noise_hbm.at[1, 0, 0, :train], noise_train_ref),
        ),
        sems,
    )
    nodes, cols = sums_ref.shape
    pieces = -(-cols // LOW)
    tiles, slots = src_ref.shape
    own_ref[...] = jnp.zeros_like(own_ref)
    ghost_ref[...] = jnp.zeros_like(ghost_ref)
    count = count_ref[0, 0]

    def sixteen(values):
        wide = jnp.broadcast_to(values.astype(f32)[:, None, :], (tiles, 16, slots))
        return wide.reshape(tiles * 16, slots).astype(bf16)

    src = src_ref[...]
    dst = dst_ref[...]
    tile_ids = lax.broadcasted_iota(jnp.int32, (tiles, slots), 0)
    high_ref[...] = sixteen(src // LOW)
    spot_ref[...] = sixteen(jnp.where((dst < BLOCK) & (tile_ids < count), dst, -1))
    low = (src % LOW - LOW // 2).astype(f32).T
    for tile in range(tiles):
        low_ref[tile] = jnp.broadcast_to(low[:, tile : tile + 1], (slots, 128)).astype(bf16)
    ids = lax.broadcasted_iota(jnp.int32, (BLOCK, slots), 0).astype(f32).astype(bf16)
    lanes = lax.broadcasted_iota(jnp.int32, (slots, 128), 1).astype(f32)
    lanes = [(lanes + first).astype(bf16) for first in range(-LOW // 2, LOW // 2, 128)]
    one = jnp.ones((), bf16)
    zero = jnp.zeros((), bf16)

    def counts(tile):
        rows = pl.ds(pl.multiple_of(tile * 16, 16), 16)
        high, spot = high_ref[rows, :], spot_ref[rows, :]
        tall = jnp.concatenate([spot] * (BLOCK // 16), 0)
        spot_one = jnp.where(ids == tall, one, zero)
        spots = []
        for piece in range(pieces):
            here = jnp.where(high == piece, one, zero)
            hot = spot_one * jnp.concatenate([here] * (BLOCK // 16), 0)
            spots.append(hot.astype(f8))
        low = low_ref[tile]
        low_hot = [jnp.where(low == ids, one, zero).astype(f8) for ids in lanes]
        return dot(jnp.concatenate(spots, 0), jnp.concatenate(low_hot, 1))

    def turn(add, step, carry):
        first = step * GROUP
        outs = [counts(first + inner) for inner in range(GROUP)]
        for inner, out in enumerate(outs):
            base = pl.multiple_of(blocks_ref[0, 0, first + inner] * BLOCK, BLOCK)
            for piece in range(pieces):
                add(pl.ds(base, BLOCK), piece * LOW, out[piece * BLOCK : (piece + 1) * BLOCK])
        return carry

    def add_short(rows, at, values):
        ref, at = (own_ref, at) if at < nodes else (ghost_ref, at - nodes)
        size = min(LOW, ref.shape[1] - at)
        ref[rows, at : at + size] += values[:, :size].astype(bf16)

    def add_long(rows, at, values):
        size = min(LOW, cols - at)
        sums_ref[rows, at : at + size] += values[:, :size]

    steps = (count + GROUP - 1) // GROUP
    copies[0].wait()
    lax.fori_loop(0, steps, functools.partial(turn, add_short), 0)
    top = ghost_ref[:BLOCK, :256]
    for first in range(0, nodes, BLOCK):
        for ref in (own_ref, ghost_ref):
            for at in range(0, ref.shape[1], 256):
                top = jnp.maximum(top, ref[first : first + BLOCK, at : at + 256])
    big = jnp.max(top.astype(f32)) >= 256.0
    flag_ref[...] = jnp.where(big, 1.0, 0.0) + jnp.zeros_like(flag_ref)

    @pl.when(big)
    def _():
        sums_ref[...] = jnp.zeros_like(sums_ref)
        lax.fori_loop(0, steps, functools.partial(turn, add_long), 0)
        own_ref[...] = sums_ref[:, :nodes].astype(bf16)
        ghost_ref[...] = sums_ref[:, nodes:].astype(bf16)

    own_copy = pltpu.make_async_copy(own_ref, own_hbm, sems.at[3])
    own_copy.start()
    own_train_ref[...] = own_ref[:train, :]
    for copy in copies[1:]:
        copy.wait()
    part_ref[...] = dot(own_ref[...], start_ref[...]) + noise_ref[...].astype(f32)

    @pl.when(big)
    def _():
        own_rest = (sums_ref[:, :nodes] - own_ref[...].astype(f32)).astype(bf16)
        part_ref[...] += dot(own_rest, start_ref[...])
        rest_ref[:, :nodes] = own_rest
        pltpu.sync_copy(rest_ref.at[:, :nodes], own_rest_ref)
        rest_ref[:, : cols - nodes] = (sums_ref[:, nodes:] - ghost_ref[...].astype(f32)).astype(bf16)
        pltpu.sync_copy(rest_ref.at[:, : cols - nodes], ghost_rest_ref)

    own_copy.wait()


def aggregate(flag_ref, first_ref, parts, sums_ref, rest_ref):
    rows = sums_ref.shape[0]
    for cut in blocks_of(rows, 256):
        total = sum(dot(count_ref[cut, :], table) for count_ref, _, table in parts)
        for inner in blocks_of(total.shape[0], 32):
            at = slice(cut.start + inner.start, cut.start + inner.stop)
            sums_ref[at, :] = first_ref[at, :].astype(f32) + total[inner]

    @pl.when(jnp.max(flag_ref[...]) > 0.0)
    def _():
        for count_ref, rest_hbm, table in parts:
            held = rest_ref.at[:, : count_ref.shape[1]]
            pltpu.sync_copy(rest_hbm.at[:rows], held)
            sums_ref[...] += dot(held[...], table)


def near_rows(place_ref, table_ref, each, near_ref, first):
    chips, _, width = near_ref.shape
    size = table_ref.shape[1] - each
    for chip in range(chips):
        member = 2 * chip + place_ref[0] % 2
        near_ref[chip, first : first + size, :] = table_ref[pl.ds(member, 1), each:, :].reshape(
            size, width
        )


def hop_kernel(
    flag_ref,
    part_ref,
    ghost_ref,
    rest_hbm,
    table_ref,
    rows_ref,
    old_ref,
    labels_ref,
    start_ref,
    out_hbm,
    side_ref,
    near_ref,
    sums_ref,
    rest_ref,
    turn_ref,
    pick_ref,
    staged_ref,
    sem,
):
    width = start_ref.shape[1]
    parts, each = rows_ref.shape
    table = table_ref[:, :each, :].reshape(-1, width)
    choose(rows_ref, turn_ref, pick_ref)
    aggregate(flag_ref, part_ref, ((ghost_ref, rest_hbm, table),), sums_ref, rest_ref)
    for cut in blocks_of(start_ref.shape[0], 32):
        start_ref[cut, :] = normalize(sums_ref[cut, :])
    sent = dot(pick_ref[...], start_ref[...]).astype(bf16)
    train = labels_ref.shape[1]
    for part in range(parts):
        staged_ref[part, :each] = sent[part * each : (part + 1) * each]
        staged_ref[part, each:] = start_ref[:train, :]
    out_copy = pltpu.make_async_copy(staged_ref, out_hbm, sem)
    out_copy.start()
    near_ref[...] = table_ref[:, each:, :]
    side_ref[:train, :] = old_ref[...]
    side_ref[train : 2 * train, :] = start_ref[:train, :]
    turn_ref[:1, :train] = labels_ref[...]
    side_ref[2 * train :, :128] = turn_ref[:16, :].astype(f32).astype(bf16)
    out_copy.wait()


def train_kernel(
    flag_ref,
    place_ref,
    own_ref,
    ghost_ref,
    own_rest_hbm,
    ghost_rest_hbm,
    noise_ref,
    start_ref,
    table_ref,
    *refs,
):
    near0_ref, *piece_refs = refs[: -10]
    out_hbm, side_hbm, near_hbm, sums_ref, rest_ref, turn_ref, staged_ref = refs[-10:-3]
    side_ref, near_ref, sems = refs[-3:]
    train, width = sums_ref.shape
    each = table_ref.shape[1] - train
    table = table_ref[:, :each, :].reshape(-1, width)
    parts = (
        (own_ref, own_rest_hbm, start_ref[...]),
        (ghost_ref, ghost_rest_hbm, table),
    )
    aggregate(flag_ref, noise_ref, parts, sums_ref, rest_ref)
    last = jnp.broadcast_to(normalize(sums_ref[...])[None], staged_ref.shape)
    out_copy = post(last, staged_ref, out_hbm, sems.at[0])
    length = piece_refs[0].shape[0] - 16
    groups = len(piece_refs)
    if groups > 1:
        near_rows(place_ref, near0_ref, 0, near_ref, 0)
        near_rows(place_ref, table_ref, each, near_ref, train)
        near_copy = pltpu.make_async_copy(near_ref, near_hbm, sems.at[2])
        near_copy.start()
        for shift, ref in enumerate(piece_refs):
            if shift:
                side_ref[(shift - 1) * length : shift * length, :] = ref[:length, :]
            group = lax.rem(place_ref[1] + shift, groups)
            turn_ref[pl.ds(group, 1), :] = ref[length:, :128].astype(f32)[:1]
        side_ref[(groups - 1) * length :, :128] = turn_ref[:16, :].astype(bf16)
        side_copy = pltpu.make_async_copy(side_ref, side_hbm, sems.at[1])
        side_copy.start()
        side_copy.wait()
        near_copy.wait()
    out_copy.wait()


def last_kernel(
    flag_ref,
    token_ref,
    own_hbm,
    own_rest_hbm,
    ghost_rest_hbm,
    noise_hbm,
    weight_hbm,
    ghost_ref,
    table_ref,
    start_ref,
    out_hbm,
    weight_ref,
    own_ref,
    noise_ref,
    sums_ref,
    rest_ref,
    out_ref,
    sems,
):
    copies = fetch(
        (
            (own_hbm, own_ref),
            (noise_hbm.at[1, 0, 0], noise_ref),
            (weight_hbm, weight_ref),
        ),
        sems,
    )
    width = out_ref.shape[-1]
    ghosts = ghost_ref.shape[1]
    table = table_ref[:, : ghosts // table_ref.shape[0], :].reshape(ghosts, width)
    out_ref[0, 0, 0] = start_ref[...]
    copies[0].wait()
    copies[1].wait()
    parts = (
        (own_ref, own_rest_hbm, start_ref[...]),
        (ghost_ref, ghost_rest_hbm, table),
    )
    aggregate(flag_ref, noise_ref, parts, sums_ref, rest_ref)
    for cut in blocks_of(sums_ref.shape[0], 32):
        out_ref[1, 0, 0, cut, :] = normalize(sums_ref[cut, :])
    out_copy = pltpu.make_async_copy(out_ref, out_hbm, sems.at[3])
    out_copy.start()
    copies[2].wait()
    out_copy.wait()


def shares(ref, first, share):
    return ref[:, pl.ds(pl.multiple_of(first, 128), share)].astype(f32)


def lanes_sum(values):
    total = None
    for piece in range(values.shape[1] // 128):
        part = values[:, piece * 128 : (piece + 1) * 128].astype(f32)
        total = part * part if total is None else total + part * part
    return total


def classify_kernel(
    many,
    place_ref,
    label_ref,
    zero_ref,
    one_ref,
    two_ref,
    side_refs,
    w_first_hbm,
    w_second_hbm,
    w_third_hbm,
    n_first_hbm,
    n_second_hbm,
    n_third_hbm,
    g_first_ref,
    g_second_ref,
    g_third_ref,
    send_ref,
    side_hbm,
    near_hbm,
    near_ref,
    w_first_ref,
    w_second_ref,
    w_third_ref,
    n_first_ref,
    n_second_ref,
    n_third_ref,
    in_ref,
    w_third_pad_ref,
    turn_ref,
    column_ref,
    h_one_ref,
    h_two_ref,
    slope_one_ref,
    slope_two_ref,
    d_one_ref,
    d_two_ref,
    d_three_ref,
    sems,
):
    classes = w_third_ref.shape[0]
    hid = w_second_ref.shape[0]
    width = two_ref.shape[2]
    wide = w_third_pad_ref.shape[0]
    train = two_ref.shape[1]
    scale = noise_mult * clip_bound
    place = place_ref[0]
    pairs = (
        (w_first_hbm, w_first_ref),
        (w_second_hbm, w_second_ref),
        (w_third_hbm, w_third_ref),
        (n_first_hbm, n_first_ref),
        (n_second_hbm, n_second_ref),
        (n_third_hbm, n_third_ref),
    )

    def set_noise():
        g_first_ref[...] = scale * n_first_ref[...]
        g_second_ref[...] = scale * n_second_ref[...]
        g_third_ref[...] = scale * n_third_ref[...]

    def pad():
        w_third_pad_ref[...] = jnp.zeros_like(w_third_pad_ref)
        w_third_pad_ref[:classes, :] = w_third_ref[...]

    def column(row, turned, lane):
        column_ref[row : row + train, :] = jnp.broadcast_to(
            turned[:train, lane : lane + 1], (train, 128)
        ).astype(jnp.int32)

    if many:

        @pl.when(pl.program_id(0) == 0)
        def _():
            for copy in fetch(pairs, sems):
                copy.wait()
            set_noise()
            pad()

        groups = label_ref.shape[0]
        turn_ref[:groups, :train] = label_ref[...].astype(f32)
        turned = turn_ref[...].T
        for group in range(groups):
            column(group * train, turned, group)
        for hop, ref in enumerate((zero_ref, one_ref)):
            in_ref[:, hop * width : (hop + 1) * width] = ref[...].reshape(-1, width)
    else:
        chips = len(side_refs)
        copies = fetch(((side_hbm, side_refs[0]), (near_hbm, near_ref)) + pairs[1:], sems)
        groups = two_ref.shape[0] // chips
        rows = groups * train
        for shift, ref in [*enumerate(side_refs)][::-1]:
            if shift == 0:
                copies[0].wait()
            part = lax.rem(place // 2 - shift + chips, chips)
            at = pl.multiple_of(part * rows, rows)
            for after in range(1, groups):
                row = at + lax.rem(place_ref[1] + after, groups) * train
                for hop in range(2):
                    first = (2 * (after - 1) + hop) * train
                    in_ref[
                        pl.ds(pl.multiple_of(row, train), train), hop * width : (hop + 1) * width
                    ] = ref[first : first + train, :]
            turn_ref[pl.ds(pl.multiple_of(part * 16, 16), 16), :] = ref[2 * (rows - train) :, :128].astype(f32)
        copies[1].wait()
        for chip in range(chips):
            row = pl.multiple_of(chip * rows + place_ref[1] * train, train)
            for hop in range(2):
                in_ref[pl.ds(row, train), hop * width : (hop + 1) * width] = near_ref[
                    chip, hop * train : (hop + 1) * train, :
                ]
        turned = turn_ref[...].T
        for part in range(chips):
            for group in range(groups):
                column((part * groups + group) * train, turned, part * 16 + group)
    in_ref[:, 2 * width :] = two_ref[...].reshape(-1, width)

    def activate(values, at, cols, h_ref, slope_ref):
        sigma = 0.5 + 0.5 * jnp.tanh(0.5 * values)
        out = values * sigma
        slope_ref[at, cols] = sigma + out * (1.0 - sigma)
        h_ref[at, cols] = out.astype(bf16)
        return lanes_sum(out)

    def back(values, at, cols, slope_ref, d_ref):
        out = values * slope_ref[at, cols]
        d_ref[at, cols] = out.astype(bf16)
        return lanes_sum(out)

    def layer(product, finish, *refs):
        sums = []
        values = product(cuts[0])
        for at, cut in enumerate(cuts):
            ahead = product(cuts[at + 1]) if at + 1 < len(cuts) else None
            for rows in blocks_of(values.shape[0], 32):
                here = slice(cut.start + rows.start, cut.start + rows.stop)
                sums.append(
                    sum(
                        finish(values[rows, cols], here, cols, *refs)
                        for cols in blocks_of(values.shape[1], 256)
                    )
                )
            values = ahead
        return jnp.concatenate(sums, 0)

    step = min(512, in_ref.shape[0])
    cuts = [slice(at, at + step) for at in range(0, in_ref.shape[0], step)]
    sq_in = jnp.concatenate([lanes_sum(in_ref[at, :]) for at in blocks_of(in_ref.shape[0], 32)], 0)
    sq_one = layer(
        lambda cut: dot(in_ref[cut, :], w_first_ref[...]), activate, h_one_ref, slope_one_ref
    )
    if not many:
        copies[2].wait()
    sq_two = layer(
        lambda cut: dot(h_one_ref[cut, :], w_second_ref[...]), activate, h_two_ref, slope_two_ref
    )
    if not many:
        copies[3].wait()
        pad()
    logits = dot_nt(h_two_ref[...], w_third_pad_ref[...])
    sums = []
    for at in blocks_of(logits.shape[0], 32):
        ids = lax.broadcasted_iota(jnp.int32, (at.stop - at.start, wide), 1)
        expo = jnp.where(ids < classes, jnp.exp(logits[at]), 0.0)
        probs = expo / jnp.sum(expo, -1, keepdims=True)
        label = column_ref[at, :1]
        d_three = (probs - jnp.where(ids == label, 1.0, 0.0)).astype(bf16)
        d_three_ref[at, :] = d_three
        sums.append(lanes_sum(d_three))
    sq_dthree = jnp.concatenate(sums, 0)
    sq_dtwo = layer(
        lambda cut: dot(d_three_ref[cut, :], w_third_pad_ref[...]), back, slope_two_ref, d_two_ref
    )
    sq_done = layer(
        lambda cut: dot_nt(d_two_ref[cut, :], w_second_ref[...]), back, slope_one_ref, d_one_ref
    )

    def total(values):
        return jnp.sum(values, -1, keepdims=True)

    norm = jnp.sqrt(
        total(sq_in) * total(sq_done)
        + total(sq_one) * total(sq_dtwo)
        + total(sq_two) * total(sq_dthree)
    )
    factor = clip_bound / jnp.maximum(norm, clip_bound)

    if not many:
        for copy in copies[4:]:
            copy.wait()
        set_noise()
    share_one, share = g_first_ref.shape[0], g_second_ref.shape[0]
    places = [place] if many else [place, place + 1 - 2 * (place % 2)]

    def left(ref, share):
        if share % 128 == 0:
            picked = [shares(ref, at * share, share) for at in places]
            return (jnp.concatenate(picked, 1) * factor).astype(bf16)
        length, count = ref.shape[1], share * len(places)
        most = 128 - math.gcd(count, 128)
        size = min(length, -(-(count + most) // 128) * 128)
        first = [at * share for at in places]
        least = functools.reduce(jnp.minimum, first)
        start = jnp.minimum(least // 128 * 128, length - size)
        rows = lax.broadcasted_iota(jnp.int32, (size, count), 0)
        cols = lax.broadcasted_iota(jnp.int32, (size, count), 1)
        wanted = cols + (first[0] - start)
        for at, other in enumerate(first[1:], 1):
            wanted = jnp.where(cols >= at * share, cols - at * share + (other - start), wanted)
        window = ref[:, pl.ds(pl.multiple_of(start, 128), size)]
        picked = dot(window, jnp.where(rows == wanted, 1.0, 0.0).astype(bf16))
        return (picked * factor).astype(bf16)

    sum_one = dot_tn(left(in_ref, share_one), d_one_ref[...])
    sum_two = dot_tn(left(h_one_ref, share), d_two_ref[...])
    sum_three = dot_tn(d_three_ref[...], left(h_two_ref, share))
    g_first_ref[...] += sum_one[:share_one]
    g_second_ref[...] += sum_two[:share]
    g_third_ref[...] += sum_three[:classes, :share]
    if not many:
        send_ref[:share_one, :] = sum_one[share_one:].astype(bf16)
        send_ref[share_one : share_one + share, :] = sum_two[share:].astype(bf16)
        first = share_one + share
        for at in range(0, classes, 32):
            cols = slice(at // 32 * share, (at // 32 + 1) * share)
            send_ref[first : first + 32, cols] = sum_three[at : at + 32, share:].astype(bf16)


def finish_kernel(got_ref, one_ref, two_ref, three_ref, g_first_ref, g_second_ref, g_third_ref):
    share_one, share = one_ref.shape[0], two_ref.shape[0]
    g_first_ref[...] = one_ref[...] + got_ref[:share_one, :].astype(f32)
    g_second_ref[...] = two_ref[...] + got_ref[share_one : share_one + share, :].astype(f32)
    first = share_one + share
    classes = three_ref.shape[0]
    for at in range(0, classes, 32):
        size = min(32, classes - at)
        cols = slice(at // 32 * share, (at // 32 + 1) * share)
        got = got_ref[first : first + 32, cols].astype(f32)
        g_third_ref[at : at + size, :] = three_ref[at : at + size, :] + got[:size]


def call(kernel, mib, outs, ins, scratch):
    def shape_of(shape, dtype, space):
        if space is None or space is HBM:
            return (space or VMEM)(shape, dtype)
        return jax.ShapeDtypeStruct(shape, dtype)

    def block(space):
        return pl.BlockSpec(memory_space=VMEM if space is None else space)

    def held(value, space):
        if space is None or space is HBM:
            return pltpu.with_memory_space_constraint(value, space or VMEM)
        return value

    return pl.pallas_call(
        kernel,
        out_shape=[shape_of(*out) for out in outs],
        in_specs=[block(space) for _, space in ins],
        out_specs=[block(space) for _, _, space in outs],
        scratch_shapes=scratch,
        compiler_params=params(mib),
    )(*[held(value, space) for value, space in ins])


def local(
    axes,
    feats,
    hop_noise,
    send_rows,
    tile_block,
    tile_src,
    tile_dst,
    tile_count,
    labels,
    w_first,
    w_second,
    w_third,
    noise_first,
    noise_second,
    noise_third,
):
    nodes, width = feats.shape[2:]
    parts, each = send_rows.shape[2:]
    ghosts = parts * each
    tiles = tile_src.shape[2]
    slots = tile_src.shape[3]
    train = labels.shape[2]
    classes = w_third.shape[1]
    hid = w_second.shape[0]
    d_in = w_first.shape[0]
    cols = nodes + ghosts
    rows = send_rows.reshape(parts, each)
    turn = VMEM((128, 128), jnp.int32)
    pick = VMEM((ghosts, nodes), bf16)
    dom = axes[:-1]
    members = lax.axis_size(axes)
    few = len(axes) == 3
    copies = members // 2 if few else 1

    def every(value, *names):
        for name in names:
            value = lax.all_gather(value, name, axis=0, tiled=True)
        return value

    staged = VMEM((parts, each + train, width), bf16)
    start0, out0, own0, src, dst = call(
        first_kernel,
        16,
        [
            ((nodes, width), bf16, None),
            ((parts, each + train, width), bf16, HBM),
            ((train, width), bf16, None),
            ((tiles, slots), jnp.int32, None),
            ((tiles, slots), jnp.int32, None),
        ],
        [(feats, HBM), (send_rows, HBM), (tile_src, HBM), (tile_dst, HBM)],
        [
            VMEM((nodes, width), bf16),
            VMEM((parts, each), jnp.int32),
            turn,
            pick,
            staged,
            DMA((5,)),
        ],
    )
    table0 = lax.all_to_all(out0, dom, split_axis=0, concat_axis=0, tiled=True)
    own, ghost, own_train, noise_train, part1, flag, own_rest, ghost_rest = call(
        build_kernel,
        28,
        [
            ((nodes, nodes), bf16, HBM),
            ((nodes, ghosts), bf16, None),
            ((train, nodes), bf16, None),
            ((train, width), bf16, None),
            ((nodes, width), f32, None),
            ((8, 128), f32, None),
            ((nodes, nodes), bf16, HBM),
            ((nodes, ghosts), bf16, HBM),
        ],
        [
            (tile_block, HBM),
            (tile_count, SMEM),
            (src, None),
            (dst, None),
            (hop_noise, HBM),
            (start0, None),
        ],
        [
            VMEM((nodes, width), bf16),
            VMEM((tiles, slots, 128), bf16),
            VMEM((tiles * 16, slots), bf16),
            VMEM((tiles * 16, slots), bf16),
            VMEM((nodes, cols), f32),
            VMEM((nodes, max(nodes, ghosts)), bf16),
            VMEM((nodes, nodes), bf16),
            SMEM(tile_block.shape, jnp.int32),
            DMA((4,)),
        ],
    )
    place = lax.axis_index(dom).reshape(1).astype(jnp.int32)

    def here():
        along = 0
        for name in dom:
            along = along * lax.axis_size(name) + lax.axis_index(name)
        return along, lax.axis_index("grp")

    def train_here(flag_ref, *refs):
        train_kernel(flag_ref, here(), *refs)

    start1, out1, side, near0 = call(
        hop_kernel,
        16,
        [
            ((nodes, width), bf16, None),
            ((parts, each + train, width), bf16, HBM),
            ((2 * train + 16, width), bf16, None),
            ((parts, train, width), bf16, None),
        ],
        [
            (flag, None),
            (part1, None),
            (ghost, None),
            (ghost_rest, HBM),
            (table0, None),
            (rows, VMEM),
            (own0, None),
            (labels.reshape(1, train), VMEM),
        ],
        [VMEM((nodes, width), f32), VMEM((nodes, ghosts), bf16), turn, pick, staged, DMA(())],
    )
    table1 = lax.all_to_all(out1, dom, split_axis=0, concat_axis=0, tiled=True)
    grp = lax.axis_size("grp")

    def shifted(value, name, size, step):
        return [
            lax.ppermute(value, name, [((at + step * shift) % size, at) for at in range(size)])
            for shift in range(1, size)
        ]

    sides = [side] + (shifted(side, "grp", grp, 1) if few else [])
    side_shape = ((len(sides) - 1) * 2 * train + 16, width)
    near_shape = (parts // 2, 2 * train, width)
    last, side, near = call(
        train_here,
        12,
        [
            ((copies, train, width), bf16, HBM),
            (side_shape, bf16, HBM),
            (near_shape, bf16, HBM),
        ],
        [
            (flag, None),
            (own_train, None),
            (ghost, None),
            (own_rest, HBM),
            (ghost_rest, HBM),
            (noise_train, None),
            (start1, None),
            (table1, None),
            (near0, None),
        ]
        + [(value, None) for value in sides],
        [
            VMEM((train, width), f32),
            VMEM((train, max(nodes, ghosts)), bf16),
            VMEM((128, 128), f32),
            VMEM((copies, train, width), bf16),
            VMEM(side_shape, bf16),
            VMEM(near_shape, bf16),
            DMA((3,)),
        ],
    )
    if few:
        every2 = lax.all_to_all(last, ("chip", "grp"), split_axis=0, concat_axis=0, tiled=True)
        sides = [side] + shifted(side, "chip", parts // 2, -1)
    else:
        every0, every1, every2 = (
            every(value, axes) for value in (own0[None], start1[None, :train], last)
        )
        every_label = every(labels.reshape(1, train), axes)
    wide = (classes + 255) // 256 * 256
    hop_feats, held_first = call(
        last_kernel,
        28,
        [
            ((2, 1, 1, nodes, width), bf16, HBM),
            (w_first.shape, bf16, None),
        ],
        [
            (flag, None),
            (side, HBM),
            (own, HBM),
            (own_rest, HBM),
            (ghost_rest, HBM),
            (hop_noise, HBM),
            (w_first, HBM),
            (ghost, None),
            (table1, None),
            (start1, None),
        ],
        [
            VMEM((nodes, nodes), bf16),
            VMEM((nodes, width), bf16),
            VMEM((nodes, width), f32),
            VMEM((nodes, max(nodes, ghosts)), bf16),
            VMEM((2, 1, 1, nodes, width), bf16),
            DMA((4,)),
        ],
    )
    chunk = train * (copies if few else min(members, 32))
    groups = chunk // train
    noises = (noise_first, noise_second, noise_third.T)
    fixed = (w_first, w_second, w_third.T) + noises
    scratch = [VMEM(value.shape, value.dtype) for value in fixed]
    scratch += [
        VMEM((chunk, d_in), bf16),
        VMEM((wide, hid), bf16),
        VMEM((128, 128), f32),
        VMEM((chunk, 128), jnp.int32),
        VMEM((chunk, hid), bf16),
        VMEM((chunk, hid), bf16),
        VMEM((chunk, hid), f32),
        VMEM((chunk, hid), f32),
        VMEM((chunk, hid), bf16),
        VMEM((chunk, hid), bf16),
        VMEM((chunk, wide), bf16),
        DMA((16,)),
    ]
    if few:
        chips = parts // 2

        def classify(*refs):
            sides_in, rest = refs[:chips], refs[chips:]
            near_hbm, two_ref, first_ref, *outs = rest[:12]
            held, near_ref, *rest = rest[12:]
            classify_kernel(
                False,
                here(),
                None,
                None,
                None,
                two_ref,
                (held,) + sides_in[1:],
                first_ref,
                *outs,
                sides_in[0],
                near_hbm,
                near_ref,
                first_ref,
                *rest,
            )

        rows = noise_first.shape[0] + noise_second.shape[0] + 32
        *own_sums, other = call(
            classify,
            44,
            [(value.shape, f32, None) for value in noises] + [((rows, hid), bf16, None)],
            [(side, HBM)]
            + [(value, None) for value in sides[1:]]
            + [(near, HBM), (every2, None), (held_first, None)]
            + [(value, HBM) for value in fixed[1:]],
            [VMEM(side_shape, bf16), VMEM(near_shape, bf16)] + scratch[1:],
        )
        got = lax.ppermute(other, "core", [(0, 1), (1, 0)])
        first, second, third = call(
            finish_kernel,
            16,
            [(value.shape, f32, VMEM) for value in noises],
            [(got, None)] + [(value, None) for value in own_sums],
            [],
        )
    else:

        ins = (every_label, every0, every1, every2)

        def classify(place_ref, label_ref, zero_ref, one_ref, two_ref, *rest):
            classify_kernel(
                True,
                place_ref,
                label_ref,
                zero_ref,
                one_ref,
                two_ref,
                None,
                *rest[:9],
                None,
                None,
                None,
                None,
                *rest[9:],
            )

        def whole(value):
            return pl.BlockSpec(value.shape, lambda i: (0, 0))

        def piece(value):
            return pl.BlockSpec(
                (groups,) + value.shape[1:], lambda i: (i,) + (0,) * (value.ndim - 1)
            )

        first, second, third = pl.pallas_call(
            classify,
            grid=(members // groups,),
            out_shape=[jax.ShapeDtypeStruct(value.shape, f32) for value in noises],
            in_specs=[pl.BlockSpec(memory_space=SMEM)]
            + [piece(value) for value in ins]
            + [pl.BlockSpec(memory_space=HBM) for value in fixed],
            out_specs=[whole(value) for value in noises],
            scratch_shapes=scratch,
            compiler_params=params(56),
        )(place, *ins, *fixed)
    return (hop_feats, first, second, third.T)


def solution(mesh):
    dom, grp = mesh.shape["dom"], mesh.shape["grp"]
    names = ("dom", "grp")
    if dom * grp <= FEW and dom <= 8 and dom % 2 == 0:
        names = ("chip", "core", "grp")
        mesh = jax.sharding.Mesh(mesh.devices.reshape(dom // 2, 2, grp), names)
    doms, grps = names[:-1], "grp"
    in_specs = (
        P(doms, grps, None, None),
        P(None, doms, grps, None, None),
        P(doms, grps, None, None),
        P(doms, grps, None),
        P(doms, grps, None, None),
        P(doms, grps, None, None),
        P(doms, grps),
        P(doms, grps, None),
        P(),
        P(),
        P(),
        P(doms, None),
        P(doms, None),
        P(doms, None),
    )
    out_specs = (P(None, doms, grps, None, None), P(doms, None), P(doms, None), P(doms, None))
    return jax.shard_map(
        functools.partial(local, names),
        mesh=mesh,
        in_specs=in_specs,
        out_specs=out_specs,
        check_vma=False,
    )
```
